32 devices in a mesh: seq: 4 (over z), fsdp: 8 (over y, x, core).
Axes of the slice: x: 2, y: 2, z: 4, core: 2. Of those that a mesh axis runs over, the one named last changes fastest.
Arguments:
- inputs: bfloat16 [16, 1024, 1024], P('fsdp', 'seq'), may hold values from -6 to 6
- lengths: int32 [16], P('fsdp'), may hold values from 1 to 1024, 12288 in all
- cotangent: bfloat16 [16, 1024, 1024], P('fsdp', 'seq'), may hold values from -6 to 6
- query_weight: bfloat16 [1024, 1024], P('fsdp'), may hold values from -0.046875 to 0.046875
- key_weight: bfloat16 [1024, 1024], P('fsdp'), may hold values from -0.1875 to 0.1875
- value_weight: bfloat16 [1024, 1024], P('fsdp'), may hold values from -0.1875 to 0.1875
- output_weight: bfloat16 [1024, 1024], P('fsdp'), may hold values from -0.75 to 0.75
- up_weight: bfloat16 [4096, 1024], P('fsdp'), may hold values from -0.1875 to 0.1875
- down_weight: bfloat16 [4096, 1024], P('fsdp'), may hold values from -0.125 to 0.125
- attn_gain: float32 [1024], replicated, may hold values from 0.25 to 1.75
- ffn_gain: float32 [1024], replicated, may hold values from 0.25 to 1.75
- bias_table: float32 [32, 16], replicated, may hold values from -4 to 4
Outputs:
- layer_out: bfloat16 [16, 1024, 1024], P('fsdp', 'seq')
- input_grad: float32 [16, 1024, 1024], P('fsdp', 'seq')
- query_grad: float32 [1024, 1024], P(('seq', 'fsdp'))
- key_grad: float32 [1024, 1024], P(('seq', 'fsdp'))
- value_grad: float32 [1024, 1024], P(('seq', 'fsdp'))
- output_grad: float32 [1024, 1024], P(('seq', 'fsdp'))
- up_grad: float32 [4096, 1024], P(('seq', 'fsdp'))
- down_grad: float32 [4096, 1024], P(('seq', 'fsdp'))
- attn_gain_grad: float32 [1024], P('fsdp')
- ffn_gain_grad: float32 [1024], P('fsdp')
- bias_grad: float32 [32, 16], P('fsdp')
The draws below stay inside these ranges and needn't reach their ends.
Inputs may be any that keep to these rules, and one draw needn't show every extreme that they name: lengths of the sequences; the longest is exactly 1024, and all of them sum to 12288.
All inputs are finite; a program needn't handle non-finite values. No bound on the sum of `lengths` on one device may be relied on, other than what follows from the above.
Results may differ from the reference program's by a relative error of at most 0.014.
The reference program's roundings to bfloat16 on the way count: a program that leaves them out, or rounds other values in their place, can miss the bound.
Values may be sent and summed in bfloat16 or wider, within the bound.
A program may use at most 256 MiB of HBM per device.

```python
import math
import jax
import jax.numpy as jnp
import numpy as np
from jax import lax

D = 1024
HEADS = 16
HEAD_DIM = 64
FF = 4096
BUCKETS = 32
SLOTS = 1024
SEQS = 16


def level_of(stream_key, dims, cuts, least, top_value):
    def one(position, shards_of):
        heights = jax.random.uniform(jax.random.fold_in(jax.random.fold_in(stream_key, 6), position), (shards_of,), jnp.float32, least / len(cuts), top_value / len(cuts))
        return jnp.repeat(jnp.exp(heights), dims[position] // shards_of).reshape((-1,) + (1,) * (len(dims) - position - 1))

    loudness = one(*cuts[0])
    for cut in cuts[1:]:
        loudness = loudness * one(*cut)
    return loudness


def split_up(number_of, total, bound, slope):
    loads = [(1 << 20) // math.isqrt(standing ** slope) + 1 for standing in range(2, number_of + 1)]
    surplus, counts = total - bound - (number_of - 1), [1] * (number_of - 1)
    while surplus > 0:
        candidates = [i for i in range(number_of - 1) if counts[i] < bound]
        whole, remaining = sum([loads[i] for i in candidates]), surplus
        for i in candidates:
            extra = min(bound - counts[i], max(1, remaining * loads[i] // whole), surplus)
            counts[i] = counts[i] + extra
            surplus = surplus - extra
    return np.array([bound] + counts)


def uneven(key, count, total, bound, skew):
    if count == 2:
        one = jax.random.randint(key, (), max(1, total - bound), min(bound, total - 1) + 1)
        return jnp.stack([one, total - one])
    sizes = jnp.asarray(split_up(count, total, bound, skew), jnp.int32)
    couples = (count - 1) // 2
    giver, receiver = sizes[1:1 + 2 * couples:2], sizes[2:2 + 2 * couples:2]
    room = jnp.minimum(giver - 1, bound - receiver)
    moved = jax.random.randint(jax.random.fold_in(key, 1), (couples,), 0, 1 << 20) % (room + 1)
    sizes = sizes.at[1:1 + 2 * couples:2].set(giver - moved).at[2:2 + 2 * couples:2].set(receiver + moved)
    return sizes[jax.random.permutation(jax.random.fold_in(key, 2), count)]


def gaussian(rng, extent, deviation, limit, pieces=(), kind=jnp.bfloat16):
    entries = deviation * jax.random.normal(rng, extent, jnp.float32)
    if pieces:
        entries = entries * level_of(rng, extent, pieces, -0.22, 0.18)
    return jnp.clip(entries, -limit, limit).astype(kind)


def setup_inputs(seed: int = 0) -> dict:
    keys = jax.random.split(jax.random.key(seed), 13)
    inputs = gaussian(keys[0], (SEQS, SLOTS, D), 1.0, 6.0, ((0, 8), (1, 4)))
    lengths = uneven(keys[1], SEQS, 3 * SEQS * SLOTS // 4, SLOTS, 2).astype(jnp.int32)
    cotangent = gaussian(keys[2], (SEQS, SLOTS, D), 1.0, 6.0, ((0, 8), (1, 4)))
    query_weight = gaussian(keys[3], (HEADS * HEAD_DIM, D), (D * HEAD_DIM // 4) ** -0.5, 0.046875, ((0, 8),))
    key_weight = gaussian(keys[4], (HEADS * HEAD_DIM, D), D ** -0.5, 0.1875, ((0, 8),))
    value_weight = gaussian(keys[5], (HEADS * HEAD_DIM, D), D ** -0.5, 0.1875, ((0, 8),))
    output_weight = gaussian(keys[6], (HEADS * HEAD_DIM, D), (HEADS * HEAD_DIM // 16) ** -0.5, 0.75, ((0, 8),))
    up_weight = gaussian(keys[7], (FF, D), D ** -0.5, 0.1875, ((0, 8),))
    down_weight = gaussian(keys[8], (FF, D), (FF // 2) ** -0.5, 0.125, ((0, 8),))
    attn_gain = jnp.clip(1.0 + 0.15 * jax.random.normal(keys[9], (D,), jnp.float32), 0.25, 1.75)
    ffn_gain = jnp.clip(1.0 + 0.15 * jax.random.normal(keys[10], (D,), jnp.float32), 0.25, 1.75)
    bias_table = gaussian(keys[11], (BUCKETS, HEADS), 1.0, 4.0, (), jnp.float32)
    return {"inputs": inputs, "lengths": lengths, "cotangent": cotangent, "query_weight": query_weight, "key_weight": key_weight, "value_weight": value_weight, "output_weight": output_weight, "up_weight": up_weight, "down_weight": down_weight, "attn_gain": attn_gain, "ffn_gain": ffn_gain, "bias_table": bias_table}


NEGATIVE = -1000000000.0
EPSILON = 1e-06
HIGHEST = lax.Precision.HIGHEST
THRESHOLDS = (1, 2, 3, 4, 5, 6, 7, 8, 12, 16, 23, 32, 46, 64, 91)

@jax.custom_vjp
def low(v):
    return lax.optimization_barrier(v.astype(jnp.bfloat16)).astype(jnp.float32)

@jax.custom_vjp
def low_back(v):
    return v

def low_keep(v):
    return (low(v), None)

def low_pass(kept, grad):
    return (grad,)

def back_keep(v):
    return (v, None)

def back_low(kept, grad):
    return (low(grad),)
low.defvjp(low_keep, low_pass)
low_back.defvjp(back_keep, back_low)

def bucket_of(relative):
    distance = jnp.abs(relative)
    magnitude = jnp.zeros(relative.shape, jnp.int32)
    for threshold in THRESHOLDS:
        magnitude = magnitude + (distance >= threshold).astype(jnp.int32)
    return magnitude + jnp.where(relative > 0, BUCKETS // 2, 0).astype(jnp.int32)

def layer(sequence, length, query_weight, key_weight, value_weight, output_weight, up_weight, down_weight, attn_gain, ffn_gain, bias_table):
    positions = jnp.arange(SLOTS, dtype=jnp.int32)
    valid = positions < length
    rms_one = lax.rsqrt(lax.optimization_barrier(jnp.mean(sequence * sequence, axis=1, keepdims=True)) + EPSILON)
    normed_one = low(sequence * rms_one * attn_gain)

    def project(weight):
        product = jnp.dot(normed_one, weight.T, precision=HIGHEST)
        return low(low_back(product)).reshape(SLOTS, HEADS, HEAD_DIM)
    queries = project(query_weight)
    keys_all = project(key_weight)
    values_all = project(value_weight)
    relative = positions[None, :] - positions[:, None]
    position_bias = jnp.transpose(jnp.take(bias_table, bucket_of(relative), axis=0), (2, 0, 1))
    logits = jnp.einsum('qhd,khd->hqk', queries, keys_all, precision=HIGHEST) + position_bias
    scores = jnp.where(valid[None, None, :], low_back(logits), NEGATIVE)
    row_peak = lax.optimization_barrier(jnp.max(scores, axis=2, keepdims=True))
    exponent = jnp.exp(scores - row_peak)
    attention = low(exponent / lax.optimization_barrier(jnp.sum(exponent, axis=2, keepdims=True)))
    context = jnp.einsum('hqk,khd->qhd', attention, values_all, precision=HIGHEST).reshape(SLOTS, HEADS * HEAD_DIM)
    context = low(low_back(context))
    hidden_one = sequence + low_back(jnp.dot(context, output_weight, precision=HIGHEST))
    rms_two = lax.rsqrt(lax.optimization_barrier(jnp.mean(hidden_one * hidden_one, axis=1, keepdims=True)) + EPSILON)
    normed_two = low(hidden_one * rms_two * ffn_gain)
    before = low_back(jnp.dot(normed_two, up_weight.T, precision=HIGHEST))
    active = low(jax.nn.gelu(before, approximate=False))
    result = hidden_one + low_back(jnp.dot(active, down_weight, precision=HIGHEST))
    return jnp.where(valid[:, None], result, 0.0)

def reference(inputs, lengths, cotangent, query_weight, key_weight, value_weight, output_weight, up_weight, down_weight, attn_gain, ffn_gain, bias_table):
    params = (query_weight.astype(jnp.float32), key_weight.astype(jnp.float32), value_weight.astype(jnp.float32), output_weight.astype(jnp.float32), up_weight.astype(jnp.float32), down_weight.astype(jnp.float32), attn_gain.astype(jnp.float32), ffn_gain.astype(jnp.float32), bias_table.astype(jnp.float32))

    def one_sequence(totals, packed):
        sequence, length, incoming = packed

        def forward(sequence_in, *weights):
            return layer(sequence_in, length, *weights)
        outputs, pullback = jax.vjp(forward, sequence.astype(jnp.float32), *params)
        gradients = pullback(incoming.astype(jnp.float32))
        totals = jax.tree.map(lambda summed, update: summed + update, totals, tuple(gradients[1:]))
        return (totals, (outputs.astype(jnp.bfloat16), gradients[0]))
    initial = tuple((jnp.zeros_like(weight) for weight in params))
    totals, (layer_out, input_grad) = lax.scan(one_sequence, initial, (inputs, lengths, cotangent))
    return (layer_out, input_grad, totals[0], totals[1], totals[2], totals[3], totals[4], totals[5], totals[6], totals[7], totals[8])
```

```python
import jax
import jax.numpy as jnp
from jax import lax
from jax.experimental import pallas as pl
from jax.experimental.pallas import tpu as pltpu
from jax.sharding import PartitionSpec as P

HEADS = 16
HEAD_DIM = 64
BUCKETS = 32
NEGATIVE = -1000000000.0
EPSILON = 1e-06
THRESHOLDS = (1, 2, 3, 4, 5, 6, 7, 8, 12, 16, 23, 32, 46, 64, 91)
ROOT_HALF = 0.7071067811865476
NORMAL_PEAK = 0.3989422804014327
LANES = 128
QUERY_ROWS = 256
HALF_ROWS = QUERY_ROWS // 2
LOW = jnp.bfloat16
WIDE = jnp.float32
BOTH = ("seq", "fsdp")

NN = (((1,), (0,)), ((), ()))
NT = (((1,), (1,)), ((), ()))
TN = (((0,), (0,)), ((), ()))


def dot(left, right, dims=NN):
    return lax.dot_general(left, right, dims, preferred_element_type=WIDE)


def bucket_of(relative):
    distance = jnp.abs(relative)
    magnitude = jnp.zeros(relative.shape, jnp.int32)
    for threshold in THRESHOLDS:
        magnitude = magnitude + (distance >= threshold).astype(jnp.int32)
    return magnitude + jnp.where(relative > 0, BUCKETS // 2, 0).astype(jnp.int32)


def gelu_parts(value):
    cumulative = 0.5 * (1.0 + lax.erf(value * ROOT_HALF))
    slope = cumulative + value * jnp.exp(-0.5 * value * value) * NORMAL_PEAK
    return (value * cumulative, slope)


def near_tables(columns):
    side = jnp.arange(HALF_ROWS, dtype=jnp.int32)
    tiles = []
    for shift in (-1, 0, 1):
        buckets = bucket_of(side[None, :] - side[:, None] + HALF_ROWS * shift)
        tile = jnp.zeros((columns.shape[1],) + buckets.shape, WIDE)
        for number in range(BUCKETS):
            tile = jnp.where((buckets == number)[None], columns[number][:, None, None], tile)
        tiles.append(tile)
    flat = [jnp.broadcast_to(columns[number][:, None, None], tiles[0].shape) for number in (15, 31)]
    before, centre, after = tiles
    wide = jnp.concatenate(
        [
            jnp.concatenate([before, centre, after, flat[1]], axis=2),
            jnp.concatenate([flat[0], before, centre, after], axis=2),
        ],
        axis=1,
    )
    return (wide, jnp.swapaxes(wide, 1, 2))


def spare_lanes(length, rows):
    blocks = rows // QUERY_ROWS
    key = lax.broadcasted_iota(jnp.int32, (rows, LANES), 0)
    lane = lax.rem(lax.broadcasted_iota(jnp.int32, (rows, LANES), 1), HEAD_DIM)
    hidden = jnp.where((lane == 0) & (key >= length), NEGATIVE, 0.0)
    left = (lane >= 1) & (lane <= blocks) & (key < QUERY_ROWS * (lane - 1) - HALF_ROWS)
    start = QUERY_ROWS * (lane - 1 - blocks) + 3 * HALF_ROWS
    right = (lane > blocks) & (lane <= 2 * blocks) & (key >= start)
    return jnp.where(left | right, 1.0, hidden).astype(LOW)


def split_heads(pair, spare, out):
    low_half = lax.broadcasted_iota(jnp.int32, pair.shape, 1) < HEAD_DIM
    out[0] = jnp.where(low_half, pair, spare)
    out[1] = jnp.where(low_half, spare, pair)


def attend_kernel(
    length_ref, ends_ref, query_ref, key_ref, value_ref, near_ref, context_ref, log_ref, bias, keys, values
):
    rows = query_ref.shape[0]
    pair = pl.program_id(0)
    split_heads(key_ref[...], spare_lanes(length_ref[0], rows), keys)
    split_heads(value_ref[...], jnp.zeros((rows, LANES), LOW), values)
    near_start = rows - QUERY_ROWS - HALF_ROWS
    near_end = near_start + 2 * QUERY_ROWS
    for head in range(2):
        left, right = (ends_ref[2 * pair + head, 0], ends_ref[2 * pair + head, 1])
        bias[head, :, :near_start] = jnp.full((QUERY_ROWS, near_start), left, WIDE)
        bias[head, :, near_start:near_end] = near_ref[head]
        bias[head, :, near_end:] = jnp.full((QUERY_ROWS, bias.shape[2] - near_end), right, WIDE)
    lane = lax.broadcasted_iota(jnp.int32, (QUERY_ROWS, LANES), 1)
    ones = jnp.where(lax.rem(lane, HEAD_DIM) == 0, 1.0, 0.0).astype(LOW)

    def block(number, carry):
        start = pl.multiple_of(number * QUERY_ROWS, QUERY_ROWS)
        offset = pl.multiple_of(rows - QUERY_ROWS - number * QUERY_ROWS, LANES)
        both = query_ref[pl.ds(start, QUERY_ROWS), :]
        total = jnp.zeros((QUERY_ROWS, LANES), WIDE)
        for head in range(2):
            mine = lane < HEAD_DIM if head == 0 else lane >= HEAD_DIM
            logits = dot(jnp.where(mine, both, ones), keys[head], NT)
            logits = logits + bias[head, :, pl.ds(offset, rows)]
            peak = jnp.max(logits, axis=1, keepdims=True)
            exponent = jnp.exp(logits - peak)
            row_sum = jnp.sum(exponent, axis=1, keepdims=True)
            weights_low = (exponent * (1.0 / row_sum)).astype(LOW)
            total = total + dot(weights_low, values[head])
            logs = jnp.broadcast_to(peak + jnp.log(row_sum), (QUERY_ROWS, LANES))
            log_ref[0, head : head + 1, pl.ds(start, QUERY_ROWS)] = logs.T[0:1, :]
        context_ref[pl.ds(start, QUERY_ROWS), :] = total.astype(LOW)
        return carry

    lax.fori_loop(0, rows // QUERY_ROWS, block, 0)


def attend(length, ends, query, key, value, near):
    rows, width = query.shape
    pairs = width // LANES
    smem = pl.BlockSpec(memory_space=pltpu.SMEM)
    columns = pl.BlockSpec((rows, LANES), lambda pair: (0, pair))
    return pl.pallas_call(
        attend_kernel,
        grid=(pairs,),
        in_specs=[smem, smem, columns, columns, columns]
        + [pl.BlockSpec((2, QUERY_ROWS, 2 * QUERY_ROWS), lambda pair: (pair, 0, 0))],
        out_specs=[columns, pl.BlockSpec((1, 2, rows), lambda pair: (pair, 0, 0))],
        out_shape=[
            jax.ShapeDtypeStruct((rows, width), LOW),
            jax.ShapeDtypeStruct((pairs, 2, rows), WIDE),
        ],
        scratch_shapes=[
            pltpu.VMEM((2, QUERY_ROWS, 2 * rows - QUERY_ROWS), WIDE),
            pltpu.VMEM((2, rows, LANES), LOW),
            pltpu.VMEM((2, rows, LANES), LOW),
        ],
        compiler_params=pltpu.CompilerParams(vmem_limit_bytes=40 << 20),
        cost_estimate=pl.CostEstimate(
            flops=24 * rows * rows * width, bytes_accessed=8 * rows * width, transcendentals=2 * pairs * rows * rows
        ),
        name="attend",
    )(length, ends, query, key, value, near)


def attend_grad_kernel(
    length_ref,
    ends_ref,
    query_ref,
    key_ref,
    value_ref,
    grad_ref,
    log_ref,
    near_ref,
    query_grad_ref,
    key_grad_ref,
    value_grad_ref,
    tiles_ref,
    far_ref,
    bias,
    keys,
    values,
    padded,
    key_total,
    value_total,
):
    rows = query_ref.shape[0]
    blocks = rows // QUERY_ROWS
    pair = pl.program_id(0)
    split_heads(key_ref[...], spare_lanes(length_ref[0], rows), keys)
    split_heads(value_ref[...], jnp.zeros((rows, LANES), LOW), values)
    near_start = rows - QUERY_ROWS - HALF_ROWS
    near_end = near_start + 2 * QUERY_ROWS
    for head in range(2):
        left, right = (ends_ref[2 * pair + head, 0], ends_ref[2 * pair + head, 1])
        bias[head, :near_start, :] = jnp.full((near_start, QUERY_ROWS), left, WIDE)
        bias[head, near_start:near_end, :] = near_ref[head]
        bias[head, near_end:, :] = jnp.full((bias.shape[1] - near_end, QUERY_ROWS), right, WIDE)
        padded[head, :HALF_ROWS, :] = jnp.zeros((HALF_ROWS, QUERY_ROWS), LOW)
        padded[head, rows + HALF_ROWS :, :] = jnp.zeros((HALF_ROWS, QUERY_ROWS), LOW)
    key_total[...] = jnp.zeros_like(key_total)
    value_total[...] = jnp.zeros_like(value_total)
    tiles_ref[...] = jnp.zeros_like(tiles_ref)
    lane = lax.broadcasted_iota(jnp.int32, (QUERY_ROWS, LANES), 1)
    ones = jnp.where(lax.rem(lane, HEAD_DIM) == 0, 1.0, 0.0).astype(LOW)
    zero = jnp.zeros((), LOW)

    def block(number, carry):
        start = pl.multiple_of(number * QUERY_ROWS, QUERY_ROWS)
        offset = pl.multiple_of(rows - QUERY_ROWS - number * QUERY_ROWS, LANES)
        both = query_ref[pl.ds(start, QUERY_ROWS), :]
        grad = grad_ref[pl.ds(start, QUERY_ROWS), :]
        parts = []
        for head in range(2):
            mine = lane < HEAD_DIM if head == 0 else lane >= HEAD_DIM
            logits = dot(keys[head], jnp.where(mine, both, ones), NT)
            logits = logits + bias[head, pl.ds(offset, rows), :]
            probs = jnp.exp(logits - log_ref[0, head : head + 1, pl.ds(start, QUERY_ROWS)])
            prob_grad = dot(values[head], grad, NT)
            weighted = probs * prob_grad
            inner = jnp.sum(weighted, axis=0, keepdims=True)
            score = (weighted - probs * inner).astype(LOW)
            value_total[...] += dot(probs.astype(LOW), jnp.where(mine, grad, zero))
            key_total[...] += dot(score, jnp.where(mine, both, zero))
            padded[head, HALF_ROWS : HALF_ROWS + rows, :] = score
            part = dot(score, keys[head], TN)
            parts.append(part)
            far_ref[0, head, pl.ds(number, 1), :] = jnp.sum(part, axis=0, keepdims=True)
            close = padded[head, pl.ds(start, 2 * QUERY_ROWS), :].astype(WIDE)
            quarter = [close[HALF_ROWS * step : HALF_ROWS * (step + 1)] for step in range(4)]
            for step in range(3):
                tiles_ref[head, step] += quarter[step][:, :HALF_ROWS] + quarter[step + 1][:, HALF_ROWS:]
            corner = jnp.sum(quarter[0][:, HALF_ROWS:], axis=0, keepdims=True)
            far_ref[0, head, pl.ds(blocks + number, 1), :] = corner
            corner = jnp.sum(quarter[3][:, :HALF_ROWS], axis=0, keepdims=True)
            far_ref[0, head, pl.ds(2 * blocks + number, 1), :] = corner
        chosen = jnp.where(lane < HEAD_DIM, parts[0], parts[1])
        query_grad_ref[pl.ds(start, QUERY_ROWS), :] = chosen.astype(LOW)
        return carry

    lax.fori_loop(0, blocks, block, 0)
    key_grad_ref[...] = key_total[...].astype(LOW)
    value_grad_ref[...] = value_total[...].astype(LOW)


def attend_grad(length, ends, query, key, value, grad, logs, near):
    rows, width = query.shape
    pairs = width // LANES
    blocks = rows // QUERY_ROWS
    smem = pl.BlockSpec(memory_space=pltpu.SMEM)
    columns = pl.BlockSpec((rows, LANES), lambda pair: (0, pair))
    shape = jax.ShapeDtypeStruct
    return pl.pallas_call(
        attend_grad_kernel,
        grid=(pairs,),
        in_specs=[smem, smem, columns, columns, columns, columns]
        + [pl.BlockSpec((1, 2, rows), lambda pair: (pair, 0, 0))]
        + [pl.BlockSpec((2, 2 * QUERY_ROWS, QUERY_ROWS), lambda pair: (pair, 0, 0))],
        out_specs=[columns, columns, columns]
        + [pl.BlockSpec((2, 3, HALF_ROWS, HALF_ROWS), lambda pair: (pair, 0, 0, 0))]
        + [pl.BlockSpec((1, 2, 3 * blocks, LANES), lambda pair: (pair, 0, 0, 0))],
        out_shape=[shape((rows, width), LOW)] * 3
        + [shape((2 * pairs, 3, HALF_ROWS, HALF_ROWS), WIDE), shape((pairs, 2, 3 * blocks, LANES), WIDE)],
        scratch_shapes=[
            pltpu.VMEM((2, 2 * rows - QUERY_ROWS, QUERY_ROWS), WIDE),
            pltpu.VMEM((2, rows, LANES), LOW),
            pltpu.VMEM((2, rows, LANES), LOW),
            pltpu.VMEM((2, rows + QUERY_ROWS, QUERY_ROWS), LOW),
            pltpu.VMEM((rows, LANES), WIDE),
            pltpu.VMEM((rows, LANES), WIDE),
        ],
        compiler_params=pltpu.CompilerParams(vmem_limit_bytes=48 << 20),
        cost_estimate=pl.CostEstimate(
            flops=44 * rows * rows * width, bytes_accessed=14 * rows * width, transcendentals=2 * pairs * rows * rows
        ),
        name="attend_grad",
    )(length, ends, query, key, value, grad, logs, near)


def bucket_sums(tiles, far):
    heads = tiles.shape[0]
    pairs = far.shape[0]
    blocks = far.shape[2] // 3
    side = jnp.arange(HALF_ROWS, dtype=jnp.int32)
    relative = jnp.stack([side[:, None] - side[None, :] + HALF_ROWS * shift for shift in (-1, 0, 1)])
    buckets = bucket_of(relative)
    sums = jnp.stack(
        [jnp.sum(jnp.where((buckets == number)[None], tiles, 0.0), axis=(1, 2, 3)) for number in range(BUCKETS)]
    )
    corners = jnp.sum(far.reshape(pairs, 2, 3, blocks, LANES)[:, :, 1:], axis=(3, 4))
    left, right = (corners[:, :, 0], corners[:, :, 1])
    for number in range(blocks):
        spare = [far[:, head, number, HEAD_DIM * (1 - head) + 1 :] for head in range(2)]
        left = left + jnp.stack([one[:, number] for one in spare], axis=1)
        right = right + jnp.stack([one[:, blocks + number] for one in spare], axis=1)
    ends = jnp.zeros((BUCKETS, heads), WIDE)
    ends = ends.at[BUCKETS // 2 - 1].set(left.reshape(heads)).at[BUCKETS - 1].set(right.reshape(heads))
    return sums + ends


def flip(value, bit):
    size = lax.axis_size("fsdp")
    return lax.ppermute(value, "fsdp", [(one, one ^ bit) for one in range(size)])


def other_core(value):
    return flip(value, 1)


def after(value, *first):
    return lax.optimization_barrier((value,) + first)[0]


def rounds_of(inverse):
    depth, size = (lax.axis_size("seq"), lax.axis_size("fsdp"))
    held = depth // 2
    rounds = []
    for step in range(held):
        pairs = []
        for place in range(depth):
            for index in range(size):
                target = (index % 2) * held + (place + step) % held
                there = target * size + index - index % 2 + place // held
                here = place * size + index
                pairs.append((there, here) if inverse else (here, there))
        rounds.append(pairs)
    return rounds


def to_sequence(blocks):
    held, span, width = blocks.shape
    place = lax.axis_index("seq")
    out = jnp.zeros((held, span, width), blocks.dtype)
    for step, pairs in enumerate(rounds_of(False)):
        sent = lax.dynamic_index_in_dim(blocks, (place + step) % held, 0, keepdims=False)
        got = lax.ppermute(sent, BOTH, pairs)
        out = lax.dynamic_update_index_in_dim(out, got, (place + held - step) % held, 0)
    return out.reshape(held * span, width)


def to_slots(rows, held):
    span, width = (rows.shape[0] // held, rows.shape[1])
    place = lax.axis_index("seq")
    blocks = rows.reshape(held, span, width)
    out = jnp.zeros(blocks.shape, rows.dtype)
    for step, pairs in enumerate(rounds_of(True)):
        sent = lax.dynamic_index_in_dim(blocks, (place + held - step) % held, 0, keepdims=False)
        got = lax.ppermute(sent, BOTH, pairs)
        out = lax.dynamic_update_index_in_dim(out, got, (place + step) % held, 0)
    return out


def whole(mine, core):
    other = other_core(mine)
    return jnp.where(
        core == 0, jnp.concatenate([mine, other], axis=0), jnp.concatenate([other, mine], axis=0)
    )


def fold(partial, core):
    half = partial.shape[0] // 2
    sent = lax.dynamic_slice_in_dim(partial, (1 - core) * half, half, 0)
    kept = lax.dynamic_slice_in_dim(partial, core * half, half, 0)
    return kept + other_core(sent)


def gather_plane(mine, first=()):
    mine = after(mine, *first)
    chip = lax.axis_index("fsdp") // 2
    half = mine.shape[0] // 2
    beside = flip(mine, 2)
    above = flip(mine, 4)
    across_one = flip(above[:half], 2)
    across_two = flip(beside[half:], 4)
    out = jnp.zeros((4,) + mine.shape, mine.dtype)
    out = lax.dynamic_update_index_in_dim(out, mine, chip, 0)
    out = lax.dynamic_update_index_in_dim(out, beside, chip ^ 1, 0)
    out = lax.dynamic_update_index_in_dim(out, above, chip ^ 2, 0)
    out = lax.dynamic_update_slice(out, across_one[None], (chip ^ 3, 0, 0))
    out = lax.dynamic_update_slice(out, across_two[None], (chip ^ 3, half, 0))
    return (out, (across_one, across_two))


def fast_plane():
    return lax.axis_size("fsdp") == 8 and lax.axis_size("seq") == 4


def own_head_rows(weight, core):
    width = weight.shape[1]
    return lax.dynamic_index_in_dim(weight.reshape(4, 2, -1, width), core, 1, keepdims=False).reshape(-1, width)


def add_low(left, right):
    return (left.astype(WIDE) + right.astype(WIDE)).astype(LOW)


def pick(value, index, axis):
    return lax.dynamic_index_in_dim(value, index, axis, keepdims=False)


def spread_depth(value):
    depth = lax.axis_size("seq")
    place = lax.axis_index("seq")
    total = pick(value, place, 0).astype(WIDE)
    for step in range(1, depth):
        sent = pick(value, (place + step) % depth, 0)
        got = lax.ppermute(sent, "seq", [(one, (one + step) % depth) for one in range(depth)])
        total = total + got.astype(WIDE)
    return total


def scatter_plane(parts, first=()):
    chip = lax.axis_index("fsdp") // 2
    x, y = (chip % 2, chip // 2)
    one, two = parts
    one_got = flip(after(pick(one, 1 - x, 2), *first), 2)
    two_got = flip(after(pick(two, 1 - y, 1), *first), 4)
    one = add_low(pick(one, x, 2), one_got)
    two = add_low(pick(two, y, 1), two_got)
    one_last = flip(pick(one, 1 - y, 1), 4)
    two_last = flip(pick(two, 1 - x, 1), 2)
    return (add_low(pick(one, y, 1), one_last), add_low(pick(two, x, 1), two_last)), (one_last, two_last)


def shards(
    inputs,
    lengths,
    cotangent,
    query_weight,
    key_weight,
    value_weight,
    output_weight,
    up_weight,
    down_weight,
    attn_gain,
    ffn_gain,
    bias_table,
):
    held, span, width = inputs.shape
    depth, size = (lax.axis_size("seq"), lax.axis_size("fsdp"))
    place, index = (lax.axis_index("seq"), lax.axis_index("fsdp"))
    core = index % 2
    rows = held * span
    inner = HEADS * HEAD_DIM
    fast = fast_plane()

    near_lengths = jnp.where(
        core == 0,
        jnp.concatenate([lengths, other_core(lengths)]),
        jnp.concatenate([other_core(lengths), lengths]),
    )
    length = lax.dynamic_slice_in_dim(near_lengths, place, 1, 0)
    slots = core * rows + jnp.arange(rows, dtype=jnp.int32)
    mask_rows = (slots < length[0])[:, None].astype(WIDE)

    own_table = lax.dynamic_index_in_dim(bias_table.reshape(BUCKETS, 4, 2, 2), core, 2, keepdims=False)
    own_table = own_table.reshape(BUCKETS, HEADS // 2)
    near, near_turned = near_tables(own_table)
    ends = jnp.stack([own_table[BUCKETS // 2 - 1], own_table[BUCKETS - 1]], axis=1)

    ffn = up_weight.shape[0]
    if fast:
        stacked = jnp.concatenate([query_weight, key_weight, value_weight], axis=0)
        heads_low, done = gather_plane(stacked)
        heads_low = heads_low.reshape(4, 3, -1, width)
        own_three = [heads_low[:, number].reshape(-1, width) for number in range(3)]
        own_output, done = gather_plane(output_weight, done)
        own_output = own_output.reshape(-1, width)
        far_output = other_core(own_output)
        cut = jnp.stack([up_weight, down_weight]).reshape(2, 2, 2, -1, width)
        swapped = other_core(pick(cut, 1 - core, 2))
        kept = pick(cut, core, 2)
        cut = jnp.where(
            core == 0, jnp.stack([kept, swapped], axis=1), jnp.stack([swapped, kept], axis=1)
        )
        own_up, done = gather_plane(cut[0].reshape(-1, width), done)
        own_down, done = gather_plane(cut[1].reshape(-1, width), done)
        own_up = own_up.reshape(-1, width)
        own_down = own_down.reshape(-1, width)
    else:
        own_three = [
            own_head_rows(lax.all_gather(one, "fsdp", axis=0, tiled=True), core)
            for one in (query_weight, key_weight, value_weight)
        ]
        full = lax.all_gather(output_weight, "fsdp", axis=0, tiled=True)
        own_output = own_head_rows(full, core)
        far_output = own_head_rows(full, 1 - core)
        own_up, own_down = (
            pick(
                lax.all_gather(one, "fsdp", axis=0, tiled=True).reshape(depth, size // 2, 2, -1, width), core, 2
            ).reshape(-1, width)
            for one in (up_weight, down_weight)
        )

    source_low = to_sequence(inputs)
    source = source_low.astype(WIDE)
    rms_one = lax.rsqrt(jnp.mean(source * source, axis=1, keepdims=True) + EPSILON)
    scaled_one = source * rms_one
    normed_one = whole((scaled_one * attn_gain).astype(LOW), core)
    query, key, value = [dot(normed_one, one, NT).astype(LOW) for one in own_three]
    context, logs = attend(length, ends, query, key, value, near)
    near_context = lax.dynamic_slice_in_dim(context, core * rows, rows, 0)
    far_context = other_core(lax.dynamic_slice_in_dim(context, (1 - core) * rows, rows, 0))
    hidden_one = source + (dot(near_context, own_output) + dot(far_context, far_output))
    rms_two = lax.rsqrt(jnp.mean(hidden_one * hidden_one, axis=1, keepdims=True) + EPSILON)
    scaled_two = hidden_one * rms_two
    normed_two = whole((scaled_two * ffn_gain).astype(LOW), core)
    grad_out = to_sequence(cotangent).astype(WIDE) * mask_rows
    grad_low = whole(grad_out.astype(LOW), core)
    active, slope = gelu_parts(dot(normed_two, own_up, NT))
    active = active.astype(LOW)
    mlp_out = fold(dot(active, own_down), core)
    layer_rows = ((hidden_one + mlp_out) * mask_rows).astype(LOW)
    layer_out = to_slots(layer_rows, held)

    pre_grad = (dot(grad_low, own_down, NT) * slope).astype(LOW)
    normed_grad = fold(dot(pre_grad, own_up), core)
    up_part = dot(pre_grad, normed_two, TN).astype(LOW)
    down_part = dot(active, grad_low, TN).astype(LOW)
    gained_two = ffn_gain * normed_grad
    hidden_grad = grad_out + rms_two * (
        gained_two - scaled_two * jnp.mean(gained_two * scaled_two, axis=1, keepdims=True)
    )
    ffn_gain_part = jnp.sum(normed_grad * scaled_two, axis=0)
    hidden_low = hidden_grad.astype(LOW)
    near_grad = dot(hidden_low, own_output, NT).astype(LOW)
    far_grad = other_core(dot(hidden_low, far_output, NT).astype(LOW))
    context_grad = jnp.where(
        core == 0,
        jnp.concatenate([near_grad, far_grad], axis=0),
        jnp.concatenate([far_grad, near_grad], axis=0),
    )
    near_output_part = dot(near_context, hidden_low, TN).astype(LOW)
    far_output_part = dot(far_context, hidden_low, TN).astype(LOW)

    query_low, key_low, value_low, tiles, far = attend_grad(
        length, ends, query, key, value, context_grad, logs, near_turned
    )
    lows = (query_low, key_low, value_low)
    normed_one_grad = dot(query_low, own_three[0]) + dot(key_low, own_three[1]) + dot(value_low, own_three[2])
    normed_one_grad = fold(normed_one_grad, core)
    three_parts = [dot(one, normed_one, TN).astype(LOW) for one in lows]
    gained_one = attn_gain * normed_one_grad
    input_grad = hidden_grad + rms_one * (
        gained_one - scaled_one * jnp.mean(gained_one * scaled_one, axis=1, keepdims=True)
    )
    attn_gain_part = jnp.sum(normed_one_grad * scaled_one, axis=0)
    input_grad = to_slots(input_grad.astype(LOW), held).astype(WIDE)

    if fast:
        blocks = (depth, 2, 2, -1, width)
        (up_some, down_some), done = scatter_plane((up_part.reshape(blocks), down_part.reshape(blocks)))
        up_grad, down_grad = (spread_depth(up_some), spread_depth(down_some))

        def to_parity(kept, sent):
            return jnp.where(
                core == 0, jnp.stack([kept, sent], axis=1), jnp.stack([sent, kept], axis=1)
            )

        three = jnp.stack(three_parts).reshape(3, 4, 2, 2, -1, width)
        three_got = other_core(pick(three, 1 - core, 3))
        three_kept = pick(three, core, 3)
        outs = [to_parity(three_kept[number], three_got[number]) for number in range(3)]
        near_part = near_output_part.reshape(4, 2, 2, -1, width)
        far_part = far_output_part.reshape(4, 2, 2, -1, width)
        got = other_core(jnp.stack([pick(far_part, 1 - core, 2), pick(near_part, 1 - core, 2)]))
        outs.append(
            to_parity(add_low(pick(near_part, core, 2), got[0]), add_low(pick(far_part, core, 2), got[1]))
        )
        one = jnp.concatenate(outs[:2], axis=3)
        two = jnp.concatenate(outs[2:], axis=3)
        (one, two), done = scatter_plane((one, two), done)
        attention = spread_depth(jnp.concatenate([one, two], axis=1))
        attention = attention.reshape(4, -1, width)
        query_grad, key_grad, value_grad, output_grad = [attention[number] for number in range(4)]
    else:

        def summed(value):
            return lax.psum_scatter(value, BOTH, scatter_dimension=0, tiled=True).astype(WIDE)

        def own_only(value, shape):
            blank = jnp.zeros_like(value)
            pair = jnp.where(core == 0, jnp.stack([value, blank], axis=1), jnp.stack([blank, value], axis=1))
            return pair.reshape(-1, width)

        up_grad, down_grad = [
            summed(own_only(one.reshape(depth * (size // 2), -1, width), None)) for one in (up_part, down_part)
        ]
        query_grad, key_grad, value_grad = [summed(own_only(one.reshape(4, -1, width), None)) for one in three_parts]
        near_part, far_part = (near_output_part.reshape(4, -1, width), far_output_part.reshape(4, -1, width))
        pair = jnp.where(
            core == 0, jnp.stack([near_part, far_part], axis=1), jnp.stack([far_part, near_part], axis=1)
        )
        output_grad = summed(pair.reshape(-1, width))

    bias_own = bucket_sums(tiles, far).reshape(BUCKETS, 4, 1, 2)
    bias_full = lax.dynamic_update_slice(
        jnp.zeros((BUCKETS, 4, 2, 2), WIDE), bias_own, (0, 0, core, 0)
    ).reshape(BUCKETS, HEADS)
    attn_gain_sum, ffn_gain_sum, bias_sum = lax.psum((attn_gain_part, ffn_gain_part, bias_full), BOTH)
    gain_rows = width // size
    bucket_rows = BUCKETS // size
    attn_gain_grad = lax.dynamic_slice_in_dim(attn_gain_sum, index * gain_rows, gain_rows, 0)
    ffn_gain_grad = lax.dynamic_slice_in_dim(ffn_gain_sum, index * gain_rows, gain_rows, 0)
    bias_grad = lax.dynamic_slice_in_dim(bias_sum, index * bucket_rows, bucket_rows, 0)
    return (
        layer_out,
        input_grad,
        query_grad,
        key_grad,
        value_grad,
        output_grad,
        up_grad,
        down_grad,
        attn_gain_grad,
        ffn_gain_grad,
        bias_grad,
    )


def solution(mesh):
    placed = (
        P("fsdp", "seq", None),
        P("fsdp"),
        P("fsdp", "seq", None),
        P("fsdp", None),
        P("fsdp", None),
        P("fsdp", None),
        P("fsdp", None),
        P("fsdp", None),
        P("fsdp", None),
        P(),
        P(),
        P(),
    )
    return jax.shard_map(
        shards,
        mesh=mesh,
        in_specs=placed,
        out_specs=(
            P("fsdp", "seq", None),
            P("fsdp", "seq", None),
            P(("seq", "fsdp"), None),
            P(("seq", "fsdp"), None),
            P(("seq", "fsdp"), None),
            P(("seq", "fsdp"), None),
            P(("seq", "fsdp"), None),
            P(("seq", "fsdp"), None),
            P("fsdp"),
            P("fsdp"),
            P("fsdp", None),
        ),
        check_vma=False,
    )
```

```python
import functools

import jax
import jax.numpy as jnp
import numpy as np
from jax import lax
from jax.experimental import pallas as pl
from jax.experimental.pallas import tpu as pltpu
from jax.sharding import PartitionSpec as P

HEADS = 16
HEAD_DIM = 64
BUCKETS = 32
NEGATIVE = -1000000000.0
EPSILON = 1e-06
THRESHOLDS = (1, 2, 3, 4, 5, 6, 7, 8, 12, 16, 23, 32, 46, 64, 91)
ROOT_HALF = 0.7071067811865476
NORMAL_PEAK = 0.3989422804014327
LANES = 128
QUERY_ROWS = 256
HALF_ROWS = QUERY_ROWS // 2
LOW = jnp.bfloat16
WIDE = jnp.float32
BOTH = ("seq", "fsdp")

NN = (((1,), (0,)), ((), ()))
NT = (((1,), (1,)), ((), ()))
TN = (((0,), (0,)), ((), ()))


def dot(left, right, dims=NN):
    return lax.dot_general(left, right, dims, preferred_element_type=WIDE)


def gelu_parts(value):
    cumulative = 0.5 * (1.0 + lax.erf(value * ROOT_HALF))
    slope = cumulative + value * jnp.exp(-0.5 * value * value) * NORMAL_PEAK
    return (value * cumulative, slope)


CORE, ALONG_X, ALONG_Y = (1, 2, 4)


def partner(bit):
    index = lax.axis_index("fsdp")
    return index + bit - 2 * bit * ((index // bit) % 2)


def chip_of(*bits):
    index = lax.axis_index("fsdp")
    for bit in bits:
        index = index + bit - 2 * bit * ((index // bit) % 2)
    return index // 2


def send(source, target, sems, number, bit):
    return pltpu.make_async_remote_copy(
        src_ref=source,
        dst_ref=target,
        send_sem=sems.at[0, number],
        recv_sem=sems.at[1, number],
        device_id={"fsdp": partner(bit)},
        device_id_type=pl.DeviceIdType.MESH,
    )


def greet(bits):
    barrier = pltpu.get_barrier_semaphore()
    for bit in bits:
        pl.semaphore_signal(
            barrier, inc=1, device_id={"fsdp": partner(bit)}, device_id_type=pl.DeviceIdType.MESH
        )
    pl.semaphore_wait(barrier, len(bits))


def bucket_columns(distances):
    distances = np.asarray(distances)
    magnitude = sum((np.abs(distances) >= threshold).astype(np.int32) for threshold in THRESHOLDS)
    buckets = magnitude + np.where(distances > 0, BUCKETS // 2, 0)
    return (buckets[None, :] == np.arange(BUCKETS)[:, None]).astype(np.float32)


def near_bias(columns):
    chosen = jnp.asarray(bucket_columns(np.arange(2 * QUERY_ROWS) - HALF_ROWS))
    line = lax.dot_general(columns, chosen, TN, precision=lax.Precision.HIGHEST, preferred_element_type=WIDE)
    return line[:, None, :]


def near_block(line):
    shape = (QUERY_ROWS, 2 * QUERY_ROWS)
    turned = pltpu.roll(jnp.broadcast_to(line, shape), 0, 1, stride=1, stride_axis=0)
    row = lax.broadcasted_iota(jnp.int32, shape, 0)
    column = lax.broadcasted_iota(jnp.int32, shape, 1)
    return jnp.where(column < row, line[:, :1], turned)


def diagonal_sums(tile):
    side = tile.shape[1]
    row = lax.broadcasted_iota(jnp.int32, tile.shape, 0)
    step = 1
    while step < side:
        tile = jnp.where((row // step) % 2 == 1, pltpu.roll(tile, side - step, 1), tile)
        step *= 2
    return jnp.sum(tile, axis=0, keepdims=True)


def spare_lanes(length, rows):
    blocks = rows // QUERY_ROWS
    key = lax.broadcasted_iota(jnp.int32, (rows, LANES), 0)
    lane = lax.rem(lax.broadcasted_iota(jnp.int32, (rows, LANES), 1), HEAD_DIM)
    hidden = jnp.where((lane == 0) & (key >= length), NEGATIVE, 0.0)
    left = (lane >= 1) & (lane <= blocks) & (key < QUERY_ROWS * (lane - 1) - HALF_ROWS)
    start = QUERY_ROWS * (lane - 1 - blocks) + 3 * HALF_ROWS
    right = (lane > blocks) & (lane <= 2 * blocks) & (key >= start)
    return jnp.where(left | right, 1.0, hidden).astype(LOW)


def split_heads(pair, spare, out):
    low_half = lax.broadcasted_iota(jnp.int32, pair.shape, 1) < HEAD_DIM
    out[0] = jnp.where(low_half, pair, spare)
    out[1] = jnp.where(low_half, spare, pair)


def gather_moves(mine, wholes, sems):
    chip = chip_of()
    direct = []
    for number, (one, whole_one) in enumerate(zip(mine, wholes)):
        for place, bit in enumerate((ALONG_X, ALONG_Y)):
            direct.append(send(one, whole_one.at[chip], sems, 2 * number + place, bit))
    first = wholes[0]
    half = first.shape[1] // 2
    onward = []
    for place, (bit, came) in enumerate(((ALONG_X, ALONG_Y), (ALONG_Y, ALONG_X))):
        piece = first.at[chip_of(came), pl.ds(place * half, half)]
        onward.append(send(piece, piece, sems, 2 * len(mine) + place, bit))
    return (direct, onward)


def attend_kernel(gathered, length_ref, query_ref, key_ref, value_ref, near_ref, *refs):
    mine, refs = (refs[:gathered], refs[gathered:])
    context_ref, log_ref = refs[:2]
    wholes, refs = (refs[2 : 2 + gathered], refs[2 + gathered :])
    bias, keys, values = refs[:3]
    rows = query_ref.shape[0]
    if gathered:
        sems, local = refs[3:]
        pair = pl.program_id(0)
        direct, onward = gather_moves(mine, wholes, sems)
        own = pltpu.make_async_copy(mine[0], wholes[0].at[chip_of()], local)

        @pl.when(pair == 0)
        def _():
            greet((ALONG_X, ALONG_Y))
            own.start()
            for one in direct:
                one.start()

        @pl.when(pair == 1)
        def _():
            for one in direct[:2]:
                one.wait_recv()
            for one in onward:
                one.start()

        @pl.when(pair == pl.num_programs(0) - 1)
        def _():
            own.wait()
            for one in direct:
                one.wait_send()
            for one in direct[2:]:
                one.wait_recv()
            for one in onward:
                one.wait()

    split_heads(key_ref[...], spare_lanes(length_ref[0], rows), keys)
    split_heads(value_ref[...], jnp.zeros((rows, LANES), LOW), values)
    near_start = rows - QUERY_ROWS - HALF_ROWS
    near_end = near_start + 2 * QUERY_ROWS
    for head in range(2):
        line = near_ref[head]
        bias[head, :, :near_start] = jnp.broadcast_to(line[:, :1], (QUERY_ROWS, near_start))
        bias[head, :, near_start:near_end] = near_block(line)
        bias[head, :, near_end:] = jnp.broadcast_to(line[:, -1:], (QUERY_ROWS, bias.shape[2] - near_end))
    lane = lax.broadcasted_iota(jnp.int32, (QUERY_ROWS, LANES), 1)
    ones = jnp.where(lax.rem(lane, HEAD_DIM) == 0, 1.0, 0.0).astype(LOW)

    def block(number, carry):
        start = pl.multiple_of(number * QUERY_ROWS, QUERY_ROWS)
        offset = pl.multiple_of(rows - QUERY_ROWS - number * QUERY_ROWS, LANES)
        both = query_ref[pl.ds(start, QUERY_ROWS), :]
        total = jnp.zeros((QUERY_ROWS, LANES), WIDE)
        for head in range(2):
            mine = lane < HEAD_DIM if head == 0 else lane >= HEAD_DIM
            logits = dot(jnp.where(mine, both, ones), keys[head], NT)
            logits = logits + bias[head, :, pl.ds(offset, rows)]
            peak = jnp.max(logits, axis=1, keepdims=True)
            exponent = jnp.exp(logits - peak)
            row_sum = jnp.sum(exponent, axis=1, keepdims=True)
            weights_low = (exponent * (1.0 / row_sum)).astype(LOW)
            total = total + dot(weights_low, values[head])
            logs = jnp.broadcast_to(peak + jnp.log(row_sum), (QUERY_ROWS, LANES))
            log_ref[0, head : head + 1, pl.ds(start, QUERY_ROWS)] = logs.T[0:1, :]
        context_ref[pl.ds(start, QUERY_ROWS), :] = total.astype(LOW)
        return carry

    lax.fori_loop(0, rows // QUERY_ROWS, block, 0)


def attend(length, query, key, value, near, mine=()):
    rows, width = query.shape
    pairs = width // LANES
    anywhere = pl.BlockSpec(memory_space=pl.ANY)
    gathered = len(mine)
    smem = pl.BlockSpec(memory_space=pltpu.SMEM)
    columns = pl.BlockSpec((rows, LANES), lambda pair: (0, pair))
    return pl.pallas_call(
        functools.partial(attend_kernel, gathered),
        grid=(pairs,),
        in_specs=[smem, columns, columns, columns]
        + [pl.BlockSpec((2, 1, 2 * QUERY_ROWS), lambda pair: (pair, 0, 0))]
        + [anywhere] * gathered,
        out_specs=[columns, pl.BlockSpec((1, 2, rows), lambda pair: (pair, 0, 0))] + [anywhere] * gathered,
        out_shape=[
            jax.ShapeDtypeStruct((rows, width), LOW),
            jax.ShapeDtypeStruct((pairs, 2, rows), WIDE),
        ]
        + [jax.ShapeDtypeStruct((4,) + one.shape, LOW) for one in mine],
        scratch_shapes=[
            pltpu.VMEM((2, QUERY_ROWS, 2 * rows - QUERY_ROWS), WIDE),
            pltpu.VMEM((2, rows, LANES), LOW),
            pltpu.VMEM((2, rows, LANES), LOW),
        ]
        + ([pltpu.SemaphoreType.DMA((2, 2 * gathered + 2)), pltpu.SemaphoreType.DMA] if gathered else []),
        compiler_params=pltpu.CompilerParams(
            vmem_limit_bytes=40 << 20,
            **({"collective_id": 1, "has_side_effects": True} if gathered else {}),
        ),
        cost_estimate=pl.CostEstimate(
            flops=24 * rows * rows * width, bytes_accessed=8 * rows * width, transcendentals=2 * pairs * rows * rows
        ),
        name="attend",
    )(length, query, key, value, near, *mine)


def attend_grad_kernel(
    length_ref,
    query_ref,
    key_ref,
    value_ref,
    grad_ref,
    log_ref,
    near_ref,
    query_grad_ref,
    key_grad_ref,
    value_grad_ref,
    sums_ref,
    bias,
    keys,
    values,
    padded,
    key_total,
    value_total,
    tiles,
):
    rows = query_ref.shape[0]
    blocks = rows // QUERY_ROWS
    split_heads(key_ref[...], spare_lanes(length_ref[0], rows), keys)
    split_heads(value_ref[...], jnp.zeros((rows, LANES), LOW), values)
    near_start = rows - QUERY_ROWS - HALF_ROWS
    near_end = near_start + 2 * QUERY_ROWS
    for head in range(2):
        line = near_ref[head]
        bias[head, :near_start, :] = jnp.broadcast_to(line[:, :1], (near_start, QUERY_ROWS))
        bias[head, near_start:near_end, :] = near_block(line).T
        bias[head, near_end:, :] = jnp.broadcast_to(line[:, -1:], (bias.shape[1] - near_end, QUERY_ROWS))
        padded[head, :HALF_ROWS, :] = jnp.zeros((HALF_ROWS, QUERY_ROWS), LOW)
        padded[head, rows + HALF_ROWS :, :] = jnp.zeros((HALF_ROWS, QUERY_ROWS), LOW)
    key_total[...] = jnp.zeros_like(key_total)
    value_total[...] = jnp.zeros_like(value_total)
    tiles[...] = jnp.zeros_like(tiles)
    sums_ref[...] = jnp.zeros_like(sums_ref)
    spot = lax.broadcasted_iota(jnp.int32, (1, LANES), 1)
    lane = lax.broadcasted_iota(jnp.int32, (QUERY_ROWS, LANES), 1)
    ones = jnp.where(lax.rem(lane, HEAD_DIM) == 0, 1.0, 0.0).astype(LOW)
    zero = jnp.zeros((), LOW)

    def block(number, carry):
        start = pl.multiple_of(number * QUERY_ROWS, QUERY_ROWS)
        offset = pl.multiple_of(rows - QUERY_ROWS - number * QUERY_ROWS, LANES)
        both = query_ref[pl.ds(start, QUERY_ROWS), :]
        grad = grad_ref[pl.ds(start, QUERY_ROWS), :]
        parts = []
        for head in range(2):
            mine = lane < HEAD_DIM if head == 0 else lane >= HEAD_DIM
            logits = dot(keys[head], jnp.where(mine, both, ones), NT)
            logits = logits + bias[head, pl.ds(offset, rows), :]
            probs = jnp.exp(logits - log_ref[0, head : head + 1, pl.ds(start, QUERY_ROWS)])
            prob_grad = dot(values[head], grad, NT)
            weighted = probs * prob_grad
            inner = jnp.sum(weighted, axis=0, keepdims=True)
            score = (weighted - probs * inner).astype(LOW)
            value_total[...] += dot(probs.astype(LOW), jnp.where(mine, grad, zero))
            key_total[...] += dot(score, jnp.where(mine, both, zero))
            padded[head, HALF_ROWS : HALF_ROWS + rows, :] = score
            part = dot(score, keys[head], TN)
            parts.append(part)
            columns = jnp.sum(part, axis=0, keepdims=True)
            spare = HEAD_DIM * (1 - head) + 1 + number
            close = padded[head, pl.ds(start, 2 * QUERY_ROWS), :].astype(WIDE)
            quarter = [close[HALF_ROWS * step : HALF_ROWS * (step + 1)] for step in range(4)]
            for step in range(3):
                tiles[head, step] += quarter[step][:, :HALF_ROWS] + quarter[step + 1][:, HALF_ROWS:]
            left = jnp.sum(quarter[0][:, HALF_ROWS:], axis=0, keepdims=True)
            right = jnp.sum(quarter[3][:, :HALF_ROWS], axis=0, keepdims=True)
            left = left + jnp.where(spot == spare, columns, 0.0)
            right = right + jnp.where(spot == spare + blocks, columns, 0.0)
            sums_ref[0, 4 * head + 2 : 4 * head + 3, :] += left
            sums_ref[0, 4 * head + 3 : 4 * head + 4, :] += right
        chosen = jnp.where(lane < HEAD_DIM, parts[0], parts[1])
        query_grad_ref[pl.ds(start, QUERY_ROWS), :] = chosen.astype(LOW)
        return carry

    lax.fori_loop(0, blocks, block, 0)
    key_grad_ref[...] = key_total[...].astype(LOW)
    value_grad_ref[...] = value_total[...].astype(LOW)
    shape = (HALF_ROWS, HALF_ROWS)
    upper = lax.broadcasted_iota(jnp.int32, shape, 0) <= lax.broadcasted_iota(jnp.int32, shape, 1)
    for head in range(2):
        before, centre, behind = (tiles[head, step] for step in range(3))
        sums_ref[0, 4 * head : 4 * head + 1, :] = diagonal_sums(jnp.where(upper, centre, before))
        sums_ref[0, 4 * head + 1 : 4 * head + 2, :] = diagonal_sums(jnp.where(upper, behind, centre))
        left = jnp.sum(jnp.where(upper, before, 0.0), axis=0, keepdims=True)
        right = jnp.sum(jnp.where(upper, 0.0, behind), axis=0, keepdims=True)
        sums_ref[0, 4 * head + 2 : 4 * head + 3, :] += left
        sums_ref[0, 4 * head + 3 : 4 * head + 4, :] += right


def attend_grad(length, query, key, value, grad, logs, near):
    rows, width = query.shape
    pairs = width // LANES
    smem = pl.BlockSpec(memory_space=pltpu.SMEM)
    columns = pl.BlockSpec((rows, LANES), lambda pair: (0, pair))
    shape = jax.ShapeDtypeStruct
    return pl.pallas_call(
        attend_grad_kernel,
        grid=(pairs,),
        in_specs=[smem, columns, columns, columns, columns]
        + [pl.BlockSpec((1, 2, rows), lambda pair: (pair, 0, 0))]
        + [pl.BlockSpec((2, 1, 2 * QUERY_ROWS), lambda pair: (pair, 0, 0))],
        out_specs=[columns, columns, columns] + [pl.BlockSpec((1, 8, LANES), lambda pair: (pair, 0, 0))],
        out_shape=[shape((rows, width), LOW)] * 3 + [shape((pairs, 8, LANES), WIDE)],
        scratch_shapes=[
            pltpu.VMEM((2, 2 * rows - QUERY_ROWS, QUERY_ROWS), WIDE),
            pltpu.VMEM((2, rows, LANES), LOW),
            pltpu.VMEM((2, rows, LANES), LOW),
            pltpu.VMEM((2, rows + QUERY_ROWS, QUERY_ROWS), LOW),
            pltpu.VMEM((rows, LANES), WIDE),
            pltpu.VMEM((rows, LANES), WIDE),
            pltpu.VMEM((2, 3, HALF_ROWS, HALF_ROWS), WIDE),
        ],
        compiler_params=pltpu.CompilerParams(vmem_limit_bytes=48 << 20),
        cost_estimate=pl.CostEstimate(
            flops=44 * rows * rows * width, bytes_accessed=14 * rows * width, transcendentals=2 * pairs * rows * rows
        ),
        name="attend_grad",
    )(length, query, key, value, grad, logs, near)


def bucket_sums(sums):
    pairs = sums.shape[0]
    side = np.arange(LANES)
    far = np.full((LANES,), 2 * HALF_ROWS)
    chosen = bucket_columns(np.concatenate([-side, HALF_ROWS - side, -far, far]))
    return lax.dot_general(
        jnp.asarray(chosen),
        sums.reshape(2 * pairs, 4 * LANES),
        NT,
        precision=lax.Precision.HIGHEST,
        preferred_element_type=WIDE,
    )


def feed_kernel(pieces, normed_ref, grad_ref, *refs):
    moved = pieces > 1
    kinds = 2
    mine, refs = (refs[:kinds], refs[kinds:])
    if moved:
        wholes, refs = (refs[:kinds], refs[kinds:])
    parts, refs = (refs[:kinds], refs[kinds:])
    out_ref, back_ref = refs[:2]
    refs = refs[2:]
    if moved:
        fars, refs = (refs[:kinds], refs[kinds:])
    slots, stages, refs = (refs[:2], refs[2:4], refs[4:])
    arrived, stored = refs[:2]
    step, steps = (pl.program_id(0), pl.num_programs(0))
    unit = slots[0].shape[1]
    slot = lax.rem(step, 2)

    if moved:
        sems = refs[2]
        half = unit // 2
        moves = []
        for kind in range(kinds):
            for place, (bit, came) in enumerate(((ALONG_X, ALONG_Y), (ALONG_Y, ALONG_X))):
                there = pl.ds(place * half, half)
                source = wholes[kind].at[chip_of(came), there]
                moves.append(send(source, fars[kind].at[there], sems, 2 * kind + place, bit))
        sources = [
            mine,
            [one.at[chip_of(ALONG_X)] for one in wholes],
            [one.at[chip_of(ALONG_Y)] for one in wholes],
            fars,
        ]
        places = [chip_of(), chip_of(ALONG_X), chip_of(ALONG_Y), chip_of(ALONG_X, ALONG_Y)]

        def fetch(block, into):
            for number, pair in enumerate(sources):

                @pl.when(block == number)
                def _():
                    for kind in range(kinds):
                        pltpu.make_async_copy(pair[kind], slots[kind].at[into], arrived.at[kind, into]).start()

        def store(block, kind, from_slot, act):
            for number, place in enumerate(places):

                @pl.when(block == number)
                def _():
                    act(
                        pltpu.make_async_copy(
                            stages[kind].at[from_slot],
                            parts[kind].at[pl.ds(pl.multiple_of(place * unit, unit), unit)],
                            stored.at[kind, from_slot],
                        )
                    )
    else:

        def fetch(block, into):
            rows = pl.ds(pl.multiple_of(block * unit, unit), unit)
            for kind in range(kinds):
                pltpu.make_async_copy(mine[kind].at[rows], slots[kind].at[into], arrived.at[kind, into]).start()

        def store(block, kind, from_slot, act):
            rows = pl.ds(pl.multiple_of(block * unit, unit), unit)
            act(pltpu.make_async_copy(stages[kind].at[from_slot], parts[kind].at[rows], stored.at[kind, from_slot]))

    @pl.when(step == 0)
    def _():
        if moved:
            greet((ALONG_X, ALONG_Y))
            for one in moves:
                one.start()
        fetch(0, 0)
        out_ref[...] = jnp.zeros_like(out_ref)
        back_ref[...] = jnp.zeros_like(back_ref)

    @pl.when(step + 1 < steps - moved)
    def _():
        fetch(step + 1, 1 - slot)

    for kind in range(kinds):
        pltpu.make_async_copy(slots[kind].at[slot], slots[kind].at[slot], arrived.at[kind, slot]).wait()
    up, down = (slots[0][slot], slots[1][slot])
    normed, grad = (normed_ref[...], grad_ref[...])
    active, slope = gelu_parts(dot(normed, up, NT))
    active = active.astype(LOW)
    pre_grad = (dot(grad, down, NT) * slope).astype(LOW)
    out_ref[...] += dot(active, down)
    back_ref[...] += dot(pre_grad, up)

    @pl.when(step >= 2)
    def _():
        for kind in range(kinds):
            store(step - 2, kind, slot, lambda copy: copy.wait())

    stages[0][slot] = dot(pre_grad, normed, TN).astype(LOW)
    stages[1][slot] = dot(active, grad, TN).astype(LOW)
    for kind in range(kinds):
        store(step, kind, slot, lambda copy: copy.start())

    if moved:

        @pl.when(step == steps - 2)
        def _():
            for one in moves:
                one.wait()
            fetch(step + 1, 1 - slot)

    @pl.when(step == steps - 1)
    def _():
        for kind in range(kinds):
            store(step - 1, kind, 1 - slot, lambda copy: copy.wait())
            store(step, kind, slot, lambda copy: copy.wait())


def feed(normed, grad, mine, wholes=()):
    rows, width = normed.shape
    moved = bool(wholes)
    unit = mine[0].shape[0] if moved else mine[0].shape[0] // 4
    anywhere = pl.BlockSpec(memory_space=pl.ANY)
    fixed = pl.BlockSpec((rows, width), lambda step: (0, 0))
    return pl.pallas_call(
        functools.partial(feed_kernel, 4 if moved else 1),
        grid=(4,),
        in_specs=[fixed, fixed] + [anywhere] * (4 if moved else 2),
        out_specs=[anywhere, anywhere, fixed, fixed] + ([anywhere, anywhere] if moved else []),
        out_shape=[jax.ShapeDtypeStruct((4 * unit, width), LOW)] * 2
        + [jax.ShapeDtypeStruct((rows, width), WIDE)] * 2
        + ([jax.ShapeDtypeStruct((unit, width), LOW)] * 2 if moved else []),
        scratch_shapes=[pltpu.VMEM((2, unit, width), LOW)] * 4
        + [pltpu.SemaphoreType.DMA((2, 2)), pltpu.SemaphoreType.DMA((2, 2))]
        + ([pltpu.SemaphoreType.DMA((2, 4))] if moved else []),
        compiler_params=pltpu.CompilerParams(
            vmem_limit_bytes=56 << 20,
            **({"collective_id": 2, "has_side_effects": True} if moved else {}),
        ),
        cost_estimate=pl.CostEstimate(
            flops=48 * unit * rows * width,
            bytes_accessed=32 * unit * width + 12 * rows * width,
            transcendentals=8 * unit * rows,
        ),
        name="feed",
    )(normed, grad, *mine, *wholes)[:4]


def flip(value, bit):
    size = lax.axis_size("fsdp")
    return lax.ppermute(value, "fsdp", [(one, one ^ bit) for one in range(size)])


def other_core(value):
    return flip(value, 1)


def after(value, *first):
    return lax.optimization_barrier((value,) + first)[0]


def rounds_of(inverse):
    depth, size = (lax.axis_size("seq"), lax.axis_size("fsdp"))
    held = depth // 2
    rounds = []
    for step in range(held):
        pairs = []
        for place in range(depth):
            for index in range(size):
                target = (index % 2) * held + (place + step) % held
                there = target * size + index - index % 2 + place // held
                here = place * size + index
                pairs.append((there, here) if inverse else (here, there))
        rounds.append(pairs)
    return rounds


def to_sequence(blocks):
    held, span, width = blocks.shape
    place = lax.axis_index("seq")
    out = jnp.zeros((held, span, width), blocks.dtype)
    for step, pairs in enumerate(rounds_of(False)):
        sent = lax.dynamic_index_in_dim(blocks, (place + step) % held, 0, keepdims=False)
        got = lax.ppermute(sent, BOTH, pairs)
        out = lax.dynamic_update_index_in_dim(out, got, (place + held - step) % held, 0)
    return out.reshape(held * span, width)


def to_slots(rows, held):
    span, width = (rows.shape[0] // held, rows.shape[1])
    place = lax.axis_index("seq")
    blocks = rows.reshape(held, span, width)
    out = jnp.zeros(blocks.shape, rows.dtype)
    for step, pairs in enumerate(rounds_of(True)):
        sent = lax.dynamic_index_in_dim(blocks, (place + held - step) % held, 0, keepdims=False)
        got = lax.ppermute(sent, BOTH, pairs)
        out = lax.dynamic_update_index_in_dim(out, got, (place + step) % held, 0)
    return out


def whole(mine, core):
    other = other_core(mine)
    return jnp.where(
        core == 0, jnp.concatenate([mine, other], axis=0), jnp.concatenate([other, mine], axis=0)
    )


def fold(partial, core):
    half = partial.shape[0] // 2
    sent = lax.dynamic_slice_in_dim(partial, (1 - core) * half, half, 0)
    kept = lax.dynamic_slice_in_dim(partial, core * half, half, 0)
    return kept + other_core(sent)


def gather_near(mine):
    return (flip(mine, 2), flip(mine, 4))


def gather_far(beside, above):
    half = beside.shape[0] // 2
    return (flip(above[:half], 2), flip(beside[half:], 4))


def in_order(mine, beside, above, far):
    chip = lax.axis_index("fsdp") // 2
    out = jnp.zeros((4,) + mine.shape, mine.dtype)
    out = lax.dynamic_update_index_in_dim(out, mine, chip, 0)
    out = lax.dynamic_update_index_in_dim(out, beside, chip ^ 1, 0)
    out = lax.dynamic_update_index_in_dim(out, above, chip ^ 2, 0)
    out = lax.dynamic_update_slice(out, far[0][None], (chip ^ 3, 0, 0))
    return lax.dynamic_update_slice(out, far[1][None], (chip ^ 3, mine.shape[0] // 2, 0))


def fast_plane():
    return lax.axis_size("fsdp") == 8 and lax.axis_size("seq") == 4


def own_head_rows(weight, core):
    width = weight.shape[1]
    return lax.dynamic_index_in_dim(weight.reshape(4, 2, -1, width), core, 1, keepdims=False).reshape(-1, width)


def add_low(left, right):
    return (left.astype(WIDE) + right.astype(WIDE)).astype(LOW)


def pick(value, index, axis):
    return lax.dynamic_index_in_dim(value, index, axis, keepdims=False)


def spread_depth(value):
    depth = lax.axis_size("seq")
    place = lax.axis_index("seq")
    total = pick(value, place, 0).astype(WIDE)
    for step in range(1, depth):
        sent = pick(value, (place + step) % depth, 0)
        got = lax.ppermute(sent, "seq", [(one, (one + step) % depth) for one in range(depth)])
        total = total + got.astype(WIDE)
    return total


def scatter_plane(one, two):
    chip = lax.axis_index("fsdp") // 2
    x, y = (chip % 2, chip // 2)
    one_got = flip(pick(one, 1 - x, 2), 2)
    two_got = flip(pick(two, 1 - y, 1), 4)
    one = add_low(pick(one, x, 2), one_got)
    two = add_low(pick(two, y, 1), two_got)
    one_last = flip(pick(one, 1 - y, 1), 4)
    two_last = flip(pick(two, 1 - x, 1), 2)
    return (add_low(pick(one, y, 1), one_last), add_low(pick(two, x, 1), two_last))


def shards(
    inputs,
    lengths,
    cotangent,
    query_weight,
    key_weight,
    value_weight,
    output_weight,
    up_weight,
    down_weight,
    attn_gain,
    ffn_gain,
    bias_table,
):
    held, span, width = inputs.shape
    depth, size = (lax.axis_size("seq"), lax.axis_size("fsdp"))
    place, index = (lax.axis_index("seq"), lax.axis_index("fsdp"))
    core = index % 2
    rows = held * span
    inner = HEADS * HEAD_DIM
    fast = fast_plane()

    near_lengths = jnp.where(
        core == 0,
        jnp.concatenate([lengths, other_core(lengths)]),
        jnp.concatenate([other_core(lengths), lengths]),
    )
    length = lax.dynamic_slice_in_dim(near_lengths, place, 1, 0)
    slots = core * rows + jnp.arange(rows, dtype=jnp.int32)
    mask_rows = (slots < length[0])[:, None].astype(WIDE)

    own_table = lax.dynamic_index_in_dim(bias_table.reshape(BUCKETS, 4, 2, 2), core, 2, keepdims=False)
    own_table = own_table.reshape(BUCKETS, HEADS // 2)
    near = near_bias(own_table)

    ffn = up_weight.shape[0]
    if fast:
        stacked = jnp.concatenate([query_weight, key_weight, value_weight], axis=0)
        cut = jnp.stack([up_weight, down_weight]).reshape(2, 2, 2, -1, width)
        swapped = other_core(pick(cut, 1 - core, 2))
        kept = pick(cut, core, 2)
        cut = jnp.where(
            core == 0, jnp.stack([kept, swapped], axis=1), jnp.stack([swapped, kept], axis=1)
        ).reshape(2, -1, width)
        up_mine, down_mine = (cut[0], cut[1])
        beside, above = gather_near(stacked)
        far = gather_far(beside, above)
        heads_low = in_order(stacked, beside, above, far).reshape(4, 3, -1, width)
        own_three = [heads_low[:, number].reshape(-1, width) for number in range(3)]
    else:
        own_three = [
            own_head_rows(lax.all_gather(one, "fsdp", axis=0, tiled=True), core)
            for one in (query_weight, key_weight, value_weight)
        ]
        full = lax.all_gather(output_weight, "fsdp", axis=0, tiled=True)
        own_output = own_head_rows(full, core)
        far_output = own_head_rows(full, 1 - core)
        own_up, own_down = (
            pick(
                lax.all_gather(one, "fsdp", axis=0, tiled=True).reshape(depth, size // 2, 2, -1, width), core, 2
            ).reshape(-1, width)
            for one in (up_weight, down_weight)
        )

    source_low = to_sequence(inputs)
    source = source_low.astype(WIDE)
    rms_one = lax.rsqrt(jnp.mean(source * source, axis=1, keepdims=True) + EPSILON)
    scaled_one = source * rms_one
    normed_one = whole((scaled_one * attn_gain).astype(LOW), core)
    query, key, value = [dot(normed_one, one, NT).astype(LOW) for one in own_three]
    if fast:
        mine = (output_weight, up_mine, down_mine)
        context, logs, own_output, *wholes = attend(length, query, key, value, near, mine)
        own_output = own_output.reshape(-1, width)
        far_output = other_core(own_output)
        mine = mine[1:]
    else:
        context, logs = attend(length, query, key, value, near)
        mine, wholes = ((own_up, own_down), ())
    near_context = lax.dynamic_slice_in_dim(context, core * rows, rows, 0)
    far_context = other_core(lax.dynamic_slice_in_dim(context, (1 - core) * rows, rows, 0))
    hidden_one = source + (dot(near_context, own_output) + dot(far_context, far_output))
    rms_two = lax.rsqrt(jnp.mean(hidden_one * hidden_one, axis=1, keepdims=True) + EPSILON)
    scaled_two = hidden_one * rms_two
    normed_two = whole((scaled_two * ffn_gain).astype(LOW), core)
    grad_out = to_sequence(cotangent).astype(WIDE) * mask_rows
    grad_low = whole(grad_out.astype(LOW), core)
    up_part, down_part, mlp_part, normed_part = feed(normed_two, grad_low, mine, wholes)
    normed_grad = fold(normed_part, core)
    mlp_out = fold(mlp_part, core)
    layer_rows = ((hidden_one + mlp_out) * mask_rows).astype(LOW)
    layer_out = to_slots(layer_rows, held)

    gained_two = ffn_gain * normed_grad
    hidden_grad = grad_out + rms_two * (
        gained_two - scaled_two * jnp.mean(gained_two * scaled_two, axis=1, keepdims=True)
    )
    ffn_gain_part = jnp.sum(normed_grad * scaled_two, axis=0)
    hidden_low = hidden_grad.astype(LOW)
    near_grad = dot(hidden_low, own_output, NT).astype(LOW)
    far_grad = other_core(dot(hidden_low, far_output, NT).astype(LOW))
    context_grad = jnp.where(
        core == 0,
        jnp.concatenate([near_grad, far_grad], axis=0),
        jnp.concatenate([far_grad, near_grad], axis=0),
    )
    near_output_part = dot(near_context, hidden_low, TN).astype(LOW)
    far_output_part = dot(far_context, hidden_low, TN).astype(LOW)

    query_low, key_low, value_low, distance_sums = attend_grad(
        length, query, key, value, context_grad, logs, near
    )
    lows = (query_low, key_low, value_low)
    normed_one_grad = dot(query_low, own_three[0]) + dot(key_low, own_three[1]) + dot(value_low, own_three[2])
    normed_one_grad = fold(normed_one_grad, core)
    three_parts = [dot(one, normed_one, TN).astype(LOW) for one in lows]
    gained_one = attn_gain * normed_one_grad
    input_grad = hidden_grad + rms_one * (
        gained_one - scaled_one * jnp.mean(gained_one * scaled_one, axis=1, keepdims=True)
    )
    attn_gain_part = jnp.sum(normed_one_grad * scaled_one, axis=0)
    input_grad = to_slots(input_grad.astype(LOW), held).astype(WIDE)

    if fast:
        blocks = (depth, 2, 2, -1, width)
        up_some, down_some = scatter_plane(up_part.reshape(blocks), down_part.reshape(blocks))
        up_grad, down_grad = (spread_depth(up_some), spread_depth(down_some))

        def to_parity(kept, sent):
            return jnp.where(
                core == 0, jnp.stack([kept, sent], axis=1), jnp.stack([sent, kept], axis=1)
            )

        three = jnp.stack(three_parts).reshape(3, 4, 2, 2, -1, width)
        three_got = other_core(pick(three, 1 - core, 3))
        three_kept = pick(three, core, 3)
        outs = [to_parity(three_kept[number], three_got[number]) for number in range(3)]
        near_part = near_output_part.reshape(4, 2, 2, -1, width)
        far_part = far_output_part.reshape(4, 2, 2, -1, width)
        got = other_core(jnp.stack([pick(far_part, 1 - core, 2), pick(near_part, 1 - core, 2)]))
        outs.append(
            to_parity(add_low(pick(near_part, core, 2), got[0]), add_low(pick(far_part, core, 2), got[1]))
        )
        one = jnp.concatenate(outs[:2], axis=3)
        two = jnp.concatenate(outs[2:], axis=3)
        one, two = scatter_plane(one, two)
        attention = spread_depth(jnp.concatenate([one, two], axis=1))
        attention = attention.reshape(4, -1, width)
        query_grad, key_grad, value_grad, output_grad = [attention[number] for number in range(4)]
    else:

        def summed(value):
            return lax.psum_scatter(value, BOTH, scatter_dimension=0, tiled=True).astype(WIDE)

        def own_only(value, shape):
            blank = jnp.zeros_like(value)
            pair = jnp.where(core == 0, jnp.stack([value, blank], axis=1), jnp.stack([blank, value], axis=1))
            return pair.reshape(-1, width)

        up_grad, down_grad = [
            summed(own_only(one.reshape(depth * (size // 2), -1, width), None)) for one in (up_part, down_part)
        ]
        query_grad, key_grad, value_grad = [summed(own_only(one.reshape(4, -1, width), None)) for one in three_parts]
        near_part, far_part = (near_output_part.reshape(4, -1, width), far_output_part.reshape(4, -1, width))
        pair = jnp.where(
            core == 0, jnp.stack([near_part, far_part], axis=1), jnp.stack([far_part, near_part], axis=1)
        )
        output_grad = summed(pair.reshape(-1, width))

    bias_own = bucket_sums(distance_sums).reshape(BUCKETS, 4, 1, 2)
    bias_full = lax.dynamic_update_slice(
        jnp.zeros((BUCKETS, 4, 2, 2), WIDE), bias_own, (0, 0, core, 0)
    ).reshape(BUCKETS, HEADS)
    if fast:
        small = jnp.concatenate([attn_gain_part, ffn_gain_part, bias_full.reshape(-1)]).reshape(-1, LANES)
        for bit in (1, 2, 4):
            small = small + flip(small, bit)
        moved = [
            lax.ppermute(small, "seq", [(one, (one + step) % depth) for one in range(depth)])
            for step in range(1, depth)
        ]
        small = sum(moved, small).reshape(-1)
        attn_gain_sum, ffn_gain_sum = (small[:width], small[width : 2 * width])
        bias_sum = small[2 * width :].reshape(BUCKETS, HEADS)
    else:
        attn_gain_sum, ffn_gain_sum, bias_sum = lax.psum((attn_gain_part, ffn_gain_part, bias_full), BOTH)
    gain_rows = width // size
    bucket_rows = BUCKETS // size
    attn_gain_grad = lax.dynamic_slice_in_dim(attn_gain_sum, index * gain_rows, gain_rows, 0)
    ffn_gain_grad = lax.dynamic_slice_in_dim(ffn_gain_sum, index * gain_rows, gain_rows, 0)
    bias_grad = lax.dynamic_slice_in_dim(bias_sum, index * bucket_rows, bucket_rows, 0)
    return (
        layer_out,
        input_grad,
        query_grad,
        key_grad,
        value_grad,
        output_grad,
        up_grad,
        down_grad,
        attn_gain_grad,
        ffn_gain_grad,
        bias_grad,
    )


def solution(mesh):
    placed = (
        P("fsdp", "seq", None),
        P("fsdp"),
        P("fsdp", "seq", None),
        P("fsdp", None),
        P("fsdp", None),
        P("fsdp", None),
        P("fsdp", None),
        P("fsdp", None),
        P("fsdp", None),
        P(),
        P(),
        P(),
    )
    return jax.shard_map(
        shards,
        mesh=mesh,
        in_specs=placed,
        out_specs=(
            P("fsdp", "seq", None),
            P("fsdp", "seq", None),
            P(("seq", "fsdp"), None),
            P(("seq", "fsdp"), None),
            P(("seq", "fsdp"), None),
            P(("seq", "fsdp"), None),
            P(("seq", "fsdp"), None),
            P(("seq", "fsdp"), None),
            P("fsdp"),
            P("fsdp"),
            P("fsdp", None),
        ),
        check_vma=False,
    )
```

```python
import functools

import jax
import jax.numpy as jnp
import numpy as np
from jax import lax
from jax.experimental import pallas as pl
from jax.experimental.pallas import tpu as pltpu
from jax.sharding import PartitionSpec as P

HEADS = 16
HEAD_DIM = 64
BUCKETS = 32
NEGATIVE = -1000000000.0
EPSILON = 1e-06
THRESHOLDS = (1, 2, 3, 4, 5, 6, 7, 8, 12, 16, 23, 32, 46, 64, 91)
ROOT_HALF = 0.7071067811865476
NORMAL_PEAK = 0.3989422804014327
LANES = 128
QUERY_ROWS = 256
HALF_ROWS = QUERY_ROWS // 2
LOW = jnp.bfloat16
WIDE = jnp.float32
BOTH = ("seq", "fsdp")

NN = (((1,), (0,)), ((), ()))
NT = (((1,), (1,)), ((), ()))
TN = (((0,), (0,)), ((), ()))


def dot(left, right, dims=NN):
    return lax.dot_general(left, right, dims, preferred_element_type=WIDE)


def gelu_parts(value):
    cumulative = 0.5 * (1.0 + lax.erf(value * ROOT_HALF))
    slope = cumulative + value * jnp.exp(-0.5 * value * value) * NORMAL_PEAK
    return (value * cumulative, slope)


CORE, ALONG_X, ALONG_Y = (1, 2, 4)


def partner(bit):
    index = lax.axis_index("fsdp")
    return index + bit - 2 * bit * ((index // bit) % 2)


def chip_of(*bits):
    index = lax.axis_index("fsdp")
    for bit in bits:
        index = index + bit - 2 * bit * ((index // bit) % 2)
    return index // 2


def send(source, target, sems, number, bit):
    return pltpu.make_async_remote_copy(
        src_ref=source,
        dst_ref=target,
        send_sem=sems.at[0, number],
        recv_sem=sems.at[1, number],
        device_id={"fsdp": partner(bit)},
        device_id_type=pl.DeviceIdType.MESH,
    )


def greet(bits):
    barrier = pltpu.get_barrier_semaphore()
    for bit in bits:
        pl.semaphore_signal(
            barrier, inc=1, device_id={"fsdp": partner(bit)}, device_id_type=pl.DeviceIdType.MESH
        )
    pl.semaphore_wait(barrier, len(bits))


def bucket_columns(distances):
    distances = np.asarray(distances)
    magnitude = sum((np.abs(distances) >= threshold).astype(np.int32) for threshold in THRESHOLDS)
    buckets = magnitude + np.where(distances > 0, BUCKETS // 2, 0)
    return (buckets[None, :] == np.arange(BUCKETS)[:, None]).astype(np.float32)


def near_bias(columns):
    chosen = jnp.asarray(bucket_columns(np.arange(2 * QUERY_ROWS) - HALF_ROWS))
    line = lax.dot_general(columns, chosen, TN, precision=lax.Precision.HIGHEST, preferred_element_type=WIDE)
    return line[:, None, :]


def near_block(line):
    shape = (QUERY_ROWS, 2 * QUERY_ROWS)
    turned = pltpu.roll(jnp.broadcast_to(line, shape), 0, 1, stride=1, stride_axis=0)
    row = lax.broadcasted_iota(jnp.int32, shape, 0)
    column = lax.broadcasted_iota(jnp.int32, shape, 1)
    return jnp.where(column < row, line[:, :1], turned)


def diagonal_sums(tile):
    side = tile.shape[1]
    row = lax.broadcasted_iota(jnp.int32, tile.shape, 0)
    step = 1
    while step < side:
        tile = jnp.where((row // step) % 2 == 1, pltpu.roll(tile, side - step, 1), tile)
        step *= 2
    return jnp.sum(tile, axis=0, keepdims=True)


def spare_lanes(length, rows):
    blocks = rows // QUERY_ROWS
    key = lax.broadcasted_iota(jnp.int32, (rows, LANES), 0)
    lane = lax.rem(lax.broadcasted_iota(jnp.int32, (rows, LANES), 1), HEAD_DIM)
    hidden = jnp.where((lane == 0) & (key >= length), NEGATIVE, 0.0)
    left = (lane >= 1) & (lane <= blocks) & (key < QUERY_ROWS * (lane - 1) - HALF_ROWS)
    start = QUERY_ROWS * (lane - 1 - blocks) + 3 * HALF_ROWS
    right = (lane > blocks) & (lane <= 2 * blocks) & (key >= start)
    return jnp.where(left | right, 1.0, hidden).astype(LOW)


def split_heads(pair, spare, out):
    low_half = lax.broadcasted_iota(jnp.int32, pair.shape, 1) < HEAD_DIM
    out[0] = jnp.where(low_half, pair, spare)
    out[1] = jnp.where(low_half, spare, pair)


def gather_moves(mine, wholes, sems):
    chip = chip_of()
    direct = []
    for number, (one, whole_one) in enumerate(zip(mine, wholes)):
        for place, bit in enumerate((ALONG_X, ALONG_Y)):
            direct.append(send(one, whole_one.at[chip], sems, 2 * number + place, bit))
    first = wholes[0]
    half = first.shape[1] // 2
    onward = []
    for place, (bit, came) in enumerate(((ALONG_X, ALONG_Y), (ALONG_Y, ALONG_X))):
        piece = first.at[chip_of(came), pl.ds(place * half, half)]
        onward.append(send(piece, piece, sems, 2 * len(mine) + place, bit))
    return (direct, onward)


def attend_kernel(gathered, length_ref, query_ref, key_ref, value_ref, near_ref, *refs):
    mine, refs = (refs[:gathered], refs[gathered:])
    context_ref, log_ref = refs[:2]
    wholes, refs = (refs[2 : 2 + gathered], refs[2 + gathered :])
    bias, keys, values = refs[:3]
    rows = query_ref.shape[0]
    if gathered:
        sems, local = refs[3:]
        pair = pl.program_id(0)
        direct, onward = gather_moves(mine, wholes, sems)
        own = pltpu.make_async_copy(mine[0], wholes[0].at[chip_of()], local)

        @pl.when(pair == 0)
        def _():
            greet((ALONG_X, ALONG_Y))
            own.start()
            for one in direct:
                one.start()

        @pl.when(pair == 1)
        def _():
            for one in direct[:2]:
                one.wait_recv()
            for one in onward:
                one.start()

        @pl.when(pair == pl.num_programs(0) - 1)
        def _():
            own.wait()
            for one in direct:
                one.wait_send()
            for one in direct[2:]:
                one.wait_recv()
            for one in onward:
                one.wait()

    split_heads(key_ref[...], spare_lanes(length_ref[0], rows), keys)
    split_heads(value_ref[...], jnp.zeros((rows, LANES), LOW), values)
    near_start = rows - QUERY_ROWS - HALF_ROWS
    near_end = near_start + 2 * QUERY_ROWS
    for head in range(2):
        line = near_ref[head]
        bias[head, :, :near_start] = jnp.broadcast_to(line[:, :1], (QUERY_ROWS, near_start))
        bias[head, :, near_start:near_end] = near_block(line)
        bias[head, :, near_end:] = jnp.broadcast_to(line[:, -1:], (QUERY_ROWS, bias.shape[2] - near_end))
    lane = lax.broadcasted_iota(jnp.int32, (QUERY_ROWS, LANES), 1)
    ones = jnp.where(lax.rem(lane, HEAD_DIM) == 0, 1.0, 0.0).astype(LOW)

    def block(number, carry):
        start = pl.multiple_of(number * QUERY_ROWS, QUERY_ROWS)
        offset = pl.multiple_of(rows - QUERY_ROWS - number * QUERY_ROWS, LANES)
        both = query_ref[pl.ds(start, QUERY_ROWS), :]
        total = jnp.zeros((QUERY_ROWS, LANES), WIDE)
        for head in range(2):
            mine = lane < HEAD_DIM if head == 0 else lane >= HEAD_DIM
            logits = dot(jnp.where(mine, both, ones), keys[head], NT)
            logits = logits + bias[head, :, pl.ds(offset, rows)]
            peak = jnp.max(logits, axis=1, keepdims=True)
            exponent = jnp.exp(logits - peak)
            row_sum = jnp.sum(exponent, axis=1, keepdims=True)
            weights_low = (exponent * (1.0 / row_sum)).astype(LOW)
            total = total + dot(weights_low, values[head])
            logs = jnp.broadcast_to(peak + jnp.log(row_sum), (QUERY_ROWS, LANES))
            log_ref[0, head : head + 1, pl.ds(start, QUERY_ROWS)] = logs.T[0:1, :]
        context_ref[pl.ds(start, QUERY_ROWS), :] = total.astype(LOW)
        return carry

    lax.fori_loop(0, rows // QUERY_ROWS, block, 0)


def attend(length, query, key, value, near, mine=()):
    rows, width = query.shape
    pairs = width // LANES
    anywhere = pl.BlockSpec(memory_space=pl.ANY)
    gathered = len(mine)
    smem = pl.BlockSpec(memory_space=pltpu.SMEM)
    columns = pl.BlockSpec((rows, LANES), lambda pair: (0, pair))
    return pl.pallas_call(
        functools.partial(attend_kernel, gathered),
        grid=(pairs,),
        in_specs=[smem, columns, columns, columns]
        + [pl.BlockSpec((2, 1, 2 * QUERY_ROWS), lambda pair: (pair, 0, 0))]
        + [anywhere] * gathered,
        out_specs=[columns, pl.BlockSpec((1, 2, rows), lambda pair: (pair, 0, 0))] + [anywhere] * gathered,
        out_shape=[
            jax.ShapeDtypeStruct((rows, width), LOW),
            jax.ShapeDtypeStruct((pairs, 2, rows), WIDE),
        ]
        + [jax.ShapeDtypeStruct((4,) + one.shape, LOW) for one in mine],
        scratch_shapes=[
            pltpu.VMEM((2, QUERY_ROWS, 2 * rows - QUERY_ROWS), WIDE),
            pltpu.VMEM((2, rows, LANES), LOW),
            pltpu.VMEM((2, rows, LANES), LOW),
        ]
        + ([pltpu.SemaphoreType.DMA((2, 2 * gathered + 2)), pltpu.SemaphoreType.DMA] if gathered else []),
        compiler_params=pltpu.CompilerParams(
            vmem_limit_bytes=40 << 20,
            **({"collective_id": 1, "has_side_effects": True} if gathered else {}),
        ),
        cost_estimate=pl.CostEstimate(
            flops=24 * rows * rows * width, bytes_accessed=8 * rows * width, transcendentals=2 * pairs * rows * rows
        ),
        name="attend",
    )(length, query, key, value, near, *mine)


def attend_grad_kernel(
    length_ref,
    query_ref,
    key_ref,
    value_ref,
    grad_ref,
    log_ref,
    near_ref,
    query_grad_ref,
    key_grad_ref,
    value_grad_ref,
    sums_ref,
    bias,
    keys,
    values,
    padded,
    key_total,
    value_total,
    tiles,
):
    rows = query_ref.shape[0]
    blocks = rows // QUERY_ROWS
    split_heads(key_ref[...], spare_lanes(length_ref[0], rows), keys)
    split_heads(value_ref[...], jnp.zeros((rows, LANES), LOW), values)
    near_start = rows - QUERY_ROWS - HALF_ROWS
    near_end = near_start + 2 * QUERY_ROWS
    for head in range(2):
        line = near_ref[head]
        bias[head, :near_start, :] = jnp.broadcast_to(line[:, :1], (near_start, QUERY_ROWS))
        bias[head, near_start:near_end, :] = near_block(line).T
        bias[head, near_end:, :] = jnp.broadcast_to(line[:, -1:], (bias.shape[1] - near_end, QUERY_ROWS))
        padded[head, :HALF_ROWS, :] = jnp.zeros((HALF_ROWS, QUERY_ROWS), LOW)
        padded[head, rows + HALF_ROWS :, :] = jnp.zeros((HALF_ROWS, QUERY_ROWS), LOW)
    key_total[...] = jnp.zeros_like(key_total)
    value_total[...] = jnp.zeros_like(value_total)
    tiles[...] = jnp.zeros_like(tiles)
    sums_ref[...] = jnp.zeros_like(sums_ref)
    spot = lax.broadcasted_iota(jnp.int32, (1, LANES), 1)
    lane = lax.broadcasted_iota(jnp.int32, (QUERY_ROWS, LANES), 1)
    ones = jnp.where(lax.rem(lane, HEAD_DIM) == 0, 1.0, 0.0).astype(LOW)
    zero = jnp.zeros((), LOW)

    def block(number, carry):
        start = pl.multiple_of(number * QUERY_ROWS, QUERY_ROWS)
        offset = pl.multiple_of(rows - QUERY_ROWS - number * QUERY_ROWS, LANES)
        both = query_ref[pl.ds(start, QUERY_ROWS), :]
        grad = grad_ref[pl.ds(start, QUERY_ROWS), :]
        parts = []
        for head in range(2):
            mine = lane < HEAD_DIM if head == 0 else lane >= HEAD_DIM
            logits = dot(keys[head], jnp.where(mine, both, ones), NT)
            logits = logits + bias[head, pl.ds(offset, rows), :]
            probs = jnp.exp(logits - log_ref[0, head : head + 1, pl.ds(start, QUERY_ROWS)])
            prob_grad = dot(values[head], grad, NT)
            weighted = probs * prob_grad
            inner = jnp.sum(weighted, axis=0, keepdims=True)
            score = (weighted - probs * inner).astype(LOW)
            value_total[...] += dot(probs.astype(LOW), jnp.where(mine, grad, zero))
            key_total[...] += dot(score, jnp.where(mine, both, zero))
            padded[head, HALF_ROWS : HALF_ROWS + rows, :] = score
            part = dot(score, keys[head], TN)
            parts.append(part)
            columns = jnp.sum(part, axis=0, keepdims=True)
            spare = HEAD_DIM * (1 - head) + 1 + number
            close = padded[head, pl.ds(start, 2 * QUERY_ROWS), :].astype(WIDE)
            quarter = [close[HALF_ROWS * step : HALF_ROWS * (step + 1)] for step in range(4)]
            for step in range(3):
                tiles[head, step] += quarter[step][:, :HALF_ROWS] + quarter[step + 1][:, HALF_ROWS:]
            left = jnp.sum(quarter[0][:, HALF_ROWS:], axis=0, keepdims=True)
            right = jnp.sum(quarter[3][:, :HALF_ROWS], axis=0, keepdims=True)
            left = left + jnp.where(spot == spare, columns, 0.0)
            right = right + jnp.where(spot == spare + blocks, columns, 0.0)
            sums_ref[0, 4 * head + 2 : 4 * head + 3, :] += left
            sums_ref[0, 4 * head + 3 : 4 * head + 4, :] += right
        chosen = jnp.where(lane < HEAD_DIM, parts[0], parts[1])
        query_grad_ref[pl.ds(start, QUERY_ROWS), :] = chosen.astype(LOW)
        return carry

    lax.fori_loop(0, blocks, block, 0)
    key_grad_ref[...] = key_total[...].astype(LOW)
    value_grad_ref[...] = value_total[...].astype(LOW)
    shape = (HALF_ROWS, HALF_ROWS)
    upper = lax.broadcasted_iota(jnp.int32, shape, 0) <= lax.broadcasted_iota(jnp.int32, shape, 1)
    for head in range(2):
        before, centre, behind = (tiles[head, step] for step in range(3))
        sums_ref[0, 4 * head : 4 * head + 1, :] = diagonal_sums(jnp.where(upper, centre, before))
        sums_ref[0, 4 * head + 1 : 4 * head + 2, :] = diagonal_sums(jnp.where(upper, behind, centre))
        left = jnp.sum(jnp.where(upper, before, 0.0), axis=0, keepdims=True)
        right = jnp.sum(jnp.where(upper, 0.0, behind), axis=0, keepdims=True)
        sums_ref[0, 4 * head + 2 : 4 * head + 3, :] += left
        sums_ref[0, 4 * head + 3 : 4 * head + 4, :] += right


def attend_grad(length, query, key, value, grad, logs, near):
    rows, width = query.shape
    pairs = width // LANES
    smem = pl.BlockSpec(memory_space=pltpu.SMEM)
    columns = pl.BlockSpec((rows, LANES), lambda pair: (0, pair))
    shape = jax.ShapeDtypeStruct
    return pl.pallas_call(
        attend_grad_kernel,
        grid=(pairs,),
        in_specs=[smem, columns, columns, columns, columns]
        + [pl.BlockSpec((1, 2, rows), lambda pair: (pair, 0, 0))]
        + [pl.BlockSpec((2, 1, 2 * QUERY_ROWS), lambda pair: (pair, 0, 0))],
        out_specs=[columns, columns, columns] + [pl.BlockSpec((1, 8, LANES), lambda pair: (pair, 0, 0))],
        out_shape=[shape((rows, width), LOW)] * 3 + [shape((pairs, 8, LANES), WIDE)],
        scratch_shapes=[
            pltpu.VMEM((2, 2 * rows - QUERY_ROWS, QUERY_ROWS), WIDE),
            pltpu.VMEM((2, rows, LANES), LOW),
            pltpu.VMEM((2, rows, LANES), LOW),
            pltpu.VMEM((2, rows + QUERY_ROWS, QUERY_ROWS), LOW),
            pltpu.VMEM((rows, LANES), WIDE),
            pltpu.VMEM((rows, LANES), WIDE),
            pltpu.VMEM((2, 3, HALF_ROWS, HALF_ROWS), WIDE),
        ],
        compiler_params=pltpu.CompilerParams(vmem_limit_bytes=48 << 20),
        cost_estimate=pl.CostEstimate(
            flops=44 * rows * rows * width, bytes_accessed=14 * rows * width, transcendentals=2 * pairs * rows * rows
        ),
        name="attend_grad",
    )(length, query, key, value, grad, logs, near)


def bucket_sums(sums):
    side = np.arange(LANES)
    far = np.full((LANES,), 2 * HALF_ROWS)
    chosen = bucket_columns(np.concatenate([-side, HALF_ROWS - side, -far, far]))
    return lax.dot_general(
        jnp.asarray(chosen), sums, NT, precision=lax.Precision.HIGHEST, preferred_element_type=WIDE
    )


def feed_kernel(pieces, normed_ref, grad_ref, *refs):
    moved = pieces > 1
    kinds = 2
    mine, refs = (refs[:kinds], refs[kinds:])
    if moved:
        wholes, refs = (refs[:kinds], refs[kinds:])
    parts, refs = (refs[:kinds], refs[kinds:])
    out_ref, back_ref = refs[:2]
    refs = refs[2:]
    if moved:
        fars, refs = (refs[:kinds], refs[kinds:])
    slots, stages, refs = (refs[:2], refs[2:4], refs[4:])
    arrived, stored = refs[:2]
    step, steps = (pl.program_id(0), pl.num_programs(0))
    unit = slots[0].shape[1]
    slot = lax.rem(step, 2)

    if moved:
        sems = refs[2]
        half = unit // 2
        moves = []
        for kind in range(kinds):
            for place, (bit, came) in enumerate(((ALONG_X, ALONG_Y), (ALONG_Y, ALONG_X))):
                there = pl.ds(place * half, half)
                source = wholes[kind].at[chip_of(came), there]
                moves.append(send(source, fars[kind].at[there], sems, 2 * kind + place, bit))
        sources = [
            mine,
            [one.at[chip_of(ALONG_X)] for one in wholes],
            [one.at[chip_of(ALONG_Y)] for one in wholes],
            fars,
        ]
        places = [chip_of(), chip_of(ALONG_X), chip_of(ALONG_Y), chip_of(ALONG_X, ALONG_Y)]

        def fetch(block, into):
            for number, pair in enumerate(sources):

                @pl.when(block == number)
                def _():
                    for kind in range(kinds):
                        pltpu.make_async_copy(pair[kind], slots[kind].at[into], arrived.at[kind, into]).start()

        def store(block, kind, from_slot, act):
            for number, place in enumerate(places):

                @pl.when(block == number)
                def _():
                    act(
                        pltpu.make_async_copy(
                            stages[kind].at[from_slot],
                            parts[kind].at[pl.ds(pl.multiple_of(place * unit, unit), unit)],
                            stored.at[kind, from_slot],
                        )
                    )
    else:

        def fetch(block, into):
            rows = pl.ds(pl.multiple_of(block * unit, unit), unit)
            for kind in range(kinds):
                pltpu.make_async_copy(mine[kind].at[rows], slots[kind].at[into], arrived.at[kind, into]).start()

        def store(block, kind, from_slot, act):
            rows = pl.ds(pl.multiple_of(block * unit, unit), unit)
            act(pltpu.make_async_copy(stages[kind].at[from_slot], parts[kind].at[rows], stored.at[kind, from_slot]))

    @pl.when(step == 0)
    def _():
        if moved:
            greet((ALONG_X, ALONG_Y))
            for one in moves:
                one.start()
        fetch(0, 0)
        out_ref[...] = jnp.zeros_like(out_ref)
        back_ref[...] = jnp.zeros_like(back_ref)

    @pl.when(step + 1 < steps - moved)
    def _():
        fetch(step + 1, 1 - slot)

    for kind in range(kinds):
        pltpu.make_async_copy(slots[kind].at[slot], slots[kind].at[slot], arrived.at[kind, slot]).wait()
    up, down = (slots[0][slot], slots[1][slot])
    normed, grad = (normed_ref[...], grad_ref[...])
    active, slope = gelu_parts(dot(normed, up, NT))
    active = active.astype(LOW)
    pre_grad = (dot(grad, down, NT) * slope).astype(LOW)
    out_ref[...] += dot(active, down)
    back_ref[...] += dot(pre_grad, up)

    @pl.when(step >= 2)
    def _():
        for kind in range(kinds):
            store(step - 2, kind, slot, lambda copy: copy.wait())

    stages[0][slot] = dot(pre_grad, normed, TN).astype(LOW)
    stages[1][slot] = dot(active, grad, TN).astype(LOW)
    for kind in range(kinds):
        store(step, kind, slot, lambda copy: copy.start())

    if moved:

        @pl.when(step == steps - 2)
        def _():
            for one in moves:
                one.wait()
            fetch(step + 1, 1 - slot)

    @pl.when(step == steps - 1)
    def _():
        for kind in range(kinds):
            store(step - 1, kind, 1 - slot, lambda copy: copy.wait())
            store(step, kind, slot, lambda copy: copy.wait())


def feed(normed, grad, mine, wholes=()):
    rows, width = normed.shape
    moved = bool(wholes)
    unit = mine[0].shape[0] if moved else mine[0].shape[0] // 4
    anywhere = pl.BlockSpec(memory_space=pl.ANY)
    fixed = pl.BlockSpec((rows, width), lambda step: (0, 0))
    return pl.pallas_call(
        functools.partial(feed_kernel, 4 if moved else 1),
        grid=(4,),
        in_specs=[fixed, fixed] + [anywhere] * (4 if moved else 2),
        out_specs=[anywhere, anywhere, fixed, fixed] + ([anywhere, anywhere] if moved else []),
        out_shape=[jax.ShapeDtypeStruct((4 * unit, width), LOW)] * 2
        + [jax.ShapeDtypeStruct((rows, width), WIDE)] * 2
        + ([jax.ShapeDtypeStruct((unit, width), LOW)] * 2 if moved else []),
        scratch_shapes=[pltpu.VMEM((2, unit, width), LOW)] * 4
        + [pltpu.SemaphoreType.DMA((2, 2)), pltpu.SemaphoreType.DMA((2, 2))]
        + ([pltpu.SemaphoreType.DMA((2, 4))] if moved else []),
        compiler_params=pltpu.CompilerParams(
            vmem_limit_bytes=56 << 20,
            **({"collective_id": 2, "has_side_effects": True} if moved else {}),
        ),
        cost_estimate=pl.CostEstimate(
            flops=48 * unit * rows * width,
            bytes_accessed=32 * unit * width + 12 * rows * width,
            transcendentals=8 * unit * rows,
        ),
        name="feed",
    )(normed, grad, *mine, *wholes)[:4]


def push(source, target, sems, number, place, index):
    return pltpu.make_async_remote_copy(
        src_ref=source,
        dst_ref=target,
        send_sem=sems.at[(0,) + number],
        recv_sem=sems.at[(1,) + number],
        device_id={"seq": place, "fsdp": index},
        device_id_type=pl.DeviceIdType.MESH,
    )


def greet_column(depth):
    barrier = pltpu.get_barrier_semaphore()
    place, index = (lax.axis_index("seq"), lax.axis_index("fsdp"))

    def signal(there, which):
        pl.semaphore_signal(
            barrier, inc=1, device_id={"seq": there, "fsdp": which}, device_id_type=pl.DeviceIdType.MESH
        )

    signal(place, partner(ALONG_X))
    signal(place, partner(ALONG_Y))
    signal(place, partner(CORE))
    for step in range(1, depth):
        signal(lax.rem(place + step, depth), index)
        signal(lax.rem(place + step, depth), partner(CORE))
    pl.semaphore_wait(barrier, 2 * depth + 1)


def add_rows(target, source):
    target[...] = (target[...].astype(WIDE) + source[...].astype(WIDE)).astype(LOW)


def backward_kernel(
    depth,
    length_ref,
    query_ref,
    key_ref,
    value_ref,
    grad_ref,
    log_ref,
    near_ref,
    normed_ref,
    weight_ref,
    source_ref,
    hidden_ref,
    gain_ref,
    small_ref,
    output_ref,
    layer_ref,
    up_ref,
    down_ref,
    layer_out_ref,
    input_grad_ref,
    heads_out_ref,
    units_out_ref,
    small_out_ref,
    bias,
    spare,
    keys,
    values,
    padded,
    key_total,
    value_total,
    tiles,
    lows,
    part,
    x_block,
    y_block,
    x_came,
    y_came,
    x_last,
    y_last,
    heads_came,
    units,
    units_came,
    units_last,
    units_far,
    fold_sent,
    fold_came,
    row_sent,
    row_came,
    small,
    small_came,
    swap_sems,
    first_sems,
    second_sems,
    third_sems,
    unit_first_sems,
    unit_second_sems,
    unit_third_sems,
    fold_sems,
    row_sems,
    layer_sems,
    small_sems,
    local_sems,
):
    rows = query_ref.shape[0]
    width = normed_ref.shape[1]
    inner = query_ref.shape[1]
    held = depth // 2
    step = pl.program_id(0)
    last = depth - 1
    place, index = (lax.axis_index("seq"), lax.axis_index("fsdp"))
    core, x, y = (lax.rem(index, 2), lax.rem(index // 2, 2), index // 4)
    column = index - core

    def owner(block):
        return lax.rem(place + 1 + block, depth)

    def beside(source, target, sems, number, bit):
        return push(source, target, sems, number, place, partner(bit))


    def row_moves(source, target, sems, piece, started=True):
        there, which = (core * held + piece, column + place // held)
        slot = lax.rem(place, held)
        home = (there == place) & (which == index)

        @pl.when(home)
        def _():
            move = pltpu.make_async_copy(source, target.at[slot], sems.at[1, piece, slot])
            if started:
                move.start()

        @pl.when(jnp.logical_not(home))
        def _():
            move = push(source, target.at[slot], sems, (piece, slot), there, which)
            if started:
                move.start()
            else:
                move.wait_send()

    def rows_came(target, sems):
        for slot in range(held):
            number = (lax.rem(place, held), slot)
            push(target.at[slot], target.at[slot], sems, number, place, partner(CORE)).wait_recv()


    def unit_sources(block):
        return (
            (up_ref.at[owner(block), :, 1 - x], up_ref.at[owner(block), :, x], ALONG_X),
            (down_ref.at[owner(block), 1 - y], down_ref.at[owner(block), y], ALONG_Y),
        )

    def units_start(block):
        for kind, (away, own, bit) in enumerate(unit_sources(block)):
            beside(away, units_came.at[kind, block], unit_first_sems, (kind, block), bit).start()
            pltpu.make_async_copy(own, units.at[kind, block], local_sems.at[kind, block]).start()

    def unit_seconds(block):
        return (
            (units.at[0, block, 1 - y], units.at[0, block, y], ALONG_Y),
            (units.at[1, block, 1 - x], units.at[1, block, x], ALONG_X),
        )

    def units_first(block):
        for kind, (away, own, bit) in enumerate(unit_sources(block)):
            pltpu.make_async_copy(own, units.at[kind, block], local_sems.at[kind, block]).wait()
            beside(away, units_came.at[kind, block], unit_first_sems, (kind, block), bit).wait()
            add_rows(units.at[kind, block], units_came.at[kind, block])
        for kind, (away, own, bit) in enumerate(unit_seconds(block)):
            beside(away, units_last.at[kind, block], unit_second_sems, (kind, block), bit).start()

    def unit_thirds(block):
        return [
            push(own, units_far.at[block, kind], unit_third_sems, (kind, block), owner(block), index)
            for kind, (away, own, bit) in enumerate(unit_seconds(block))
        ]

    def units_second(block, mine=False):
        for kind, (away, own, bit) in enumerate(unit_seconds(block)):
            beside(away, units_last.at[kind, block], unit_second_sems, (kind, block), bit).wait()
            add_rows(own, units_last.at[kind, block])
        if not mine:
            for one in unit_thirds(block):
                one.start()


    def swaps(block):
        moves = [
            beside(part.at[kind, :, 1 - core], x_block.at[block, :, core, kind], swap_sems, (kind, block), CORE)
            for kind in range(2)
        ]
        moves.append(beside(part.at[2, :, 1 - core], y_block.at[block, core, :, 0], swap_sems, (2, block), CORE))
        return moves

    def output_copy(block):
        return pltpu.make_async_copy(output_ref.at[owner(block)], y_block.at[block, :, :, 1], local_sems.at[2, block])

    def firsts(block):
        return (
            beside(x_block.at[block, 1 - x], x_came.at[block], first_sems, (0, block), ALONG_X),
            beside(y_block.at[block, 1 - y], y_came.at[block], first_sems, (1, block), ALONG_Y),
        )

    def seconds(block):
        return (
            beside(x_block.at[block, x, 1 - y], x_last.at[block], second_sems, (0, block), ALONG_Y),
            beside(y_block.at[block, y, 1 - x], y_last.at[block], second_sems, (1, block), ALONG_X),
        )

    def thirds(block):
        return [
            push(own, heads_came.at[block, kind], third_sems, (kind, block), owner(block), index)
            for kind, own in enumerate((x_block.at[block, x, y], y_block.at[block, y, x]))
        ]

    def heads_start(block):
        for one in swaps(block):
            one.wait_recv()
        output_copy(block).wait()
        for one in firsts(block):
            one.start()

    def heads_first(block):
        for one in firsts(block):
            one.wait()
        add_rows(x_block.at[block, x], x_came.at[block])
        add_rows(y_block.at[block, y], y_came.at[block])
        for one in seconds(block):
            one.start()

    def heads_second(block, mine=False):
        for one in seconds(block):
            one.wait()
        add_rows(x_block.at[block, x, y], x_last.at[block])
        add_rows(y_block.at[block, y, x], y_last.at[block])
        if not mine:
            for one in thirds(block):
                one.start()

    @pl.when(step == 0)
    def _():
        greet_column(depth)
        for block in range(depth):
            units_start(block)
        for block in range(depth):
            output_copy(block).start()
        for piece in range(held):
            row_moves(layer_ref.at[piece], layer_out_ref, layer_sems, piece)
        spare[...] = spare_lanes(length_ref[0], rows)
        for head in range(2):
            padded[head, :HALF_ROWS, :] = jnp.zeros((HALF_ROWS, QUERY_ROWS), LOW)
            padded[head, rows + HALF_ROWS :, :] = jnp.zeros((HALF_ROWS, QUERY_ROWS), LOW)

    @pl.when(step >= 1)
    def _():
        units_first(step - 1)

    @pl.when(step >= 2)
    def _():
        units_second(step - 2)

    pair = owner(step)
    lanes = pl.ds(pl.multiple_of(pair * LANES, LANES), LANES)
    split_heads(key_ref[:, lanes], spare[...], keys)
    split_heads(value_ref[:, lanes], jnp.zeros((rows, LANES), LOW), values)
    near_start = rows - QUERY_ROWS - HALF_ROWS
    near_end = near_start + 2 * QUERY_ROWS
    for head in range(2):
        line = near_ref[2 * pair + head]
        bias[head, :near_start, :] = jnp.broadcast_to(line[:, :1], (near_start, QUERY_ROWS))
        bias[head, near_start:near_end, :] = near_block(line).T
        bias[head, near_end:, :] = jnp.broadcast_to(line[:, -1:], (bias.shape[1] - near_end, QUERY_ROWS))
    key_total[...] = jnp.zeros_like(key_total)
    value_total[...] = jnp.zeros_like(value_total)
    tiles[...] = jnp.zeros_like(tiles)
    sums = small.at[0, pl.ds(pl.multiple_of(16 + 8 * pair, 8), 8)]
    sums[...] = jnp.zeros((8, LANES), WIDE)
    spot = lax.broadcasted_iota(jnp.int32, (1, LANES), 1)
    lane = lax.broadcasted_iota(jnp.int32, (QUERY_ROWS, LANES), 1)
    ones = jnp.where(lax.rem(lane, HEAD_DIM) == 0, 1.0, 0.0).astype(LOW)
    zero = jnp.zeros((), LOW)
    blocks = rows // QUERY_ROWS

    def block(number, carry):
        start = pl.multiple_of(number * QUERY_ROWS, QUERY_ROWS)
        offset = pl.multiple_of(rows - QUERY_ROWS - number * QUERY_ROWS, LANES)
        both = query_ref[pl.ds(start, QUERY_ROWS), lanes]
        grad = grad_ref[pl.ds(start, QUERY_ROWS), lanes]
        parts = []
        for head in range(2):
            mine = lane < HEAD_DIM if head == 0 else lane >= HEAD_DIM
            logits = dot(keys[head], jnp.where(mine, both, ones), NT)
            logits = logits + bias[head, pl.ds(offset, rows), :]
            probs = jnp.exp(logits - log_ref[pair, head : head + 1, pl.ds(start, QUERY_ROWS)])
            prob_grad = dot(values[head], grad, NT)
            weighted = probs * prob_grad
            total = jnp.sum(weighted, axis=0, keepdims=True)
            score = (weighted - probs * total).astype(LOW)
            value_total[...] += dot(probs.astype(LOW), jnp.where(mine, grad, zero))
            key_total[...] += dot(score, jnp.where(mine, both, zero))
            padded[head, HALF_ROWS : HALF_ROWS + rows, :] = score
            one = dot(score, keys[head], TN)
            parts.append(one)
            columns = jnp.sum(one, axis=0, keepdims=True)
            first = HEAD_DIM * (1 - head) + 1 + number
            close = padded[head, pl.ds(start, 2 * QUERY_ROWS), :].astype(WIDE)
            quarter = [close[HALF_ROWS * turn : HALF_ROWS * (turn + 1)] for turn in range(4)]
            for turn in range(3):
                tiles[head, turn] += quarter[turn][:, :HALF_ROWS] + quarter[turn + 1][:, HALF_ROWS:]
            left = jnp.sum(quarter[0][:, HALF_ROWS:], axis=0, keepdims=True)
            right = jnp.sum(quarter[3][:, :HALF_ROWS], axis=0, keepdims=True)
            left = left + jnp.where(spot == first, columns, 0.0)
            right = right + jnp.where(spot == first + blocks, columns, 0.0)
            sums[4 * head + 2 : 4 * head + 3, :] += left
            sums[4 * head + 3 : 4 * head + 4, :] += right
        chosen = jnp.where(lane < HEAD_DIM, parts[0], parts[1])
        lows[pl.ds(start, QUERY_ROWS), lanes] = chosen.astype(LOW)
        return carry

    lax.fori_loop(0, blocks, block, 0)
    lows[:, pl.ds(pl.multiple_of(inner + pair * LANES, LANES), LANES)] = key_total[...].astype(LOW)
    lows[:, pl.ds(pl.multiple_of(2 * inner + pair * LANES, LANES), LANES)] = value_total[...].astype(LOW)
    shape = (HALF_ROWS, HALF_ROWS)
    upper = lax.broadcasted_iota(jnp.int32, shape, 0) <= lax.broadcasted_iota(jnp.int32, shape, 1)
    for head in range(2):
        before, centre, behind = (tiles[head, turn] for turn in range(3))
        sums[4 * head : 4 * head + 1, :] = diagonal_sums(jnp.where(upper, centre, before))
        sums[4 * head + 1 : 4 * head + 2, :] = diagonal_sums(jnp.where(upper, behind, centre))
        sums[4 * head + 2 : 4 * head + 3, :] += jnp.sum(jnp.where(upper, before, 0.0), axis=0, keepdims=True)
        sums[4 * head + 3 : 4 * head + 4, :] += jnp.sum(jnp.where(upper, 0.0, behind), axis=0, keepdims=True)

    @pl.when(step >= 1)
    def _():
        for one in swaps(step - 1):
            one.wait_send()

    for kind in range(3):
        columns = lows[:, pl.ds(pl.multiple_of(kind * inner + pair * LANES, LANES), LANES)]
        product = dot(columns, normed_ref[...], TN).astype(LOW)
        part[kind] = product.reshape(part.shape[1:])
    for one in swaps(step):
        one.start()
    for half in range(2):
        for kind in range(2):
            x_block[step, half, core, kind] = part[kind, half, core]
        y_block[step, core, half, 0] = part[2, half, core]

    @pl.when(step >= 1)
    def _():
        heads_start(step - 1)

    @pl.when(step >= 2)
    def _():
        heads_first(step - 2)

    @pl.when(step >= 3)
    def _():
        heads_second(step - 3)

    @pl.when(step == last)
    def _():
        span = rows // 2 // held
        for piece in range(held):
            away = pl.ds(pl.multiple_of((1 - core) * (rows // 2) + piece * span, span), span)
            fold_sent[piece] = dot(lows[away, :], weight_ref[...]).astype(LOW)
            beside(fold_sent.at[piece], fold_came.at[piece], fold_sems, (piece,), CORE).start()
        for one in swaps(last):
            one.wait_send()
        heads_start(last)
        units_first(last)
        units_second(last - 1)
        heads_first(last - 1)
        heads_second(last - 2)

        gain_total = jnp.zeros((1, width), WIDE)
        for piece in range(held):
            here = pl.ds(pl.multiple_of(core * (rows // 2) + piece * span, span), span)
            product = dot(lows[here, :], weight_ref[...])
            beside(fold_sent.at[piece], fold_came.at[piece], fold_sems, (piece,), CORE).wait()
            product = product + fold_came[piece].astype(WIDE)
            local = slice(piece * span, (piece + 1) * span)
            source = source_ref[local, :].astype(WIDE)
            rms = lax.rsqrt(jnp.mean(source * source, axis=1, keepdims=True) + EPSILON)
            scaled = source * rms
            gain_total = gain_total + jnp.sum(product * scaled, axis=0, keepdims=True)
            gained = gain_ref[...] * product
            inside = jnp.mean(gained * scaled, axis=1, keepdims=True)
            row_sent[piece] = (hidden_ref[local, :] + rms * (gained - scaled * inside)).astype(LOW)
            row_moves(row_sent.at[piece], row_came, row_sems, piece)
            if piece == 0:
                heads_first(last)
                units_second(last, True)
                heads_second(last - 1)
        heads_second(last, True)

        for number in range(width // LANES):
            small[0, number : number + 1, :] = gain_total[:, number * LANES : (number + 1) * LANES]
        small[0, 8:16, :] = small_ref[...]
        for turn, bit in enumerate((ALONG_X, ALONG_Y)):
            move = beside(small.at[turn], small_came.at[turn], small_sems, (turn,), bit)
            move.start()
            move.wait()
            small[turn + 1] = small[turn] + small_came[turn]
        moves = [
            push(small.at[2], small_came.at[1 + turn], small_sems, (1 + turn,), lax.rem(place + turn, depth), index)
            for turn in range(1, depth)
        ]
        for one in moves:
            one.start()

        for block in range(last):
            for one in unit_thirds(block) + thirds(block):
                one.wait()
        units_out_ref[0] = units[0, last, y].astype(WIDE) + sum(units_far[one, 0].astype(WIDE) for one in range(depth - 1))
        units_out_ref[1] = units[1, last, x].astype(WIDE) + sum(units_far[one, 1].astype(WIDE) for one in range(depth - 1))
        heads_out_ref[0:2] = x_block[last, x, y].astype(WIDE) + sum(
            heads_came[one, 0].astype(WIDE) for one in range(depth - 1)
        )
        heads_out_ref[2:4] = y_block[last, y, x].astype(WIDE) + sum(
            heads_came[one, 1].astype(WIDE) for one in range(depth - 1)
        )
        for one in moves:
            one.wait()
        small[3] = small[2] + sum(small_came[1 + turn] for turn in range(1, depth))
        move = beside(small.at[3], small_came.at[depth + 1], small_sems, (depth + 1,), CORE)
        move.start()
        move.wait()
        small_out_ref[0] = small[3]
        small_out_ref[1] = small_came[depth + 1]

        for piece in range(held):
            row_moves(layer_ref.at[piece], layer_out_ref, layer_sems, piece, False)
            row_moves(row_sent.at[piece], row_came, row_sems, piece, False)
        rows_came(layer_out_ref, layer_sems)
        rows_came(row_came, row_sems)
        input_grad_ref[...] = row_came[...].astype(WIDE)


def backward(
    length, query, key, value, grad, logs, near, normed, weights, source, hidden, gain, ffn_gain_part, output_part, layer, ups, downs
):
    rows, inner = query.shape
    width = normed.shape[1]
    depth = lax.axis_size("seq")
    held = depth // 2
    span = rows // depth
    slim, thick = (output_part.shape[3], ups.shape[3])
    vmem, anywhere = (pl.BlockSpec(memory_space=pltpu.VMEM), pl.BlockSpec(memory_space=pl.ANY))
    shape = jax.ShapeDtypeStruct
    small_rows = 2 * (width // LANES) + 8 * depth
    sems = [(3, depth), (2, depth), (2, depth), (2, depth), (2, depth), (2, depth), (2, depth)]
    sems += [(held,), (held, held), (held, held), (depth + 2,)]
    return pl.pallas_call(
        functools.partial(backward_kernel, depth),
        grid=(depth,),
        in_specs=[pl.BlockSpec(memory_space=pltpu.SMEM)] + [vmem] * 12 + [anywhere] * 4,
        out_specs=[anywhere] + [vmem] * 4,
        out_shape=[
            shape((held, span, width), LOW),
            shape((held, span, width), WIDE),
            shape((4, slim, width), WIDE),
            shape((2, thick, width), WIDE),
            shape((2, small_rows, LANES), WIDE),
        ],
        scratch_shapes=[
            pltpu.VMEM((2, 2 * rows - QUERY_ROWS, QUERY_ROWS), WIDE),
            pltpu.VMEM((rows, LANES), LOW),
            pltpu.VMEM((2, rows, LANES), LOW),
            pltpu.VMEM((2, rows, LANES), LOW),
            pltpu.VMEM((2, rows + QUERY_ROWS, QUERY_ROWS), LOW),
            pltpu.VMEM((rows, LANES), WIDE),
            pltpu.VMEM((rows, LANES), WIDE),
            pltpu.VMEM((2, 3, HALF_ROWS, HALF_ROWS), WIDE),
            pltpu.VMEM((rows, 3 * inner), LOW),
            pltpu.VMEM((3, 2, 2, slim, width), LOW),
        ]
        + [pltpu.VMEM((depth, 2, 2, 2, slim, width), LOW)] * 2
        + [pltpu.VMEM((depth, 2, 2, slim, width), LOW)] * 2
        + [pltpu.VMEM((depth, 2, slim, width), LOW)] * 2
        + [
            pltpu.VMEM((depth - 1, 2, 2, slim, width), LOW),
            pltpu.VMEM((2, depth, 2, thick, width), LOW),
            pltpu.VMEM((2, depth, 2, thick, width), LOW),
            pltpu.VMEM((2, depth, thick, width), LOW),
            pltpu.VMEM((depth - 1, 2, thick, width), LOW),
        ]
        + [pltpu.VMEM((held, span, width), LOW)] * 4
        + [pltpu.VMEM((4, small_rows, LANES), WIDE), pltpu.VMEM((depth + 2, small_rows, LANES), WIDE)]
        + [pltpu.SemaphoreType.DMA((2,) + one) for one in sems]
        + [pltpu.SemaphoreType.DMA((3, depth))],
        compiler_params=pltpu.CompilerParams(
            vmem_limit_bytes=62 << 20, collective_id=3, has_side_effects=True
        ),
        cost_estimate=pl.CostEstimate(
            flops=60 * rows * rows * inner, bytes_accessed=14 * rows * inner, transcendentals=rows * rows * inner // 64
        ),
        name="backward",
    )(length, query, key, value, grad, logs, near, normed, weights, source, hidden, gain, ffn_gain_part, output_part, layer, ups, downs)


def flip(value, bit):
    size = lax.axis_size("fsdp")
    return lax.ppermute(value, "fsdp", [(one, one ^ bit) for one in range(size)])


def other_core(value):
    return flip(value, 1)


def after(value, *first):
    return lax.optimization_barrier((value,) + first)[0]


def rounds_of(inverse):
    depth, size = (lax.axis_size("seq"), lax.axis_size("fsdp"))
    held = depth // 2
    rounds = []
    for step in range(held):
        pairs = []
        for place in range(depth):
            for index in range(size):
                target = (index % 2) * held + (place + step) % held
                there = target * size + index - index % 2 + place // held
                here = place * size + index
                pairs.append((there, here) if inverse else (here, there))
        rounds.append(pairs)
    return rounds


def to_sequence(blocks):
    held, span, width = blocks.shape
    place = lax.axis_index("seq")
    out = jnp.zeros((held, span, width), blocks.dtype)
    for step, pairs in enumerate(rounds_of(False)):
        sent = lax.dynamic_index_in_dim(blocks, (place + step) % held, 0, keepdims=False)
        got = lax.ppermute(sent, BOTH, pairs)
        out = lax.dynamic_update_index_in_dim(out, got, (place + held - step) % held, 0)
    return out.reshape(held * span, width)


def to_slots(rows, held):
    span, width = (rows.shape[0] // held, rows.shape[1])
    place = lax.axis_index("seq")
    blocks = rows.reshape(held, span, width)
    out = jnp.zeros(blocks.shape, rows.dtype)
    for step, pairs in enumerate(rounds_of(True)):
        sent = lax.dynamic_index_in_dim(blocks, (place + held - step) % held, 0, keepdims=False)
        got = lax.ppermute(sent, BOTH, pairs)
        out = lax.dynamic_update_index_in_dim(out, got, (place + step) % held, 0)
    return out


def whole(mine, core):
    other = other_core(mine)
    return jnp.where(
        core == 0, jnp.concatenate([mine, other], axis=0), jnp.concatenate([other, mine], axis=0)
    )


def fold(partial, core):
    half = partial.shape[0] // 2
    sent = lax.dynamic_slice_in_dim(partial, (1 - core) * half, half, 0)
    kept = lax.dynamic_slice_in_dim(partial, core * half, half, 0)
    return kept + other_core(sent)


def gather_near(mine):
    return (flip(mine, 2), flip(mine, 4))


def gather_far(beside, above):
    half = beside.shape[0] // 2
    return (flip(above[:half], 2), flip(beside[half:], 4))


def in_order(mine, beside, above, far):
    chip = lax.axis_index("fsdp") // 2
    out = jnp.zeros((4,) + mine.shape, mine.dtype)
    out = lax.dynamic_update_index_in_dim(out, mine, chip, 0)
    out = lax.dynamic_update_index_in_dim(out, beside, chip ^ 1, 0)
    out = lax.dynamic_update_index_in_dim(out, above, chip ^ 2, 0)
    out = lax.dynamic_update_slice(out, far[0][None], (chip ^ 3, 0, 0))
    return lax.dynamic_update_slice(out, far[1][None], (chip ^ 3, mine.shape[0] // 2, 0))


def fast_plane():
    return lax.axis_size("fsdp") == 8 and lax.axis_size("seq") == 4


def own_head_rows(weight, core):
    width = weight.shape[1]
    return lax.dynamic_index_in_dim(weight.reshape(4, 2, -1, width), core, 1, keepdims=False).reshape(-1, width)


def add_low(left, right):
    return (left.astype(WIDE) + right.astype(WIDE)).astype(LOW)


def pick(value, index, axis):
    return lax.dynamic_index_in_dim(value, index, axis, keepdims=False)


def shards(
    inputs,
    lengths,
    cotangent,
    query_weight,
    key_weight,
    value_weight,
    output_weight,
    up_weight,
    down_weight,
    attn_gain,
    ffn_gain,
    bias_table,
):
    held, span, width = inputs.shape
    depth, size = (lax.axis_size("seq"), lax.axis_size("fsdp"))
    place, index = (lax.axis_index("seq"), lax.axis_index("fsdp"))
    core = index % 2
    rows = held * span
    inner = HEADS * HEAD_DIM
    fast = fast_plane()

    near_lengths = jnp.where(
        core == 0,
        jnp.concatenate([lengths, other_core(lengths)]),
        jnp.concatenate([other_core(lengths), lengths]),
    )
    length = lax.dynamic_slice_in_dim(near_lengths, place, 1, 0)
    slots = core * rows + jnp.arange(rows, dtype=jnp.int32)
    mask_rows = (slots < length[0])[:, None].astype(WIDE)

    own_table = lax.dynamic_index_in_dim(bias_table.reshape(BUCKETS, 4, 2, 2), core, 2, keepdims=False)
    own_table = own_table.reshape(BUCKETS, HEADS // 2)
    near = near_bias(own_table)

    ffn = up_weight.shape[0]
    if fast:
        stacked = jnp.concatenate([query_weight, key_weight, value_weight], axis=0)
        cut = jnp.stack([up_weight, down_weight]).reshape(2, 2, 2, -1, width)
        swapped = other_core(pick(cut, 1 - core, 2))
        kept = pick(cut, core, 2)
        cut = jnp.where(
            core == 0, jnp.stack([kept, swapped], axis=1), jnp.stack([swapped, kept], axis=1)
        ).reshape(2, -1, width)
        up_mine, down_mine = (cut[0], cut[1])
        beside, above = gather_near(stacked)
        far = gather_far(beside, above)
        heads_low = in_order(stacked, beside, above, far).reshape(4, 3, -1, width)
        own_three = [heads_low[:, number].reshape(-1, width) for number in range(3)]
    else:
        own_three = [
            own_head_rows(lax.all_gather(one, "fsdp", axis=0, tiled=True), core)
            for one in (query_weight, key_weight, value_weight)
        ]
        full = lax.all_gather(output_weight, "fsdp", axis=0, tiled=True)
        own_output = own_head_rows(full, core)
        far_output = own_head_rows(full, 1 - core)
        own_up, own_down = (
            pick(
                lax.all_gather(one, "fsdp", axis=0, tiled=True).reshape(depth, size // 2, 2, -1, width), core, 2
            ).reshape(-1, width)
            for one in (up_weight, down_weight)
        )

    source_low = to_sequence(inputs)
    source = source_low.astype(WIDE)
    rms_one = lax.rsqrt(jnp.mean(source * source, axis=1, keepdims=True) + EPSILON)
    scaled_one = source * rms_one
    normed_one = whole((scaled_one * attn_gain).astype(LOW), core)
    query, key, value = [dot(normed_one, one, NT).astype(LOW) for one in own_three]
    if fast:
        mine = (output_weight, up_mine, down_mine)
        context, logs, own_output, *wholes = attend(length, query, key, value, near, mine)
        own_output = own_output.reshape(-1, width)
        far_output = other_core(own_output)
        mine = mine[1:]
    else:
        context, logs = attend(length, query, key, value, near)
        mine, wholes = ((own_up, own_down), ())
    near_context = lax.dynamic_slice_in_dim(context, core * rows, rows, 0)
    far_context = other_core(lax.dynamic_slice_in_dim(context, (1 - core) * rows, rows, 0))
    hidden_one = source + (dot(near_context, own_output) + dot(far_context, far_output))
    rms_two = lax.rsqrt(jnp.mean(hidden_one * hidden_one, axis=1, keepdims=True) + EPSILON)
    scaled_two = hidden_one * rms_two
    normed_two = whole((scaled_two * ffn_gain).astype(LOW), core)
    grad_out = to_sequence(cotangent).astype(WIDE) * mask_rows
    grad_low = whole(grad_out.astype(LOW), core)
    up_part, down_part, mlp_part, normed_part = feed(normed_two, grad_low, mine, wholes)
    normed_grad = fold(normed_part, core)
    mlp_out = fold(mlp_part, core)
    layer_rows = ((hidden_one + mlp_out) * mask_rows).astype(LOW)

    gained_two = ffn_gain * normed_grad
    hidden_grad = grad_out + rms_two * (
        gained_two - scaled_two * jnp.mean(gained_two * scaled_two, axis=1, keepdims=True)
    )
    ffn_gain_part = jnp.sum(normed_grad * scaled_two, axis=0)
    hidden_low = hidden_grad.astype(LOW)
    near_grad = dot(hidden_low, own_output, NT).astype(LOW)
    far_grad = other_core(dot(hidden_low, far_output, NT).astype(LOW))
    context_grad = jnp.where(
        core == 0,
        jnp.concatenate([near_grad, far_grad], axis=0),
        jnp.concatenate([far_grad, near_grad], axis=0),
    )
    near_output_part = dot(near_context, hidden_low, TN).astype(LOW)
    far_output_part = dot(far_context, hidden_low, TN).astype(LOW)

    if fast:
        blocks = (depth, 2, 2, -1, width)

        def to_parity(kept, sent):
            return jnp.where(core == 0, jnp.stack([kept, sent], axis=1), jnp.stack([sent, kept], axis=1))

        near_part = near_output_part.reshape(4, 2, 2, -1, width)
        far_part = far_output_part.reshape(4, 2, 2, -1, width)
        got = other_core(jnp.stack([pick(far_part, 1 - core, 2), pick(near_part, 1 - core, 2)]))
        output_part = to_parity(
            add_low(pick(near_part, core, 2), got[0]), add_low(pick(far_part, core, 2), got[1])
        )
        layer_out, input_grad, heads_grad, units_grad, small = backward(
            length,
            query,
            key,
            value,
            context_grad,
            logs,
            near,
            normed_one,
            jnp.concatenate(own_three, axis=0),
            source_low,
            hidden_grad,
            attn_gain[None, :],
            ffn_gain_part.reshape(-1, LANES),
            output_part,
            layer_rows.reshape(held, span, width),
            up_part.reshape(blocks),
            down_part.reshape(blocks),
        )
        query_grad, key_grad, value_grad, output_grad = (heads_grad[number] for number in range(4))
        up_grad, down_grad = (units_grad[0], units_grad[1])
        gain_lines = width // LANES
        gains = (small[0] + small[1])[: 2 * gain_lines].reshape(2, width)
        attn_gain_sum, ffn_gain_sum = (gains[0], gains[1])
        sums = jnp.where(core == 0, small, small[::-1])[:, 2 * gain_lines :]
        sums = jnp.swapaxes(sums.reshape(2, 4, 2, 4 * LANES), 0, 1)
        bias_sum = bucket_sums(sums.reshape(HEADS, 4 * LANES))
    else:
        query_low, key_low, value_low, distance_sums = attend_grad(
            length, query, key, value, context_grad, logs, near
        )
        lows = (query_low, key_low, value_low)
        normed_one_grad = dot(query_low, own_three[0]) + dot(key_low, own_three[1]) + dot(value_low, own_three[2])
        normed_one_grad = fold(normed_one_grad, core)
        three_parts = [dot(one, normed_one, TN).astype(LOW) for one in lows]
        gained_one = attn_gain * normed_one_grad
        input_grad = hidden_grad + rms_one * (
            gained_one - scaled_one * jnp.mean(gained_one * scaled_one, axis=1, keepdims=True)
        )
        attn_gain_part = jnp.sum(normed_one_grad * scaled_one, axis=0)
        input_grad = to_slots(input_grad.astype(LOW), held).astype(WIDE)
        layer_out = to_slots(layer_rows, held)

        def summed(value):
            return lax.psum_scatter(value, BOTH, scatter_dimension=0, tiled=True).astype(WIDE)

        def own_only(value):
            blank = jnp.zeros_like(value)
            pair = jnp.where(core == 0, jnp.stack([value, blank], axis=1), jnp.stack([blank, value], axis=1))
            return summed(pair.reshape(-1, width))

        up_grad, down_grad = [own_only(one.reshape(depth * (size // 2), -1, width)) for one in (up_part, down_part)]
        query_grad, key_grad, value_grad = [own_only(one.reshape(4, -1, width)) for one in three_parts]
        near_part, far_part = (near_output_part.reshape(4, -1, width), far_output_part.reshape(4, -1, width))
        pair = jnp.where(
            core == 0, jnp.stack([near_part, far_part], axis=1), jnp.stack([far_part, near_part], axis=1)
        )
        output_grad = summed(pair.reshape(-1, width))
        bias_own = bucket_sums(distance_sums.reshape(HEADS // 2, 4 * LANES)).reshape(BUCKETS, 4, 1, 2)
        bias_full = lax.dynamic_update_slice(
            jnp.zeros((BUCKETS, 4, 2, 2), WIDE), bias_own, (0, 0, core, 0)
        ).reshape(BUCKETS, HEADS)
        attn_gain_sum, ffn_gain_sum, bias_sum = lax.psum((attn_gain_part, ffn_gain_part, bias_full), BOTH)

    gain_rows = width // size
    bucket_rows = BUCKETS // size
    attn_gain_grad = lax.dynamic_slice_in_dim(attn_gain_sum, index * gain_rows, gain_rows, 0)
    ffn_gain_grad = lax.dynamic_slice_in_dim(ffn_gain_sum, index * gain_rows, gain_rows, 0)
    bias_grad = lax.dynamic_slice_in_dim(bias_sum, index * bucket_rows, bucket_rows, 0)
    return (
        layer_out,
        input_grad,
        query_grad,
        key_grad,
        value_grad,
        output_grad,
        up_grad,
        down_grad,
        attn_gain_grad,
        ffn_gain_grad,
        bias_grad,
    )


def solution(mesh):
    placed = (
        P("fsdp", "seq", None),
        P("fsdp"),
        P("fsdp", "seq", None),
        P("fsdp", None),
        P("fsdp", None),
        P("fsdp", None),
        P("fsdp", None),
        P("fsdp", None),
        P("fsdp", None),
        P(),
        P(),
        P(),
    )
    return jax.shard_map(
        shards,
        mesh=mesh,
        in_specs=placed,
        out_specs=(
            P("fsdp", "seq", None),
            P("fsdp", "seq", None),
            P(("seq", "fsdp"), None),
            P(("seq", "fsdp"), None),
            P(("seq", "fsdp"), None),
            P(("seq", "fsdp"), None),
            P(("seq", "fsdp"), None),
            P(("seq", "fsdp"), None),
            P("fsdp"),
            P("fsdp"),
            P("fsdp", None),
        ),
        check_vma=False,
    )
```

```python
import functools

import jax
import jax.numpy as jnp
import numpy as np
from jax import lax
from jax.experimental import pallas as pl
from jax.experimental.pallas import tpu as pltpu
from jax.sharding import PartitionSpec as P

HEADS = 16
HEAD_DIM = 64
BUCKETS = 32
NEGATIVE = -1000000000.0
EPSILON = 1e-06
THRESHOLDS = (1, 2, 3, 4, 5, 6, 7, 8, 12, 16, 23, 32, 46, 64, 91)
ROOT_HALF = 0.7071067811865476
NORMAL_PEAK = 0.3989422804014327
LANES = 128
QUERY_ROWS = 256
HALF_ROWS = QUERY_ROWS // 2
LOW = jnp.bfloat16
WIDE = jnp.float32
BOTH = ("seq", "fsdp")

NN = (((1,), (0,)), ((), ()))
NT = (((1,), (1,)), ((), ()))
TN = (((0,), (0,)), ((), ()))


def dot(left, right, dims=NN):
    return lax.dot_general(left, right, dims, preferred_element_type=WIDE)


def inverse_root(value):
    root = lax.rsqrt(value)
    return root * (1.5 - 0.5 * value * root * root)


def gelu_parts(value):
    cumulative = 0.5 * (1.0 + lax.erf(value * ROOT_HALF))
    slope = cumulative + value * jnp.exp(-0.5 * value * value) * NORMAL_PEAK
    return (value * cumulative, slope)


CORE, ALONG_X, ALONG_Y = (1, 2, 4)


def partner(bit):
    index = lax.axis_index("fsdp")
    return index + bit - 2 * bit * ((index // bit) % 2)


def chip_of(*bits):
    index = lax.axis_index("fsdp")
    for bit in bits:
        index = index + bit - 2 * bit * ((index // bit) % 2)
    return index // 2


def send(source, target, sems, number, bit):
    return pltpu.make_async_remote_copy(
        src_ref=source,
        dst_ref=target,
        send_sem=sems.at[0, number],
        recv_sem=sems.at[1, number],
        device_id={"fsdp": partner(bit)},
        device_id_type=pl.DeviceIdType.MESH,
    )


def greet(bits):
    barrier = pltpu.get_barrier_semaphore()
    for bit in bits:
        pl.semaphore_signal(
            barrier, inc=1, device_id={"fsdp": partner(bit)}, device_id_type=pl.DeviceIdType.MESH
        )
    pl.semaphore_wait(barrier, len(bits))


def bucket_columns(distances):
    distances = np.asarray(distances)
    magnitude = sum((np.abs(distances) >= threshold).astype(np.int32) for threshold in THRESHOLDS)
    buckets = magnitude + np.where(distances > 0, BUCKETS // 2, 0)
    return (buckets[None, :] == np.arange(BUCKETS)[:, None]).astype(np.float32)


def near_bias(columns):
    chosen = jnp.asarray(bucket_columns(np.arange(2 * QUERY_ROWS) - HALF_ROWS))
    line = lax.dot_general(columns, chosen, TN, precision=lax.Precision.HIGHEST, preferred_element_type=WIDE)
    return line[:, None, :]


def near_block(line):
    shape = (QUERY_ROWS, 2 * QUERY_ROWS)
    turned = pltpu.roll(jnp.broadcast_to(line, shape), 0, 1, stride=1, stride_axis=0)
    row = lax.broadcasted_iota(jnp.int32, shape, 0)
    column = lax.broadcasted_iota(jnp.int32, shape, 1)
    return jnp.where(column < row, line[:, :1], turned)


def diagonal_sums(tile):
    side = tile.shape[1]
    row = lax.broadcasted_iota(jnp.int32, tile.shape, 0)
    step = 1
    while step < side:
        tile = jnp.where((row // step) % 2 == 1, pltpu.roll(tile, side - step, 1), tile)
        step *= 2
    return jnp.sum(tile, axis=0, keepdims=True)


def spare_lanes(length, rows):
    blocks = rows // QUERY_ROWS
    key = lax.broadcasted_iota(jnp.int32, (rows, LANES), 0)
    lane = lax.rem(lax.broadcasted_iota(jnp.int32, (rows, LANES), 1), HEAD_DIM)
    hidden = jnp.where((lane == 0) & (key >= length), NEGATIVE, 0.0)
    left = (lane >= 1) & (lane <= blocks) & (key < QUERY_ROWS * (lane - 1) - HALF_ROWS)
    start = QUERY_ROWS * (lane - 1 - blocks) + 3 * HALF_ROWS
    right = (lane > blocks) & (lane <= 2 * blocks) & (key >= start)
    return jnp.where(left | right, 1.0, hidden).astype(LOW)


def split_heads(pair, spare, out):
    low_half = lax.broadcasted_iota(jnp.int32, pair.shape, 1) < HEAD_DIM
    out[0] = jnp.where(low_half, pair, spare)
    out[1] = jnp.where(low_half, spare, pair)


def attend_kernel(
    length_ref, query_ref, key_ref, value_ref, near_ref, context_ref, log_ref, bias, keys, values
):
    rows = query_ref.shape[0]
    split_heads(key_ref[...], spare_lanes(length_ref[0], rows), keys)
    split_heads(value_ref[...], jnp.zeros((rows, LANES), LOW), values)
    near_start = rows - QUERY_ROWS - HALF_ROWS
    near_end = near_start + 2 * QUERY_ROWS
    for head in range(2):
        line = near_ref[head]
        bias[head, :, :near_start] = jnp.broadcast_to(line[:, :1], (QUERY_ROWS, near_start))
        bias[head, :, near_start:near_end] = near_block(line)
        bias[head, :, near_end:] = jnp.broadcast_to(line[:, -1:], (QUERY_ROWS, bias.shape[2] - near_end))
    lane = lax.broadcasted_iota(jnp.int32, (QUERY_ROWS, LANES), 1)
    ones = jnp.where(lax.rem(lane, HEAD_DIM) == 0, 1.0, 0.0).astype(LOW)

    def block(number, carry):
        start = pl.multiple_of(number * QUERY_ROWS, QUERY_ROWS)
        offset = pl.multiple_of(rows - QUERY_ROWS - number * QUERY_ROWS, LANES)
        both = query_ref[pl.ds(start, QUERY_ROWS), :]
        total = jnp.zeros((QUERY_ROWS, LANES), WIDE)
        for head in range(2):
            mine = lane < HEAD_DIM if head == 0 else lane >= HEAD_DIM
            logits = dot(jnp.where(mine, both, ones), keys[head], NT)
            logits = logits + bias[head, :, pl.ds(offset, rows)]
            peak = jnp.max(logits, axis=1, keepdims=True)
            exponent = jnp.exp(logits - peak)
            row_sum = jnp.sum(exponent, axis=1, keepdims=True)
            weights_low = (exponent * (1.0 / row_sum)).astype(LOW)
            total = total + dot(weights_low, values[head])
            logs = jnp.broadcast_to(peak + jnp.log(row_sum), (QUERY_ROWS, LANES))
            log_ref[0, head : head + 1, pl.ds(start, QUERY_ROWS)] = logs.T[0:1, :]
        context_ref[pl.ds(start, QUERY_ROWS), :] = total.astype(LOW)
        return carry

    lax.fori_loop(0, rows // QUERY_ROWS, block, 0)


def attend(length, query, key, value, near):
    rows, width = query.shape
    pairs = width // LANES
    smem = pl.BlockSpec(memory_space=pltpu.SMEM)
    columns = pl.BlockSpec((rows, LANES), lambda pair: (0, pair))
    return pl.pallas_call(
        attend_kernel,
        grid=(pairs,),
        in_specs=[smem, columns, columns, columns]
        + [pl.BlockSpec((2, 1, 2 * QUERY_ROWS), lambda pair: (pair, 0, 0))],
        out_specs=[columns, pl.BlockSpec((1, 2, rows), lambda pair: (pair, 0, 0))],
        out_shape=[
            jax.ShapeDtypeStruct((rows, width), LOW),
            jax.ShapeDtypeStruct((pairs, 2, rows), WIDE),
        ],
        scratch_shapes=[
            pltpu.VMEM((2, QUERY_ROWS, 2 * rows - QUERY_ROWS), WIDE),
            pltpu.VMEM((2, rows, LANES), LOW),
            pltpu.VMEM((2, rows, LANES), LOW),
        ],
        compiler_params=pltpu.CompilerParams(vmem_limit_bytes=40 << 20),
        cost_estimate=pl.CostEstimate(
            flops=24 * rows * rows * width, bytes_accessed=8 * rows * width, transcendentals=2 * pairs * rows * rows
        ),
        name="attend",
    )(length, query, key, value, near)


def attend_grad_kernel(
    length_ref,
    query_ref,
    key_ref,
    value_ref,
    grad_ref,
    log_ref,
    near_ref,
    query_grad_ref,
    key_grad_ref,
    value_grad_ref,
    sums_ref,
    bias,
    keys,
    values,
    padded,
    key_total,
    value_total,
    tiles,
):
    rows = query_ref.shape[0]
    blocks = rows // QUERY_ROWS
    split_heads(key_ref[...], spare_lanes(length_ref[0], rows), keys)
    split_heads(value_ref[...], jnp.zeros((rows, LANES), LOW), values)
    near_start = rows - QUERY_ROWS - HALF_ROWS
    near_end = near_start + 2 * QUERY_ROWS
    for head in range(2):
        line = near_ref[head]
        bias[head, :near_start, :] = jnp.broadcast_to(line[:, :1], (near_start, QUERY_ROWS))
        bias[head, near_start:near_end, :] = near_block(line).T
        bias[head, near_end:, :] = jnp.broadcast_to(line[:, -1:], (bias.shape[1] - near_end, QUERY_ROWS))
        padded[head, :HALF_ROWS, :] = jnp.zeros((HALF_ROWS, QUERY_ROWS), LOW)
        padded[head, rows + HALF_ROWS :, :] = jnp.zeros((HALF_ROWS, QUERY_ROWS), LOW)
    key_total[...] = jnp.zeros_like(key_total)
    value_total[...] = jnp.zeros_like(value_total)
    tiles[...] = jnp.zeros_like(tiles)
    sums_ref[...] = jnp.zeros_like(sums_ref)
    spot = lax.broadcasted_iota(jnp.int32, (1, LANES), 1)
    lane = lax.broadcasted_iota(jnp.int32, (QUERY_ROWS, LANES), 1)
    ones = jnp.where(lax.rem(lane, HEAD_DIM) == 0, 1.0, 0.0).astype(LOW)
    zero = jnp.zeros((), LOW)

    def block(number, carry):
        start = pl.multiple_of(number * QUERY_ROWS, QUERY_ROWS)
        offset = pl.multiple_of(rows - QUERY_ROWS - number * QUERY_ROWS, LANES)
        both = query_ref[pl.ds(start, QUERY_ROWS), :]
        grad = grad_ref[pl.ds(start, QUERY_ROWS), :]
        parts = []
        for head in range(2):
            mine = lane < HEAD_DIM if head == 0 else lane >= HEAD_DIM
            logits = dot(keys[head], jnp.where(mine, both, ones), NT)
            logits = logits + bias[head, pl.ds(offset, rows), :]
            probs = jnp.exp(logits - log_ref[0, head : head + 1, pl.ds(start, QUERY_ROWS)])
            prob_grad = dot(values[head], grad, NT)
            weighted = probs * prob_grad
            inner = jnp.sum(weighted, axis=0, keepdims=True)
            score = (weighted - probs * inner).astype(LOW)
            value_total[...] += dot(probs.astype(LOW), jnp.where(mine, grad, zero))
            key_total[...] += dot(score, jnp.where(mine, both, zero))
            padded[head, HALF_ROWS : HALF_ROWS + rows, :] = score
            part = dot(score, keys[head], TN)
            parts.append(part)
            columns = jnp.sum(part, axis=0, keepdims=True)
            spare = HEAD_DIM * (1 - head) + 1 + number
            close = padded[head, pl.ds(start, 2 * QUERY_ROWS), :].astype(WIDE)
            quarter = [close[HALF_ROWS * step : HALF_ROWS * (step + 1)] for step in range(4)]
            for step in range(3):
                tiles[head, step] += quarter[step][:, :HALF_ROWS] + quarter[step + 1][:, HALF_ROWS:]
            left = jnp.sum(quarter[0][:, HALF_ROWS:], axis=0, keepdims=True)
            right = jnp.sum(quarter[3][:, :HALF_ROWS], axis=0, keepdims=True)
            left = left + jnp.where(spot == spare, columns, 0.0)
            right = right + jnp.where(spot == spare + blocks, columns, 0.0)
            sums_ref[0, 4 * head + 2 : 4 * head + 3, :] += left
            sums_ref[0, 4 * head + 3 : 4 * head + 4, :] += right
        chosen = jnp.where(lane < HEAD_DIM, parts[0], parts[1])
        query_grad_ref[pl.ds(start, QUERY_ROWS), :] = chosen.astype(LOW)
        return carry

    lax.fori_loop(0, blocks, block, 0)
    key_grad_ref[...] = key_total[...].astype(LOW)
    value_grad_ref[...] = value_total[...].astype(LOW)
    shape = (HALF_ROWS, HALF_ROWS)
    upper = lax.broadcasted_iota(jnp.int32, shape, 0) <= lax.broadcasted_iota(jnp.int32, shape, 1)
    for head in range(2):
        before, centre, behind = (tiles[head, step] for step in range(3))
        sums_ref[0, 4 * head : 4 * head + 1, :] = diagonal_sums(jnp.where(upper, centre, before))
        sums_ref[0, 4 * head + 1 : 4 * head + 2, :] = diagonal_sums(jnp.where(upper, behind, centre))
        left = jnp.sum(jnp.where(upper, before, 0.0), axis=0, keepdims=True)
        right = jnp.sum(jnp.where(upper, 0.0, behind), axis=0, keepdims=True)
        sums_ref[0, 4 * head + 2 : 4 * head + 3, :] += left
        sums_ref[0, 4 * head + 3 : 4 * head + 4, :] += right


def attend_grad(length, query, key, value, grad, logs, near):
    rows, width = query.shape
    pairs = width // LANES
    smem = pl.BlockSpec(memory_space=pltpu.SMEM)
    columns = pl.BlockSpec((rows, LANES), lambda pair: (0, pair))
    shape = jax.ShapeDtypeStruct
    return pl.pallas_call(
        attend_grad_kernel,
        grid=(pairs,),
        in_specs=[smem, columns, columns, columns, columns]
        + [pl.BlockSpec((1, 2, rows), lambda pair: (pair, 0, 0))]
        + [pl.BlockSpec((2, 1, 2 * QUERY_ROWS), lambda pair: (pair, 0, 0))],
        out_specs=[columns, columns, columns] + [pl.BlockSpec((1, 8, LANES), lambda pair: (pair, 0, 0))],
        out_shape=[shape((rows, width), LOW)] * 3 + [shape((pairs, 8, LANES), WIDE)],
        scratch_shapes=[
            pltpu.VMEM((2, 2 * rows - QUERY_ROWS, QUERY_ROWS), WIDE),
            pltpu.VMEM((2, rows, LANES), LOW),
            pltpu.VMEM((2, rows, LANES), LOW),
            pltpu.VMEM((2, rows + QUERY_ROWS, QUERY_ROWS), LOW),
            pltpu.VMEM((rows, LANES), WIDE),
            pltpu.VMEM((rows, LANES), WIDE),
            pltpu.VMEM((2, 3, HALF_ROWS, HALF_ROWS), WIDE),
        ],
        compiler_params=pltpu.CompilerParams(vmem_limit_bytes=48 << 20),
        cost_estimate=pl.CostEstimate(
            flops=44 * rows * rows * width, bytes_accessed=14 * rows * width, transcendentals=2 * pairs * rows * rows
        ),
        name="attend_grad",
    )(length, query, key, value, grad, logs, near)


def bucket_sums(sums):
    side = np.arange(LANES)
    far = np.full((LANES,), 2 * HALF_ROWS)
    chosen = bucket_columns(np.concatenate([-side, HALF_ROWS - side, -far, far]))
    return lax.dot_general(
        jnp.asarray(chosen), sums, NT, precision=lax.Precision.HIGHEST, preferred_element_type=WIDE
    )


def feed_kernel(normed_ref, grad_ref, up_ref, down_ref, up_part_ref, down_part_ref, out_ref, back_ref):
    @pl.when(pl.program_id(0) == 0)
    def _():
        out_ref[...] = jnp.zeros_like(out_ref)
        back_ref[...] = jnp.zeros_like(back_ref)

    up, down = (up_ref[...], down_ref[...])
    normed, grad = (normed_ref[...], grad_ref[...])
    active, slope = gelu_parts(dot(normed, up, NT))
    active = active.astype(LOW)
    pre_grad = (dot(grad, down, NT) * slope).astype(LOW)
    out_ref[...] += dot(active, down)
    back_ref[...] += dot(pre_grad, up)
    up_part_ref[...] = dot(pre_grad, normed, TN).astype(LOW)
    down_part_ref[...] = dot(active, grad, TN).astype(LOW)


def feed(normed, grad, up, down):
    rows, width = normed.shape
    unit = up.shape[0] // 4
    fixed = pl.BlockSpec((rows, width), lambda step: (0, 0))
    block = pl.BlockSpec((unit, width), lambda step: (step, 0))
    return pl.pallas_call(
        feed_kernel,
        grid=(4,),
        in_specs=[fixed, fixed, block, block],
        out_specs=[block, block, fixed, fixed],
        out_shape=[jax.ShapeDtypeStruct((4 * unit, width), LOW)] * 2
        + [jax.ShapeDtypeStruct((rows, width), WIDE)] * 2,
        compiler_params=pltpu.CompilerParams(vmem_limit_bytes=56 << 20),
        name="feed",
    )(normed, grad, up, down)


def push(source, target, sems, number, place, index, there=None):
    return pltpu.make_async_remote_copy(
        src_ref=source,
        dst_ref=target,
        send_sem=sems.at[(0,) + number],
        recv_sem=sems.at[(1,) + (there or number)],
        device_id={"seq": place, "fsdp": index},
        device_id_type=pl.DeviceIdType.MESH,
    )


def greet_column(depth):
    barrier = pltpu.get_barrier_semaphore()
    place, index = (lax.axis_index("seq"), lax.axis_index("fsdp"))

    def signal(there, which):
        pl.semaphore_signal(
            barrier, inc=1, device_id={"seq": there, "fsdp": which}, device_id_type=pl.DeviceIdType.MESH
        )

    signal(place, partner(ALONG_X))
    signal(place, partner(ALONG_Y))
    signal(place, partner(CORE))
    for step in range(1, depth):
        signal(lax.rem(place + step, depth), index)
        signal(lax.rem(place + step, depth), partner(CORE))
    pl.semaphore_wait(barrier, 2 * depth + 1)


def slots_moves(source, target, sems, depth, act):
    held = depth // 2
    place, index = (lax.axis_index("seq"), lax.axis_index("fsdp"))
    core = lax.rem(index, 2)
    slot = lax.rem(place, held)
    for sequence in range(held):
        there, which = (core * held + sequence, index - core + place // held)
        home = (there == place) & (which == index)

        @pl.when(home)
        def _():
            if act == "start":
                pltpu.make_async_copy(source.at[sequence], target.at[slot], sems.at[1, slot]).start()

        @pl.when(jnp.logical_not(home))
        def _():
            move = push(source.at[sequence], target.at[slot], sems, (sequence,), there, which, (slot,))
            if act == "start":
                move.start()
            else:
                move.wait_send()


def slots_came(target, sems, slot):
    push(target.at[slot], target.at[slot], sems, (slot,), lax.axis_index("seq"), partner(CORE)).wait_recv()


def enter_kernel(
    depth,
    inputs_ref,
    query_ref,
    key_ref,
    value_ref,
    up_ref,
    down_ref,
    gain_ref,
    normed_out_ref,
    query_out_ref,
    key_out_ref,
    value_out_ref,
    source_out_ref,
    weights_out_ref,
    up_out_ref,
    down_out_ref,
    normed_ref,
    source_ref,
    weights_ref,
    slot_sems,
    near_sems,
    far_sems,
    cut_sems,
    row_sems,
    local_sems,
):
    held = depth // 2
    span = source_ref.shape[1]
    rows = normed_ref.shape[0]
    index = lax.axis_index("fsdp")
    core = lax.rem(index, 2)
    chip = chip_of()
    mine = (query_ref, key_ref, value_ref)
    half = query_ref.shape[0] // 2
    greet_column(depth)
    slots_moves(inputs_ref, source_ref, slot_sems, depth, "start")
    direct = [
        send(one, weights_ref.at[chip, kind], near_sems, 2 * kind + turn, bit)
        for kind, one in enumerate(mine)
        for turn, bit in enumerate((ALONG_X, ALONG_Y))
    ]
    for one in direct:
        one.start()
    local = [
        pltpu.make_async_copy(one, weights_ref.at[chip, kind], local_sems.at[kind]) for kind, one in enumerate(mine)
    ]
    cuts = []
    for kind, (whole_one, out) in enumerate(((up_ref, up_out_ref), (down_ref, down_out_ref))):
        cuts.append(send(whole_one.at[:, 1 - core], out.at[core], cut_sems, kind, CORE))
        local.append(pltpu.make_async_copy(whole_one.at[:, core], out.at[core], local_sems.at[3 + kind]))
    for one in cuts + local:
        one.start()
    for one in direct:
        one.wait_recv()
    onward = []
    for turn, (bit, came) in enumerate(((ALONG_X, ALONG_Y), (ALONG_Y, ALONG_X))):
        piece = weights_ref.at[chip_of(came), :, pl.ds(turn * half, half)]
        onward.append(send(piece, piece, far_sems, turn, bit))
    for one in onward:
        one.start()

    moves = []
    for slot in range(held):
        slots_came(source_ref, slot_sems, slot)
        source = source_ref[slot].astype(WIDE)
        rms = inverse_root(jnp.mean(source * source, axis=1, keepdims=True) + EPSILON)
        here = pl.ds(pl.multiple_of(core * (rows // 2) + slot * span, span), span)
        normed_ref[here, :] = (source * rms * gain_ref[...]).astype(LOW)
        moves.append(send(normed_ref.at[here], normed_ref.at[here], row_sems, slot, CORE))
        moves[-1].start()
    for one in moves:
        one.wait()
    for one in local[:3]:
        one.wait()

    def project(number):
        weight = weights_ref[number].reshape(-1, weights_ref.shape[3])
        product = dot(normed_ref[...], weight, NT).astype(LOW)
        lanes = pl.ds(pl.multiple_of(number * LANES, LANES), LANES)
        for kind, out in enumerate((query_out_ref, key_out_ref, value_out_ref)):
            out[:, lanes] = product[:, kind * LANES : (kind + 1) * LANES]

    def some(turn, carry):
        project(lax.rem(chip + turn, 4))
        return carry

    for one in onward:
        one.wait()
    stored = [
        pltpu.make_async_copy(one, there, local_sems.at[5 + number])
        for number, (one, there) in enumerate(
            ((normed_ref, normed_out_ref), (source_ref, source_out_ref), (weights_ref, weights_out_ref))
        )
    ]
    for one in stored:
        one.start()
    lax.fori_loop(0, 4, some, 0)
    for one in stored:
        one.wait()
    for one in direct:
        one.wait_send()
    for one in cuts + local[3:]:
        one.wait()
    slots_moves(inputs_ref, source_ref, slot_sems, depth, "end")


def enter(inputs, projections, up, down, gain):
    held, span, width = inputs.shape
    depth = lax.axis_size("seq")
    rows = 2 * held * span
    slim = projections[0].shape[0]
    thick = up.shape[0] // 4
    vmem, anywhere = (pl.BlockSpec(memory_space=pltpu.VMEM), pl.BlockSpec(memory_space=pltpu.HBM))
    shape = jax.ShapeDtypeStruct
    return pl.pallas_call(
        functools.partial(enter_kernel, depth),
        in_specs=[anywhere] * 6 + [vmem],
        out_specs=[anywhere] + [vmem] * 3 + [anywhere] * 4,
        out_shape=[shape((rows, width), LOW)]
        + [shape((rows, 4 * slim), LOW)] * 3
        + [shape((held, span, width), LOW), shape((4, 3, slim, width), LOW)]
        + [shape((2, 2, thick, width), LOW)] * 2,
        scratch_shapes=[
            pltpu.VMEM((rows, width), LOW),
            pltpu.VMEM((held, span, width), LOW),
            pltpu.VMEM((4, 3, slim, width), LOW),
            pltpu.SemaphoreType.DMA((2, held)),
            pltpu.SemaphoreType.DMA((2, 6)),
            pltpu.SemaphoreType.DMA((2, 2)),
            pltpu.SemaphoreType.DMA((2, 2)),
            pltpu.SemaphoreType.DMA((2, held)),
            pltpu.SemaphoreType.DMA((8,)),
        ],
        compiler_params=pltpu.CompilerParams(vmem_limit_bytes=62 << 20, collective_id=4, has_side_effects=True),
        cost_estimate=pl.CostEstimate(flops=24 * rows * slim * width, bytes_accessed=16 << 20, transcendentals=0),
        name="enter",
    )(inputs, *projections, up.reshape(2, 2, thick, width), down.reshape(2, 2, thick, width), gain)


def through_kernel(
    depth,
    length_ref,
    query_ref,
    key_ref,
    value_ref,
    near_ref,
    source_ref,
    gain_ref,
    output_ref,
    up_ref,
    down_ref,
    cotangent_ref,
    log_ref,
    context_ref,
    hidden_ref,
    far_context_out_ref,
    own_output_out_ref,
    far_output_out_ref,
    normed_ref,
    grad_ref,
    ups_ref,
    downs_ref,
    bias,
    keys,
    values,
    context,
    came,
    far_context_ref,
    own_output_ref,
    far_output_ref,
    normed,
    grad,
    slot_sems,
    near_sems,
    far_sems,
    core_sems,
    context_sems,
    local,
):
    rows = query_ref.shape[0]
    width = source_ref.shape[1]
    pair = pl.program_id(0)
    last = depth - 1
    held = depth // 2
    core = lax.rem(lax.axis_index("fsdp"), 2)
    chip = chip_of()
    own = pl.ds(pl.multiple_of(core * (rows // 2), rows // 2), rows // 2)
    other = pl.ds(pl.multiple_of((1 - core) * (rows // 2), rows // 2), rows // 2)
    half = output_ref.shape[0] // 2
    direct = []
    unit = up_ref.shape[0] // 2
    for first in (None, 0, unit):
        for one, there in ((output_ref, own_output_ref),) if first is None else ((up_ref, ups_ref), (down_ref, downs_ref)):
            for bit in (ALONG_X, ALONG_Y):
                source, target = (one, there.at[chip])
                if first is not None:
                    source, target = (source.at[pl.ds(first, unit)], target.at[pl.ds(first, unit)])
                direct.append(send(source, target, near_sems, len(direct), bit))
    onward = []
    for turn, (bit, from_bit) in enumerate(((ALONG_X, ALONG_Y), (ALONG_Y, ALONG_X))):
        piece = own_output_ref.at[chip_of(from_bit), pl.ds(turn * half, half)]
        onward.append(send(piece, piece, far_sems, turn, bit))
    keep = pltpu.make_async_copy(output_ref, own_output_ref.at[chip], local.at[0])
    swap = send(own_output_ref, far_output_ref, core_sems, 0, CORE)
    both_cores = [
        (send(one, there.at[own], core_sems, 1 + number, CORE), pltpu.make_async_copy(one, there.at[own], local.at[1 + number]))
        for number, (one, there) in enumerate(((grad, grad_ref), (normed, normed_ref)))
    ]
    stored = [
        pltpu.make_async_copy(one, there, local.at[3 + number])
        for number, (one, there) in enumerate(
            (
                (own_output_ref, own_output_out_ref),
                (far_output_ref, far_output_out_ref),
                (far_context_ref, far_context_out_ref),
            )
        )
    ]

    def context_move(number):
        lanes = pl.ds(pl.multiple_of(number * LANES, LANES), LANES)
        return send(context.at[other, lanes], far_context_ref.at[:, lanes], context_sems, number, CORE)

    @pl.when(pair == 0)
    def _():
        greet_column(depth)
        for one in direct[:4]:
            one.start()
        keep.start()
        slots_moves(cotangent_ref, came, slot_sems, depth, "start")

    @pl.when(pair == 1)
    def _():
        for one in direct[:2]:
            one.wait_recv()
        for one in onward + direct[4:]:
            one.start()

    @pl.when(pair == last)
    def _():
        for one in onward:
            one.wait()
        keep.wait()
        swap.start()
        stored[0].start()
        slot_ids = core * (rows // 2) + lax.broadcasted_iota(jnp.int32, (rows // 2, 1), 0)
        valid = (slot_ids < length_ref[0]).astype(WIDE)
        for slot in range(held):
            slots_came(came, slot_sems, slot)
        grad[...] = (came[...].reshape(rows // 2, width).astype(WIDE) * valid).astype(LOW)
        for one in both_cores[0]:
            one.start()

    lanes = pl.ds(pl.multiple_of(pair * LANES, LANES), LANES)
    split_heads(key_ref[...], spare_lanes(length_ref[0], rows), keys)
    split_heads(value_ref[...], jnp.zeros((rows, LANES), LOW), values)
    near_start = rows - QUERY_ROWS - HALF_ROWS
    near_end = near_start + 2 * QUERY_ROWS
    for head in range(2):
        line = near_ref[head]
        bias[head, :, :near_start] = jnp.broadcast_to(line[:, :1], (QUERY_ROWS, near_start))
        bias[head, :, near_start:near_end] = near_block(line)
        bias[head, :, near_end:] = jnp.broadcast_to(line[:, -1:], (QUERY_ROWS, bias.shape[2] - near_end))
    lane = lax.broadcasted_iota(jnp.int32, (QUERY_ROWS, LANES), 1)
    ones = jnp.where(lax.rem(lane, HEAD_DIM) == 0, 1.0, 0.0).astype(LOW)

    def block(number, carry):
        start = pl.multiple_of(number * QUERY_ROWS, QUERY_ROWS)
        offset = pl.multiple_of(rows - QUERY_ROWS - number * QUERY_ROWS, LANES)
        both = query_ref[pl.ds(start, QUERY_ROWS), :]
        total = jnp.zeros((QUERY_ROWS, LANES), WIDE)
        for head in range(2):
            mine = lane < HEAD_DIM if head == 0 else lane >= HEAD_DIM
            logits = dot(jnp.where(mine, both, ones), keys[head], NT)
            logits = logits + bias[head, :, pl.ds(offset, rows)]
            peak = jnp.max(logits, axis=1, keepdims=True)
            exponent = jnp.exp(logits - peak)
            row_sum = jnp.sum(exponent, axis=1, keepdims=True)
            weights_low = (exponent * (1.0 / row_sum)).astype(LOW)
            total = total + dot(weights_low, values[head])
            logs = jnp.broadcast_to(peak + jnp.log(row_sum), (QUERY_ROWS, LANES))
            log_ref[0, head : head + 1, pl.ds(start, QUERY_ROWS)] = logs.T[0:1, :]
        context[pl.ds(start, QUERY_ROWS), lanes] = total.astype(LOW)
        return carry

    lax.fori_loop(0, rows // QUERY_ROWS, block, 0)
    context_move(pair).start()
    context_ref[:, lanes] = context[own, lanes]

    @pl.when(pair == last)
    def _():
        swap.wait()
        for number in range(last + 1):
            context_move(number).wait()
        for one in stored[1:]:
            one.start()
        inner = context_ref.shape[1]
        attended = dot(context_ref[...], own_output_ref[...].reshape(inner, width))
        attended = attended + dot(far_context_ref[...], far_output_ref[...].reshape(inner, width))
        hidden = source_ref[...].astype(WIDE) + attended
        hidden_ref[...] = hidden
        rms = inverse_root(jnp.mean(hidden * hidden, axis=1, keepdims=True) + EPSILON)
        normed[...] = (hidden * rms * gain_ref[...]).astype(LOW)
        for one in both_cores[1]:
            one.start()
        for one in direct:
            one.wait_send()
        for one in direct[2:]:
            one.wait_recv()
        slots_moves(cotangent_ref, came, slot_sems, depth, "end")
        for one in both_cores[0] + both_cores[1]:
            one.wait()
        for one in stored:
            one.wait()


def through(length, query, key, value, near, source, gain, output, up, down, cotangent):
    rows, inner = query.shape
    held, span, width = cotangent.shape
    depth = lax.axis_size("seq")
    pairs = inner // LANES
    vmem, anywhere = (pl.BlockSpec(memory_space=pltpu.VMEM), pl.BlockSpec(memory_space=pltpu.HBM))
    columns = pl.BlockSpec((rows, LANES), lambda pair: (0, pair))
    shape = jax.ShapeDtypeStruct
    outputs = (4,) + output.shape
    return pl.pallas_call(
        functools.partial(through_kernel, depth),
        grid=(pairs,),
        in_specs=[pl.BlockSpec(memory_space=pltpu.SMEM), columns, columns, columns]
        + [pl.BlockSpec((2, 1, 2 * QUERY_ROWS), lambda pair: (pair, 0, 0)), vmem, vmem]
        + [anywhere] * 4,
        out_specs=[pl.BlockSpec((1, 2, rows), lambda pair: (pair, 0, 0))] + [vmem] * 2 + [anywhere] * 7,
        out_shape=[shape((pairs, 2, rows), WIDE)]
        + [shape((rows // 2, inner), LOW), shape((rows // 2, width), WIDE), shape((rows // 2, inner), LOW)]
        + [shape(outputs, LOW)] * 2
        + [shape((rows, width), LOW)] * 2
        + [shape((4,) + up.shape, LOW)] * 2,
        scratch_shapes=[
            pltpu.VMEM((2, QUERY_ROWS, 2 * rows - QUERY_ROWS), WIDE),
            pltpu.VMEM((2, rows, LANES), LOW),
            pltpu.VMEM((2, rows, LANES), LOW),
            pltpu.VMEM((rows, inner), LOW),
            pltpu.VMEM((held, span, width), LOW),
            pltpu.VMEM((rows // 2, inner), LOW),
            pltpu.VMEM(outputs, LOW),
            pltpu.VMEM(outputs, LOW),
            pltpu.VMEM((rows // 2, width), LOW),
            pltpu.VMEM((rows // 2, width), LOW),
            pltpu.SemaphoreType.DMA((2, held)),
            pltpu.SemaphoreType.DMA((2, 10)),
            pltpu.SemaphoreType.DMA((2, 2)),
            pltpu.SemaphoreType.DMA((2, 3)),
            pltpu.SemaphoreType.DMA((2, pairs)),
            pltpu.SemaphoreType.DMA((6,)),
        ],
        compiler_params=pltpu.CompilerParams(vmem_limit_bytes=62 << 20, collective_id=1, has_side_effects=True),
        cost_estimate=pl.CostEstimate(
            flops=24 * rows * rows * inner, bytes_accessed=8 * rows * inner, transcendentals=2 * pairs * rows * rows
        ),
        name="through",
    )(length, query, key, value, near, source, gain, output, up, down, cotangent)


def row_moves(source, target, sems, depth, piece, started=True):
    held = depth // 2
    place, index = (lax.axis_index("seq"), lax.axis_index("fsdp"))
    core = lax.rem(index, 2)
    there, which = (core * held + piece, index - core + place // held)
    slot = lax.rem(place, held)
    home = (there == place) & (which == index)

    @pl.when(home)
    def _():
        if started:
            pltpu.make_async_copy(source, target.at[slot], sems.at[1, piece, slot]).start()

    @pl.when(jnp.logical_not(home))
    def _():
        move = push(source, target.at[slot], sems, (piece, slot), there, which)
        if started:
            move.start()
        else:
            move.wait_send()


def rows_came(target, sems, depth):
    held = depth // 2
    place = lax.axis_index("seq")
    for slot in range(held):
        number = (lax.rem(place, held), slot)
        push(target.at[slot], target.at[slot], sems, number, place, partner(CORE)).wait_recv()


def middle_kernel(
    depth,
    length_ref,
    normed_ref,
    grad_ref,
    hidden_ref,
    gain_ref,
    output_ref,
    far_output_ref,
    context_ref,
    far_context_ref,
    up_ref,
    down_ref,
    ups_ref,
    downs_ref,
    up_part_ref,
    down_part_ref,
    up_came_ref,
    down_came_ref,
    far_up_ref,
    far_down_ref,
    context_grad_ref,
    hidden_grad_ref,
    layer_ref,
    gain_part_ref,
    output_part_ref,
    near_grad,
    out_total,
    back_total,
    out_came,
    back_came,
    up_slots,
    down_slots,
    up_stages,
    down_stages,
    parts,
    parts_came,
    far_grad,
    arrived,
    stored,
    far_sems,
    unit_sems,
    fold_sems,
    core_sems,
    kept,
):
    rows, width = normed_ref.shape
    mine, wholes, fars = ((up_ref, down_ref), (ups_ref, downs_ref), (far_up_ref, far_down_ref))
    results, came = ((up_part_ref, down_part_ref), (up_came_ref, down_came_ref))
    slots, stages = ((up_slots, down_slots), (up_stages, down_stages))
    kinds = range(2)
    step = pl.program_id(0)
    last = depth - 1
    index = lax.axis_index("fsdp")
    core, x, y = (lax.rem(index, 2), lax.rem(index // 2, 2), index // 4)
    unit = up_slots.shape[1]
    half = unit // 2
    slot = lax.rem(step, 2)
    places = [chip_of(), chip_of(ALONG_X), chip_of(ALONG_Y), chip_of(ALONG_X, ALONG_Y)]

    moves = []
    for kind in kinds:
        for place, (bit, from_bit) in enumerate(((ALONG_X, ALONG_Y), (ALONG_Y, ALONG_X))):
            there = pl.ds(place * half, half)
            source = wholes[kind].at[chip_of(from_bit), there]
            moves.append(send(source, fars[kind].at[there], far_sems, 2 * kind + place, bit))
    sources = [
        mine,
        [one.at[places[1]] for one in wholes],
        [one.at[places[2]] for one in wholes],
        fars,
    ]

    def fetch(block, into):
        for number, pair in enumerate(sources):

            @pl.when(block == number)
            def _():
                for kind in kinds:
                    pltpu.make_async_copy(pair[kind], slots[kind].at[into], arrived.at[kind, into]).start()

    def store(number, kind):
        return pltpu.make_async_copy(
            stages[kind].at[number % 2], results[kind].at[places[number]], stored.at[kind, number % 2]
        )

    def first_sum(number, kind):
        block = places[number]
        if kind == 0:
            source, bit = (results[0].at[block, :, 1 - x], ALONG_X)
        else:
            source, bit = (results[1].at[block, 1 - y], ALONG_Y)
        return send(source, came[kind].at[block], unit_sems, last * kind + number, bit)

    def own_rows(which):
        return pl.ds(pl.multiple_of(which * (rows // 2), rows // 2), rows // 2)

    folds = [
        send(one.at[own_rows(1 - core)], there, fold_sems, number, CORE)
        for number, (one, there) in enumerate(((back_total, back_came), (out_total, out_came)))
    ]

    @pl.when(step == 0)
    def _():
        greet_column(depth)
        for one in moves:
            one.start()
        fetch(0, 0)
        out_total[...] = jnp.zeros_like(out_total)
        back_total[...] = jnp.zeros_like(back_total)

    @pl.when(step + 1 < last)
    def _():
        fetch(step + 1, 1 - slot)

    for number in range(last):

        @pl.when(step == number + 1)
        def _():
            for kind in kinds:
                store(number, kind).wait()
                first_sum(number, kind).start()

    for kind in kinds:
        pltpu.make_async_copy(slots[kind].at[slot], slots[kind].at[slot], arrived.at[kind, slot]).wait()
    up, down = (slots[0][slot], slots[1][slot])
    normed, grad = (normed_ref[...], grad_ref[...])
    active, slope = gelu_parts(dot(normed, up, NT))
    active = active.astype(LOW)
    pre_grad = (dot(grad, down, NT) * slope).astype(LOW)
    back_total[...] += dot(pre_grad, up)
    out_total[...] += dot(active, down)
    shape = up_stages.shape[1:]
    stages[0][slot] = dot(pre_grad, normed, TN).astype(LOW).reshape(shape)
    stages[1][slot] = dot(active, grad, TN).astype(LOW).reshape(shape)
    for number in range(last + 1):

        @pl.when(step == number)
        def _():
            for kind in kinds:
                store(number, kind).start()

    @pl.when(step == last - 1)
    def _():
        for one in moves:
            one.wait()
        fetch(last, last % 2)

    @pl.when(step == last)
    def _():
        for one in folds:
            one.start()
        folds[0].wait()
        normed_grad = back_total[own_rows(core), :] + back_came[...]
        hidden = hidden_ref[...]
        rms = inverse_root(jnp.mean(hidden * hidden, axis=1, keepdims=True) + EPSILON)
        scaled = hidden * rms
        gained = gain_ref[...] * normed_grad
        inside = jnp.mean(gained * scaled, axis=1, keepdims=True)
        hidden_grad = grad_ref[own_rows(core), :].astype(WIDE) + rms * (gained - scaled * inside)
        gain_part_ref[...] = jnp.sum(normed_grad * scaled, axis=0, keepdims=True)
        hidden_grad_ref[...] = hidden_grad
        hidden_low = hidden_grad.astype(LOW)
        far_grad[...] = dot(hidden_low, far_output_ref[...], NT).astype(LOW)
        move = send(far_grad, context_grad_ref.at[own_rows(core)], core_sems, 0, CORE)
        move.start()
        part_shape = parts.shape[1:]
        parts[0] = dot(context_ref[...], hidden_low, TN).astype(LOW).reshape(part_shape)
        parts[1] = dot(far_context_ref[...], hidden_low, TN).astype(LOW).reshape(part_shape)
        others = [
            send(parts.at[kind, :, :, 1 - core], parts_came.at[kind], core_sems, 1 + kind, CORE) for kind in kinds
        ]
        for one in others:
            one.start()
        near_grad[...] = dot(hidden_low, output_ref[...], NT).astype(LOW)
        keep = pltpu.make_async_copy(near_grad, context_grad_ref.at[own_rows(core)], kept)
        keep.start()
        folds[1].wait()
        slot_ids = core * (rows // 2) + lax.broadcasted_iota(jnp.int32, (rows // 2, 1), 0)
        valid = (slot_ids < length_ref[0]).astype(WIDE)
        layer_rows = (hidden + (out_total[own_rows(core), :] + out_came[...])) * valid
        layer_ref[...] = layer_rows.astype(LOW).reshape(layer_ref.shape)
        for one in others:
            one.wait()
        for turn in range(depth):
            near = parts[0, turn, :, core].astype(WIDE) + parts_came[1, turn].astype(WIDE)
            output_part_ref[turn, core] = near.astype(LOW)
            far = parts[1, turn, :, core].astype(WIDE) + parts_came[0, turn].astype(WIDE)
            output_part_ref[turn, 1 - core] = far.astype(LOW)
        for kind in kinds:
            store(last, kind).wait()
        move.wait()
        keep.wait()
        for number in range(last):
            for kind in kinds:
                first_sum(number, kind).wait()


def middle(length, normed, grad, hidden, gain, outputs, contexts, mine, wholes):
    rows, width = normed.shape
    inner = outputs[0].shape[0]
    unit = mine[0].shape[0]
    depth = lax.axis_size("seq")
    held = depth // 2
    thick, slim = (unit // 4, inner // 16)
    vmem, anywhere = (pl.BlockSpec(memory_space=pltpu.VMEM), pl.BlockSpec(memory_space=pltpu.HBM))
    shape = jax.ShapeDtypeStruct
    part = (depth, 2, 2, thick, width)
    return pl.pallas_call(
        functools.partial(middle_kernel, depth),
        grid=(depth,),
        in_specs=[pl.BlockSpec(memory_space=pltpu.SMEM)] + [vmem] * 8 + [anywhere] * 4,
        out_specs=[anywhere] * 7 + [vmem] * 4,
        out_shape=[shape(part, LOW)] * 2
        + [shape((depth, 2, thick, width), LOW)] * 2
        + [shape((unit, width), LOW)] * 2
        + [
            shape((rows, inner), LOW),
            shape((rows // 2, width), WIDE),
            shape((held, rows // depth, width), LOW),
            shape((1, width), WIDE),
            shape((4, 2, 2, slim, width), LOW),
        ],
        scratch_shapes=[pltpu.VMEM((rows // 2, inner), LOW)]
        + [pltpu.VMEM((rows, width), WIDE)] * 2
        + [pltpu.VMEM((rows // 2, width), WIDE)] * 2
        + [pltpu.VMEM((2, unit, width), LOW)] * 2
        + [pltpu.VMEM((2, 2, 2, thick, width), LOW)] * 2
        + [
            pltpu.VMEM((2, 4, 2, 2, slim, width), LOW),
            pltpu.VMEM((2, 4, 2, slim, width), LOW),
            pltpu.VMEM((rows // 2, inner), LOW),
            pltpu.SemaphoreType.DMA((2, 2)),
            pltpu.SemaphoreType.DMA((2, 2)),
            pltpu.SemaphoreType.DMA((2, 4)),
            pltpu.SemaphoreType.DMA((2, 2 * (depth - 1))),
            pltpu.SemaphoreType.DMA((2, 2)),
            pltpu.SemaphoreType.DMA((2, 3)),
            pltpu.SemaphoreType.DMA,
        ],
        compiler_params=pltpu.CompilerParams(vmem_limit_bytes=62 << 20, collective_id=2, has_side_effects=True),
        cost_estimate=pl.CostEstimate(
            flops=52 * unit * rows * width,
            bytes_accessed=32 * unit * width + 12 * rows * width,
            transcendentals=8 * unit * rows,
        ),
        name="middle",
    )(length, normed, grad, hidden, gain, *outputs, *contexts, *mine, *wholes)


def add_rows(target, source):
    target[...] = (target[...].astype(WIDE) + source[...].astype(WIDE)).astype(LOW)


def backward_kernel(
    depth,
    length_ref,
    query_ref,
    key_ref,
    value_ref,
    grad_ref,
    log_ref,
    near_ref,
    normed_ref,
    weight_ref,
    source_ref,
    hidden_ref,
    gain_ref,
    small_ref,
    output_ref,
    layer_ref,
    up_ref,
    down_ref,
    up_came_ref,
    down_came_ref,
    layer_out_ref,
    input_grad_ref,
    heads_out_ref,
    units_out_ref,
    small_out_ref,
    bias,
    spare,
    keys,
    values,
    padded,
    key_total,
    value_total,
    tiles,
    lows,
    part,
    x_block,
    y_block,
    x_came,
    y_came,
    x_last,
    y_last,
    heads_came,
    units,
    units_came,
    units_last,
    units_far,
    fold_sent,
    fold_came,
    row_sent,
    row_came,
    small,
    small_came,
    swap_sems,
    first_sems,
    second_sems,
    third_sems,
    late_sems,
    unit_second_sems,
    unit_third_sems,
    fold_sems,
    row_sems,
    layer_sems,
    small_sems,
    early_sems,
    local_sems,
):
    rows = query_ref.shape[0]
    width = normed_ref.shape[1]
    held = depth // 2
    step = pl.program_id(0)
    last = depth - 1
    place, index = (lax.axis_index("seq"), lax.axis_index("fsdp"))
    core, x, y = (lax.rem(index, 2), lax.rem(index // 2, 2), index // 4)
    column = index - core

    def owner(block):
        return lax.rem(place + 1 + block, depth)

    def beside(source, target, sems, number, bit):
        return push(source, target, sems, number, place, partner(bit))


    def unit_place(hop):
        return chip_of(*(bit for bit in (ALONG_X, ALONG_Y) if hop & (bit // 2)))

    def unit_source(kind, hop):
        block = unit_place(hop)
        if kind == 0:
            return (up_ref.at[block, :, 1 - x], up_ref.at[block, :, x], ALONG_X)
        return (down_ref.at[block, 1 - y], down_ref.at[block, y], ALONG_Y)

    def unit_came(kind, hop):
        return units_came.at[kind, hop]

    def unit_own(kind, hop):
        return pltpu.make_async_copy(unit_source(kind, hop)[1], units.at[kind, hop], local_sems.at[kind, hop])

    def unit_early(kind, hop):
        there = (up_came_ref, down_came_ref)[kind].at[unit_place(hop)]
        return pltpu.make_async_copy(there, units_came.at[kind, hop], early_sems.at[kind, hop])

    def unit_late(kind, hop):
        away, _, bit = unit_source(kind, hop)
        return beside(away, units_came.at[kind, late[kind]], late_sems, (kind,), bit)

    late = (2, 1)

    def units_start():
        for kind in range(2):
            unit_late(kind, 3).start()
        for kind in range(2):
            for hop in range(4):
                unit_own(kind, hop).start()
                if hop != late[kind]:
                    unit_early(kind, hop).start()

    def unit_halves(kind, hop):
        if kind == 0:
            return (units.at[0, hop, 1 - y], units.at[0, hop, y], ALONG_Y)
        return (units.at[1, hop, 1 - x], units.at[1, hop, x], ALONG_X)

    def unit_second(kind, hop):
        away, _, bit = unit_halves(kind, hop)
        there = hop ^ (bit // 2)
        return push(
            away, units_last.at[kind, there], unit_second_sems, (kind, hop), place, partner(bit), (kind, there)
        )

    def unit_first(kind, hop):
        unit_own(kind, hop).wait()
        if hop == late[kind]:
            unit_late(kind, 3).wait()
        else:
            unit_early(kind, hop).wait()
        add_rows(units.at[kind, hop], units_came.at[kind, hop])
        unit_second(kind, hop).start()


    def unit_pass(kind, hop):
        block = unit_place(hop)
        ahead = block > place
        there = jnp.where(ahead, place + 1, place - 1)
        side = jnp.where(ahead, 0, 1)
        own = unit_halves(kind, hop)[1]
        far = units_far.at[kind, block, side]
        return push(own, far, unit_third_sems, (kind, block, 0), there, index, (kind, block, side))

    def unit_arrived(kind, block, side):
        far = units_far.at[kind, block, side]
        return push(far, far, unit_third_sems, (kind, block, side), place, partner(CORE))

    def unit_summed(kind, hop):
        unit_second(kind, hop).wait_send()
        unit_second(kind, hop ^ (2 - kind)).wait_recv()
        add_rows(unit_halves(kind, hop)[1], units_last.at[kind, hop])
        block = unit_place(hop)

        @pl.when(((place == 0) | (place == last)) & (block != place))
        def _():
            unit_pass(kind, hop).start()

    def unit_onward(kind, hop, turn):
        block = unit_place(hop)
        ahead = block > place
        outer = jnp.where(ahead, place, last - place)

        @pl.when((block != place) & (outer == turn + 1))
        def _():
            side = jnp.where(ahead, 0, 1)
            unit_arrived(kind, block, side).wait_recv()
            add_rows(unit_halves(kind, hop)[1], units_far.at[kind, block, side])
            unit_pass(kind, hop).start()

    def unit_finish(kind, hop):
        block = unit_place(hop)

        @pl.when(block != place)
        def _():
            unit_pass(kind, hop).wait_send()

        @pl.when(block == place)
        def _():
            units_out_ref[kind] = unit_halves(kind, hop)[1][...].astype(WIDE)
            for side, there in enumerate((place > 0, place < last)):

                @pl.when(there)
                def _():
                    unit_arrived(kind, block, side).wait_recv()
                    units_out_ref[kind] += units_far[kind, block, side].astype(WIDE)


    def swaps(block):
        moves = [
            beside(part.at[kind, :, 1 - core], x_block.at[block, :, core, kind], swap_sems, (kind, block), CORE)
            for kind in range(2)
        ]
        moves.append(beside(part.at[2, :, 1 - core], y_block.at[block, core, :, 0], swap_sems, (2, block), CORE))
        return moves

    def output_copy(block):
        return pltpu.make_async_copy(output_ref.at[owner(block)], y_block.at[block, :, :, 1], local_sems.at[2, block])

    def firsts(block):
        return (
            beside(x_block.at[block, 1 - x], x_came.at[block], first_sems, (0, block), ALONG_X),
            beside(y_block.at[block, 1 - y], y_came.at[block], first_sems, (1, block), ALONG_Y),
        )

    def seconds(block):
        return (
            beside(x_block.at[block, x, 1 - y], x_last.at[block], second_sems, (0, block), ALONG_Y),
            beside(y_block.at[block, y, 1 - x], y_last.at[block], second_sems, (1, block), ALONG_X),
        )

    def thirds(block):
        return [
            push(own, heads_came.at[block, kind], third_sems, (kind, block), owner(block), index)
            for kind, own in enumerate((x_block.at[block, x, y], y_block.at[block, y, x]))
        ]

    def heads_start(block):
        for one in swaps(block):
            one.wait_recv()
        output_copy(block).wait()
        for one in firsts(block):
            one.start()

    def heads_first(block):
        for one in firsts(block):
            one.wait()
        add_rows(x_block.at[block, x], x_came.at[block])
        add_rows(y_block.at[block, y], y_came.at[block])
        for one in seconds(block):
            one.start()

    def heads_second(block, mine=False):
        for one in seconds(block):
            one.wait()
        add_rows(x_block.at[block, x, y], x_last.at[block])
        add_rows(y_block.at[block, y, x], y_last.at[block])
        if not mine:
            for one in thirds(block):
                one.start()

    @pl.when(step == 0)
    def _():
        greet_column(depth)
        units_start()
        for block in range(depth):
            output_copy(block).start()
        for piece in range(held):
            row_moves(layer_ref.at[piece], layer_out_ref, layer_sems, depth, piece)
        spare[...] = spare_lanes(length_ref[0], rows)
        for head in range(2):
            padded[head, :HALF_ROWS, :] = jnp.zeros((HALF_ROWS, QUERY_ROWS), LOW)
            padded[head, rows + HALF_ROWS :, :] = jnp.zeros((HALF_ROWS, QUERY_ROWS), LOW)

    def advance(number):
        def at(turn, tick, act):
            @pl.when((step == turn) & (number == tick))
            def _():
                act()

        ready = [(kind, hop) for kind in range(2) for hop in range(4) if hop != late[kind]]
        both_ready = [(0, 1), (0, 3), (1, 2), (1, 3)]
        others = [(0, 0), (0, 2), (1, 0), (1, 1)]
        at(0, 1, lambda: [unit_first(*one) for one in ready])
        at(1, 0, lambda: [unit_first(kind, late[kind]) for kind in range(2)])
        at(1, 1, lambda: [unit_summed(*one) for one in both_ready])
        at(2, 0, lambda: [unit_summed(*one) for one in others])
        at(2, 1, lambda: [unit_onward(*one, 0) for one in both_ready])
        at(3, 0, lambda: [unit_onward(*one, 0) for one in others])
        at(3, 1, lambda: [unit_onward(*one, 1) for one in both_ready])
        at(3, 3, lambda: [unit_onward(*one, 1) for one in others])

        @pl.when((step >= 1) & (number == 1))
        def _():
            heads_start(step - 1)

        @pl.when((step >= 2) & (number == 0))
        def _():
            heads_first(step - 2)

        @pl.when((step >= 2) & (number == 2))
        def _():
            heads_second(step - 2)

    pair = owner(step)
    lanes = pl.ds(pl.multiple_of(pair * LANES, LANES), LANES)
    split_heads(key_ref[:, lanes], spare[...], keys)
    split_heads(value_ref[:, lanes], jnp.zeros((rows, LANES), LOW), values)

    def low_lanes(kind):
        return pl.ds(pl.multiple_of((3 * pair + kind) * LANES, LANES), LANES)

    near_start = rows - QUERY_ROWS - HALF_ROWS
    near_end = near_start + 2 * QUERY_ROWS
    for head in range(2):
        line = near_ref[2 * pair + head]
        bias[head, :near_start, :] = jnp.broadcast_to(line[:, :1], (near_start, QUERY_ROWS))
        bias[head, near_start:near_end, :] = near_block(line).T
        bias[head, near_end:, :] = jnp.broadcast_to(line[:, -1:], (bias.shape[1] - near_end, QUERY_ROWS))
    key_total[...] = jnp.zeros_like(key_total)
    value_total[...] = jnp.zeros_like(value_total)
    tiles[...] = jnp.zeros_like(tiles)
    sums = small.at[0, pl.ds(pl.multiple_of(16 + 8 * pair, 8), 8)]
    sums[...] = jnp.zeros((8, LANES), WIDE)
    spot = lax.broadcasted_iota(jnp.int32, (1, LANES), 1)
    lane = lax.broadcasted_iota(jnp.int32, (QUERY_ROWS, LANES), 1)
    ones = jnp.where(lax.rem(lane, HEAD_DIM) == 0, 1.0, 0.0).astype(LOW)
    zero = jnp.zeros((), LOW)
    blocks = rows // QUERY_ROWS

    def block(number, carry):
        start = pl.multiple_of(number * QUERY_ROWS, QUERY_ROWS)
        offset = pl.multiple_of(rows - QUERY_ROWS - number * QUERY_ROWS, LANES)
        advance(number)
        both = query_ref[pl.ds(start, QUERY_ROWS), lanes]
        grad = grad_ref[pl.ds(start, QUERY_ROWS), lanes]
        parts = []
        for head in range(2):
            mine = lane < HEAD_DIM if head == 0 else lane >= HEAD_DIM
            logits = dot(keys[head], jnp.where(mine, both, ones), NT)
            logits = logits + bias[head, pl.ds(offset, rows), :]
            probs = jnp.exp(logits - log_ref[pair, head : head + 1, pl.ds(start, QUERY_ROWS)])
            prob_grad = dot(values[head], grad, NT)
            weighted = probs * prob_grad
            total = jnp.sum(weighted, axis=0, keepdims=True)
            score = (weighted - probs * total).astype(LOW)
            value_total[...] += dot(probs.astype(LOW), jnp.where(mine, grad, zero))
            key_total[...] += dot(score, jnp.where(mine, both, zero))
            padded[head, HALF_ROWS : HALF_ROWS + rows, :] = score
            one = dot(score, keys[head], TN)
            parts.append(one)
            columns = jnp.sum(one, axis=0, keepdims=True)
            first = HEAD_DIM * (1 - head) + 1 + number
            close = padded[head, pl.ds(start, 2 * QUERY_ROWS), :].astype(WIDE)
            quarter = [close[HALF_ROWS * turn : HALF_ROWS * (turn + 1)] for turn in range(4)]
            for turn in range(3):
                tiles[head, turn] += quarter[turn][:, :HALF_ROWS] + quarter[turn + 1][:, HALF_ROWS:]
            left = jnp.sum(quarter[0][:, HALF_ROWS:], axis=0, keepdims=True)
            right = jnp.sum(quarter[3][:, :HALF_ROWS], axis=0, keepdims=True)
            left = left + jnp.where(spot == first, columns, 0.0)
            right = right + jnp.where(spot == first + blocks, columns, 0.0)
            sums[4 * head + 2 : 4 * head + 3, :] += left
            sums[4 * head + 3 : 4 * head + 4, :] += right
        chosen = jnp.where(lane < HEAD_DIM, parts[0], parts[1])
        lows[pl.ds(start, QUERY_ROWS), low_lanes(0)] = chosen.astype(LOW)
        return carry

    lax.fori_loop(0, blocks, block, 0)
    lows[:, low_lanes(1)] = key_total[...].astype(LOW)
    lows[:, low_lanes(2)] = value_total[...].astype(LOW)
    shape = (HALF_ROWS, HALF_ROWS)
    upper = lax.broadcasted_iota(jnp.int32, shape, 0) <= lax.broadcasted_iota(jnp.int32, shape, 1)
    for head in range(2):
        before, centre, behind = (tiles[head, turn] for turn in range(3))
        sums[4 * head : 4 * head + 1, :] = diagonal_sums(jnp.where(upper, centre, before))
        sums[4 * head + 1 : 4 * head + 2, :] = diagonal_sums(jnp.where(upper, behind, centre))
        sums[4 * head + 2 : 4 * head + 3, :] += jnp.sum(jnp.where(upper, before, 0.0), axis=0, keepdims=True)
        sums[4 * head + 3 : 4 * head + 4, :] += jnp.sum(jnp.where(upper, 0.0, behind), axis=0, keepdims=True)

    @pl.when(step >= 1)
    def _():
        for one in swaps(step - 1):
            one.wait_send()

    for kind in range(3):
        product = dot(lows[:, low_lanes(kind)], normed_ref[...], TN).astype(LOW)
        part[kind] = product.reshape(part.shape[1:])
    for one in swaps(step):
        one.start()
    for half in range(2):
        for kind in range(2):
            x_block[step, half, core, kind] = part[kind, half, core]
        y_block[step, core, half, 0] = part[2, half, core]

    @pl.when(step == last)
    def _():
        span = rows // 2 // held
        for piece in range(held):
            away = pl.ds(pl.multiple_of((1 - core) * (rows // 2) + piece * span, span), span)
            fold_sent[piece] = dot(lows[away, :], weight_ref[...]).astype(LOW)
            beside(fold_sent.at[piece], fold_came.at[piece], fold_sems, (piece,), CORE).start()
        for one in swaps(last):
            one.wait_send()
        heads_start(last)
        heads_first(last - 1)

        gain_total = jnp.zeros((1, width), WIDE)
        for piece in range(held):
            here = pl.ds(pl.multiple_of(core * (rows // 2) + piece * span, span), span)
            product = dot(lows[here, :], weight_ref[...])
            beside(fold_sent.at[piece], fold_came.at[piece], fold_sems, (piece,), CORE).wait()
            product = product + fold_came[piece].astype(WIDE)
            local = slice(piece * span, (piece + 1) * span)
            source = source_ref[local, :].astype(WIDE)
            rms = inverse_root(jnp.mean(source * source, axis=1, keepdims=True) + EPSILON)
            scaled = source * rms
            gain_total = gain_total + jnp.sum(product * scaled, axis=0, keepdims=True)
            gained = gain_ref[...] * product
            inside = jnp.mean(gained * scaled, axis=1, keepdims=True)
            row_sent[piece] = (hidden_ref[local, :] + rms * (gained - scaled * inside)).astype(LOW)
            row_moves(row_sent.at[piece], row_came, row_sems, depth, piece)
            if piece == 0:
                heads_second(last - 1)
                heads_first(last)
        heads_second(last, True)

        for number in range(width // LANES):
            small[0, number : number + 1, :] = gain_total[:, number * LANES : (number + 1) * LANES]
        small[0, 8:16, :] = small_ref[...]
        for turn, bit in enumerate((ALONG_X, ALONG_Y)):
            move = beside(small.at[turn], small_came.at[turn], small_sems, (turn,), bit)
            move.start()
            move.wait()
            small[turn + 1] = small[turn] + small_came[turn]
        moves = [
            push(small.at[2], small_came.at[1 + turn], small_sems, (1 + turn,), lax.rem(place + turn, depth), index)
            for turn in range(1, depth)
        ]
        for one in moves:
            one.start()

        for block in range(last):
            for one in thirds(block):
                one.wait()
        for kind in range(2):
            for hop in range(4):
                unit_finish(kind, hop)
        heads_out_ref[0:2] = x_block[last, x, y].astype(WIDE) + sum(
            heads_came[one, 0].astype(WIDE) for one in range(depth - 1)
        )
        heads_out_ref[2:4] = y_block[last, y, x].astype(WIDE) + sum(
            heads_came[one, 1].astype(WIDE) for one in range(depth - 1)
        )
        for one in moves:
            one.wait()
        small[3] = small[2] + sum(small_came[1 + turn] for turn in range(1, depth))
        move = beside(small.at[3], small_came.at[depth + 1], small_sems, (depth + 1,), CORE)
        move.start()
        move.wait()
        small_out_ref[0] = small[3]
        small_out_ref[1] = small_came[depth + 1]

        for piece in range(held):
            row_moves(layer_ref.at[piece], layer_out_ref, layer_sems, depth, piece, False)
            row_moves(row_sent.at[piece], row_came, row_sems, depth, piece, False)
        rows_came(layer_out_ref, layer_sems, depth)
        rows_came(row_came, row_sems, depth)
        input_grad_ref[...] = row_came[...].astype(WIDE)


def backward(
    length, query, key, value, grad, logs, near, normed, weights, source, hidden, gain, ffn_gain_part, output_part, layer, *units
):
    rows, inner = query.shape
    width = normed.shape[1]
    depth = lax.axis_size("seq")
    held = depth // 2
    span = rows // depth
    slim, thick = (output_part.shape[3], units[0].shape[3])
    vmem, anywhere = (pl.BlockSpec(memory_space=pltpu.VMEM), pl.BlockSpec(memory_space=pltpu.HBM))
    shape = jax.ShapeDtypeStruct
    small_rows = 2 * (width // LANES) + 8 * depth
    sems = [(3, depth), (2, depth), (2, depth), (2, depth), (2,), (2, depth), (2, depth, 2)]
    sems += [(held,), (held, held), (held, held), (depth + 2,)]
    return pl.pallas_call(
        functools.partial(backward_kernel, depth),
        grid=(depth,),
        in_specs=[pl.BlockSpec(memory_space=pltpu.SMEM)] + [vmem] * 12 + [anywhere] * 6,
        out_specs=[anywhere] + [vmem] * 4,
        out_shape=[
            shape((held, span, width), LOW),
            shape((held, span, width), WIDE),
            shape((4, slim, width), WIDE),
            shape((2, thick, width), WIDE),
            shape((2, small_rows, LANES), WIDE),
        ],
        scratch_shapes=[
            pltpu.VMEM((2, 2 * rows - QUERY_ROWS, QUERY_ROWS), WIDE),
            pltpu.VMEM((rows, LANES), LOW),
            pltpu.VMEM((2, rows, LANES), LOW),
            pltpu.VMEM((2, rows, LANES), LOW),
            pltpu.VMEM((2, rows + QUERY_ROWS, QUERY_ROWS), LOW),
            pltpu.VMEM((rows, LANES), WIDE),
            pltpu.VMEM((rows, LANES), WIDE),
            pltpu.VMEM((2, 3, HALF_ROWS, HALF_ROWS), WIDE),
            pltpu.VMEM((rows, 3 * inner), LOW),
            pltpu.VMEM((3, 2, 2, slim, width), LOW),
        ]
        + [pltpu.VMEM((depth, 2, 2, 2, slim, width), LOW)] * 2
        + [pltpu.VMEM((depth, 2, 2, slim, width), LOW)] * 2
        + [pltpu.VMEM((depth, 2, slim, width), LOW)] * 2
        + [
            pltpu.VMEM((depth - 1, 2, 2, slim, width), LOW),
            pltpu.VMEM((2, depth, 2, thick, width), LOW),
            pltpu.VMEM((2, depth, 2, thick, width), LOW),
            pltpu.VMEM((2, depth, thick, width), LOW),
            pltpu.VMEM((2, depth, 2, thick, width), LOW),
        ]
        + [pltpu.VMEM((held, span, width), LOW)] * 4
        + [pltpu.VMEM((4, small_rows, LANES), WIDE), pltpu.VMEM((depth + 2, small_rows, LANES), WIDE)]
        + [pltpu.SemaphoreType.DMA((2,) + one) for one in sems]
        + [pltpu.SemaphoreType.DMA((2, depth)), pltpu.SemaphoreType.DMA((3, depth))],
        compiler_params=pltpu.CompilerParams(
            vmem_limit_bytes=62 << 20, collective_id=3, has_side_effects=True
        ),
        cost_estimate=pl.CostEstimate(
            flops=60 * rows * rows * inner, bytes_accessed=14 * rows * inner, transcendentals=rows * rows * inner // 64
        ),
        name="backward",
    )(length, query, key, value, grad, logs, near, normed, weights, source, hidden, gain, ffn_gain_part, output_part, layer, *units)


def flip(value, bit):
    size = lax.axis_size("fsdp")
    return lax.ppermute(value, "fsdp", [(one, one ^ bit) for one in range(size)])


def other_core(value):
    return flip(value, 1)


def rounds_of(inverse):
    depth, size = (lax.axis_size("seq"), lax.axis_size("fsdp"))
    held = depth // 2
    rounds = []
    for step in range(held):
        pairs = []
        for place in range(depth):
            for index in range(size):
                target = (index % 2) * held + (place + step) % held
                there = target * size + index - index % 2 + place // held
                here = place * size + index
                pairs.append((there, here) if inverse else (here, there))
        rounds.append(pairs)
    return rounds


def to_sequence(blocks):
    held, span, width = blocks.shape
    place = lax.axis_index("seq")
    out = jnp.zeros((held, span, width), blocks.dtype)
    for step, pairs in enumerate(rounds_of(False)):
        sent = lax.dynamic_index_in_dim(blocks, (place + step) % held, 0, keepdims=False)
        got = lax.ppermute(sent, BOTH, pairs)
        out = lax.dynamic_update_index_in_dim(out, got, (place + held - step) % held, 0)
    return out.reshape(held * span, width)


def to_slots(rows, held):
    span, width = (rows.shape[0] // held, rows.shape[1])
    place = lax.axis_index("seq")
    blocks = rows.reshape(held, span, width)
    out = jnp.zeros(blocks.shape, rows.dtype)
    for step, pairs in enumerate(rounds_of(True)):
        sent = lax.dynamic_index_in_dim(blocks, (place + held - step) % held, 0, keepdims=False)
        got = lax.ppermute(sent, BOTH, pairs)
        out = lax.dynamic_update_index_in_dim(out, got, (place + step) % held, 0)
    return out


def whole(mine, core):
    other = other_core(mine)
    return jnp.where(
        core == 0, jnp.concatenate([mine, other], axis=0), jnp.concatenate([other, mine], axis=0)
    )


def fold(partial, core):
    half = partial.shape[0] // 2
    sent = lax.dynamic_slice_in_dim(partial, (1 - core) * half, half, 0)
    kept = lax.dynamic_slice_in_dim(partial, core * half, half, 0)
    return kept + other_core(sent)


def fast_plane():
    return lax.axis_size("fsdp") == 8 and lax.axis_size("seq") == 4


def own_head_rows(weight, core):
    width = weight.shape[1]
    return lax.dynamic_index_in_dim(weight.reshape(4, 2, -1, width), core, 1, keepdims=False).reshape(-1, width)


def add_low(left, right):
    return (left.astype(WIDE) + right.astype(WIDE)).astype(LOW)


def pick(value, index, axis):
    return lax.dynamic_index_in_dim(value, index, axis, keepdims=False)


def shards(
    inputs,
    lengths,
    cotangent,
    query_weight,
    key_weight,
    value_weight,
    output_weight,
    up_weight,
    down_weight,
    attn_gain,
    ffn_gain,
    bias_table,
):
    held, span, width = inputs.shape
    depth, size = (lax.axis_size("seq"), lax.axis_size("fsdp"))
    place, index = (lax.axis_index("seq"), lax.axis_index("fsdp"))
    core = index % 2
    rows = held * span
    inner = HEADS * HEAD_DIM
    fast = fast_plane()

    near_lengths = jnp.where(
        core == 0,
        jnp.concatenate([lengths, other_core(lengths)]),
        jnp.concatenate([other_core(lengths), lengths]),
    )
    length = lax.dynamic_slice_in_dim(near_lengths, place, 1, 0)

    own_table = lax.dynamic_index_in_dim(bias_table.reshape(BUCKETS, 4, 2, 2), core, 2, keepdims=False)
    own_table = own_table.reshape(BUCKETS, HEADS // 2)
    near = near_bias(own_table)

    if fast:
        normed_one, query, key, value, source_low, weights, up_mine, down_mine = enter(
            inputs, (query_weight, key_weight, value_weight), up_weight, down_weight, attn_gain[None, :]
        )
        source_low = source_low.reshape(rows, width)
        mine = (up_mine.reshape(-1, width), down_mine.reshape(-1, width))
        logs, near_context, hidden_one, far_context, own_output, far_output, normed_two, grad_low, *wholes = through(
            length,
            query,
            key,
            value,
            near,
            source_low,
            ffn_gain[None, :],
            output_weight,
            *mine,
            cotangent,
        )
        own_output, far_output = (own_output.reshape(-1, width), far_output.reshape(-1, width))
    else:
        own_three = [
            own_head_rows(lax.all_gather(one, "fsdp", axis=0, tiled=True), core)
            for one in (query_weight, key_weight, value_weight)
        ]
        full = lax.all_gather(output_weight, "fsdp", axis=0, tiled=True)
        own_output = own_head_rows(full, core)
        far_output = own_head_rows(full, 1 - core)
        own_up, own_down = (
            pick(
                lax.all_gather(one, "fsdp", axis=0, tiled=True).reshape(depth, size // 2, 2, -1, width), core, 2
            ).reshape(-1, width)
            for one in (up_weight, down_weight)
        )
        mask_rows = (core * rows + jnp.arange(rows, dtype=jnp.int32) < length[0])[:, None].astype(WIDE)
        source_low = to_sequence(inputs)
        source = source_low.astype(WIDE)
        rms_one = lax.rsqrt(jnp.mean(source * source, axis=1, keepdims=True) + EPSILON)
        scaled_one = source * rms_one
        normed_one = whole((scaled_one * attn_gain).astype(LOW), core)
        query, key, value = [dot(normed_one, one, NT).astype(LOW) for one in own_three]
        context, logs = attend(length, query, key, value, near)
        mine = (own_up, own_down)
        near_context = lax.dynamic_slice_in_dim(context, core * rows, rows, 0)
        far_context = other_core(lax.dynamic_slice_in_dim(context, (1 - core) * rows, rows, 0))
        hidden_one = source + (dot(near_context, own_output) + dot(far_context, far_output))
        rms_two = lax.rsqrt(jnp.mean(hidden_one * hidden_one, axis=1, keepdims=True) + EPSILON)
        scaled_two = hidden_one * rms_two
        normed_two = whole((scaled_two * ffn_gain).astype(LOW), core)
        grad_out = to_sequence(cotangent).astype(WIDE) * mask_rows
        grad_low = whole(grad_out.astype(LOW), core)

    if fast:
        up_part, down_part, up_came, down_came, _, _, context_grad, hidden_grad, layer_rows, ffn_gain_part, output_part = middle(
            length,
            normed_two,
            grad_low,
            hidden_one,
            ffn_gain[None, :],
            (own_output, far_output),
            (near_context, far_context),
            mine,
            wholes,
        )
    else:
        up_part, down_part, mlp_part, normed_part = feed(normed_two, grad_low, *mine)
        normed_grad = fold(normed_part, core)
        layer_rows = ((hidden_one + fold(mlp_part, core)) * mask_rows).astype(LOW)
        gained_two = ffn_gain * normed_grad
        hidden_grad = grad_out + rms_two * (
            gained_two - scaled_two * jnp.mean(gained_two * scaled_two, axis=1, keepdims=True)
        )
        ffn_gain_part = jnp.sum(normed_grad * scaled_two, axis=0)
        hidden_low = hidden_grad.astype(LOW)
        near_grad = dot(hidden_low, own_output, NT).astype(LOW)
        far_grad = other_core(dot(hidden_low, far_output, NT).astype(LOW))
        context_grad = jnp.where(
            core == 0,
            jnp.concatenate([near_grad, far_grad], axis=0),
            jnp.concatenate([far_grad, near_grad], axis=0),
        )
        near_output_part = dot(near_context, hidden_low, TN).astype(LOW)
        far_output_part = dot(far_context, hidden_low, TN).astype(LOW)

    if fast:
        layer_out, input_grad, heads_grad, units_grad, small = backward(
            length,
            query,
            key,
            value,
            context_grad,
            logs,
            near,
            normed_one,
            weights.reshape(-1, width),
            source_low,
            hidden_grad,
            attn_gain[None, :],
            ffn_gain_part.reshape(-1, LANES),
            output_part,
            layer_rows,
            up_part,
            down_part,
            up_came,
            down_came,
        )
        query_grad, key_grad, value_grad, output_grad = (heads_grad[number] for number in range(4))
        up_grad, down_grad = (units_grad[0], units_grad[1])
        gain_lines = width // LANES
        gains = (small[0] + small[1])[: 2 * gain_lines].reshape(2, width)
        attn_gain_sum, ffn_gain_sum = (gains[0], gains[1])
        sums = jnp.where(core == 0, small, small[::-1])[:, 2 * gain_lines :]
        sums = jnp.swapaxes(sums.reshape(2, 4, 2, 4 * LANES), 0, 1)
        bias_sum = bucket_sums(sums.reshape(HEADS, 4 * LANES))
    else:
        query_low, key_low, value_low, distance_sums = attend_grad(
            length, query, key, value, context_grad, logs, near
        )
        lows = (query_low, key_low, value_low)
        normed_one_grad = dot(query_low, own_three[0]) + dot(key_low, own_three[1]) + dot(value_low, own_three[2])
        normed_one_grad = fold(normed_one_grad, core)
        three_parts = [dot(one, normed_one, TN).astype(LOW) for one in lows]
        gained_one = attn_gain * normed_one_grad
        input_grad = hidden_grad + rms_one * (
            gained_one - scaled_one * jnp.mean(gained_one * scaled_one, axis=1, keepdims=True)
        )
        attn_gain_part = jnp.sum(normed_one_grad * scaled_one, axis=0)
        input_grad = to_slots(input_grad.astype(LOW), held).astype(WIDE)
        layer_out = to_slots(layer_rows, held)

        def summed(value):
            return lax.psum_scatter(value, BOTH, scatter_dimension=0, tiled=True).astype(WIDE)

        def own_only(value):
            blank = jnp.zeros_like(value)
            pair = jnp.where(core == 0, jnp.stack([value, blank], axis=1), jnp.stack([blank, value], axis=1))
            return summed(pair.reshape(-1, width))

        up_grad, down_grad = [own_only(one.reshape(depth * (size // 2), -1, width)) for one in (up_part, down_part)]
        query_grad, key_grad, value_grad = [own_only(one.reshape(4, -1, width)) for one in three_parts]
        near_part, far_part = (near_output_part.reshape(4, -1, width), far_output_part.reshape(4, -1, width))
        pair = jnp.where(
            core == 0, jnp.stack([near_part, far_part], axis=1), jnp.stack([far_part, near_part], axis=1)
        )
        output_grad = summed(pair.reshape(-1, width))
        bias_own = bucket_sums(distance_sums.reshape(HEADS // 2, 4 * LANES)).reshape(BUCKETS, 4, 1, 2)
        bias_full = lax.dynamic_update_slice(
            jnp.zeros((BUCKETS, 4, 2, 2), WIDE), bias_own, (0, 0, core, 0)
        ).reshape(BUCKETS, HEADS)
        attn_gain_sum, ffn_gain_sum, bias_sum = lax.psum((attn_gain_part, ffn_gain_part, bias_full), BOTH)

    gain_rows = width // size
    bucket_rows = BUCKETS // size
    attn_gain_grad = lax.dynamic_slice_in_dim(attn_gain_sum, index * gain_rows, gain_rows, 0)
    ffn_gain_grad = lax.dynamic_slice_in_dim(ffn_gain_sum, index * gain_rows, gain_rows, 0)
    bias_grad = lax.dynamic_slice_in_dim(bias_sum, index * bucket_rows, bucket_rows, 0)
    return (
        layer_out,
        input_grad,
        query_grad,
        key_grad,
        value_grad,
        output_grad,
        up_grad,
        down_grad,
        attn_gain_grad,
        ffn_gain_grad,
        bias_grad,
    )


def solution(mesh):
    placed = (
        P("fsdp", "seq", None),
        P("fsdp"),
        P("fsdp", "seq", None),
        P("fsdp", None),
        P("fsdp", None),
        P("fsdp", None),
        P("fsdp", None),
        P("fsdp", None),
        P("fsdp", None),
        P(),
        P(),
        P(),
    )
    return jax.shard_map(
        shards,
        mesh=mesh,
        in_specs=placed,
        out_specs=(
            P("fsdp", "seq", None),
            P("fsdp", "seq", None),
            P(("seq", "fsdp"), None),
            P(("seq", "fsdp"), None),
            P(("seq", "fsdp"), None),
            P(("seq", "fsdp"), None),
            P(("seq", "fsdp"), None),
            P(("seq", "fsdp"), None),
            P("fsdp"),
            P("fsdp"),
            P("fsdp", None),
        ),
        check_vma=False,
    )
```

```python
import functools

import jax
import jax.numpy as jnp
import numpy as np
from jax import lax
from jax.experimental import pallas as pl
from jax.experimental.pallas import tpu as pltpu
from jax.sharding import PartitionSpec as P

HEADS = 16
HEAD_DIM = 64
BUCKETS = 32
NEGATIVE = -1000000000.0
EPSILON = 1e-06
THRESHOLDS = (1, 2, 3, 4, 5, 6, 7, 8, 12, 16, 23, 32, 46, 64, 91)
ROOT_HALF = 0.7071067811865476
NORMAL_PEAK = 0.3989422804014327
LANES = 128
QUERY_ROWS = 256
HALF_ROWS = QUERY_ROWS // 2
LOW = jnp.bfloat16
WIDE = jnp.float32
BOTH = ("seq", "fsdp")

NN = (((1,), (0,)), ((), ()))
NT = (((1,), (1,)), ((), ()))
TN = (((0,), (0,)), ((), ()))


def dot(left, right, dims=NN):
    return lax.dot_general(left, right, dims, preferred_element_type=WIDE)


def inverse_root(value):
    root = lax.rsqrt(value)
    return root * (1.5 - 0.5 * value * root * root)


def gelu_parts(value):
    cumulative = 0.5 * (1.0 + lax.erf(value * ROOT_HALF))
    slope = cumulative + value * jnp.exp(-0.5 * value * value) * NORMAL_PEAK
    return (value * cumulative, slope)


CORE, ALONG_X, ALONG_Y = (1, 2, 4)


def partner(bit):
    index = lax.axis_index("fsdp")
    return index + bit - 2 * bit * ((index // bit) % 2)


def chip_of(*bits):
    index = lax.axis_index("fsdp")
    for bit in bits:
        index = index + bit - 2 * bit * ((index // bit) % 2)
    return index // 2


def send(source, target, sems, number, bit):
    return pltpu.make_async_remote_copy(
        src_ref=source,
        dst_ref=target,
        send_sem=sems.at[0, number],
        recv_sem=sems.at[1, number],
        device_id={"fsdp": partner(bit)},
        device_id_type=pl.DeviceIdType.MESH,
    )


def greet(bits):
    barrier = pltpu.get_barrier_semaphore()
    for bit in bits:
        pl.semaphore_signal(
            barrier, inc=1, device_id={"fsdp": partner(bit)}, device_id_type=pl.DeviceIdType.MESH
        )
    pl.semaphore_wait(barrier, len(bits))


def bucket_columns(distances):
    distances = np.asarray(distances)
    magnitude = sum((np.abs(distances) >= threshold).astype(np.int32) for threshold in THRESHOLDS)
    buckets = magnitude + np.where(distances > 0, BUCKETS // 2, 0)
    return (buckets[None, :] == np.arange(BUCKETS)[:, None]).astype(np.float32)


def near_bias(columns):
    chosen = jnp.asarray(bucket_columns(np.arange(2 * QUERY_ROWS) - HALF_ROWS))
    line = lax.dot_general(columns, chosen, TN, precision=lax.Precision.HIGHEST, preferred_element_type=WIDE)
    return line[:, None, :]


def near_block(line):
    shape = (QUERY_ROWS, 2 * QUERY_ROWS)
    turned = pltpu.roll(jnp.broadcast_to(line, shape), 0, 1, stride=1, stride_axis=0)
    row = lax.broadcasted_iota(jnp.int32, shape, 0)
    column = lax.broadcasted_iota(jnp.int32, shape, 1)
    return jnp.where(column < row, line[:, :1], turned)


def diagonal_sums(tile):
    side = tile.shape[1]
    row = lax.broadcasted_iota(jnp.int32, tile.shape, 0)
    step = 1
    while step < side:
        tile = jnp.where((row // step) % 2 == 1, pltpu.roll(tile, side - step, 1), tile)
        step *= 2
    return jnp.sum(tile, axis=0, keepdims=True)


def spare_lanes(length, rows):
    blocks = rows // QUERY_ROWS
    key = lax.broadcasted_iota(jnp.int32, (rows, LANES), 0)
    lane = lax.rem(lax.broadcasted_iota(jnp.int32, (rows, LANES), 1), HEAD_DIM)
    hidden = jnp.where((lane == 0) & (key >= length), NEGATIVE, 0.0)
    left = (lane >= 1) & (lane <= blocks) & (key < QUERY_ROWS * (lane - 1) - HALF_ROWS)
    start = QUERY_ROWS * (lane - 1 - blocks) + 3 * HALF_ROWS
    right = (lane > blocks) & (lane <= 2 * blocks) & (key >= start)
    return jnp.where(left | right, 1.0, hidden).astype(LOW)


def split_heads(pair, spare, out):
    low_half = lax.broadcasted_iota(jnp.int32, pair.shape, 1) < HEAD_DIM
    out[0] = jnp.where(low_half, pair, spare)
    out[1] = jnp.where(low_half, spare, pair)


def attend_kernel(
    length_ref, query_ref, key_ref, value_ref, near_ref, context_ref, log_ref, bias, keys, values
):
    rows = query_ref.shape[0]
    split_heads(key_ref[...], spare_lanes(length_ref[0], rows), keys)
    split_heads(value_ref[...], jnp.zeros((rows, LANES), LOW), values)
    near_start = rows - QUERY_ROWS - HALF_ROWS
    near_end = near_start + 2 * QUERY_ROWS
    for head in range(2):
        line = near_ref[head]
        bias[head, :, :near_start] = jnp.broadcast_to(line[:, :1], (QUERY_ROWS, near_start))
        bias[head, :, near_start:near_end] = near_block(line)
        bias[head, :, near_end:] = jnp.broadcast_to(line[:, -1:], (QUERY_ROWS, bias.shape[2] - near_end))
    lane = lax.broadcasted_iota(jnp.int32, (QUERY_ROWS, LANES), 1)
    ones = jnp.where(lax.rem(lane, HEAD_DIM) == 0, 1.0, 0.0).astype(LOW)

    def block(number, carry):
        start = pl.multiple_of(number * QUERY_ROWS, QUERY_ROWS)
        offset = pl.multiple_of(rows - QUERY_ROWS - number * QUERY_ROWS, LANES)
        both = query_ref[pl.ds(start, QUERY_ROWS), :]
        total = jnp.zeros((QUERY_ROWS, LANES), WIDE)
        for head in range(2):
            mine = lane < HEAD_DIM if head == 0 else lane >= HEAD_DIM
            logits = dot(jnp.where(mine, both, ones), keys[head], NT)
            logits = logits + bias[head, :, pl.ds(offset, rows)]
            peak = jnp.max(logits, axis=1, keepdims=True)
            exponent = jnp.exp(logits - peak)
            row_sum = jnp.sum(exponent, axis=1, keepdims=True)
            weights_low = (exponent * (1.0 / row_sum)).astype(LOW)
            total = total + dot(weights_low, values[head])
            logs = jnp.broadcast_to(peak + jnp.log(row_sum), (QUERY_ROWS, LANES))
            log_ref[0, head : head + 1, pl.ds(start, QUERY_ROWS)] = logs.T[0:1, :]
        context_ref[pl.ds(start, QUERY_ROWS), :] = total.astype(LOW)
        return carry

    lax.fori_loop(0, rows // QUERY_ROWS, block, 0)


def attend(length, query, key, value, near):
    rows, width = query.shape
    pairs = width // LANES
    smem = pl.BlockSpec(memory_space=pltpu.SMEM)
    columns = pl.BlockSpec((rows, LANES), lambda pair: (0, pair))
    return pl.pallas_call(
        attend_kernel,
        grid=(pairs,),
        in_specs=[smem, columns, columns, columns]
        + [pl.BlockSpec((2, 1, 2 * QUERY_ROWS), lambda pair: (pair, 0, 0))],
        out_specs=[columns, pl.BlockSpec((1, 2, rows), lambda pair: (pair, 0, 0))],
        out_shape=[
            jax.ShapeDtypeStruct((rows, width), LOW),
            jax.ShapeDtypeStruct((pairs, 2, rows), WIDE),
        ],
        scratch_shapes=[
            pltpu.VMEM((2, QUERY_ROWS, 2 * rows - QUERY_ROWS), WIDE),
            pltpu.VMEM((2, rows, LANES), LOW),
            pltpu.VMEM((2, rows, LANES), LOW),
        ],
        compiler_params=pltpu.CompilerParams(vmem_limit_bytes=40 << 20),
        cost_estimate=pl.CostEstimate(
            flops=24 * rows * rows * width, bytes_accessed=8 * rows * width, transcendentals=2 * pairs * rows * rows
        ),
        name="attend",
    )(length, query, key, value, near)


def attend_grad_kernel(
    length_ref,
    query_ref,
    key_ref,
    value_ref,
    grad_ref,
    log_ref,
    near_ref,
    query_grad_ref,
    key_grad_ref,
    value_grad_ref,
    sums_ref,
    bias,
    keys,
    values,
    padded,
    key_total,
    value_total,
    tiles,
):
    rows = query_ref.shape[0]
    blocks = rows // QUERY_ROWS
    split_heads(key_ref[...], spare_lanes(length_ref[0], rows), keys)
    split_heads(value_ref[...], jnp.zeros((rows, LANES), LOW), values)
    near_start = rows - QUERY_ROWS - HALF_ROWS
    near_end = near_start + 2 * QUERY_ROWS
    for head in range(2):
        line = near_ref[head]
        bias[head, :near_start, :] = jnp.broadcast_to(line[:, :1], (near_start, QUERY_ROWS))
        bias[head, near_start:near_end, :] = near_block(line).T
        bias[head, near_end:, :] = jnp.broadcast_to(line[:, -1:], (bias.shape[1] - near_end, QUERY_ROWS))
        padded[head, :HALF_ROWS, :] = jnp.zeros((HALF_ROWS, QUERY_ROWS), LOW)
        padded[head, rows + HALF_ROWS :, :] = jnp.zeros((HALF_ROWS, QUERY_ROWS), LOW)
    key_total[...] = jnp.zeros_like(key_total)
    value_total[...] = jnp.zeros_like(value_total)
    tiles[...] = jnp.zeros_like(tiles)
    sums_ref[...] = jnp.zeros_like(sums_ref)
    spot = lax.broadcasted_iota(jnp.int32, (1, LANES), 1)
    lane = lax.broadcasted_iota(jnp.int32, (QUERY_ROWS, LANES), 1)
    ones = jnp.where(lax.rem(lane, HEAD_DIM) == 0, 1.0, 0.0).astype(LOW)
    zero = jnp.zeros((), LOW)

    def block(number, carry):
        start = pl.multiple_of(number * QUERY_ROWS, QUERY_ROWS)
        offset = pl.multiple_of(rows - QUERY_ROWS - number * QUERY_ROWS, LANES)
        both = query_ref[pl.ds(start, QUERY_ROWS), :]
        grad = grad_ref[pl.ds(start, QUERY_ROWS), :]
        parts = []
        for head in range(2):
            mine = lane < HEAD_DIM if head == 0 else lane >= HEAD_DIM
            logits = dot(keys[head], jnp.where(mine, both, ones), NT)
            logits = logits + bias[head, pl.ds(offset, rows), :]
            probs = jnp.exp(logits - log_ref[0, head : head + 1, pl.ds(start, QUERY_ROWS)])
            prob_grad = dot(values[head], grad, NT)
            weighted = probs * prob_grad
            inner = jnp.sum(weighted, axis=0, keepdims=True)
            score = (weighted - probs * inner).astype(LOW)
            value_total[...] += dot(probs.astype(LOW), jnp.where(mine, grad, zero))
            key_total[...] += dot(score, jnp.where(mine, both, zero))
            padded[head, HALF_ROWS : HALF_ROWS + rows, :] = score
            part = dot(score, keys[head], TN)
            parts.append(part)
            columns = jnp.sum(part, axis=0, keepdims=True)
            spare = HEAD_DIM * (1 - head) + 1 + number
            close = padded[head, pl.ds(start, 2 * QUERY_ROWS), :].astype(WIDE)
            quarter = [close[HALF_ROWS * step : HALF_ROWS * (step + 1)] for step in range(4)]
            for step in range(3):
                tiles[head, step] += quarter[step][:, :HALF_ROWS] + quarter[step + 1][:, HALF_ROWS:]
            left = jnp.sum(quarter[0][:, HALF_ROWS:], axis=0, keepdims=True)
            right = jnp.sum(quarter[3][:, :HALF_ROWS], axis=0, keepdims=True)
            left = left + jnp.where(spot == spare, columns, 0.0)
            right = right + jnp.where(spot == spare + blocks, columns, 0.0)
            sums_ref[0, 4 * head + 2 : 4 * head + 3, :] += left
            sums_ref[0, 4 * head + 3 : 4 * head + 4, :] += right
        chosen = jnp.where(lane < HEAD_DIM, parts[0], parts[1])
        query_grad_ref[pl.ds(start, QUERY_ROWS), :] = chosen.astype(LOW)
        return carry

    lax.fori_loop(0, blocks, block, 0)
    key_grad_ref[...] = key_total[...].astype(LOW)
    value_grad_ref[...] = value_total[...].astype(LOW)
    shape = (HALF_ROWS, HALF_ROWS)
    upper = lax.broadcasted_iota(jnp.int32, shape, 0) <= lax.broadcasted_iota(jnp.int32, shape, 1)
    for head in range(2):
        before, centre, behind = (tiles[head, step] for step in range(3))
        sums_ref[0, 4 * head : 4 * head + 1, :] = diagonal_sums(jnp.where(upper, centre, before))
        sums_ref[0, 4 * head + 1 : 4 * head + 2, :] = diagonal_sums(jnp.where(upper, behind, centre))
        left = jnp.sum(jnp.where(upper, before, 0.0), axis=0, keepdims=True)
        right = jnp.sum(jnp.where(upper, 0.0, behind), axis=0, keepdims=True)
        sums_ref[0, 4 * head + 2 : 4 * head + 3, :] += left
        sums_ref[0, 4 * head + 3 : 4 * head + 4, :] += right


def attend_grad(length, query, key, value, grad, logs, near):
    rows, width = query.shape
    pairs = width // LANES
    smem = pl.BlockSpec(memory_space=pltpu.SMEM)
    columns = pl.BlockSpec((rows, LANES), lambda pair: (0, pair))
    shape = jax.ShapeDtypeStruct
    return pl.pallas_call(
        attend_grad_kernel,
        grid=(pairs,),
        in_specs=[smem, columns, columns, columns, columns]
        + [pl.BlockSpec((1, 2, rows), lambda pair: (pair, 0, 0))]
        + [pl.BlockSpec((2, 1, 2 * QUERY_ROWS), lambda pair: (pair, 0, 0))],
        out_specs=[columns, columns, columns] + [pl.BlockSpec((1, 8, LANES), lambda pair: (pair, 0, 0))],
        out_shape=[shape((rows, width), LOW)] * 3 + [shape((pairs, 8, LANES), WIDE)],
        scratch_shapes=[
            pltpu.VMEM((2, 2 * rows - QUERY_ROWS, QUERY_ROWS), WIDE),
            pltpu.VMEM((2, rows, LANES), LOW),
            pltpu.VMEM((2, rows, LANES), LOW),
            pltpu.VMEM((2, rows + QUERY_ROWS, QUERY_ROWS), LOW),
            pltpu.VMEM((rows, LANES), WIDE),
            pltpu.VMEM((rows, LANES), WIDE),
            pltpu.VMEM((2, 3, HALF_ROWS, HALF_ROWS), WIDE),
        ],
        compiler_params=pltpu.CompilerParams(vmem_limit_bytes=48 << 20),
        cost_estimate=pl.CostEstimate(
            flops=44 * rows * rows * width, bytes_accessed=14 * rows * width, transcendentals=2 * pairs * rows * rows
        ),
        name="attend_grad",
    )(length, query, key, value, grad, logs, near)


def bucket_sums(sums):
    side = np.arange(LANES)
    far = np.full((LANES,), 2 * HALF_ROWS)
    chosen = bucket_columns(np.concatenate([-side, HALF_ROWS - side, -far, far]))
    return lax.dot_general(
        jnp.asarray(chosen), sums, NT, precision=lax.Precision.HIGHEST, preferred_element_type=WIDE
    )


def feed_kernel(normed_ref, grad_ref, up_ref, down_ref, up_part_ref, down_part_ref, out_ref, back_ref):
    @pl.when(pl.program_id(0) == 0)
    def _():
        out_ref[...] = jnp.zeros_like(out_ref)
        back_ref[...] = jnp.zeros_like(back_ref)

    up, down = (up_ref[...], down_ref[...])
    normed, grad = (normed_ref[...], grad_ref[...])
    active, slope = gelu_parts(dot(normed, up, NT))
    active = active.astype(LOW)
    pre_grad = (dot(grad, down, NT) * slope).astype(LOW)
    out_ref[...] += dot(active, down)
    back_ref[...] += dot(pre_grad, up)
    up_part_ref[...] = dot(pre_grad, normed, TN).astype(LOW)
    down_part_ref[...] = dot(active, grad, TN).astype(LOW)


def feed(normed, grad, up, down):
    rows, width = normed.shape
    unit = up.shape[0] // 4
    fixed = pl.BlockSpec((rows, width), lambda step: (0, 0))
    block = pl.BlockSpec((unit, width), lambda step: (step, 0))
    return pl.pallas_call(
        feed_kernel,
        grid=(4,),
        in_specs=[fixed, fixed, block, block],
        out_specs=[block, block, fixed, fixed],
        out_shape=[jax.ShapeDtypeStruct((4 * unit, width), LOW)] * 2
        + [jax.ShapeDtypeStruct((rows, width), WIDE)] * 2,
        compiler_params=pltpu.CompilerParams(vmem_limit_bytes=56 << 20),
        name="feed",
    )(normed, grad, up, down)


def push(source, target, sems, number, place, index, there=None):
    return pltpu.make_async_remote_copy(
        src_ref=source,
        dst_ref=target,
        send_sem=sems.at[(0,) + number],
        recv_sem=sems.at[(1,) + (there or number)],
        device_id={"seq": place, "fsdp": index},
        device_id_type=pl.DeviceIdType.MESH,
    )


def greet_column(depth):
    barrier = pltpu.get_barrier_semaphore()
    place, index = (lax.axis_index("seq"), lax.axis_index("fsdp"))

    def signal(there, which):
        pl.semaphore_signal(
            barrier, inc=1, device_id={"seq": there, "fsdp": which}, device_id_type=pl.DeviceIdType.MESH
        )

    signal(place, partner(ALONG_X))
    signal(place, partner(ALONG_Y))
    signal(place, partner(CORE))
    for step in range(1, depth):
        signal(lax.rem(place + step, depth), index)
        signal(lax.rem(place + step, depth), partner(CORE))
    pl.semaphore_wait(barrier, 2 * depth + 1)


def slots_moves(source, target, sems, depth, act):
    held = depth // 2
    place, index = (lax.axis_index("seq"), lax.axis_index("fsdp"))
    core = lax.rem(index, 2)
    slot = lax.rem(place, held)
    for sequence in range(held):
        there, which = (core * held + sequence, index - core + place // held)
        home = (there == place) & (which == index)

        @pl.when(home)
        def _():
            if act == "start":
                pltpu.make_async_copy(source.at[sequence], target.at[slot], sems.at[1, slot]).start()

        @pl.when(jnp.logical_not(home))
        def _():
            move = push(source.at[sequence], target.at[slot], sems, (sequence,), there, which, (slot,))
            if act == "start":
                move.start()
            else:
                move.wait_send()


def slots_came(target, sems, slot):
    push(target.at[slot], target.at[slot], sems, (slot,), lax.axis_index("seq"), partner(CORE)).wait_recv()


def enter_kernel(
    depth,
    inputs_ref,
    query_ref,
    key_ref,
    value_ref,
    up_ref,
    down_ref,
    gain_ref,
    normed_out_ref,
    query_out_ref,
    key_out_ref,
    value_out_ref,
    source_out_ref,
    weights_out_ref,
    up_out_ref,
    down_out_ref,
    normed_ref,
    source_ref,
    weights_ref,
    kept,
    slot_sems,
    near_sems,
    far_sems,
    cut_sems,
    row_sems,
    local_sems,
):
    held = depth // 2
    span = source_ref.shape[1]
    rows = normed_ref.shape[0]
    index = lax.axis_index("fsdp")
    core = lax.rem(index, 2)
    chip = chip_of()
    mine = (query_ref, key_ref, value_ref)
    half = query_ref.shape[0] // 2
    greet_column(depth)
    slots_moves(inputs_ref, source_ref, slot_sems, depth, "start")
    direct = [
        send(one, weights_ref.at[chip, kind], near_sems, 2 * kind + turn, bit)
        for kind, one in enumerate(mine)
        for turn, bit in enumerate((ALONG_X, ALONG_Y))
    ]
    for one in direct:
        one.start()
    local = [
        pltpu.make_async_copy(one, weights_ref.at[chip, kind], local_sems.at[kind]) for kind, one in enumerate(mine)
    ]
    cuts = []
    for kind, (whole_one, out) in enumerate(((up_ref, up_out_ref), (down_ref, down_out_ref))):
        cuts.append(send(whole_one.at[:, 1 - core], out.at[core], cut_sems, kind, CORE))
        local.append(pltpu.make_async_copy(whole_one.at[:, core], kept.at[kind], local_sems.at[3 + kind]))
    for one in cuts + local:
        one.start()
    for one in direct:
        one.wait_recv()
    onward = []
    for turn, (bit, came) in enumerate(((ALONG_X, ALONG_Y), (ALONG_Y, ALONG_X))):
        piece = weights_ref.at[chip_of(came), :, pl.ds(turn * half, half)]
        onward.append(send(piece, piece, far_sems, turn, bit))
    for one in onward:
        one.start()

    moves = []
    for slot in range(held):
        slots_came(source_ref, slot_sems, slot)
        source = source_ref[slot].astype(WIDE)
        rms = inverse_root(jnp.mean(source * source, axis=1, keepdims=True) + EPSILON)
        here = pl.ds(pl.multiple_of(core * (rows // 2) + slot * span, span), span)
        normed_ref[here, :] = (source * rms * gain_ref[...]).astype(LOW)
        moves.append(send(normed_ref.at[here], normed_ref.at[here], row_sems, slot, CORE))
        moves[-1].start()
    for one in moves:
        one.wait()
    for one in local:
        one.wait()

    def project(number):
        weight = weights_ref[number].reshape(-1, weights_ref.shape[3])
        product = dot(normed_ref[...], weight, NT).astype(LOW)
        lanes = pl.ds(pl.multiple_of(number * LANES, LANES), LANES)
        for kind, out in enumerate((query_out_ref, key_out_ref, value_out_ref)):
            out[:, lanes] = product[:, kind * LANES : (kind + 1) * LANES]

    def some(turn, carry):
        project(jnp.where(turn == 0, chip, jnp.where(turn == 1, chip_of(ALONG_X), chip_of(ALONG_Y))))
        return carry

    lax.fori_loop(0, 3, some, 0)
    for one in onward:
        one.wait()
    stored = [
        pltpu.make_async_copy(one, there, local_sems.at[5 + number])
        for number, (one, there) in enumerate(
            (
                (normed_ref, normed_out_ref),
                (source_ref, source_out_ref),
                (weights_ref, weights_out_ref),
                (kept.at[0], up_out_ref.at[core]),
                (kept.at[1], down_out_ref.at[core]),
            )
        )
    ]
    for one in stored:
        one.start()
    project(chip_of(ALONG_X, ALONG_Y))
    for one in stored:
        one.wait()
    for one in direct:
        one.wait_send()
    for one in cuts:
        one.wait()
    slots_moves(inputs_ref, source_ref, slot_sems, depth, "end")


def enter(inputs, projections, up, down, gain):
    held, span, width = inputs.shape
    depth = lax.axis_size("seq")
    rows = 2 * held * span
    slim = projections[0].shape[0]
    thick = up.shape[0] // 4
    vmem, anywhere = (pl.BlockSpec(memory_space=pltpu.VMEM), pl.BlockSpec(memory_space=pltpu.HBM))
    shape = jax.ShapeDtypeStruct
    return pl.pallas_call(
        functools.partial(enter_kernel, depth),
        in_specs=[anywhere] * 6 + [vmem],
        out_specs=[anywhere] + [vmem] * 3 + [anywhere] * 4,
        out_shape=[shape((rows, width), LOW)]
        + [shape((rows, 4 * slim), LOW)] * 3
        + [shape((held, span, width), LOW), shape((4, 3, slim, width), LOW)]
        + [shape((2, 2, thick, width), LOW)] * 2,
        scratch_shapes=[
            pltpu.VMEM((rows, width), LOW),
            pltpu.VMEM((held, span, width), LOW),
            pltpu.VMEM((4, 3, slim, width), LOW),
            pltpu.VMEM((2, 2, thick, width), LOW),
            pltpu.SemaphoreType.DMA((2, held)),
            pltpu.SemaphoreType.DMA((2, 6)),
            pltpu.SemaphoreType.DMA((2, 2)),
            pltpu.SemaphoreType.DMA((2, 2)),
            pltpu.SemaphoreType.DMA((2, held)),
            pltpu.SemaphoreType.DMA((10,)),
        ],
        compiler_params=pltpu.CompilerParams(vmem_limit_bytes=62 << 20, collective_id=4, has_side_effects=True),
        cost_estimate=pl.CostEstimate(flops=24 * rows * slim * width, bytes_accessed=16 << 20, transcendentals=0),
        name="enter",
    )(inputs, *projections, up.reshape(2, 2, thick, width), down.reshape(2, 2, thick, width), gain)


def through_kernel(
    depth,
    length_ref,
    query_ref,
    key_ref,
    value_ref,
    near_ref,
    source_ref,
    gain_ref,
    output_ref,
    up_ref,
    down_ref,
    cotangent_ref,
    log_ref,
    context_ref,
    hidden_ref,
    far_context_out_ref,
    own_output_out_ref,
    far_output_out_ref,
    normed_ref,
    grad_ref,
    ups_ref,
    downs_ref,
    bias,
    keys,
    values,
    context,
    came,
    far_context_ref,
    own_output_ref,
    far_output_ref,
    normed,
    grad,
    slot_sems,
    near_sems,
    far_sems,
    deep_sems,
    core_sems,
    context_sems,
    local,
):
    rows = query_ref.shape[0]
    width = source_ref.shape[1]
    pair = pl.program_id(0)
    last = depth - 1
    held = depth // 2
    core = lax.rem(lax.axis_index("fsdp"), 2)
    chip = chip_of()
    own = pl.ds(pl.multiple_of(core * (rows // 2), rows // 2), rows // 2)
    other = pl.ds(pl.multiple_of((1 - core) * (rows // 2), rows // 2), rows // 2)
    half = output_ref.shape[0] // 2
    place, index = (lax.axis_index("seq"), lax.axis_index("fsdp"))
    parity = lax.rem(place, 2)
    unit = down_ref.shape[0] // 2
    mine = pl.ds(pl.multiple_of(parity * unit, unit), unit)
    direct = []
    for one, there in (
        (output_ref, own_output_ref.at[chip]),
        (down_ref.at[mine], downs_ref.at[chip, mine]),
        (up_ref, ups_ref.at[chip]),
    ):
        for bit in (ALONG_X, ALONG_Y):
            direct.append(send(one, there, near_sems, len(direct), bit))
    exchange = [
        push(
            downs_ref.at[chip_of(bit), mine],
            downs_ref.at[chip_of(bit), mine],
            deep_sems,
            (number,),
            place + 1 - 2 * parity,
            index,
        )
        for number, bit in enumerate((ALONG_X, ALONG_Y))
    ]
    onward = []
    for turn, (bit, from_bit) in enumerate(((ALONG_X, ALONG_Y), (ALONG_Y, ALONG_X))):
        piece = own_output_ref.at[chip_of(from_bit), pl.ds(turn * half, half)]
        onward.append(send(piece, piece, far_sems, turn, bit))
    keep = pltpu.make_async_copy(output_ref, own_output_ref.at[chip], local.at[0])
    swap = send(own_output_ref, far_output_ref, core_sems, 0, CORE)
    both_cores = [
        (send(one, there.at[own], core_sems, 1 + number, CORE), pltpu.make_async_copy(one, there.at[own], local.at[1 + number]))
        for number, (one, there) in enumerate(((grad, grad_ref), (normed, normed_ref)))
    ]
    stored = [
        pltpu.make_async_copy(one, there, local.at[3 + number])
        for number, (one, there) in enumerate(
            (
                (own_output_ref, own_output_out_ref),
                (far_output_ref, far_output_out_ref),
                (far_context_ref, far_context_out_ref),
            )
        )
    ]

    def context_move(number):
        lanes = pl.ds(pl.multiple_of(number * LANES, LANES), LANES)
        return send(context.at[other, lanes], far_context_ref.at[:, lanes], context_sems, number, CORE)

    @pl.when(pair == 0)
    def _():
        greet_column(depth)
        for one in direct[:4]:
            one.start()
        keep.start()
        slots_moves(cotangent_ref, came, slot_sems, depth, "start")

    @pl.when(pair == 1)
    def _():
        for one in direct[:2]:
            one.wait_recv()
        for one in onward + direct[4:]:
            one.start()

    @pl.when(pair == last - 1)
    def _():
        for one in direct[2:4]:
            one.wait_recv()
        for one in exchange:
            one.start()

    @pl.when(pair == last)
    def _():
        for one in onward:
            one.wait()
        keep.wait()
        swap.start()
        stored[0].start()
        slot_ids = core * (rows // 2) + lax.broadcasted_iota(jnp.int32, (rows // 2, 1), 0)
        valid = (slot_ids < length_ref[0]).astype(WIDE)
        for slot in range(held):
            slots_came(came, slot_sems, slot)
        grad[...] = (came[...].reshape(rows // 2, width).astype(WIDE) * valid).astype(LOW)
        for one in both_cores[0]:
            one.start()

    lanes = pl.ds(pl.multiple_of(pair * LANES, LANES), LANES)
    split_heads(key_ref[...], spare_lanes(length_ref[0], rows), keys)
    split_heads(value_ref[...], jnp.zeros((rows, LANES), LOW), values)
    near_start = rows - QUERY_ROWS - HALF_ROWS
    near_end = near_start + 2 * QUERY_ROWS
    for head in range(2):
        line = near_ref[head]
        bias[head, :, :near_start] = jnp.broadcast_to(line[:, :1], (QUERY_ROWS, near_start))
        bias[head, :, near_start:near_end] = near_block(line)
        bias[head, :, near_end:] = jnp.broadcast_to(line[:, -1:], (QUERY_ROWS, bias.shape[2] - near_end))
    lane = lax.broadcasted_iota(jnp.int32, (QUERY_ROWS, LANES), 1)
    ones = jnp.where(lax.rem(lane, HEAD_DIM) == 0, 1.0, 0.0).astype(LOW)

    def block(number, carry):
        start = pl.multiple_of(number * QUERY_ROWS, QUERY_ROWS)
        offset = pl.multiple_of(rows - QUERY_ROWS - number * QUERY_ROWS, LANES)
        both = query_ref[pl.ds(start, QUERY_ROWS), :]
        total = jnp.zeros((QUERY_ROWS, LANES), WIDE)
        for head in range(2):
            mine = lane < HEAD_DIM if head == 0 else lane >= HEAD_DIM
            logits = dot(jnp.where(mine, both, ones), keys[head], NT)
            logits = logits + bias[head, :, pl.ds(offset, rows)]
            peak = jnp.max(logits, axis=1, keepdims=True)
            exponent = jnp.exp(logits - peak)
            row_sum = jnp.sum(exponent, axis=1, keepdims=True)
            weights_low = (exponent * (1.0 / row_sum)).astype(LOW)
            total = total + dot(weights_low, values[head])
            logs = jnp.broadcast_to(peak + jnp.log(row_sum), (QUERY_ROWS, LANES))
            log_ref[0, head : head + 1, pl.ds(start, QUERY_ROWS)] = logs.T[0:1, :]
        context[pl.ds(start, QUERY_ROWS), lanes] = total.astype(LOW)
        return carry

    lax.fori_loop(0, rows // QUERY_ROWS, block, 0)
    context_move(pair).start()
    context_ref[:, lanes] = context[own, lanes]

    @pl.when(pair == last)
    def _():
        swap.wait()
        for number in range(last + 1):
            context_move(number).wait()
        for one in stored[1:]:
            one.start()
        inner = context_ref.shape[1]
        attended = dot(context_ref[...], own_output_ref[...].reshape(inner, width))
        attended = attended + dot(far_context_ref[...], far_output_ref[...].reshape(inner, width))
        hidden = source_ref[...].astype(WIDE) + attended
        hidden_ref[...] = hidden
        rms = inverse_root(jnp.mean(hidden * hidden, axis=1, keepdims=True) + EPSILON)
        normed[...] = (hidden * rms * gain_ref[...]).astype(LOW)
        for one in both_cores[1]:
            one.start()
        for one in direct:
            one.wait_send()
        for one in direct[4:]:
            one.wait_recv()
        for one in exchange:
            one.wait()
        slots_moves(cotangent_ref, came, slot_sems, depth, "end")
        for one in both_cores[0] + both_cores[1]:
            one.wait()
        for one in stored:
            one.wait()


def through(length, query, key, value, near, source, gain, output, up, down, cotangent):
    rows, inner = query.shape
    held, span, width = cotangent.shape
    depth = lax.axis_size("seq")
    pairs = inner // LANES
    vmem, anywhere = (pl.BlockSpec(memory_space=pltpu.VMEM), pl.BlockSpec(memory_space=pltpu.HBM))
    columns = pl.BlockSpec((rows, LANES), lambda pair: (0, pair))
    shape = jax.ShapeDtypeStruct
    outputs = (4,) + output.shape
    return pl.pallas_call(
        functools.partial(through_kernel, depth),
        grid=(pairs,),
        in_specs=[pl.BlockSpec(memory_space=pltpu.SMEM), columns, columns, columns]
        + [pl.BlockSpec((2, 1, 2 * QUERY_ROWS), lambda pair: (pair, 0, 0)), vmem, vmem]
        + [anywhere] * 4,
        out_specs=[pl.BlockSpec((1, 2, rows), lambda pair: (pair, 0, 0))] + [vmem] * 2 + [anywhere] * 7,
        out_shape=[shape((pairs, 2, rows), WIDE)]
        + [shape((rows // 2, inner), LOW), shape((rows // 2, width), WIDE), shape((rows // 2, inner), LOW)]
        + [shape(outputs, LOW)] * 2
        + [shape((rows, width), LOW)] * 2
        + [shape((4,) + up.shape, LOW)] * 2,
        scratch_shapes=[
            pltpu.VMEM((2, QUERY_ROWS, 2 * rows - QUERY_ROWS), WIDE),
            pltpu.VMEM((2, rows, LANES), LOW),
            pltpu.VMEM((2, rows, LANES), LOW),
            pltpu.VMEM((rows, inner), LOW),
            pltpu.VMEM((held, span, width), LOW),
            pltpu.VMEM((rows // 2, inner), LOW),
            pltpu.VMEM(outputs, LOW),
            pltpu.VMEM(outputs, LOW),
            pltpu.VMEM((rows // 2, width), LOW),
            pltpu.VMEM((rows // 2, width), LOW),
            pltpu.SemaphoreType.DMA((2, held)),
            pltpu.SemaphoreType.DMA((2, 6)),
            pltpu.SemaphoreType.DMA((2, 2)),
            pltpu.SemaphoreType.DMA((2, 2)),
            pltpu.SemaphoreType.DMA((2, 3)),
            pltpu.SemaphoreType.DMA((2, pairs)),
            pltpu.SemaphoreType.DMA((6,)),
        ],
        compiler_params=pltpu.CompilerParams(vmem_limit_bytes=62 << 20, collective_id=1, has_side_effects=True),
        cost_estimate=pl.CostEstimate(
            flops=24 * rows * rows * inner, bytes_accessed=8 * rows * inner, transcendentals=2 * pairs * rows * rows
        ),
        name="through",
    )(length, query, key, value, near, source, gain, output, up, down, cotangent)


def row_moves(source, target, sems, depth, piece, started=True):
    held = depth // 2
    place, index = (lax.axis_index("seq"), lax.axis_index("fsdp"))
    core = lax.rem(index, 2)
    there, which = (core * held + piece, index - core + place // held)
    slot = lax.rem(place, held)
    home = (there == place) & (which == index)

    @pl.when(home)
    def _():
        if started:
            pltpu.make_async_copy(source, target.at[slot], sems.at[1, piece, slot]).start()

    @pl.when(jnp.logical_not(home))
    def _():
        move = push(source, target.at[slot], sems, (piece, slot), there, which)
        if started:
            move.start()
        else:
            move.wait_send()


def rows_came(target, sems, depth):
    held = depth // 2
    place = lax.axis_index("seq")
    for slot in range(held):
        number = (lax.rem(place, held), slot)
        push(target.at[slot], target.at[slot], sems, number, place, partner(CORE)).wait_recv()


def middle_kernel(
    depth,
    length_ref,
    normed_ref,
    grad_ref,
    hidden_ref,
    gain_ref,
    output_ref,
    far_output_ref,
    context_ref,
    far_context_ref,
    up_ref,
    down_ref,
    ups_ref,
    downs_ref,
    up_part_ref,
    down_part_ref,
    up_came_ref,
    down_came_ref,
    far_up_ref,
    far_down_ref,
    context_grad_ref,
    hidden_grad_ref,
    layer_ref,
    gain_part_ref,
    output_part_ref,
    near_grad,
    out_total,
    back_total,
    fold_sent,
    fold_came,
    up_slots,
    down_slots,
    up_stages,
    down_stages,
    parts,
    parts_came,
    far_grad,
    arrived,
    stored,
    far_sems,
    unit_sems,
    fold_sems,
    core_sems,
    kept,
):
    rows, width = normed_ref.shape
    mine, wholes, fars = ((up_ref, down_ref), (ups_ref, downs_ref), (far_up_ref, far_down_ref))
    results, came = ((up_part_ref, down_part_ref), (up_came_ref, down_came_ref))
    slots, stages = ((up_slots, down_slots), (up_stages, down_stages))
    kinds = range(2)
    step = pl.program_id(0)
    last = depth - 1
    index = lax.axis_index("fsdp")
    core, x, y = (lax.rem(index, 2), lax.rem(index // 2, 2), index // 4)
    unit = up_slots.shape[1]
    half = unit // 2
    slot = lax.rem(step, 2)
    places = [chip_of(), chip_of(ALONG_X), chip_of(ALONG_Y), chip_of(ALONG_X, ALONG_Y)]

    place = lax.axis_index("seq")
    parity = lax.rem(place, 2)
    moves, exchange = ([], [])
    for turn, (bit, from_bit) in enumerate(((ALONG_X, ALONG_Y), (ALONG_Y, ALONG_X))):
        there = pl.ds(pl.multiple_of(turn * half + parity * (half // 2), half // 2), half // 2)
        moves.append(send(downs_ref.at[chip_of(from_bit), there], far_down_ref.at[there], far_sems, turn, bit))
        far = far_down_ref.at[there]
        exchange.append(push(far, far, far_sems, (4 + turn,), place + 1 - 2 * parity, index))
    for turn, (bit, from_bit) in enumerate(((ALONG_X, ALONG_Y), (ALONG_Y, ALONG_X))):
        there = pl.ds(turn * half, half)
        moves.append(send(ups_ref.at[chip_of(from_bit), there], far_up_ref.at[there], far_sems, 2 + turn, bit))
    sources = [
        mine,
        [one.at[places[1]] for one in wholes],
        [one.at[places[2]] for one in wholes],
        fars,
    ]

    def fetch(block, into):
        for number, pair in enumerate(sources):

            @pl.when(block == number)
            def _():
                for kind in kinds:
                    pltpu.make_async_copy(pair[kind], slots[kind].at[into], arrived.at[kind, into]).start()

    def store(number, kind):
        return pltpu.make_async_copy(
            stages[kind].at[number % 2], results[kind].at[places[number]], stored.at[kind, number % 2]
        )

    def first_sum(number, kind):
        block = places[number]
        if kind == 0:
            source, bit = (results[0].at[block, :, 1 - x], ALONG_X)
        else:
            source, bit = (results[1].at[block, 1 - y], ALONG_Y)
        return send(source, came[kind].at[block], unit_sems, last * kind + number, bit)

    def own_rows(which):
        return pl.ds(pl.multiple_of(which * (rows // 2), rows // 2), rows // 2)

    folds = [send(fold_sent.at[number], fold_came.at[number], fold_sems, number, CORE) for number in range(2)]

    @pl.when(step == 0)
    def _():
        greet_column(depth)
        for one in moves:
            one.start()
        fetch(0, 0)
        out_total[...] = jnp.zeros_like(out_total)
        back_total[...] = jnp.zeros_like(back_total)

    @pl.when(step + 1 < last)
    def _():
        fetch(step + 1, 1 - slot)

    @pl.when(step == 1)
    def _():
        for one in moves[:2]:
            one.wait()
        for one in exchange:
            one.start()

    for number in range(last):

        @pl.when(step == number + 1)
        def _():
            for kind in kinds:
                store(number, kind).wait()
                first_sum(number, kind).start()

    for kind in kinds:
        pltpu.make_async_copy(slots[kind].at[slot], slots[kind].at[slot], arrived.at[kind, slot]).wait()
    up, down = (slots[0][slot], slots[1][slot])
    normed, grad = (normed_ref[...], grad_ref[...])
    active, slope = gelu_parts(dot(normed, up, NT))
    active = active.astype(LOW)
    pre_grad = (dot(grad, down, NT) * slope).astype(LOW)
    back_total[...] += dot(pre_grad, up)
    out_total[...] += dot(active, down)

    @pl.when(step == last)
    def _():
        for number, total in enumerate((back_total, out_total)):
            fold_sent[number] = total[own_rows(1 - core), :].astype(LOW)
            folds[number].start()

    shape = up_stages.shape[1:]
    stages[0][slot] = dot(pre_grad, normed, TN).astype(LOW).reshape(shape)
    stages[1][slot] = dot(active, grad, TN).astype(LOW).reshape(shape)
    for number in range(last + 1):

        @pl.when(step == number)
        def _():
            for kind in kinds:
                store(number, kind).start()

    @pl.when(step == last - 1)
    def _():
        for one in moves[2:] + exchange:
            one.wait()
        fetch(last, last % 2)

    @pl.when(step == last)
    def _():
        folds[0].wait()
        normed_grad = back_total[own_rows(core), :] + fold_came[0].astype(WIDE)
        hidden = hidden_ref[...]
        rms = inverse_root(jnp.mean(hidden * hidden, axis=1, keepdims=True) + EPSILON)
        scaled = hidden * rms
        gained = gain_ref[...] * normed_grad
        inside = jnp.mean(gained * scaled, axis=1, keepdims=True)
        hidden_grad = grad_ref[own_rows(core), :].astype(WIDE) + rms * (gained - scaled * inside)
        gain_part_ref[...] = jnp.sum(normed_grad * scaled, axis=0, keepdims=True)
        hidden_grad_ref[...] = hidden_grad
        hidden_low = hidden_grad.astype(LOW)
        far_grad[...] = dot(hidden_low, far_output_ref[...], NT).astype(LOW)
        move = send(far_grad, context_grad_ref.at[own_rows(core)], core_sems, 0, CORE)
        move.start()
        part_shape = parts.shape[1:]
        parts[0] = dot(context_ref[...], hidden_low, TN).astype(LOW).reshape(part_shape)
        parts[1] = dot(far_context_ref[...], hidden_low, TN).astype(LOW).reshape(part_shape)
        others = [
            send(parts.at[kind, :, :, 1 - core], parts_came.at[kind], core_sems, 1 + kind, CORE) for kind in kinds
        ]
        for one in others:
            one.start()
        near_grad[...] = dot(hidden_low, output_ref[...], NT).astype(LOW)
        keep = pltpu.make_async_copy(near_grad, context_grad_ref.at[own_rows(core)], kept)
        keep.start()
        folds[1].wait()
        slot_ids = core * (rows // 2) + lax.broadcasted_iota(jnp.int32, (rows // 2, 1), 0)
        valid = (slot_ids < length_ref[0]).astype(WIDE)
        layer_rows = (hidden + (out_total[own_rows(core), :] + fold_came[1].astype(WIDE))) * valid
        layer_ref[...] = layer_rows.astype(LOW).reshape(layer_ref.shape)
        for one in others:
            one.wait()
        for turn in range(depth):
            near = parts[0, turn, :, core].astype(WIDE) + parts_came[1, turn].astype(WIDE)
            output_part_ref[turn, core] = near.astype(LOW)
            far = parts[1, turn, :, core].astype(WIDE) + parts_came[0, turn].astype(WIDE)
            output_part_ref[turn, 1 - core] = far.astype(LOW)
        for kind in kinds:
            store(last, kind).wait()
        move.wait()
        keep.wait()
        for number in range(last):
            for kind in kinds:
                first_sum(number, kind).wait()


def middle(length, normed, grad, hidden, gain, outputs, contexts, mine, wholes):
    rows, width = normed.shape
    inner = outputs[0].shape[0]
    unit = mine[0].shape[0]
    depth = lax.axis_size("seq")
    held = depth // 2
    thick, slim = (unit // 4, inner // 16)
    vmem, anywhere = (pl.BlockSpec(memory_space=pltpu.VMEM), pl.BlockSpec(memory_space=pltpu.HBM))
    shape = jax.ShapeDtypeStruct
    part = (depth, 2, 2, thick, width)
    return pl.pallas_call(
        functools.partial(middle_kernel, depth),
        grid=(depth,),
        in_specs=[pl.BlockSpec(memory_space=pltpu.SMEM)] + [vmem] * 8 + [anywhere] * 4,
        out_specs=[anywhere] * 7 + [vmem] * 4,
        out_shape=[shape(part, LOW)] * 2
        + [shape((depth, 2, thick, width), LOW)] * 2
        + [shape((unit, width), LOW)] * 2
        + [
            shape((rows, inner), LOW),
            shape((rows // 2, width), WIDE),
            shape((held, rows // depth, width), LOW),
            shape((1, width), WIDE),
            shape((4, 2, 2, slim, width), LOW),
        ],
        scratch_shapes=[pltpu.VMEM((rows // 2, inner), LOW)]
        + [pltpu.VMEM((rows, width), WIDE)] * 2
        + [pltpu.VMEM((2, rows // 2, width), LOW)] * 2
        + [pltpu.VMEM((2, unit, width), LOW)] * 2
        + [pltpu.VMEM((2, 2, 2, thick, width), LOW)] * 2
        + [
            pltpu.VMEM((2, 4, 2, 2, slim, width), LOW),
            pltpu.VMEM((2, 4, 2, slim, width), LOW),
            pltpu.VMEM((rows // 2, inner), LOW),
            pltpu.SemaphoreType.DMA((2, 2)),
            pltpu.SemaphoreType.DMA((2, 2)),
            pltpu.SemaphoreType.DMA((2, 6)),
            pltpu.SemaphoreType.DMA((2, 2 * (depth - 1))),
            pltpu.SemaphoreType.DMA((2, 2)),
            pltpu.SemaphoreType.DMA((2, 3)),
            pltpu.SemaphoreType.DMA,
        ],
        compiler_params=pltpu.CompilerParams(vmem_limit_bytes=62 << 20, collective_id=2, has_side_effects=True),
        cost_estimate=pl.CostEstimate(
            flops=52 * unit * rows * width,
            bytes_accessed=32 * unit * width + 12 * rows * width,
            transcendentals=8 * unit * rows,
        ),
        name="middle",
    )(length, normed, grad, hidden, gain, *outputs, *contexts, *mine, *wholes)


def add_rows(target, source):
    target[...] = (target[...].astype(WIDE) + source[...].astype(WIDE)).astype(LOW)


def backward_kernel(
    depth,
    length_ref,
    query_ref,
    key_ref,
    value_ref,
    grad_ref,
    log_ref,
    near_ref,
    normed_ref,
    weight_ref,
    source_ref,
    hidden_ref,
    gain_ref,
    small_ref,
    output_ref,
    layer_ref,
    up_ref,
    down_ref,
    up_came_ref,
    down_came_ref,
    layer_out_ref,
    input_grad_ref,
    heads_out_ref,
    units_out_ref,
    small_out_ref,
    bias,
    spare,
    keys,
    values,
    padded,
    key_total,
    value_total,
    tiles,
    lows,
    part,
    x_block,
    y_block,
    x_came,
    y_came,
    x_last,
    y_last,
    heads_came,
    units,
    units_came,
    units_last,
    units_far,
    fold_sent,
    fold_came,
    row_sent,
    row_came,
    small,
    small_came,
    swap_sems,
    first_sems,
    second_sems,
    third_sems,
    late_sems,
    unit_second_sems,
    unit_third_sems,
    fold_sems,
    row_sems,
    layer_sems,
    small_sems,
    early_sems,
    local_sems,
):
    rows = query_ref.shape[0]
    width = normed_ref.shape[1]
    held = depth // 2
    step = pl.program_id(0)
    last = depth - 1
    place, index = (lax.axis_index("seq"), lax.axis_index("fsdp"))
    core, x, y = (lax.rem(index, 2), lax.rem(index // 2, 2), index // 4)
    column = index - core

    def owner(block):
        return lax.rem(place + 1 + block, depth)

    def beside(source, target, sems, number, bit):
        return push(source, target, sems, number, place, partner(bit))


    def unit_place(hop):
        return chip_of(*(bit for bit in (ALONG_X, ALONG_Y) if hop & (bit // 2)))

    def unit_source(kind, hop):
        block = unit_place(hop)
        if kind == 0:
            return (up_ref.at[block, :, 1 - x], up_ref.at[block, :, x], ALONG_X)
        return (down_ref.at[block, 1 - y], down_ref.at[block, y], ALONG_Y)

    def unit_came(kind, hop):
        return units_came.at[kind, hop]

    def unit_own(kind, hop):
        return pltpu.make_async_copy(unit_source(kind, hop)[1], units.at[kind, hop], local_sems.at[kind, hop])

    def unit_early(kind, hop):
        there = (up_came_ref, down_came_ref)[kind].at[unit_place(hop)]
        return pltpu.make_async_copy(there, units_came.at[kind, hop], early_sems.at[kind, hop])

    def unit_late(kind, hop):
        away, _, bit = unit_source(kind, hop)
        return beside(away, units_came.at[kind, late[kind]], late_sems, (kind,), bit)

    late = (2, 1)

    def units_start():
        for kind in range(2):
            unit_late(kind, 3).start()
        for kind in range(2):
            for hop in range(4):
                unit_own(kind, hop).start()
                if hop != late[kind]:
                    unit_early(kind, hop).start()

    def unit_halves(kind, hop):
        if kind == 0:
            return (units.at[0, hop, 1 - y], units.at[0, hop, y], ALONG_Y)
        return (units.at[1, hop, 1 - x], units.at[1, hop, x], ALONG_X)

    def unit_second(kind, hop):
        away, _, bit = unit_halves(kind, hop)
        there = hop ^ (bit // 2)
        return push(
            away, units_last.at[kind, there], unit_second_sems, (kind, hop), place, partner(bit), (kind, there)
        )

    def unit_first(kind, hop):
        unit_own(kind, hop).wait()
        if hop == late[kind]:
            unit_late(kind, 3).wait()
        else:
            unit_early(kind, hop).wait()
        add_rows(units.at[kind, hop], units_came.at[kind, hop])
        unit_second(kind, hop).start()


    def unit_arrived(kind, block, slot):
        far = units_far.at[kind, block, slot]
        return push(far, far, unit_third_sems, (kind, block, slot), place, partner(CORE))

    def unit_direct(kind, hop):
        block = unit_place(hop)
        slot = lax.rem(block + 2 * depth - place - 1, depth)
        own = unit_halves(kind, hop)[1]
        return push(
            own, units_far.at[kind, block, slot], unit_third_sems, (kind, block, 0), block, index, (kind, block, slot)
        )

    def unit_summed(kind, hop):
        unit_second(kind, hop).wait_send()
        unit_second(kind, hop ^ (2 - kind)).wait_recv()
        add_rows(unit_halves(kind, hop)[1], units_last.at[kind, hop])

        @pl.when(unit_place(hop) != place)
        def _():
            unit_direct(kind, hop).start()

    def unit_finish(kind, hop):
        block = unit_place(hop)

        @pl.when(block != place)
        def _():
            unit_direct(kind, hop).wait_send()

        @pl.when(block == place)
        def _():
            total = unit_halves(kind, hop)[1][...].astype(WIDE)
            for slot in range(depth - 1):
                unit_arrived(kind, block, slot).wait_recv()
                total = total + units_far[kind, block, slot].astype(WIDE)
            units_out_ref[kind] = total


    def swaps(block):
        moves = [
            beside(part.at[kind, :, 1 - core], x_block.at[block, :, core, kind], swap_sems, (kind, block), CORE)
            for kind in range(2)
        ]
        moves.append(beside(part.at[2, :, 1 - core], y_block.at[block, core, :, 0], swap_sems, (2, block), CORE))
        return moves

    def output_copy(block):
        return pltpu.make_async_copy(output_ref.at[owner(block)], y_block.at[block, :, :, 1], local_sems.at[2, block])

    def firsts(block):
        return (
            beside(x_block.at[block, 1 - x], x_came.at[block], first_sems, (0, block), ALONG_X),
            beside(y_block.at[block, 1 - y], y_came.at[block], first_sems, (1, block), ALONG_Y),
        )

    def seconds(block):
        return (
            beside(x_block.at[block, x, 1 - y], x_last.at[block], second_sems, (0, block), ALONG_Y),
            beside(y_block.at[block, y, 1 - x], y_last.at[block], second_sems, (1, block), ALONG_X),
        )

    def thirds(block):
        return [
            push(own, heads_came.at[block, kind], third_sems, (kind, block), owner(block), index)
            for kind, own in enumerate((x_block.at[block, x, y], y_block.at[block, y, x]))
        ]

    def heads_start(block):
        for one in swaps(block):
            one.wait_recv()
        output_copy(block).wait()
        for one in firsts(block):
            one.start()

    def heads_first(block):
        for one in firsts(block):
            one.wait()
        add_rows(x_block.at[block, x], x_came.at[block])
        add_rows(y_block.at[block, y], y_came.at[block])
        for one in seconds(block):
            one.start()

    def heads_second(block, mine=False):
        for one in seconds(block):
            one.wait()
        add_rows(x_block.at[block, x, y], x_last.at[block])
        add_rows(y_block.at[block, y, x], y_last.at[block])
        if not mine:
            for one in thirds(block):
                one.start()

    @pl.when(step == 0)
    def _():
        greet_column(depth)
        units_start()
        for block in range(depth):
            output_copy(block).start()
        for piece in range(held):
            row_moves(layer_ref.at[piece], layer_out_ref, layer_sems, depth, piece)
        spare[...] = spare_lanes(length_ref[0], rows)
        for head in range(2):
            padded[head, :HALF_ROWS, :] = jnp.zeros((HALF_ROWS, QUERY_ROWS), LOW)
            padded[head, rows + HALF_ROWS :, :] = jnp.zeros((HALF_ROWS, QUERY_ROWS), LOW)

    both_ready = [(0, 1), (0, 3), (1, 2), (1, 3)]
    others = [(0, 0), (0, 2), (1, 0), (1, 1)]

    def advance(number):
        def at(turn, tick, act):
            @pl.when((step == turn) & (number == tick))
            def _():
                act()

        ready = both_ready + [(0, 0), (1, 0)]
        at(0, 1, lambda: [unit_first(*one) for one in ready])
        at(1, 0, lambda: [unit_first(kind, late[kind]) for kind in range(2)])
        at(1, 3, lambda: [unit_summed(*one) for one in both_ready])
        at(2, 3, lambda: [unit_summed(*one) for one in others])
        at(3, 1, lambda: heads_first(0))

        @pl.when((step >= 1) & (number == 1))
        def _():
            heads_start(step - 1)

    pair = owner(step)
    lanes = pl.ds(pl.multiple_of(pair * LANES, LANES), LANES)
    split_heads(key_ref[:, lanes], spare[...], keys)
    split_heads(value_ref[:, lanes], jnp.zeros((rows, LANES), LOW), values)

    def low_lanes(kind):
        return pl.ds(pl.multiple_of((3 * pair + kind) * LANES, LANES), LANES)

    near_start = rows - QUERY_ROWS - HALF_ROWS
    near_end = near_start + 2 * QUERY_ROWS
    for head in range(2):
        line = near_ref[2 * pair + head]
        bias[head, :near_start, :] = jnp.broadcast_to(line[:, :1], (near_start, QUERY_ROWS))
        bias[head, near_start:near_end, :] = near_block(line).T
        bias[head, near_end:, :] = jnp.broadcast_to(line[:, -1:], (bias.shape[1] - near_end, QUERY_ROWS))
    key_total[...] = jnp.zeros_like(key_total)
    value_total[...] = jnp.zeros_like(value_total)
    tiles[...] = jnp.zeros_like(tiles)
    sums = small.at[0, pl.ds(pl.multiple_of(16 + 8 * pair, 8), 8)]
    sums[...] = jnp.zeros((8, LANES), WIDE)
    spot = lax.broadcasted_iota(jnp.int32, (1, LANES), 1)
    lane = lax.broadcasted_iota(jnp.int32, (QUERY_ROWS, LANES), 1)
    ones = jnp.where(lax.rem(lane, HEAD_DIM) == 0, 1.0, 0.0).astype(LOW)
    zero = jnp.zeros((), LOW)
    blocks = rows // QUERY_ROWS

    def block(number, carry):
        start = pl.multiple_of(number * QUERY_ROWS, QUERY_ROWS)
        offset = pl.multiple_of(rows - QUERY_ROWS - number * QUERY_ROWS, LANES)
        advance(number)
        both = query_ref[pl.ds(start, QUERY_ROWS), lanes]
        grad = grad_ref[pl.ds(start, QUERY_ROWS), lanes]
        parts = []
        for head in range(2):
            mine = lane < HEAD_DIM if head == 0 else lane >= HEAD_DIM
            logits = dot(keys[head], jnp.where(mine, both, ones), NT)
            logits = logits + bias[head, pl.ds(offset, rows), :]
            probs = jnp.exp(logits - log_ref[pair, head : head + 1, pl.ds(start, QUERY_ROWS)])
            prob_grad = dot(values[head], grad, NT)
            weighted = probs * prob_grad
            total = jnp.sum(weighted, axis=0, keepdims=True)
            score = (weighted - probs * total).astype(LOW)
            value_total[...] += dot(probs.astype(LOW), jnp.where(mine, grad, zero))
            key_total[...] += dot(score, jnp.where(mine, both, zero))
            padded[head, HALF_ROWS : HALF_ROWS + rows, :] = score
            one = dot(score, keys[head], TN)
            parts.append(one)
            columns = jnp.sum(one, axis=0, keepdims=True)
            first = HEAD_DIM * (1 - head) + 1 + number
            close = padded[head, pl.ds(start, 2 * QUERY_ROWS), :].astype(WIDE)
            quarter = [close[HALF_ROWS * turn : HALF_ROWS * (turn + 1)] for turn in range(4)]
            for turn in range(3):
                tiles[head, turn] += quarter[turn][:, :HALF_ROWS] + quarter[turn + 1][:, HALF_ROWS:]
            left = jnp.sum(quarter[0][:, HALF_ROWS:], axis=0, keepdims=True)
            right = jnp.sum(quarter[3][:, :HALF_ROWS], axis=0, keepdims=True)
            left = left + jnp.where(spot == first, columns, 0.0)
            right = right + jnp.where(spot == first + blocks, columns, 0.0)
            sums[4 * head + 2 : 4 * head + 3, :] += left
            sums[4 * head + 3 : 4 * head + 4, :] += right
        chosen = jnp.where(lane < HEAD_DIM, parts[0], parts[1])
        lows[pl.ds(start, QUERY_ROWS), low_lanes(0)] = chosen.astype(LOW)
        return carry

    lax.fori_loop(0, blocks, block, 0)
    lows[:, low_lanes(1)] = key_total[...].astype(LOW)
    lows[:, low_lanes(2)] = value_total[...].astype(LOW)
    shape = (HALF_ROWS, HALF_ROWS)
    upper = lax.broadcasted_iota(jnp.int32, shape, 0) <= lax.broadcasted_iota(jnp.int32, shape, 1)
    for head in range(2):
        before, centre, behind = (tiles[head, turn] for turn in range(3))
        sums[4 * head : 4 * head + 1, :] = diagonal_sums(jnp.where(upper, centre, before))
        sums[4 * head + 1 : 4 * head + 2, :] = diagonal_sums(jnp.where(upper, behind, centre))
        sums[4 * head + 2 : 4 * head + 3, :] += jnp.sum(jnp.where(upper, before, 0.0), axis=0, keepdims=True)
        sums[4 * head + 3 : 4 * head + 4, :] += jnp.sum(jnp.where(upper, 0.0, behind), axis=0, keepdims=True)

    @pl.when(step >= 1)
    def _():
        for one in swaps(step - 1):
            one.wait_send()

    for kind in range(3):
        product = dot(lows[:, low_lanes(kind)], normed_ref[...], TN).astype(LOW)
        part[kind] = product.reshape(part.shape[1:])
    for one in swaps(step):
        one.start()
    for half in range(2):
        for kind in range(2):
            x_block[step, half, core, kind] = part[kind, half, core]
        y_block[step, core, half, 0] = part[2, half, core]

    @pl.when(step == last)
    def _():
        span = rows // 2 // held
        for piece in range(held):
            away = pl.ds(pl.multiple_of((1 - core) * (rows // 2) + piece * span, span), span)
            fold_sent[piece] = dot(lows[away, :], weight_ref[...]).astype(LOW)
            beside(fold_sent.at[piece], fold_came.at[piece], fold_sems, (piece,), CORE).start()
        heads_second(0)
        heads_first(1)
        for one in swaps(last):
            one.wait_send()
        heads_start(last)

        gain_total = jnp.zeros((1, width), WIDE)
        for piece in range(held):
            here = pl.ds(pl.multiple_of(core * (rows // 2) + piece * span, span), span)
            product = dot(lows[here, :], weight_ref[...])
            beside(fold_sent.at[piece], fold_came.at[piece], fold_sems, (piece,), CORE).wait()
            product = product + fold_came[piece].astype(WIDE)
            local = slice(piece * span, (piece + 1) * span)
            source = source_ref[local, :].astype(WIDE)
            rms = inverse_root(jnp.mean(source * source, axis=1, keepdims=True) + EPSILON)
            scaled = source * rms
            gain_total = gain_total + jnp.sum(product * scaled, axis=0, keepdims=True)
            gained = gain_ref[...] * product
            inside = jnp.mean(gained * scaled, axis=1, keepdims=True)
            row_sent[piece] = (hidden_ref[local, :] + rms * (gained - scaled * inside)).astype(LOW)
            if piece == held - 1:
                for number in range(width // LANES):
                    small[0, number : number + 1, :] = gain_total[:, number * LANES : (number + 1) * LANES]
                small[0, 8:16, :] = small_ref[...]
                moves = [
                    push(small.at[0], small_came.at[turn], small_sems, (turn,), lax.rem(place + turn, depth), index)
                    for turn in range(1, depth)
                ]
                for one in moves:
                    one.start()
            row_moves(row_sent.at[piece], row_came, row_sems, depth, piece)
            if piece == 0:
                heads_first(last - 1)
                heads_second(1)
        heads_second(last - 1)
        heads_first(last)
        heads_second(last, True)

        for one in moves:
            one.wait()
        small[1] = small[0] + sum(small_came[turn] for turn in range(1, depth))
        for turn, bit in ((1, ALONG_X), (2, ALONG_Y)):
            move = beside(small.at[turn], small_came.at[depth + turn - 1], small_sems, (depth + turn - 1,), bit)
            move.start()
            move.wait()
            small[turn + 1] = small[turn] + small_came[depth + turn - 1]
        move = beside(small.at[3], small_came.at[0], small_sems, (0,), CORE)
        move.start()
        move.wait()
        small_out_ref[core] = small[3]
        small_out_ref[1 - core] = small_came[0]

        for block in range(last):
            for one in thirds(block):
                one.wait()
        for kind in range(2):
            for hop in range(4):
                unit_finish(kind, hop)
        heads_out_ref[0:2] = x_block[last, x, y].astype(WIDE) + sum(
            heads_came[one, 0].astype(WIDE) for one in range(depth - 1)
        )
        heads_out_ref[2:4] = y_block[last, y, x].astype(WIDE) + sum(
            heads_came[one, 1].astype(WIDE) for one in range(depth - 1)
        )
        for piece in range(held):
            row_moves(layer_ref.at[piece], layer_out_ref, layer_sems, depth, piece, False)
            row_moves(row_sent.at[piece], row_came, row_sems, depth, piece, False)
        rows_came(layer_out_ref, layer_sems, depth)
        rows_came(row_came, row_sems, depth)
        input_grad_ref[...] = row_came[...].astype(WIDE)


def backward(
    length, query, key, value, grad, logs, near, normed, weights, source, hidden, gain, ffn_gain_part, output_part, layer, *units
):
    rows, inner = query.shape
    width = normed.shape[1]
    depth = lax.axis_size("seq")
    held = depth // 2
    span = rows // depth
    slim, thick = (output_part.shape[3], units[0].shape[3])
    vmem, anywhere = (pl.BlockSpec(memory_space=pltpu.VMEM), pl.BlockSpec(memory_space=pltpu.HBM))
    shape = jax.ShapeDtypeStruct
    small_rows = 2 * (width // LANES) + 8 * depth
    sems = [(3, depth), (2, depth), (2, depth), (2, depth), (2,), (2, depth), (2, depth, depth - 1)]
    sems += [(held,), (held, held), (held, held), (depth + 2,)]
    return pl.pallas_call(
        functools.partial(backward_kernel, depth),
        grid=(depth,),
        in_specs=[pl.BlockSpec(memory_space=pltpu.SMEM)] + [vmem] * 12 + [anywhere, vmem] + [anywhere] * 4,
        out_specs=[anywhere] + [vmem] * 4,
        out_shape=[
            shape((held, span, width), LOW),
            shape((held, span, width), WIDE),
            shape((4, slim, width), WIDE),
            shape((2, thick, width), WIDE),
            shape((2, small_rows, LANES), WIDE),
        ],
        scratch_shapes=[
            pltpu.VMEM((2, 2 * rows - QUERY_ROWS, QUERY_ROWS), WIDE),
            pltpu.VMEM((rows, LANES), LOW),
            pltpu.VMEM((2, rows, LANES), LOW),
            pltpu.VMEM((2, rows, LANES), LOW),
            pltpu.VMEM((2, rows + QUERY_ROWS, QUERY_ROWS), LOW),
            pltpu.VMEM((rows, LANES), WIDE),
            pltpu.VMEM((rows, LANES), WIDE),
            pltpu.VMEM((2, 3, HALF_ROWS, HALF_ROWS), WIDE),
            pltpu.VMEM((rows, 3 * inner), LOW),
            pltpu.VMEM((3, 2, 2, slim, width), LOW),
        ]
        + [pltpu.VMEM((depth, 2, 2, 2, slim, width), LOW)] * 2
        + [pltpu.VMEM((depth, 2, 2, slim, width), LOW)] * 2
        + [pltpu.VMEM((depth, 2, slim, width), LOW)] * 2
        + [
            pltpu.VMEM((depth - 1, 2, 2, slim, width), LOW),
            pltpu.VMEM((2, depth, 2, thick, width), LOW),
            pltpu.VMEM((2, depth, 2, thick, width), LOW),
            pltpu.VMEM((2, depth, thick, width), LOW),
            pltpu.VMEM((2, depth, depth - 1, thick, width), LOW),
        ]
        + [pltpu.VMEM((held, span, width), LOW)] * 4
        + [pltpu.VMEM((4, small_rows, LANES), WIDE), pltpu.VMEM((depth + 2, small_rows, LANES), WIDE)]
        + [pltpu.SemaphoreType.DMA((2,) + one) for one in sems]
        + [pltpu.SemaphoreType.DMA((2, depth)), pltpu.SemaphoreType.DMA((3, depth))],
        compiler_params=pltpu.CompilerParams(
            vmem_limit_bytes=62 << 20, collective_id=3, has_side_effects=True
        ),
        cost_estimate=pl.CostEstimate(
            flops=60 * rows * rows * inner, bytes_accessed=14 * rows * inner, transcendentals=rows * rows * inner // 64
        ),
        name="backward",
    )(length, query, key, value, grad, logs, near, normed, weights, source, hidden, gain, ffn_gain_part, output_part, layer, *units)


def flip(value, bit):
    size = lax.axis_size("fsdp")
    return lax.ppermute(value, "fsdp", [(one, one ^ bit) for one in range(size)])


def other_core(value):
    return flip(value, 1)


def rounds_of(inverse):
    depth, size = (lax.axis_size("seq"), lax.axis_size("fsdp"))
    held = depth // 2
    rounds = []
    for step in range(held):
        pairs = []
        for place in range(depth):
            for index in range(size):
                target = (index % 2) * held + (place + step) % held
                there = target * size + index - index % 2 + place // held
                here = place * size + index
                pairs.append((there, here) if inverse else (here, there))
        rounds.append(pairs)
    return rounds


def to_sequence(blocks):
    held, span, width = blocks.shape
    place = lax.axis_index("seq")
    out = jnp.zeros((held, span, width), blocks.dtype)
    for step, pairs in enumerate(rounds_of(False)):
        sent = lax.dynamic_index_in_dim(blocks, (place + step) % held, 0, keepdims=False)
        got = lax.ppermute(sent, BOTH, pairs)
        out = lax.dynamic_update_index_in_dim(out, got, (place + held - step) % held, 0)
    return out.reshape(held * span, width)


def to_slots(rows, held):
    span, width = (rows.shape[0] // held, rows.shape[1])
    place = lax.axis_index("seq")
    blocks = rows.reshape(held, span, width)
    out = jnp.zeros(blocks.shape, rows.dtype)
    for step, pairs in enumerate(rounds_of(True)):
        sent = lax.dynamic_index_in_dim(blocks, (place + held - step) % held, 0, keepdims=False)
        got = lax.ppermute(sent, BOTH, pairs)
        out = lax.dynamic_update_index_in_dim(out, got, (place + step) % held, 0)
    return out


def whole(mine, core):
    other = other_core(mine)
    return jnp.where(
        core == 0, jnp.concatenate([mine, other], axis=0), jnp.concatenate([other, mine], axis=0)
    )


def fold(partial, core):
    half = partial.shape[0] // 2
    sent = lax.dynamic_slice_in_dim(partial, (1 - core) * half, half, 0)
    kept = lax.dynamic_slice_in_dim(partial, core * half, half, 0)
    return kept + other_core(sent)


def fast_plane():
    return lax.axis_size("fsdp") == 8 and lax.axis_size("seq") == 4


def own_head_rows(weight, core):
    width = weight.shape[1]
    return lax.dynamic_index_in_dim(weight.reshape(4, 2, -1, width), core, 1, keepdims=False).reshape(-1, width)


def add_low(left, right):
    return (left.astype(WIDE) + right.astype(WIDE)).astype(LOW)


def pick(value, index, axis):
    return lax.dynamic_index_in_dim(value, index, axis, keepdims=False)


def shards(
    inputs,
    lengths,
    cotangent,
    query_weight,
    key_weight,
    value_weight,
    output_weight,
    up_weight,
    down_weight,
    attn_gain,
    ffn_gain,
    bias_table,
):
    held, span, width = inputs.shape
    depth, size = (lax.axis_size("seq"), lax.axis_size("fsdp"))
    place, index = (lax.axis_index("seq"), lax.axis_index("fsdp"))
    core = index % 2
    rows = held * span
    inner = HEADS * HEAD_DIM
    fast = fast_plane()

    near_lengths = jnp.where(
        core == 0,
        jnp.concatenate([lengths, other_core(lengths)]),
        jnp.concatenate([other_core(lengths), lengths]),
    )
    length = lax.dynamic_slice_in_dim(near_lengths, place, 1, 0)

    own_table = lax.dynamic_index_in_dim(bias_table.reshape(BUCKETS, 4, 2, 2), core, 2, keepdims=False)
    own_table = own_table.reshape(BUCKETS, HEADS // 2)
    near = near_bias(own_table)

    if fast:
        normed_one, query, key, value, source_low, weights, up_mine, down_mine = enter(
            inputs, (query_weight, key_weight, value_weight), up_weight, down_weight, attn_gain[None, :]
        )
        source_low = source_low.reshape(rows, width)
        mine = (up_mine.reshape(-1, width), down_mine.reshape(-1, width))
        logs, near_context, hidden_one, far_context, own_output, far_output, normed_two, grad_low, *wholes = through(
            length,
            query,
            key,
            value,
            near,
            source_low,
            ffn_gain[None, :],
            output_weight,
            *mine,
            cotangent,
        )
        own_output, far_output = (own_output.reshape(-1, width), far_output.reshape(-1, width))
    else:
        own_three = [
            own_head_rows(lax.all_gather(one, "fsdp", axis=0, tiled=True), core)
            for one in (query_weight, key_weight, value_weight)
        ]
        full = lax.all_gather(output_weight, "fsdp", axis=0, tiled=True)
        own_output = own_head_rows(full, core)
        far_output = own_head_rows(full, 1 - core)
        own_up, own_down = (
            pick(
                lax.all_gather(one, "fsdp", axis=0, tiled=True).reshape(depth, size // 2, 2, -1, width), core, 2
            ).reshape(-1, width)
            for one in (up_weight, down_weight)
        )
        mask_rows = (core * rows + jnp.arange(rows, dtype=jnp.int32) < length[0])[:, None].astype(WIDE)
        source_low = to_sequence(inputs)
        source = source_low.astype(WIDE)
        rms_one = lax.rsqrt(jnp.mean(source * source, axis=1, keepdims=True) + EPSILON)
        scaled_one = source * rms_one
        normed_one = whole((scaled_one * attn_gain).astype(LOW), core)
        query, key, value = [dot(normed_one, one, NT).astype(LOW) for one in own_three]
        context, logs = attend(length, query, key, value, near)
        mine = (own_up, own_down)
        near_context = lax.dynamic_slice_in_dim(context, core * rows, rows, 0)
        far_context = other_core(lax.dynamic_slice_in_dim(context, (1 - core) * rows, rows, 0))
        hidden_one = source + (dot(near_context, own_output) + dot(far_context, far_output))
        rms_two = lax.rsqrt(jnp.mean(hidden_one * hidden_one, axis=1, keepdims=True) + EPSILON)
        scaled_two = hidden_one * rms_two
        normed_two = whole((scaled_two * ffn_gain).astype(LOW), core)
        grad_out = to_sequence(cotangent).astype(WIDE) * mask_rows
        grad_low = whole(grad_out.astype(LOW), core)

    if fast:
        up_part, down_part, up_came, down_came, _, _, context_grad, hidden_grad, layer_rows, ffn_gain_part, output_part = middle(
            length,
            normed_two,
            grad_low,
            hidden_one,
            ffn_gain[None, :],
            (own_output, far_output),
            (near_context, far_context),
            mine,
            wholes,
        )
    else:
        up_part, down_part, mlp_part, normed_part = feed(normed_two, grad_low, *mine)
        normed_grad = fold(normed_part, core)
        layer_rows = ((hidden_one + fold(mlp_part, core)) * mask_rows).astype(LOW)
        gained_two = ffn_gain * normed_grad
        hidden_grad = grad_out + rms_two * (
            gained_two - scaled_two * jnp.mean(gained_two * scaled_two, axis=1, keepdims=True)
        )
        ffn_gain_part = jnp.sum(normed_grad * scaled_two, axis=0)
        hidden_low = hidden_grad.astype(LOW)
        near_grad = dot(hidden_low, own_output, NT).astype(LOW)
        far_grad = other_core(dot(hidden_low, far_output, NT).astype(LOW))
        context_grad = jnp.where(
            core == 0,
            jnp.concatenate([near_grad, far_grad], axis=0),
            jnp.concatenate([far_grad, near_grad], axis=0),
        )
        near_output_part = dot(near_context, hidden_low, TN).astype(LOW)
        far_output_part = dot(far_context, hidden_low, TN).astype(LOW)

    if fast:
        layer_out, input_grad, heads_grad, units_grad, small = backward(
            length,
            query,
            key,
            value,
            context_grad,
            logs,
            near,
            normed_one,
            weights.reshape(-1, width),
            source_low,
            hidden_grad,
            attn_gain[None, :],
            ffn_gain_part.reshape(-1, LANES),
            output_part,
            layer_rows,
            up_part,
            down_part,
            up_came,
            down_came,
        )
        query_grad, key_grad, value_grad, output_grad = (heads_grad[number] for number in range(4))
        up_grad, down_grad = (units_grad[0], units_grad[1])
        gain_lines = width // LANES
        gains = (small[0] + small[1])[: 2 * gain_lines].reshape(2, width)
        attn_gain_sum, ffn_gain_sum = (gains[0], gains[1])
        sums = jnp.swapaxes(small[:, 2 * gain_lines :].reshape(2, 4, 2, 4 * LANES), 0, 1)
        bias_sum = bucket_sums(sums.reshape(HEADS, 4 * LANES))
    else:
        query_low, key_low, value_low, distance_sums = attend_grad(
            length, query, key, value, context_grad, logs, near
        )
        lows = (query_low, key_low, value_low)
        normed_one_grad = dot(query_low, own_three[0]) + dot(key_low, own_three[1]) + dot(value_low, own_three[2])
        normed_one_grad = fold(normed_one_grad, core)
        three_parts = [dot(one, normed_one, TN).astype(LOW) for one in lows]
        gained_one = attn_gain * normed_one_grad
        input_grad = hidden_grad + rms_one * (
            gained_one - scaled_one * jnp.mean(gained_one * scaled_one, axis=1, keepdims=True)
        )
        attn_gain_part = jnp.sum(normed_one_grad * scaled_one, axis=0)
        input_grad = to_slots(input_grad.astype(LOW), held).astype(WIDE)
        layer_out = to_slots(layer_rows, held)

        def summed(value):
            return lax.psum_scatter(value, BOTH, scatter_dimension=0, tiled=True).astype(WIDE)

        def own_only(value):
            blank = jnp.zeros_like(value)
            pair = jnp.where(core == 0, jnp.stack([value, blank], axis=1), jnp.stack([blank, value], axis=1))
            return summed(pair.reshape(-1, width))

        up_grad, down_grad = [own_only(one.reshape(depth * (size // 2), -1, width)) for one in (up_part, down_part)]
        query_grad, key_grad, value_grad = [own_only(one.reshape(4, -1, width)) for one in three_parts]
        near_part, far_part = (near_output_part.reshape(4, -1, width), far_output_part.reshape(4, -1, width))
        pair = jnp.where(
            core == 0, jnp.stack([near_part, far_part], axis=1), jnp.stack([far_part, near_part], axis=1)
        )
        output_grad = summed(pair.reshape(-1, width))
        bias_own = bucket_sums(distance_sums.reshape(HEADS // 2, 4 * LANES)).reshape(BUCKETS, 4, 1, 2)
        bias_full = lax.dynamic_update_slice(
            jnp.zeros((BUCKETS, 4, 2, 2), WIDE), bias_own, (0, 0, core, 0)
        ).reshape(BUCKETS, HEADS)
        attn_gain_sum, ffn_gain_sum, bias_sum = lax.psum((attn_gain_part, ffn_gain_part, bias_full), BOTH)

    gain_rows = width // size
    bucket_rows = BUCKETS // size
    attn_gain_grad = lax.dynamic_slice_in_dim(attn_gain_sum, index * gain_rows, gain_rows, 0)
    ffn_gain_grad = lax.dynamic_slice_in_dim(ffn_gain_sum, index * gain_rows, gain_rows, 0)
    bias_grad = lax.dynamic_slice_in_dim(bias_sum, index * bucket_rows, bucket_rows, 0)
    return (
        layer_out,
        input_grad,
        query_grad,
        key_grad,
        value_grad,
        output_grad,
        up_grad,
        down_grad,
        attn_gain_grad,
        ffn_gain_grad,
        bias_grad,
    )


def solution(mesh):
    placed = (
        P("fsdp", "seq", None),
        P("fsdp"),
        P("fsdp", "seq", None),
        P("fsdp", None),
        P("fsdp", None),
        P("fsdp", None),
        P("fsdp", None),
        P("fsdp", None),
        P("fsdp", None),
        P(),
        P(),
        P(),
    )
    return jax.shard_map(
        shards,
        mesh=mesh,
        in_specs=placed,
        out_specs=(
            P("fsdp", "seq", None),
            P("fsdp", "seq", None),
            P(("seq", "fsdp"), None),
            P(("seq", "fsdp"), None),
            P(("seq", "fsdp"), None),
            P(("seq", "fsdp"), None),
            P(("seq", "fsdp"), None),
            P(("seq", "fsdp"), None),
            P("fsdp"),
            P("fsdp"),
            P("fsdp", None),
        ),
        check_vma=False,
    )
```

```python
import functools

import jax
import jax.numpy as jnp
import numpy as np
from jax import lax
from jax.experimental import pallas as pl
from jax.experimental.pallas import tpu as pltpu
from jax.sharding import PartitionSpec as P

HEADS = 16
HEAD_DIM = 64
BUCKETS = 32
NEGATIVE = -1000000000.0
EPSILON = 1e-06
THRESHOLDS = (1, 2, 3, 4, 5, 6, 7, 8, 12, 16, 23, 32, 46, 64, 91)
ROOT_HALF = 0.7071067811865476
NORMAL_PEAK = 0.3989422804014327
LANES = 128
QUERY_ROWS = 256
HALF_ROWS = QUERY_ROWS // 2
LOW = jnp.bfloat16
WIDE = jnp.float32
BOTH = ("seq", "fsdp")

NN = (((1,), (0,)), ((), ()))
NT = (((1,), (1,)), ((), ()))
TN = (((0,), (0,)), ((), ()))


def dot(left, right, dims=NN):
    return lax.dot_general(left, right, dims, preferred_element_type=WIDE)


def inverse_root(value):
    root = lax.rsqrt(value)
    return root * (1.5 - 0.5 * value * root * root)


def gelu_parts(value):
    cumulative = 0.5 * (1.0 + lax.erf(value * ROOT_HALF))
    slope = cumulative + value * jnp.exp(-0.5 * value * value) * NORMAL_PEAK
    return (value * cumulative, slope)


CORE, ALONG_X, ALONG_Y = (1, 2, 4)


def partner(bit):
    index = lax.axis_index("fsdp")
    return index + bit - 2 * bit * ((index // bit) % 2)


def chip_of(*bits):
    index = lax.axis_index("fsdp")
    for bit in bits:
        index = index + bit - 2 * bit * ((index // bit) % 2)
    return index // 2


def send(source, target, sems, number, bit):
    return pltpu.make_async_remote_copy(
        src_ref=source,
        dst_ref=target,
        send_sem=sems.at[0, number],
        recv_sem=sems.at[1, number],
        device_id={"fsdp": partner(bit)},
        device_id_type=pl.DeviceIdType.MESH,
    )


def greet(bits):
    barrier = pltpu.get_barrier_semaphore()
    for bit in bits:
        pl.semaphore_signal(
            barrier, inc=1, device_id={"fsdp": partner(bit)}, device_id_type=pl.DeviceIdType.MESH
        )
    pl.semaphore_wait(barrier, len(bits))


def bucket_columns(distances):
    distances = np.asarray(distances)
    magnitude = sum((np.abs(distances) >= threshold).astype(np.int32) for threshold in THRESHOLDS)
    buckets = magnitude + np.where(distances > 0, BUCKETS // 2, 0)
    return (buckets[None, :] == np.arange(BUCKETS)[:, None]).astype(np.float32)


def near_bias(columns):
    chosen = jnp.asarray(bucket_columns(np.arange(2 * QUERY_ROWS) - HALF_ROWS))
    line = lax.dot_general(columns, chosen, TN, precision=lax.Precision.HIGHEST, preferred_element_type=WIDE)
    return line[:, None, :]


def near_block(line):
    shape = (QUERY_ROWS, 2 * QUERY_ROWS)
    turned = pltpu.roll(jnp.broadcast_to(line, shape), 0, 1, stride=1, stride_axis=0)
    row = lax.broadcasted_iota(jnp.int32, shape, 0)
    column = lax.broadcasted_iota(jnp.int32, shape, 1)
    return jnp.where(column < row, line[:, :1], turned)


def diagonal_sums(tile):
    side = tile.shape[1]
    row = lax.broadcasted_iota(jnp.int32, tile.shape, 0)
    step = 1
    while step < side:
        tile = jnp.where((row // step) % 2 == 1, pltpu.roll(tile, side - step, 1), tile)
        step *= 2
    return jnp.sum(tile, axis=0, keepdims=True)


def spare_lanes(length, rows):
    blocks = rows // QUERY_ROWS
    key = lax.broadcasted_iota(jnp.int32, (rows, LANES), 0)
    lane = lax.rem(lax.broadcasted_iota(jnp.int32, (rows, LANES), 1), HEAD_DIM)
    hidden = jnp.where((lane == 0) & (key >= length), NEGATIVE, 0.0)
    left = (lane >= 1) & (lane <= blocks) & (key < QUERY_ROWS * (lane - 1) - HALF_ROWS)
    start = QUERY_ROWS * (lane - 1 - blocks) + 3 * HALF_ROWS
    right = (lane > blocks) & (lane <= 2 * blocks) & (key >= start)
    return jnp.where(left | right, 1.0, hidden).astype(LOW)


def split_heads(pair, spare, out):
    low_half = lax.broadcasted_iota(jnp.int32, pair.shape, 1) < HEAD_DIM
    out[0] = jnp.where(low_half, pair, spare)
    out[1] = jnp.where(low_half, spare, pair)


def attend_kernel(
    length_ref, query_ref, key_ref, value_ref, near_ref, context_ref, log_ref, bias, keys, values
):
    rows = query_ref.shape[0]
    split_heads(key_ref[...], spare_lanes(length_ref[0], rows), keys)
    split_heads(value_ref[...], jnp.zeros((rows, LANES), LOW), values)
    near_start = rows - QUERY_ROWS - HALF_ROWS
    near_end = near_start + 2 * QUERY_ROWS
    for head in range(2):
        line = near_ref[head]
        bias[head, :, :near_start] = jnp.broadcast_to(line[:, :1], (QUERY_ROWS, near_start))
        bias[head, :, near_start:near_end] = near_block(line)
        bias[head, :, near_end:] = jnp.broadcast_to(line[:, -1:], (QUERY_ROWS, bias.shape[2] - near_end))
    lane = lax.broadcasted_iota(jnp.int32, (QUERY_ROWS, LANES), 1)
    ones = jnp.where(lax.rem(lane, HEAD_DIM) == 0, 1.0, 0.0).astype(LOW)

    def block(number, carry):
        start = pl.multiple_of(number * QUERY_ROWS, QUERY_ROWS)
        offset = pl.multiple_of(rows - QUERY_ROWS - number * QUERY_ROWS, LANES)
        both = query_ref[pl.ds(start, QUERY_ROWS), :]
        total = jnp.zeros((QUERY_ROWS, LANES), WIDE)
        for head in range(2):
            mine = lane < HEAD_DIM if head == 0 else lane >= HEAD_DIM
            logits = dot(jnp.where(mine, both, ones), keys[head], NT)
            logits = logits + bias[head, :, pl.ds(offset, rows)]
            peak = jnp.max(logits, axis=1, keepdims=True)
            exponent = jnp.exp(logits - peak)
            row_sum = jnp.sum(exponent, axis=1, keepdims=True)
            weights_low = (exponent * (1.0 / row_sum)).astype(LOW)
            total = total + dot(weights_low, values[head])
            logs = jnp.broadcast_to(peak + jnp.log(row_sum), (QUERY_ROWS, LANES))
            log_ref[0, head : head + 1, pl.ds(start, QUERY_ROWS)] = logs.T[0:1, :]
        context_ref[pl.ds(start, QUERY_ROWS), :] = total.astype(LOW)
        return carry

    lax.fori_loop(0, rows // QUERY_ROWS, block, 0)


def attend(length, query, key, value, near):
    rows, width = query.shape
    pairs = width // LANES
    smem = pl.BlockSpec(memory_space=pltpu.SMEM)
    columns = pl.BlockSpec((rows, LANES), lambda pair: (0, pair))
    return pl.pallas_call(
        attend_kernel,
        grid=(pairs,),
        in_specs=[smem, columns, columns, columns]
        + [pl.BlockSpec((2, 1, 2 * QUERY_ROWS), lambda pair: (pair, 0, 0))],
        out_specs=[columns, pl.BlockSpec((1, 2, rows), lambda pair: (pair, 0, 0))],
        out_shape=[
            jax.ShapeDtypeStruct((rows, width), LOW),
            jax.ShapeDtypeStruct((pairs, 2, rows), WIDE),
        ],
        scratch_shapes=[
            pltpu.VMEM((2, QUERY_ROWS, 2 * rows - QUERY_ROWS), WIDE),
            pltpu.VMEM((2, rows, LANES), LOW),
            pltpu.VMEM((2, rows, LANES), LOW),
        ],
        compiler_params=pltpu.CompilerParams(vmem_limit_bytes=40 << 20),
        cost_estimate=pl.CostEstimate(
            flops=24 * rows * rows * width, bytes_accessed=8 * rows * width, transcendentals=2 * pairs * rows * rows
        ),
        name="attend",
    )(length, query, key, value, near)


def attend_grad_kernel(
    length_ref,
    query_ref,
    key_ref,
    value_ref,
    grad_ref,
    log_ref,
    near_ref,
    query_grad_ref,
    key_grad_ref,
    value_grad_ref,
    sums_ref,
    bias,
    keys,
    values,
    padded,
    key_total,
    value_total,
    tiles,
):
    rows = query_ref.shape[0]
    blocks = rows // QUERY_ROWS
    split_heads(key_ref[...], spare_lanes(length_ref[0], rows), keys)
    split_heads(value_ref[...], jnp.zeros((rows, LANES), LOW), values)
    near_start = rows - QUERY_ROWS - HALF_ROWS
    near_end = near_start + 2 * QUERY_ROWS
    for head in range(2):
        line = near_ref[head]
        bias[head, :near_start, :] = jnp.broadcast_to(line[:, :1], (near_start, QUERY_ROWS))
        bias[head, near_start:near_end, :] = near_block(line).T
        bias[head, near_end:, :] = jnp.broadcast_to(line[:, -1:], (bias.shape[1] - near_end, QUERY_ROWS))
        padded[head, :HALF_ROWS, :] = jnp.zeros((HALF_ROWS, QUERY_ROWS), LOW)
        padded[head, rows + HALF_ROWS :, :] = jnp.zeros((HALF_ROWS, QUERY_ROWS), LOW)
    key_total[...] = jnp.zeros_like(key_total)
    value_total[...] = jnp.zeros_like(value_total)
    tiles[...] = jnp.zeros_like(tiles)
    sums_ref[...] = jnp.zeros_like(sums_ref)
    spot = lax.broadcasted_iota(jnp.int32, (1, LANES), 1)
    lane = lax.broadcasted_iota(jnp.int32, (QUERY_ROWS, LANES), 1)
    ones = jnp.where(lax.rem(lane, HEAD_DIM) == 0, 1.0, 0.0).astype(LOW)
    zero = jnp.zeros((), LOW)

    def block(number, carry):
        start = pl.multiple_of(number * QUERY_ROWS, QUERY_ROWS)
        offset = pl.multiple_of(rows - QUERY_ROWS - number * QUERY_ROWS, LANES)
        both = query_ref[pl.ds(start, QUERY_ROWS), :]
        grad = grad_ref[pl.ds(start, QUERY_ROWS), :]
        parts = []
        for head in range(2):
            mine = lane < HEAD_DIM if head == 0 else lane >= HEAD_DIM
            logits = dot(keys[head], jnp.where(mine, both, ones), NT)
            logits = logits + bias[head, pl.ds(offset, rows), :]
            probs = jnp.exp(logits - log_ref[0, head : head + 1, pl.ds(start, QUERY_ROWS)])
            prob_grad = dot(values[head], grad, NT)
            weighted = probs * prob_grad
            inner = jnp.sum(weighted, axis=0, keepdims=True)
            score = (weighted - probs * inner).astype(LOW)
            value_total[...] += dot(probs.astype(LOW), jnp.where(mine, grad, zero))
            key_total[...] += dot(score, jnp.where(mine, both, zero))
            padded[head, HALF_ROWS : HALF_ROWS + rows, :] = score
            part = dot(score, keys[head], TN)
            parts.append(part)
            columns = jnp.sum(part, axis=0, keepdims=True)
            spare = HEAD_DIM * (1 - head) + 1 + number
            close = padded[head, pl.ds(start, 2 * QUERY_ROWS), :].astype(WIDE)
            quarter = [close[HALF_ROWS * step : HALF_ROWS * (step + 1)] for step in range(4)]
            for step in range(3):
                tiles[head, step] += quarter[step][:, :HALF_ROWS] + quarter[step + 1][:, HALF_ROWS:]
            left = jnp.sum(quarter[0][:, HALF_ROWS:], axis=0, keepdims=True)
            right = jnp.sum(quarter[3][:, :HALF_ROWS], axis=0, keepdims=True)
            left = left + jnp.where(spot == spare, columns, 0.0)
            right = right + jnp.where(spot == spare + blocks, columns, 0.0)
            sums_ref[0, 4 * head + 2 : 4 * head + 3, :] += left
            sums_ref[0, 4 * head + 3 : 4 * head + 4, :] += right
        chosen = jnp.where(lane < HEAD_DIM, parts[0], parts[1])
        query_grad_ref[pl.ds(start, QUERY_ROWS), :] = chosen.astype(LOW)
        return carry

    lax.fori_loop(0, blocks, block, 0)
    key_grad_ref[...] = key_total[...].astype(LOW)
    value_grad_ref[...] = value_total[...].astype(LOW)
    shape = (HALF_ROWS, HALF_ROWS)
    upper = lax.broadcasted_iota(jnp.int32, shape, 0) <= lax.broadcasted_iota(jnp.int32, shape, 1)
    for head in range(2):
        before, centre, behind = (tiles[head, step] for step in range(3))
        sums_ref[0, 4 * head : 4 * head + 1, :] = diagonal_sums(jnp.where(upper, centre, before))
        sums_ref[0, 4 * head + 1 : 4 * head + 2, :] = diagonal_sums(jnp.where(upper, behind, centre))
        left = jnp.sum(jnp.where(upper, before, 0.0), axis=0, keepdims=True)
        right = jnp.sum(jnp.where(upper, 0.0, behind), axis=0, keepdims=True)
        sums_ref[0, 4 * head + 2 : 4 * head + 3, :] += left
        sums_ref[0, 4 * head + 3 : 4 * head + 4, :] += right


def attend_grad(length, query, key, value, grad, logs, near):
    rows, width = query.shape
    pairs = width // LANES
    smem = pl.BlockSpec(memory_space=pltpu.SMEM)
    columns = pl.BlockSpec((rows, LANES), lambda pair: (0, pair))
    shape = jax.ShapeDtypeStruct
    return pl.pallas_call(
        attend_grad_kernel,
        grid=(pairs,),
        in_specs=[smem, columns, columns, columns, columns]
        + [pl.BlockSpec((1, 2, rows), lambda pair: (pair, 0, 0))]
        + [pl.BlockSpec((2, 1, 2 * QUERY_ROWS), lambda pair: (pair, 0, 0))],
        out_specs=[columns, columns, columns] + [pl.BlockSpec((1, 8, LANES), lambda pair: (pair, 0, 0))],
        out_shape=[shape((rows, width), LOW)] * 3 + [shape((pairs, 8, LANES), WIDE)],
        scratch_shapes=[
            pltpu.VMEM((2, 2 * rows - QUERY_ROWS, QUERY_ROWS), WIDE),
            pltpu.VMEM((2, rows, LANES), LOW),
            pltpu.VMEM((2, rows, LANES), LOW),
            pltpu.VMEM((2, rows + QUERY_ROWS, QUERY_ROWS), LOW),
            pltpu.VMEM((rows, LANES), WIDE),
            pltpu.VMEM((rows, LANES), WIDE),
            pltpu.VMEM((2, 3, HALF_ROWS, HALF_ROWS), WIDE),
        ],
        compiler_params=pltpu.CompilerParams(vmem_limit_bytes=48 << 20),
        cost_estimate=pl.CostEstimate(
            flops=44 * rows * rows * width, bytes_accessed=14 * rows * width, transcendentals=2 * pairs * rows * rows
        ),
        name="attend_grad",
    )(length, query, key, value, grad, logs, near)


def bucket_sums(sums):
    side = np.arange(LANES)
    far = np.full((LANES,), 2 * HALF_ROWS)
    chosen = bucket_columns(np.concatenate([-side, HALF_ROWS - side, -far, far]))
    return lax.dot_general(
        jnp.asarray(chosen), sums, NT, precision=lax.Precision.HIGHEST, preferred_element_type=WIDE
    )


def feed_kernel(normed_ref, grad_ref, up_ref, down_ref, up_part_ref, down_part_ref, out_ref, back_ref):
    @pl.when(pl.program_id(0) == 0)
    def _():
        out_ref[...] = jnp.zeros_like(out_ref)
        back_ref[...] = jnp.zeros_like(back_ref)

    up, down = (up_ref[...], down_ref[...])
    normed, grad = (normed_ref[...], grad_ref[...])
    active, slope = gelu_parts(dot(normed, up, NT))
    active = active.astype(LOW)
    pre_grad = (dot(grad, down, NT) * slope).astype(LOW)
    out_ref[...] += dot(active, down)
    back_ref[...] += dot(pre_grad, up)
    up_part_ref[...] = dot(pre_grad, normed, TN).astype(LOW)
    down_part_ref[...] = dot(active, grad, TN).astype(LOW)


def feed(normed, grad, up, down):
    rows, width = normed.shape
    unit = up.shape[0] // 4
    fixed = pl.BlockSpec((rows, width), lambda step: (0, 0))
    block = pl.BlockSpec((unit, width), lambda step: (step, 0))
    return pl.pallas_call(
        feed_kernel,
        grid=(4,),
        in_specs=[fixed, fixed, block, block],
        out_specs=[block, block, fixed, fixed],
        out_shape=[jax.ShapeDtypeStruct((4 * unit, width), LOW)] * 2
        + [jax.ShapeDtypeStruct((rows, width), WIDE)] * 2,
        compiler_params=pltpu.CompilerParams(vmem_limit_bytes=56 << 20),
        name="feed",
    )(normed, grad, up, down)


def push(source, target, sems, number, place, index, there=None):
    return pltpu.make_async_remote_copy(
        src_ref=source,
        dst_ref=target,
        send_sem=sems.at[(0,) + number],
        recv_sem=sems.at[(1,) + (there or number)],
        device_id={"seq": place, "fsdp": index},
        device_id_type=pl.DeviceIdType.MESH,
    )


def greet_column(depth):
    barrier = pltpu.get_barrier_semaphore()
    place, index = (lax.axis_index("seq"), lax.axis_index("fsdp"))

    def signal(there, which):
        pl.semaphore_signal(
            barrier, inc=1, device_id={"seq": there, "fsdp": which}, device_id_type=pl.DeviceIdType.MESH
        )

    signal(place, partner(ALONG_X))
    signal(place, partner(ALONG_Y))
    signal(place, partner(CORE))
    for step in range(1, depth):
        signal(lax.rem(place + step, depth), index)
        signal(lax.rem(place + step, depth), partner(CORE))
    pl.semaphore_wait(barrier, 2 * depth + 1)


def slots_moves(source, target, sems, depth, act):
    held = depth // 2
    place, index = (lax.axis_index("seq"), lax.axis_index("fsdp"))
    core = lax.rem(index, 2)
    slot = lax.rem(place, held)
    for sequence in range(held):
        there, which = (core * held + sequence, index - core + place // held)
        home = (there == place) & (which == index)

        @pl.when(home)
        def _():
            if act == "start":
                pltpu.make_async_copy(source.at[sequence], target.at[slot], sems.at[1, slot]).start()

        @pl.when(jnp.logical_not(home))
        def _():
            move = push(source.at[sequence], target.at[slot], sems, (sequence,), there, which, (slot,))
            if act == "start":
                move.start()
            else:
                move.wait_send()


def slots_came(target, sems, slot):
    push(target.at[slot], target.at[slot], sems, (slot,), lax.axis_index("seq"), partner(CORE)).wait_recv()


def enter_kernel(
    depth,
    inputs_ref,
    query_ref,
    key_ref,
    value_ref,
    up_ref,
    down_ref,
    gain_ref,
    normed_out_ref,
    query_out_ref,
    key_out_ref,
    value_out_ref,
    source_out_ref,
    weights_out_ref,
    up_out_ref,
    down_out_ref,
    normed_ref,
    source_ref,
    weights_ref,
    kept,
    slot_sems,
    near_sems,
    far_sems,
    cut_sems,
    row_sems,
    local_sems,
):
    held = depth // 2
    span = source_ref.shape[1]
    rows = normed_ref.shape[0]
    index = lax.axis_index("fsdp")
    core = lax.rem(index, 2)
    chip = chip_of()
    mine = (query_ref, key_ref, value_ref)
    half = query_ref.shape[0] // 2
    greet_column(depth)
    slots_moves(inputs_ref, source_ref, slot_sems, depth, "start")
    direct = [
        send(one, weights_ref.at[chip, kind], near_sems, 2 * kind + turn, bit)
        for kind, one in enumerate(mine)
        for turn, bit in enumerate((ALONG_X, ALONG_Y))
    ]
    for one in direct:
        one.start()
    local = [
        pltpu.make_async_copy(one, weights_ref.at[chip, kind], local_sems.at[kind]) for kind, one in enumerate(mine)
    ]
    cuts = []
    for kind, (whole_one, out) in enumerate(((up_ref, up_out_ref), (down_ref, down_out_ref))):
        cuts.append(send(whole_one.at[:, 1 - core], out.at[core], cut_sems, kind, CORE))
        local.append(pltpu.make_async_copy(whole_one.at[:, core], kept.at[kind], local_sems.at[3 + kind]))
    for one in cuts + local:
        one.start()
    for one in direct:
        one.wait_recv()
    onward = []
    for turn, (bit, came) in enumerate(((ALONG_X, ALONG_Y), (ALONG_Y, ALONG_X))):
        piece = weights_ref.at[chip_of(came), :, pl.ds(turn * half, half)]
        onward.append(send(piece, piece, far_sems, turn, bit))
    for one in onward:
        one.start()

    moves = []
    for slot in range(held):
        slots_came(source_ref, slot_sems, slot)
        source = source_ref[slot].astype(WIDE)
        rms = inverse_root(jnp.mean(source * source, axis=1, keepdims=True) + EPSILON)
        here = pl.ds(pl.multiple_of(core * (rows // 2) + slot * span, span), span)
        normed_ref[here, :] = (source * rms * gain_ref[...]).astype(LOW)
        moves.append(send(normed_ref.at[here], normed_ref.at[here], row_sems, slot, CORE))
        moves[-1].start()
    for one in moves:
        one.wait()
    for one in local:
        one.wait()

    def project(number):
        weight = weights_ref[number].reshape(-1, weights_ref.shape[3])
        product = dot(normed_ref[...], weight, NT).astype(LOW)
        lanes = pl.ds(pl.multiple_of(number * LANES, LANES), LANES)
        for kind, out in enumerate((query_out_ref, key_out_ref, value_out_ref)):
            out[:, lanes] = product[:, kind * LANES : (kind + 1) * LANES]

    def some(turn, carry):
        project(jnp.where(turn == 0, chip, jnp.where(turn == 1, chip_of(ALONG_X), chip_of(ALONG_Y))))
        return carry

    lax.fori_loop(0, 3, some, 0)
    for one in onward:
        one.wait()
    stored = [
        pltpu.make_async_copy(one, there, local_sems.at[5 + number])
        for number, (one, there) in enumerate(
            (
                (normed_ref, normed_out_ref),
                (source_ref, source_out_ref),
                (weights_ref, weights_out_ref),
                (kept.at[0], up_out_ref.at[core]),
                (kept.at[1], down_out_ref.at[core]),
            )
        )
    ]
    for one in stored:
        one.start()
    project(chip_of(ALONG_X, ALONG_Y))
    for one in stored:
        one.wait()
    for one in direct:
        one.wait_send()
    for one in cuts:
        one.wait()
    slots_moves(inputs_ref, source_ref, slot_sems, depth, "end")


def enter(inputs, projections, up, down, gain):
    held, span, width = inputs.shape
    depth = lax.axis_size("seq")
    rows = 2 * held * span
    slim = projections[0].shape[0]
    thick = up.shape[0] // 4
    vmem, anywhere = (pl.BlockSpec(memory_space=pltpu.VMEM), pl.BlockSpec(memory_space=pltpu.HBM))
    shape = jax.ShapeDtypeStruct
    return pl.pallas_call(
        functools.partial(enter_kernel, depth),
        in_specs=[anywhere] * 6 + [vmem],
        out_specs=[anywhere] + [vmem] * 3 + [anywhere] * 4,
        out_shape=[shape((rows, width), LOW)]
        + [shape((rows, 4 * slim), LOW)] * 3
        + [shape((held, span, width), LOW), shape((4, 3, slim, width), LOW)]
        + [shape((2, 2, thick, width), LOW)] * 2,
        scratch_shapes=[
            pltpu.VMEM((rows, width), LOW),
            pltpu.VMEM((held, span, width), LOW),
            pltpu.VMEM((4, 3, slim, width), LOW),
            pltpu.VMEM((2, 2, thick, width), LOW),
            pltpu.SemaphoreType.DMA((2, held)),
            pltpu.SemaphoreType.DMA((2, 6)),
            pltpu.SemaphoreType.DMA((2, 2)),
            pltpu.SemaphoreType.DMA((2, 2)),
            pltpu.SemaphoreType.DMA((2, held)),
            pltpu.SemaphoreType.DMA((10,)),
        ],
        compiler_params=pltpu.CompilerParams(vmem_limit_bytes=62 << 20, collective_id=4, has_side_effects=True),
        cost_estimate=pl.CostEstimate(flops=24 * rows * slim * width, bytes_accessed=16 << 20, transcendentals=0),
        name="enter",
    )(inputs, *projections, up.reshape(2, 2, thick, width), down.reshape(2, 2, thick, width), gain)


def through_kernel(
    depth,
    length_ref,
    query_ref,
    key_ref,
    value_ref,
    near_ref,
    source_ref,
    gain_ref,
    output_ref,
    up_ref,
    down_ref,
    cotangent_ref,
    log_ref,
    context_ref,
    hidden_ref,
    far_context_out_ref,
    own_output_out_ref,
    far_output_out_ref,
    normed_ref,
    grad_ref,
    ups_ref,
    downs_ref,
    bias,
    keys,
    values,
    context,
    came,
    far_context_ref,
    own_output_ref,
    far_output_ref,
    normed,
    grad,
    slot_sems,
    near_sems,
    far_sems,
    deep_sems,
    core_sems,
    context_sems,
    local,
):
    rows = query_ref.shape[0]
    width = source_ref.shape[1]
    pair = pl.program_id(0)
    last = depth - 1
    held = depth // 2
    core = lax.rem(lax.axis_index("fsdp"), 2)
    chip = chip_of()
    own = pl.ds(pl.multiple_of(core * (rows // 2), rows // 2), rows // 2)
    other = pl.ds(pl.multiple_of((1 - core) * (rows // 2), rows // 2), rows // 2)
    half = output_ref.shape[0] // 2
    place, index = (lax.axis_index("seq"), lax.axis_index("fsdp"))
    parity = lax.rem(place, 2)
    unit = down_ref.shape[0] // 2
    mine = pl.ds(pl.multiple_of(parity * unit, unit), unit)
    direct = []
    for one, there in (
        (output_ref, own_output_ref.at[chip]),
        (down_ref.at[mine], downs_ref.at[chip, mine]),
        (up_ref, ups_ref.at[chip]),
    ):
        for bit in (ALONG_X, ALONG_Y):
            direct.append(send(one, there, near_sems, len(direct), bit))
    exchange = [
        push(
            downs_ref.at[chip_of(bit), mine],
            downs_ref.at[chip_of(bit), mine],
            deep_sems,
            (number,),
            place + 1 - 2 * parity,
            index,
        )
        for number, bit in enumerate((ALONG_X, ALONG_Y))
    ]
    onward = []
    for turn, (bit, from_bit) in enumerate(((ALONG_X, ALONG_Y), (ALONG_Y, ALONG_X))):
        piece = own_output_ref.at[chip_of(from_bit), pl.ds(turn * half, half)]
        onward.append(send(piece, piece, far_sems, turn, bit))
    keep = pltpu.make_async_copy(output_ref, own_output_ref.at[chip], local.at[0])
    swap = send(own_output_ref, far_output_ref, core_sems, 0, CORE)
    both_cores = [
        (send(one, there.at[own], core_sems, 1 + number, CORE), pltpu.make_async_copy(one, there.at[own], local.at[1 + number]))
        for number, (one, there) in enumerate(((grad, grad_ref), (normed, normed_ref)))
    ]
    stored = [
        pltpu.make_async_copy(one, there, local.at[3 + number])
        for number, (one, there) in enumerate(
            (
                (own_output_ref, own_output_out_ref),
                (far_output_ref, far_output_out_ref),
                (far_context_ref, far_context_out_ref),
            )
        )
    ]

    def context_move(number):
        lanes = pl.ds(pl.multiple_of(number * LANES, LANES), LANES)
        return send(context.at[other, lanes], far_context_ref.at[:, lanes], context_sems, number, CORE)

    @pl.when(pair == 0)
    def _():
        greet_column(depth)
        for one in direct[:4]:
            one.start()
        keep.start()
        slots_moves(cotangent_ref, came, slot_sems, depth, "start")

    @pl.when(pair == 1)
    def _():
        for one in direct[:2]:
            one.wait_recv()
        for one in onward + direct[4:]:
            one.start()

    @pl.when(pair == last - 1)
    def _():
        for one in direct[2:4]:
            one.wait_recv()
        for one in exchange:
            one.start()

    @pl.when(pair == last)
    def _():
        for one in onward:
            one.wait()
        keep.wait()
        swap.start()
        stored[0].start()
        slot_ids = core * (rows // 2) + lax.broadcasted_iota(jnp.int32, (rows // 2, 1), 0)
        valid = (slot_ids < length_ref[0]).astype(WIDE)
        for slot in range(held):
            slots_came(came, slot_sems, slot)
        grad[...] = (came[...].reshape(rows // 2, width).astype(WIDE) * valid).astype(LOW)
        for one in both_cores[0]:
            one.start()

    lanes = pl.ds(pl.multiple_of(pair * LANES, LANES), LANES)
    split_heads(key_ref[...], spare_lanes(length_ref[0], rows), keys)
    split_heads(value_ref[...], jnp.zeros((rows, LANES), LOW), values)
    near_start = rows - QUERY_ROWS - HALF_ROWS
    near_end = near_start + 2 * QUERY_ROWS
    for head in range(2):
        line = near_ref[head]
        bias[head, :, :near_start] = jnp.broadcast_to(line[:, :1], (QUERY_ROWS, near_start))
        bias[head, :, near_start:near_end] = near_block(line)
        bias[head, :, near_end:] = jnp.broadcast_to(line[:, -1:], (QUERY_ROWS, bias.shape[2] - near_end))
    lane = lax.broadcasted_iota(jnp.int32, (QUERY_ROWS, LANES), 1)
    ones = jnp.where(lax.rem(lane, HEAD_DIM) == 0, 1.0, 0.0).astype(LOW)

    def block(number, carry):
        start = pl.multiple_of(number * QUERY_ROWS, QUERY_ROWS)
        offset = pl.multiple_of(rows - QUERY_ROWS - number * QUERY_ROWS, LANES)
        both = query_ref[pl.ds(start, QUERY_ROWS), :]
        total = jnp.zeros((QUERY_ROWS, LANES), WIDE)
        for head in range(2):
            mine = lane < HEAD_DIM if head == 0 else lane >= HEAD_DIM
            logits = dot(jnp.where(mine, both, ones), keys[head], NT)
            logits = logits + bias[head, :, pl.ds(offset, rows)]
            peak = jnp.max(logits, axis=1, keepdims=True)
            exponent = jnp.exp(logits - peak)
            row_sum = jnp.sum(exponent, axis=1, keepdims=True)
            weights_low = (exponent * (1.0 / row_sum)).astype(LOW)
            total = total + dot(weights_low, values[head])
            logs = jnp.broadcast_to(peak + jnp.log(row_sum), (QUERY_ROWS, LANES))
            log_ref[0, head : head + 1, pl.ds(start, QUERY_ROWS)] = logs.T[0:1, :]
        context[pl.ds(start, QUERY_ROWS), lanes] = total.astype(LOW)
        return carry

    lax.fori_loop(0, rows // QUERY_ROWS, block, 0)
    context_move(pair).start()
    context_ref[:, lanes] = context[own, lanes]

    @pl.when(pair == last)
    def _():
        swap.wait()
        for number in range(last + 1):
            context_move(number).wait()
        for one in stored[1:]:
            one.start()
        inner = context_ref.shape[1]
        attended = dot(context_ref[...], own_output_ref[...].reshape(inner, width))
        attended = attended + dot(far_context_ref[...], far_output_ref[...].reshape(inner, width))
        hidden = source_ref[...].astype(WIDE) + attended
        hidden_ref[...] = hidden
        rms = inverse_root(jnp.mean(hidden * hidden, axis=1, keepdims=True) + EPSILON)
        normed[...] = (hidden * rms * gain_ref[...]).astype(LOW)
        for one in both_cores[1]:
            one.start()
        for one in direct:
            one.wait_send()
        for one in direct[4:]:
            one.wait_recv()
        for one in exchange:
            one.wait()
        slots_moves(cotangent_ref, came, slot_sems, depth, "end")
        for one in both_cores[0] + both_cores[1]:
            one.wait()
        for one in stored:
            one.wait()


def through(length, query, key, value, near, source, gain, output, up, down, cotangent):
    rows, inner = query.shape
    held, span, width = cotangent.shape
    depth = lax.axis_size("seq")
    pairs = inner // LANES
    vmem, anywhere = (pl.BlockSpec(memory_space=pltpu.VMEM), pl.BlockSpec(memory_space=pltpu.HBM))
    columns = pl.BlockSpec((rows, LANES), lambda pair: (0, pair))
    shape = jax.ShapeDtypeStruct
    outputs = (4,) + output.shape
    return pl.pallas_call(
        functools.partial(through_kernel, depth),
        grid=(pairs,),
        in_specs=[pl.BlockSpec(memory_space=pltpu.SMEM), columns, columns, columns]
        + [pl.BlockSpec((2, 1, 2 * QUERY_ROWS), lambda pair: (pair, 0, 0)), vmem, vmem]
        + [anywhere] * 4,
        out_specs=[pl.BlockSpec((1, 2, rows), lambda pair: (pair, 0, 0))] + [vmem] * 2 + [anywhere] * 7,
        out_shape=[shape((pairs, 2, rows), WIDE)]
        + [shape((rows // 2, inner), LOW), shape((rows // 2, width), WIDE), shape((rows // 2, inner), LOW)]
        + [shape(outputs, LOW)] * 2
        + [shape((rows, width), LOW)] * 2
        + [shape((4,) + up.shape, LOW)] * 2,
        scratch_shapes=[
            pltpu.VMEM((2, QUERY_ROWS, 2 * rows - QUERY_ROWS), WIDE),
            pltpu.VMEM((2, rows, LANES), LOW),
            pltpu.VMEM((2, rows, LANES), LOW),
            pltpu.VMEM((rows, inner), LOW),
            pltpu.VMEM((held, span, width), LOW),
            pltpu.VMEM((rows // 2, inner), LOW),
            pltpu.VMEM(outputs, LOW),
            pltpu.VMEM(outputs, LOW),
            pltpu.VMEM((rows // 2, width), LOW),
            pltpu.VMEM((rows // 2, width), LOW),
            pltpu.SemaphoreType.DMA((2, held)),
            pltpu.SemaphoreType.DMA((2, 6)),
            pltpu.SemaphoreType.DMA((2, 2)),
            pltpu.SemaphoreType.DMA((2, 2)),
            pltpu.SemaphoreType.DMA((2, 3)),
            pltpu.SemaphoreType.DMA((2, pairs)),
            pltpu.SemaphoreType.DMA((6,)),
        ],
        compiler_params=pltpu.CompilerParams(vmem_limit_bytes=62 << 20, collective_id=1, has_side_effects=True),
        cost_estimate=pl.CostEstimate(
            flops=24 * rows * rows * inner, bytes_accessed=8 * rows * inner, transcendentals=2 * pairs * rows * rows
        ),
        name="through",
    )(length, query, key, value, near, source, gain, output, up, down, cotangent)


def row_moves(source, target, sems, depth, piece, started=True):
    held = depth // 2
    place, index = (lax.axis_index("seq"), lax.axis_index("fsdp"))
    core = lax.rem(index, 2)
    there, which = (core * held + piece, index - core + place // held)
    slot = lax.rem(place, held)
    home = (there == place) & (which == index)

    @pl.when(home)
    def _():
        if started:
            pltpu.make_async_copy(source, target.at[slot], sems.at[1, piece, slot]).start()

    @pl.when(jnp.logical_not(home))
    def _():
        move = push(source, target.at[slot], sems, (piece, slot), there, which)
        if started:
            move.start()
        else:
            move.wait_send()


def rows_came(target, sems, depth):
    held = depth // 2
    place = lax.axis_index("seq")
    for slot in range(held):
        number = (lax.rem(place, held), slot)
        push(target.at[slot], target.at[slot], sems, number, place, partner(CORE)).wait_recv()


def middle_kernel(
    depth,
    length_ref,
    normed_ref,
    grad_ref,
    hidden_in_ref,
    gain_ref,
    output_in_ref,
    far_output_in_ref,
    context_in_ref,
    far_context_in_ref,
    up_ref,
    down_ref,
    ups_ref,
    downs_ref,
    up_part_ref,
    down_part_ref,
    up_came_ref,
    down_came_ref,
    far_up_ref,
    far_down_ref,
    context_grad_ref,
    hidden_grad_ref,
    layer_ref,
    gain_part_ref,
    output_part_ref,
    hidden_ref,
    output_ref,
    far_output_ref,
    context_ref,
    far_context_ref,
    near_grad,
    out_total,
    back_total,
    fold_sent,
    fold_came,
    up_slots,
    down_slots,
    up_stages,
    down_stages,
    parts,
    parts_came,
    far_grad,
    arrived,
    stored,
    far_sems,
    unit_sems,
    fold_sems,
    core_sems,
    kept,
    later_sems,
):
    rows, width = normed_ref.shape
    mine, wholes, fars = ((up_ref, down_ref), (ups_ref, downs_ref), (far_up_ref, far_down_ref))
    results, came = ((up_part_ref, down_part_ref), (up_came_ref, down_came_ref))
    slots, stages = ((up_slots, down_slots), (up_stages, down_stages))
    kinds = range(2)
    step = pl.program_id(0)
    last = depth - 1
    index = lax.axis_index("fsdp")
    core, x, y = (lax.rem(index, 2), lax.rem(index // 2, 2), index // 4)
    unit = up_slots.shape[1]
    half = unit // 2
    slot = lax.rem(step, 2)
    places = [chip_of(), chip_of(ALONG_X), chip_of(ALONG_Y), chip_of(ALONG_X, ALONG_Y)]

    place = lax.axis_index("seq")
    parity = lax.rem(place, 2)
    moves, exchange = ([], [])
    for turn, (bit, from_bit) in enumerate(((ALONG_X, ALONG_Y), (ALONG_Y, ALONG_X))):
        there = pl.ds(pl.multiple_of(turn * half + parity * (half // 2), half // 2), half // 2)
        moves.append(send(downs_ref.at[chip_of(from_bit), there], far_down_ref.at[there], far_sems, turn, bit))
        far = far_down_ref.at[there]
        exchange.append(push(far, far, far_sems, (4 + turn,), place + 1 - 2 * parity, index))
    for turn, (bit, from_bit) in enumerate(((ALONG_X, ALONG_Y), (ALONG_Y, ALONG_X))):
        there = pl.ds(turn * half, half)
        moves.append(send(ups_ref.at[chip_of(from_bit), there], far_up_ref.at[there], far_sems, 2 + turn, bit))
    sources = [
        mine,
        [one.at[places[1]] for one in wholes],
        [one.at[places[2]] for one in wholes],
        fars,
    ]

    def fetch(block, into):
        for number, pair in enumerate(sources):

            @pl.when(block == number)
            def _():
                for kind in kinds:
                    pltpu.make_async_copy(pair[kind], slots[kind].at[into], arrived.at[kind, into]).start()

    def store(number, kind):
        return pltpu.make_async_copy(
            stages[kind].at[number % 2], results[kind].at[places[number]], stored.at[kind, number % 2]
        )

    def first_sum(number, kind):
        block = places[number]
        if kind == 0:
            source, bit = (results[0].at[block, :, 1 - x], ALONG_X)
        else:
            source, bit = (results[1].at[block, 1 - y], ALONG_Y)
        return send(source, came[kind].at[block], unit_sems, last * kind + number, bit)

    def own_rows(which):
        return pl.ds(pl.multiple_of(which * (rows // 2), rows // 2), rows // 2)

    folds = [send(fold_sent.at[number], fold_came.at[number], fold_sems, number, CORE) for number in range(2)]

    later = [
        pltpu.make_async_copy(one, there, later_sems.at[number])
        for number, (one, there) in enumerate(
            (
                (hidden_in_ref, hidden_ref),
                (output_in_ref, output_ref),
                (far_output_in_ref, far_output_ref),
                (context_in_ref, context_ref),
                (far_context_in_ref, far_context_ref),
            )
        )
    ]

    @pl.when(step == 0)
    def _():
        greet_column(depth)
        for one in moves:
            one.start()
        fetch(0, 0)
        for one in later:
            one.start()
        out_total[...] = jnp.zeros_like(out_total)
        back_total[...] = jnp.zeros_like(back_total)

    @pl.when(step + 1 < last)
    def _():
        fetch(step + 1, 1 - slot)

    @pl.when(step == 1)
    def _():
        for one in moves[:2]:
            one.wait()
        for one in exchange:
            one.start()

    for number in range(last):

        @pl.when(step == number + 1)
        def _():
            for kind in kinds:
                store(number, kind).wait()
                first_sum(number, kind).start()

    for kind in kinds:
        pltpu.make_async_copy(slots[kind].at[slot], slots[kind].at[slot], arrived.at[kind, slot]).wait()
    up, down = (slots[0][slot], slots[1][slot])
    normed, grad = (normed_ref[...], grad_ref[...])
    active, slope = gelu_parts(dot(normed, up, NT))
    active = active.astype(LOW)
    pre_grad = (dot(grad, down, NT) * slope).astype(LOW)
    back_total[...] += dot(pre_grad, up)
    out_total[...] += dot(active, down)

    @pl.when(step == last)
    def _():
        for number, total in enumerate((back_total, out_total)):
            fold_sent[number] = total[own_rows(1 - core), :].astype(LOW)
            folds[number].start()

    shape = up_stages.shape[1:]
    stages[0][slot] = dot(pre_grad, normed, TN).astype(LOW).reshape(shape)
    stages[1][slot] = dot(active, grad, TN).astype(LOW).reshape(shape)
    for number in range(last + 1):

        @pl.when(step == number)
        def _():
            for kind in kinds:
                store(number, kind).start()

    @pl.when(step == last - 1)
    def _():
        for one in moves[2:] + exchange:
            one.wait()
        fetch(last, last % 2)

    @pl.when(step == last)
    def _():
        for one in later:
            one.wait()
        folds[0].wait()
        normed_grad = back_total[own_rows(core), :] + fold_came[0].astype(WIDE)
        hidden = hidden_ref[...]
        rms = inverse_root(jnp.mean(hidden * hidden, axis=1, keepdims=True) + EPSILON)
        scaled = hidden * rms
        gained = gain_ref[...] * normed_grad
        inside = jnp.mean(gained * scaled, axis=1, keepdims=True)
        hidden_grad = grad_ref[own_rows(core), :].astype(WIDE) + rms * (gained - scaled * inside)
        gain_part_ref[...] = jnp.sum(normed_grad * scaled, axis=0, keepdims=True)
        hidden_grad_ref[...] = hidden_grad
        hidden_low = hidden_grad.astype(LOW)
        far_grad[...] = dot(hidden_low, far_output_ref[...], NT).astype(LOW)
        move = send(far_grad, context_grad_ref.at[own_rows(core)], core_sems, 0, CORE)
        move.start()
        part_shape = parts.shape[1:]
        parts[0] = dot(context_ref[...], hidden_low, TN).astype(LOW).reshape(part_shape)
        parts[1] = dot(far_context_ref[...], hidden_low, TN).astype(LOW).reshape(part_shape)
        others = [
            send(parts.at[kind, :, :, 1 - core], parts_came.at[kind], core_sems, 1 + kind, CORE) for kind in kinds
        ]
        for one in others:
            one.start()
        near_grad[...] = dot(hidden_low, output_ref[...], NT).astype(LOW)
        keep = pltpu.make_async_copy(near_grad, context_grad_ref.at[own_rows(core)], kept)
        keep.start()
        folds[1].wait()
        slot_ids = core * (rows // 2) + lax.broadcasted_iota(jnp.int32, (rows // 2, 1), 0)
        valid = (slot_ids < length_ref[0]).astype(WIDE)
        layer_rows = (hidden + (out_total[own_rows(core), :] + fold_came[1].astype(WIDE))) * valid
        layer_ref[...] = layer_rows.astype(LOW).reshape(layer_ref.shape)
        for one in others:
            one.wait()
        for turn in range(depth):
            near = parts[0, turn, :, core].astype(WIDE) + parts_came[1, turn].astype(WIDE)
            output_part_ref[turn, core] = near.astype(LOW)
            far = parts[1, turn, :, core].astype(WIDE) + parts_came[0, turn].astype(WIDE)
            output_part_ref[turn, 1 - core] = far.astype(LOW)
        for kind in kinds:
            store(last, kind).wait()
        move.wait()
        keep.wait()
        for number in range(last):
            for kind in kinds:
                first_sum(number, kind).wait()


def middle(length, normed, grad, hidden, gain, outputs, contexts, mine, wholes):
    rows, width = normed.shape
    inner = outputs[0].shape[0]
    unit = mine[0].shape[0]
    depth = lax.axis_size("seq")
    held = depth // 2
    thick, slim = (unit // 4, inner // 16)
    vmem, anywhere = (pl.BlockSpec(memory_space=pltpu.VMEM), pl.BlockSpec(memory_space=pltpu.HBM))
    shape = jax.ShapeDtypeStruct
    part = (depth, 2, 2, thick, width)
    return pl.pallas_call(
        functools.partial(middle_kernel, depth),
        grid=(depth,),
        in_specs=[pl.BlockSpec(memory_space=pltpu.SMEM)] + [vmem] * 2 + [anywhere, vmem] + [anywhere] * 8,
        out_specs=[anywhere] * 7 + [vmem] * 4,
        out_shape=[shape(part, LOW)] * 2
        + [shape((depth, 2, thick, width), LOW)] * 2
        + [shape((unit, width), LOW)] * 2
        + [
            shape((rows, inner), LOW),
            shape((rows // 2, width), WIDE),
            shape((held, rows // depth, width), LOW),
            shape((1, width), WIDE),
            shape((4, 2, 2, slim, width), LOW),
        ],
        scratch_shapes=[pltpu.VMEM(one.shape, one.dtype) for one in (hidden, *outputs, *contexts)]
        + [pltpu.VMEM((rows // 2, inner), LOW)]
        + [pltpu.VMEM((rows, width), WIDE)] * 2
        + [pltpu.VMEM((2, rows // 2, width), LOW)] * 2
        + [pltpu.VMEM((2, unit, width), LOW)] * 2
        + [pltpu.VMEM((2, 2, 2, thick, width), LOW)] * 2
        + [
            pltpu.VMEM((2, 4, 2, 2, slim, width), LOW),
            pltpu.VMEM((2, 4, 2, slim, width), LOW),
            pltpu.VMEM((rows // 2, inner), LOW),
            pltpu.SemaphoreType.DMA((2, 2)),
            pltpu.SemaphoreType.DMA((2, 2)),
            pltpu.SemaphoreType.DMA((2, 6)),
            pltpu.SemaphoreType.DMA((2, 2 * (depth - 1))),
            pltpu.SemaphoreType.DMA((2, 2)),
            pltpu.SemaphoreType.DMA((2, 3)),
            pltpu.SemaphoreType.DMA,
            pltpu.SemaphoreType.DMA((5,)),
        ],
        compiler_params=pltpu.CompilerParams(vmem_limit_bytes=62 << 20, collective_id=2, has_side_effects=True),
        cost_estimate=pl.CostEstimate(
            flops=52 * unit * rows * width,
            bytes_accessed=32 * unit * width + 12 * rows * width,
            transcendentals=8 * unit * rows,
        ),
        name="middle",
    )(length, normed, grad, hidden, gain, *outputs, *contexts, *mine, *wholes)


def add_rows(target, source):
    target[...] = (target[...].astype(WIDE) + source[...].astype(WIDE)).astype(LOW)


def backward_kernel(
    depth,
    length_ref,
    query_ref,
    key_ref,
    value_ref,
    grad_ref,
    log_ref,
    near_ref,
    normed_in_ref,
    weight_in_ref,
    source_in_ref,
    hidden_in_ref,
    gain_ref,
    small_ref,
    output_ref,
    layer_ref,
    up_ref,
    down_ref,
    up_came_ref,
    down_came_ref,
    layer_out_ref,
    row_came,
    heads_out_ref,
    units_out_ref,
    gains_out_ref,
    sums_out_ref,
    normed_ref,
    weight_ref,
    source_ref,
    hidden_ref,
    bias,
    spare,
    keys,
    values,
    padded,
    key_total,
    value_total,
    tiles,
    lows,
    part,
    x_block,
    y_block,
    x_came,
    y_came,
    x_last,
    y_last,
    heads_came,
    units,
    units_came,
    units_last,
    units_far,
    fold_sent,
    fold_came,
    row_sent,
    small,
    small_came,
    swap_sems,
    first_sems,
    second_sems,
    third_sems,
    late_sems,
    unit_second_sems,
    unit_third_sems,
    fold_sems,
    row_sems,
    layer_sems,
    small_sems,
    early_sems,
    local_sems,
    later_sems,
):
    rows = query_ref.shape[0]
    width = normed_ref.shape[1]
    held = depth // 2
    step = pl.program_id(0)
    last = depth - 1
    place, index = (lax.axis_index("seq"), lax.axis_index("fsdp"))
    core, x, y = (lax.rem(index, 2), lax.rem(index // 2, 2), index // 4)
    column = index - core

    def owner(block):
        return lax.rem(place + 1 + block, depth)

    def beside(source, target, sems, number, bit):
        return push(source, target, sems, number, place, partner(bit))


    def unit_place(hop):
        return chip_of(*(bit for bit in (ALONG_X, ALONG_Y) if hop & (bit // 2)))

    def unit_source(kind, hop):
        block = unit_place(hop)
        if kind == 0:
            return (up_ref.at[block, :, 1 - x], up_ref.at[block, :, x], ALONG_X)
        return (down_ref.at[block, 1 - y], down_ref.at[block, y], ALONG_Y)

    def unit_came(kind, hop):
        return units_came.at[kind, hop]

    def unit_own(kind, hop):
        return pltpu.make_async_copy(unit_source(kind, hop)[1], units.at[kind, hop], local_sems.at[kind, hop])

    def unit_early(kind, hop):
        there = (up_came_ref, down_came_ref)[kind].at[unit_place(hop)]
        return pltpu.make_async_copy(there, units_came.at[kind, hop], early_sems.at[kind, hop])

    def unit_late(kind, hop):
        away, _, bit = unit_source(kind, hop)
        return beside(away, units_came.at[kind, late[kind]], late_sems, (kind,), bit)

    late = (2, 1)

    def units_start():
        for kind in range(2):
            unit_late(kind, 3).start()
        for kind in range(2):
            for hop in range(4):
                unit_own(kind, hop).start()
                if hop != late[kind]:
                    unit_early(kind, hop).start()

    def unit_halves(kind, hop):
        if kind == 0:
            return (units.at[0, hop, 1 - y], units.at[0, hop, y], ALONG_Y)
        return (units.at[1, hop, 1 - x], units.at[1, hop, x], ALONG_X)

    def unit_second(kind, hop):
        away, _, bit = unit_halves(kind, hop)
        there = hop ^ (bit // 2)
        return push(
            away, units_last.at[kind, there], unit_second_sems, (kind, hop), place, partner(bit), (kind, there)
        )

    def unit_first(kind, hop):
        unit_own(kind, hop).wait()
        if hop == late[kind]:
            unit_late(kind, 3).wait()
        else:
            unit_early(kind, hop).wait()
        add_rows(units.at[kind, hop], units_came.at[kind, hop])
        unit_second(kind, hop).start()


    def unit_arrived(kind, block, slot):
        far = units_far.at[kind, block, slot]
        return push(far, far, unit_third_sems, (kind, block, slot), place, partner(CORE))

    def unit_direct(kind, hop):
        block = unit_place(hop)
        slot = lax.rem(block + 2 * depth - place - 1, depth)
        own = unit_halves(kind, hop)[1]
        return push(
            own, units_far.at[kind, block, slot], unit_third_sems, (kind, block, 0), block, index, (kind, block, slot)
        )

    def unit_summed(kind, hop):
        unit_second(kind, hop).wait_send()
        unit_second(kind, hop ^ (2 - kind)).wait_recv()
        add_rows(unit_halves(kind, hop)[1], units_last.at[kind, hop])

        @pl.when(unit_place(hop) != place)
        def _():
            unit_direct(kind, hop).start()

    def unit_finish(kind, hop):
        block = unit_place(hop)

        @pl.when(block != place)
        def _():
            unit_direct(kind, hop).wait_send()

        @pl.when(block == place)
        def _():
            total = unit_halves(kind, hop)[1][...].astype(WIDE)
            for slot in range(depth - 1):
                unit_arrived(kind, block, slot).wait_recv()
                total = total + units_far[kind, block, slot].astype(WIDE)
            units_out_ref[kind] = total


    def swaps(block):
        moves = [
            beside(part.at[kind, :, 1 - core], x_block.at[block, :, core, kind], swap_sems, (kind, block), CORE)
            for kind in range(2)
        ]
        moves.append(beside(part.at[2, :, 1 - core], y_block.at[block, core, :, 0], swap_sems, (2, block), CORE))
        return moves

    def output_copy(block):
        return pltpu.make_async_copy(output_ref.at[owner(block)], y_block.at[block, :, :, 1], local_sems.at[2, block])

    def firsts(block):
        return (
            beside(x_block.at[block, 1 - x], x_came.at[block], first_sems, (0, block), ALONG_X),
            beside(y_block.at[block, 1 - y], y_came.at[block], first_sems, (1, block), ALONG_Y),
        )

    def seconds(block):
        return (
            beside(x_block.at[block, x, 1 - y], x_last.at[block], second_sems, (0, block), ALONG_Y),
            beside(y_block.at[block, y, 1 - x], y_last.at[block], second_sems, (1, block), ALONG_X),
        )

    def thirds(block):
        return [
            push(own, heads_came.at[block, kind], third_sems, (kind, block), owner(block), index)
            for kind, own in enumerate((x_block.at[block, x, y], y_block.at[block, y, x]))
        ]

    def heads_start(block):
        for one in swaps(block):
            one.wait_recv()
        output_copy(block).wait()
        for one in firsts(block):
            one.start()

    def heads_first(block):
        for one in firsts(block):
            one.wait()
        add_rows(x_block.at[block, x], x_came.at[block])
        add_rows(y_block.at[block, y], y_came.at[block])
        for one in seconds(block):
            one.start()

    def heads_second(block, mine=False):
        for one in seconds(block):
            one.wait()
        add_rows(x_block.at[block, x, y], x_last.at[block])
        add_rows(y_block.at[block, y, x], y_last.at[block])
        if not mine:
            for one in thirds(block):
                one.start()

    later = [
        pltpu.make_async_copy(one, there, later_sems.at[number])
        for number, (one, there) in enumerate(
            (
                (normed_in_ref, normed_ref),
                (weight_in_ref, weight_ref),
                (source_in_ref, source_ref),
                (hidden_in_ref, hidden_ref),
            )
        )
    ]

    @pl.when(step == 0)
    def _():
        greet_column(depth)
        units_start()
        for one in later:
            one.start()
        for block in range(depth):
            output_copy(block).start()
        for piece in range(held):
            row_moves(layer_ref.at[piece], layer_out_ref, layer_sems, depth, piece)
        spare[...] = spare_lanes(length_ref[0], rows)
        for head in range(2):
            padded[head, :HALF_ROWS, :] = jnp.zeros((HALF_ROWS, QUERY_ROWS), LOW)
            padded[head, rows + HALF_ROWS :, :] = jnp.zeros((HALF_ROWS, QUERY_ROWS), LOW)

    both_ready = [(0, 1), (0, 3), (1, 2), (1, 3)]
    others = [(0, 0), (0, 2), (1, 0), (1, 1)]

    def advance(number):
        def at(turn, tick, act):
            @pl.when((step == turn) & (number == tick))
            def _():
                act()

        ready = both_ready + [(0, 0), (1, 0)]
        at(0, 1, lambda: [unit_first(*one) for one in ready])
        at(1, 0, lambda: [unit_first(kind, late[kind]) for kind in range(2)])
        at(1, 3, lambda: [unit_summed(*one) for one in both_ready])
        at(2, 3, lambda: [unit_summed(*one) for one in others])
        at(3, 1, lambda: heads_first(0))

        @pl.when((step >= 1) & (number == 1))
        def _():
            heads_start(step - 1)

    pair = owner(step)
    lanes = pl.ds(pl.multiple_of(pair * LANES, LANES), LANES)
    split_heads(key_ref[:, lanes], spare[...], keys)
    split_heads(value_ref[:, lanes], jnp.zeros((rows, LANES), LOW), values)

    def low_lanes(kind):
        return pl.ds(pl.multiple_of((3 * pair + kind) * LANES, LANES), LANES)

    near_start = rows - QUERY_ROWS - HALF_ROWS
    near_end = near_start + 2 * QUERY_ROWS
    for head in range(2):
        line = near_ref[2 * pair + head]
        bias[head, :near_start, :] = jnp.broadcast_to(line[:, :1], (near_start, QUERY_ROWS))
        bias[head, near_start:near_end, :] = near_block(line).T
        bias[head, near_end:, :] = jnp.broadcast_to(line[:, -1:], (bias.shape[1] - near_end, QUERY_ROWS))
    key_total[...] = jnp.zeros_like(key_total)
    value_total[...] = jnp.zeros_like(value_total)
    tiles[...] = jnp.zeros_like(tiles)
    sums = small.at[0, pl.ds(pl.multiple_of(16 + 8 * pair, 8), 8)]
    sums[...] = jnp.zeros((8, LANES), WIDE)
    spot = lax.broadcasted_iota(jnp.int32, (1, LANES), 1)
    lane = lax.broadcasted_iota(jnp.int32, (QUERY_ROWS, LANES), 1)
    ones = jnp.where(lax.rem(lane, HEAD_DIM) == 0, 1.0, 0.0).astype(LOW)
    zero = jnp.zeros((), LOW)
    blocks = rows // QUERY_ROWS

    def block(number, carry):
        start = pl.multiple_of(number * QUERY_ROWS, QUERY_ROWS)
        offset = pl.multiple_of(rows - QUERY_ROWS - number * QUERY_ROWS, LANES)
        advance(number)
        both = query_ref[pl.ds(start, QUERY_ROWS), lanes]
        grad = grad_ref[pl.ds(start, QUERY_ROWS), lanes]
        parts = []
        for head in range(2):
            mine = lane < HEAD_DIM if head == 0 else lane >= HEAD_DIM
            logits = dot(keys[head], jnp.where(mine, both, ones), NT)
            logits = logits + bias[head, pl.ds(offset, rows), :]
            probs = jnp.exp(logits - log_ref[pair, head : head + 1, pl.ds(start, QUERY_ROWS)])
            prob_grad = dot(values[head], grad, NT)
            weighted = probs * prob_grad
            total = jnp.sum(weighted, axis=0, keepdims=True)
            score = (weighted - probs * total).astype(LOW)
            value_total[...] += dot(probs.astype(LOW), jnp.where(mine, grad, zero))
            key_total[...] += dot(score, jnp.where(mine, both, zero))
            padded[head, HALF_ROWS : HALF_ROWS + rows, :] = score
            one = dot(score, keys[head], TN)
            parts.append(one)
            columns = jnp.sum(one, axis=0, keepdims=True)
            first = HEAD_DIM * (1 - head) + 1 + number
            close = padded[head, pl.ds(start, 2 * QUERY_ROWS), :].astype(WIDE)
            quarter = [close[HALF_ROWS * turn : HALF_ROWS * (turn + 1)] for turn in range(4)]
            for turn in range(3):
                tiles[head, turn] += quarter[turn][:, :HALF_ROWS] + quarter[turn + 1][:, HALF_ROWS:]
            left = jnp.sum(quarter[0][:, HALF_ROWS:], axis=0, keepdims=True)
            right = jnp.sum(quarter[3][:, :HALF_ROWS], axis=0, keepdims=True)
            left = left + jnp.where(spot == first, columns, 0.0)
            right = right + jnp.where(spot == first + blocks, columns, 0.0)
            sums[4 * head + 2 : 4 * head + 3, :] += left
            sums[4 * head + 3 : 4 * head + 4, :] += right
        chosen = jnp.where(lane < HEAD_DIM, parts[0], parts[1])
        lows[pl.ds(start, QUERY_ROWS), low_lanes(0)] = chosen.astype(LOW)
        return carry

    lax.fori_loop(0, blocks, block, 0)
    lows[:, low_lanes(1)] = key_total[...].astype(LOW)
    lows[:, low_lanes(2)] = value_total[...].astype(LOW)
    shape = (HALF_ROWS, HALF_ROWS)
    upper = lax.broadcasted_iota(jnp.int32, shape, 0) <= lax.broadcasted_iota(jnp.int32, shape, 1)
    for head in range(2):
        before, centre, behind = (tiles[head, turn] for turn in range(3))
        sums[4 * head : 4 * head + 1, :] = diagonal_sums(jnp.where(upper, centre, before))
        sums[4 * head + 1 : 4 * head + 2, :] = diagonal_sums(jnp.where(upper, behind, centre))
        sums[4 * head + 2 : 4 * head + 3, :] += jnp.sum(jnp.where(upper, before, 0.0), axis=0, keepdims=True)
        sums[4 * head + 3 : 4 * head + 4, :] += jnp.sum(jnp.where(upper, 0.0, behind), axis=0, keepdims=True)

    @pl.when(step >= 1)
    def _():
        for one in swaps(step - 1):
            one.wait_send()

    @pl.when(step == 0)
    def _():
        later[0].wait()

    for kind in range(3):
        product = dot(lows[:, low_lanes(kind)], normed_ref[...], TN).astype(LOW)
        part[kind] = product.reshape(part.shape[1:])
    for one in swaps(step):
        one.start()
    for half in range(2):
        for kind in range(2):
            x_block[step, half, core, kind] = part[kind, half, core]
        y_block[step, core, half, 0] = part[2, half, core]

    @pl.when(step == last)
    def _():
        span = rows // 2 // held
        for one in later[1:]:
            one.wait()
        for piece in range(held):
            away = pl.ds(pl.multiple_of((1 - core) * (rows // 2) + piece * span, span), span)
            fold_sent[piece] = dot(lows[away, :], weight_ref[...]).astype(LOW)
            beside(fold_sent.at[piece], fold_came.at[piece], fold_sems, (piece,), CORE).start()
        heads_second(0)
        heads_first(1)
        for one in swaps(last):
            one.wait_send()
        heads_start(last)

        gain_total = jnp.zeros((1, width), WIDE)
        for piece in range(held):
            here = pl.ds(pl.multiple_of(core * (rows // 2) + piece * span, span), span)
            product = dot(lows[here, :], weight_ref[...])
            beside(fold_sent.at[piece], fold_came.at[piece], fold_sems, (piece,), CORE).wait()
            product = product + fold_came[piece].astype(WIDE)
            local = slice(piece * span, (piece + 1) * span)
            source = source_ref[local, :].astype(WIDE)
            rms = inverse_root(jnp.mean(source * source, axis=1, keepdims=True) + EPSILON)
            scaled = source * rms
            gain_total = gain_total + jnp.sum(product * scaled, axis=0, keepdims=True)
            gained = gain_ref[...] * product
            inside = jnp.mean(gained * scaled, axis=1, keepdims=True)
            row_sent[piece] = (hidden_ref[local, :] + rms * (gained - scaled * inside)).astype(LOW)
            if piece == held - 1:
                for number in range(width // LANES):
                    small[0, number : number + 1, :] = gain_total[:, number * LANES : (number + 1) * LANES]
                small[0, 8:16, :] = small_ref[...]
                moves = [
                    push(small.at[0], small_came.at[turn], small_sems, (turn,), lax.rem(place + turn, depth), index)
                    for turn in range(1, depth)
                ]
                for one in moves:
                    one.start()
            row_moves(row_sent.at[piece], row_came, row_sems, depth, piece)
            if piece == 0:
                heads_first(last - 1)
                heads_second(1)
        heads_second(last - 1)
        heads_first(last)
        heads_second(last, True)

        for one in moves:
            one.wait()
        small[1] = small[0] + sum(small_came[turn] for turn in range(1, depth))
        for turn, bit in ((1, ALONG_X), (2, ALONG_Y)):
            move = beside(small.at[turn], small_came.at[depth + turn - 1], small_sems, (depth + turn - 1,), bit)
            move.start()
            move.wait()
            small[turn + 1] = small[turn] + small_came[depth + turn - 1]
        move = beside(small.at[3], small_came.at[0], small_sems, (0,), CORE)
        move.start()
        move.wait()
        lines = width // LANES
        for number in range(2):
            line = pl.ds(number * lines + index, 1)
            gains_out_ref[number : number + 1, :] = small[3, line, :] + small_came[0, line, :]
        sums_out_ref[core] = small[3, 2 * lines :, :]
        sums_out_ref[1 - core] = small_came[0, 2 * lines :, :]

        for block in range(last):
            for one in thirds(block):
                one.wait()
        for kind in range(2):
            for hop in range(4):
                unit_finish(kind, hop)
        heads_out_ref[0:2] = x_block[last, x, y].astype(WIDE) + sum(
            heads_came[one, 0].astype(WIDE) for one in range(depth - 1)
        )
        heads_out_ref[2:4] = y_block[last, y, x].astype(WIDE) + sum(
            heads_came[one, 1].astype(WIDE) for one in range(depth - 1)
        )
        for piece in range(held):
            row_moves(layer_ref.at[piece], layer_out_ref, layer_sems, depth, piece, False)
            row_moves(row_sent.at[piece], row_came, row_sems, depth, piece, False)
        rows_came(layer_out_ref, layer_sems, depth)
        rows_came(row_came, row_sems, depth)


def backward(
    length, query, key, value, grad, logs, near, normed, weights, source, hidden, gain, ffn_gain_part, output_part, layer, *units
):
    rows, inner = query.shape
    width = normed.shape[1]
    depth = lax.axis_size("seq")
    held = depth // 2
    span = rows // depth
    slim, thick = (output_part.shape[3], units[0].shape[3])
    vmem, anywhere = (pl.BlockSpec(memory_space=pltpu.VMEM), pl.BlockSpec(memory_space=pltpu.HBM))
    shape = jax.ShapeDtypeStruct
    small_rows = 2 * (width // LANES) + 8 * depth
    sems = [(3, depth), (2, depth), (2, depth), (2, depth), (2,), (2, depth), (2, depth, depth - 1)]
    sems += [(held,), (held, held), (held, held), (depth + 2,)]
    return pl.pallas_call(
        functools.partial(backward_kernel, depth),
        grid=(depth,),
        in_specs=[pl.BlockSpec(memory_space=pltpu.SMEM)] + [vmem] * 6 + [anywhere] * 4 + [vmem] * 2 + [anywhere, vmem] + [anywhere] * 4,
        out_specs=[anywhere] * 2 + [vmem] * 4,
        out_shape=[
            shape((held, span, width), LOW),
            shape((held, span, width), LOW),
            shape((4, slim, width), WIDE),
            shape((2, thick, width), WIDE),
            shape((2, LANES), WIDE),
            shape((2, 8 * depth, LANES), WIDE),
        ],
        scratch_shapes=[
            pltpu.VMEM(normed.shape, LOW),
            pltpu.VMEM(weights.shape, LOW),
            pltpu.VMEM(source.shape, LOW),
            pltpu.VMEM(hidden.shape, WIDE),
            pltpu.VMEM((2, 2 * rows - QUERY_ROWS, QUERY_ROWS), WIDE),
            pltpu.VMEM((rows, LANES), LOW),
            pltpu.VMEM((2, rows, LANES), LOW),
            pltpu.VMEM((2, rows, LANES), LOW),
            pltpu.VMEM((2, rows + QUERY_ROWS, QUERY_ROWS), LOW),
            pltpu.VMEM((rows, LANES), WIDE),
            pltpu.VMEM((rows, LANES), WIDE),
            pltpu.VMEM((2, 3, HALF_ROWS, HALF_ROWS), WIDE),
            pltpu.VMEM((rows, 3 * inner), LOW),
            pltpu.VMEM((3, 2, 2, slim, width), LOW),
        ]
        + [pltpu.VMEM((depth, 2, 2, 2, slim, width), LOW)] * 2
        + [pltpu.VMEM((depth, 2, 2, slim, width), LOW)] * 2
        + [pltpu.VMEM((depth, 2, slim, width), LOW)] * 2
        + [
            pltpu.VMEM((depth - 1, 2, 2, slim, width), LOW),
            pltpu.VMEM((2, depth, 2, thick, width), LOW),
            pltpu.VMEM((2, depth, 2, thick, width), LOW),
            pltpu.VMEM((2, depth, thick, width), LOW),
            pltpu.VMEM((2, depth, depth - 1, thick, width), LOW),
        ]
        + [pltpu.VMEM((held, span, width), LOW)] * 3
        + [pltpu.VMEM((4, small_rows, LANES), WIDE), pltpu.VMEM((depth + 2, small_rows, LANES), WIDE)]
        + [pltpu.SemaphoreType.DMA((2,) + one) for one in sems]
        + [pltpu.SemaphoreType.DMA((2, depth)), pltpu.SemaphoreType.DMA((3, depth)), pltpu.SemaphoreType.DMA((4,))],
        compiler_params=pltpu.CompilerParams(
            vmem_limit_bytes=62 << 20, collective_id=3, has_side_effects=True
        ),
        cost_estimate=pl.CostEstimate(
            flops=60 * rows * rows * inner, bytes_accessed=14 * rows * inner, transcendentals=rows * rows * inner // 64
        ),
        name="backward",
    )(length, query, key, value, grad, logs, near, normed, weights, source, hidden, gain, ffn_gain_part, output_part, layer, *units)


def flip(value, bit):
    size = lax.axis_size("fsdp")
    return lax.ppermute(value, "fsdp", [(one, one ^ bit) for one in range(size)])


def other_core(value):
    return flip(value, 1)


def rounds_of(inverse):
    depth, size = (lax.axis_size("seq"), lax.axis_size("fsdp"))
    held = depth // 2
    rounds = []
    for step in range(held):
        pairs = []
        for place in range(depth):
            for index in range(size):
                target = (index % 2) * held + (place + step) % held
                there = target * size + index - index % 2 + place // held
                here = place * size + index
                pairs.append((there, here) if inverse else (here, there))
        rounds.append(pairs)
    return rounds


def to_sequence(blocks):
    held, span, width = blocks.shape
    place = lax.axis_index("seq")
    out = jnp.zeros((held, span, width), blocks.dtype)
    for step, pairs in enumerate(rounds_of(False)):
        sent = lax.dynamic_index_in_dim(blocks, (place + step) % held, 0, keepdims=False)
        got = lax.ppermute(sent, BOTH, pairs)
        out = lax.dynamic_update_index_in_dim(out, got, (place + held - step) % held, 0)
    return out.reshape(held * span, width)


def to_slots(rows, held):
    span, width = (rows.shape[0] // held, rows.shape[1])
    place = lax.axis_index("seq")
    blocks = rows.reshape(held, span, width)
    out = jnp.zeros(blocks.shape, rows.dtype)
    for step, pairs in enumerate(rounds_of(True)):
        sent = lax.dynamic_index_in_dim(blocks, (place + held - step) % held, 0, keepdims=False)
        got = lax.ppermute(sent, BOTH, pairs)
        out = lax.dynamic_update_index_in_dim(out, got, (place + step) % held, 0)
    return out


def whole(mine, core):
    other = other_core(mine)
    return jnp.where(
        core == 0, jnp.concatenate([mine, other], axis=0), jnp.concatenate([other, mine], axis=0)
    )


def fold(partial, core):
    half = partial.shape[0] // 2
    sent = lax.dynamic_slice_in_dim(partial, (1 - core) * half, half, 0)
    kept = lax.dynamic_slice_in_dim(partial, core * half, half, 0)
    return kept + other_core(sent)


def fast_plane():
    return lax.axis_size("fsdp") == 8 and lax.axis_size("seq") == 4


def own_head_rows(weight, core):
    width = weight.shape[1]
    return lax.dynamic_index_in_dim(weight.reshape(4, 2, -1, width), core, 1, keepdims=False).reshape(-1, width)


def add_low(left, right):
    return (left.astype(WIDE) + right.astype(WIDE)).astype(LOW)


def pick(value, index, axis):
    return lax.dynamic_index_in_dim(value, index, axis, keepdims=False)


def shards(
    inputs,
    lengths,
    cotangent,
    query_weight,
    key_weight,
    value_weight,
    output_weight,
    up_weight,
    down_weight,
    attn_gain,
    ffn_gain,
    bias_table,
):
    held, span, width = inputs.shape
    depth, size = (lax.axis_size("seq"), lax.axis_size("fsdp"))
    place, index = (lax.axis_index("seq"), lax.axis_index("fsdp"))
    core = index % 2
    rows = held * span
    inner = HEADS * HEAD_DIM
    fast = fast_plane()

    near_lengths = jnp.where(
        core == 0,
        jnp.concatenate([lengths, other_core(lengths)]),
        jnp.concatenate([other_core(lengths), lengths]),
    )
    length = lax.dynamic_slice_in_dim(near_lengths, place, 1, 0)

    own_table = lax.dynamic_index_in_dim(bias_table.reshape(BUCKETS, 4, 2, 2), core, 2, keepdims=False)
    own_table = own_table.reshape(BUCKETS, HEADS // 2)
    near = near_bias(own_table)

    if fast:
        normed_one, query, key, value, source_low, weights, up_mine, down_mine = enter(
            inputs, (query_weight, key_weight, value_weight), up_weight, down_weight, attn_gain[None, :]
        )
        source_low = source_low.reshape(rows, width)
        mine = (up_mine.reshape(-1, width), down_mine.reshape(-1, width))
        logs, near_context, hidden_one, far_context, own_output, far_output, normed_two, grad_low, *wholes = through(
            length,
            query,
            key,
            value,
            near,
            source_low,
            ffn_gain[None, :],
            output_weight,
            *mine,
            cotangent,
        )
        own_output, far_output = (own_output.reshape(-1, width), far_output.reshape(-1, width))
    else:
        own_three = [
            own_head_rows(lax.all_gather(one, "fsdp", axis=0, tiled=True), core)
            for one in (query_weight, key_weight, value_weight)
        ]
        full = lax.all_gather(output_weight, "fsdp", axis=0, tiled=True)
        own_output = own_head_rows(full, core)
        far_output = own_head_rows(full, 1 - core)
        own_up, own_down = (
            pick(
                lax.all_gather(one, "fsdp", axis=0, tiled=True).reshape(depth, size // 2, 2, -1, width), core, 2
            ).reshape(-1, width)
            for one in (up_weight, down_weight)
        )
        mask_rows = (core * rows + jnp.arange(rows, dtype=jnp.int32) < length[0])[:, None].astype(WIDE)
        source_low = to_sequence(inputs)
        source = source_low.astype(WIDE)
        rms_one = lax.rsqrt(jnp.mean(source * source, axis=1, keepdims=True) + EPSILON)
        scaled_one = source * rms_one
        normed_one = whole((scaled_one * attn_gain).astype(LOW), core)
        query, key, value = [dot(normed_one, one, NT).astype(LOW) for one in own_three]
        context, logs = attend(length, query, key, value, near)
        mine = (own_up, own_down)
        near_context = lax.dynamic_slice_in_dim(context, core * rows, rows, 0)
        far_context = other_core(lax.dynamic_slice_in_dim(context, (1 - core) * rows, rows, 0))
        hidden_one = source + (dot(near_context, own_output) + dot(far_context, far_output))
        rms_two = lax.rsqrt(jnp.mean(hidden_one * hidden_one, axis=1, keepdims=True) + EPSILON)
        scaled_two = hidden_one * rms_two
        normed_two = whole((scaled_two * ffn_gain).astype(LOW), core)
        grad_out = to_sequence(cotangent).astype(WIDE) * mask_rows
        grad_low = whole(grad_out.astype(LOW), core)

    if fast:
        up_part, down_part, up_came, down_came, _, _, context_grad, hidden_grad, layer_rows, ffn_gain_part, output_part = middle(
            length,
            normed_two,
            grad_low,
            hidden_one,
            ffn_gain[None, :],
            (own_output, far_output),
            (near_context, far_context),
            mine,
            wholes,
        )
    else:
        up_part, down_part, mlp_part, normed_part = feed(normed_two, grad_low, *mine)
        normed_grad = fold(normed_part, core)
        layer_rows = ((hidden_one + fold(mlp_part, core)) * mask_rows).astype(LOW)
        gained_two = ffn_gain * normed_grad
        hidden_grad = grad_out + rms_two * (
            gained_two - scaled_two * jnp.mean(gained_two * scaled_two, axis=1, keepdims=True)
        )
        ffn_gain_part = jnp.sum(normed_grad * scaled_two, axis=0)
        hidden_low = hidden_grad.astype(LOW)
        near_grad = dot(hidden_low, own_output, NT).astype(LOW)
        far_grad = other_core(dot(hidden_low, far_output, NT).astype(LOW))
        context_grad = jnp.where(
            core == 0,
            jnp.concatenate([near_grad, far_grad], axis=0),
            jnp.concatenate([far_grad, near_grad], axis=0),
        )
        near_output_part = dot(near_context, hidden_low, TN).astype(LOW)
        far_output_part = dot(far_context, hidden_low, TN).astype(LOW)

    if fast:
        layer_out, input_grad, heads_grad, units_grad, gains, sums = backward(
            length,
            query,
            key,
            value,
            context_grad,
            logs,
            near,
            normed_one,
            weights.reshape(-1, width),
            source_low,
            hidden_grad,
            attn_gain[None, :],
            ffn_gain_part.reshape(-1, LANES),
            output_part,
            layer_rows,
            up_part,
            down_part,
            up_came,
            down_came,
        )
        query_grad, key_grad, value_grad, output_grad = (heads_grad[number] for number in range(4))
        up_grad, down_grad = (units_grad[0], units_grad[1])
        input_grad = input_grad.astype(WIDE)
        attn_gain_grad, ffn_gain_grad = (gains[0], gains[1])
        sums = jnp.swapaxes(sums.reshape(2, 4, 2, 4 * LANES), 0, 1)
        bias_sum = bucket_sums(sums.reshape(HEADS, 4 * LANES))
    else:
        query_low, key_low, value_low, distance_sums = attend_grad(
            length, query, key, value, context_grad, logs, near
        )
        lows = (query_low, key_low, value_low)
        normed_one_grad = dot(query_low, own_three[0]) + dot(key_low, own_three[1]) + dot(value_low, own_three[2])
        normed_one_grad = fold(normed_one_grad, core)
        three_parts = [dot(one, normed_one, TN).astype(LOW) for one in lows]
        gained_one = attn_gain * normed_one_grad
        input_grad = hidden_grad + rms_one * (
            gained_one - scaled_one * jnp.mean(gained_one * scaled_one, axis=1, keepdims=True)
        )
        attn_gain_part = jnp.sum(normed_one_grad * scaled_one, axis=0)
        input_grad = to_slots(input_grad.astype(LOW), held).astype(WIDE)
        layer_out = to_slots(layer_rows, held)

        def summed(value):
            return lax.psum_scatter(value, BOTH, scatter_dimension=0, tiled=True).astype(WIDE)

        def own_only(value):
            blank = jnp.zeros_like(value)
            pair = jnp.where(core == 0, jnp.stack([value, blank], axis=1), jnp.stack([blank, value], axis=1))
            return summed(pair.reshape(-1, width))

        up_grad, down_grad = [own_only(one.reshape(depth * (size // 2), -1, width)) for one in (up_part, down_part)]
        query_grad, key_grad, value_grad = [own_only(one.reshape(4, -1, width)) for one in three_parts]
        near_part, far_part = (near_output_part.reshape(4, -1, width), far_output_part.reshape(4, -1, width))
        pair = jnp.where(
            core == 0, jnp.stack([near_part, far_part], axis=1), jnp.stack([far_part, near_part], axis=1)
        )
        output_grad = summed(pair.reshape(-1, width))
        bias_own = bucket_sums(distance_sums.reshape(HEADS // 2, 4 * LANES)).reshape(BUCKETS, 4, 1, 2)
        bias_full = lax.dynamic_update_slice(
            jnp.zeros((BUCKETS, 4, 2, 2), WIDE), bias_own, (0, 0, core, 0)
        ).reshape(BUCKETS, HEADS)
        attn_gain_sum, ffn_gain_sum, bias_sum = lax.psum((attn_gain_part, ffn_gain_part, bias_full), BOTH)

        gain_rows = width // size
        attn_gain_grad = lax.dynamic_slice_in_dim(attn_gain_sum, index * gain_rows, gain_rows, 0)
        ffn_gain_grad = lax.dynamic_slice_in_dim(ffn_gain_sum, index * gain_rows, gain_rows, 0)
    bucket_rows = BUCKETS // size
    bias_grad = lax.dynamic_slice_in_dim(bias_sum, index * bucket_rows, bucket_rows, 0)
    return (
        layer_out,
        input_grad,
        query_grad,
        key_grad,
        value_grad,
        output_grad,
        up_grad,
        down_grad,
        attn_gain_grad,
        ffn_gain_grad,
        bias_grad,
    )


def solution(mesh):
    placed = (
        P("fsdp", "seq", None),
        P("fsdp"),
        P("fsdp", "seq", None),
        P("fsdp", None),
        P("fsdp", None),
        P("fsdp", None),
        P("fsdp", None),
        P("fsdp", None),
        P("fsdp", None),
        P(),
        P(),
        P(),
    )
    return jax.shard_map(
        shards,
        mesh=mesh,
        in_specs=placed,
        out_specs=(
            P("fsdp", "seq", None),
            P("fsdp", "seq", None),
            P(("seq", "fsdp"), None),
            P(("seq", "fsdp"), None),
            P(("seq", "fsdp"), None),
            P(("seq", "fsdp"), None),
            P(("seq", "fsdp"), None),
            P(("seq", "fsdp"), None),
            P("fsdp"),
            P("fsdp"),
            P("fsdp", None),
        ),
        check_vma=False,
    )
```

```python
import functools

import jax
import jax.numpy as jnp
import numpy as np
from jax import lax
from jax.experimental import pallas as pl
from jax.experimental.pallas import tpu as pltpu
from jax.sharding import PartitionSpec as P

HEADS = 16
HEAD_DIM = 64
BUCKETS = 32
NEGATIVE = -1000000000.0
EPSILON = 1e-06
THRESHOLDS = (1, 2, 3, 4, 5, 6, 7, 8, 12, 16, 23, 32, 46, 64, 91)
ROOT_HALF = 0.7071067811865476
NORMAL_PEAK = 0.3989422804014327
LANES = 128
QUERY_ROWS = 256
HALF_ROWS = QUERY_ROWS // 2
LOW = jnp.bfloat16
WIDE = jnp.float32
BOTH = ("seq", "fsdp")

NN = (((1,), (0,)), ((), ()))
NT = (((1,), (1,)), ((), ()))
TN = (((0,), (0,)), ((), ()))


def dot(left, right, dims=NN):
    return lax.dot_general(left, right, dims, preferred_element_type=WIDE)


def inverse_root(value):
    root = lax.rsqrt(value)
    return root * (1.5 - 0.5 * value * root * root)


def gelu_parts(value):
    cumulative = 0.5 * (1.0 + lax.erf(value * ROOT_HALF))
    slope = cumulative + value * jnp.exp(-0.5 * value * value) * NORMAL_PEAK
    return (value * cumulative, slope)


CORE, ALONG_X, ALONG_Y = (1, 2, 4)


def partner(bit):
    index = lax.axis_index("fsdp")
    return index + bit - 2 * bit * ((index // bit) % 2)


def chip_of(*bits):
    index = lax.axis_index("fsdp")
    for bit in bits:
        index = index + bit - 2 * bit * ((index // bit) % 2)
    return index // 2


def send(source, target, sems, number, bit):
    return pltpu.make_async_remote_copy(
        src_ref=source,
        dst_ref=target,
        send_sem=sems.at[0, number],
        recv_sem=sems.at[1, number],
        device_id={"fsdp": partner(bit)},
        device_id_type=pl.DeviceIdType.MESH,
    )


def greet(bits):
    barrier = pltpu.get_barrier_semaphore()
    for bit in bits:
        pl.semaphore_signal(
            barrier, inc=1, device_id={"fsdp": partner(bit)}, device_id_type=pl.DeviceIdType.MESH
        )
    pl.semaphore_wait(barrier, len(bits))


def bucket_columns(distances):
    distances = np.asarray(distances)
    magnitude = sum((np.abs(distances) >= threshold).astype(np.int32) for threshold in THRESHOLDS)
    buckets = magnitude + np.where(distances > 0, BUCKETS // 2, 0)
    return (buckets[None, :] == np.arange(BUCKETS)[:, None]).astype(np.float32)


def near_bias(columns):
    chosen = jnp.asarray(bucket_columns(np.arange(2 * QUERY_ROWS) - HALF_ROWS))
    line = lax.dot_general(columns, chosen, TN, precision=lax.Precision.HIGHEST, preferred_element_type=WIDE)
    return line[:, None, :]


def near_block(line):
    shape = (QUERY_ROWS, 2 * QUERY_ROWS)
    turned = pltpu.roll(jnp.broadcast_to(line, shape), 0, 1, stride=1, stride_axis=0)
    row = lax.broadcasted_iota(jnp.int32, shape, 0)
    column = lax.broadcasted_iota(jnp.int32, shape, 1)
    return jnp.where(column < row, line[:, :1], turned)


def diagonal_sums(tile):
    side = tile.shape[1]
    row = lax.broadcasted_iota(jnp.int32, tile.shape, 0)
    step = 1
    while step < side:
        tile = jnp.where((row // step) % 2 == 1, pltpu.roll(tile, side - step, 1), tile)
        step *= 2
    return jnp.sum(tile, axis=0, keepdims=True)


def spare_lanes(length, rows):
    blocks = rows // QUERY_ROWS
    key = lax.broadcasted_iota(jnp.int32, (rows, LANES), 0)
    lane = lax.rem(lax.broadcasted_iota(jnp.int32, (rows, LANES), 1), HEAD_DIM)
    hidden = jnp.where((lane == 0) & (key >= length), NEGATIVE, 0.0)
    left = (lane >= 1) & (lane <= blocks) & (key < QUERY_ROWS * (lane - 1) - HALF_ROWS)
    start = QUERY_ROWS * (lane - 1 - blocks) + 3 * HALF_ROWS
    right = (lane > blocks) & (lane <= 2 * blocks) & (key >= start)
    return jnp.where(left | right, 1.0, hidden).astype(LOW)


def split_heads(pair, spare, out):
    low_half = lax.broadcasted_iota(jnp.int32, pair.shape, 1) < HEAD_DIM
    out[0] = jnp.where(low_half, pair, spare)
    out[1] = jnp.where(low_half, spare, pair)


def attend_kernel(
    length_ref, query_ref, key_ref, value_ref, near_ref, context_ref, log_ref, bias, keys, values
):
    rows = query_ref.shape[0]
    split_heads(key_ref[...], spare_lanes(length_ref[0], rows), keys)
    split_heads(value_ref[...], jnp.zeros((rows, LANES), LOW), values)
    near_start = rows - QUERY_ROWS - HALF_ROWS
    near_end = near_start + 2 * QUERY_ROWS
    for head in range(2):
        line = near_ref[head]
        bias[head, :, :near_start] = jnp.broadcast_to(line[:, :1], (QUERY_ROWS, near_start))
        bias[head, :, near_start:near_end] = near_block(line)
        bias[head, :, near_end:] = jnp.broadcast_to(line[:, -1:], (QUERY_ROWS, bias.shape[2] - near_end))
    lane = lax.broadcasted_iota(jnp.int32, (QUERY_ROWS, LANES), 1)
    ones = jnp.where(lax.rem(lane, HEAD_DIM) == 0, 1.0, 0.0).astype(LOW)

    def block(number, carry):
        start = pl.multiple_of(number * QUERY_ROWS, QUERY_ROWS)
        offset = pl.multiple_of(rows - QUERY_ROWS - number * QUERY_ROWS, LANES)
        both = query_ref[pl.ds(start, QUERY_ROWS), :]
        total = jnp.zeros((QUERY_ROWS, LANES), WIDE)
        for head in range(2):
            mine = lane < HEAD_DIM if head == 0 else lane >= HEAD_DIM
            logits = dot(jnp.where(mine, both, ones), keys[head], NT)
            logits = logits + bias[head, :, pl.ds(offset, rows)]
            peak = jnp.max(logits, axis=1, keepdims=True)
            exponent = jnp.exp(logits - peak)
            row_sum = jnp.sum(exponent, axis=1, keepdims=True)
            weights_low = (exponent * (1.0 / row_sum)).astype(LOW)
            total = total + dot(weights_low, values[head])
            logs = jnp.broadcast_to(peak + jnp.log(row_sum), (QUERY_ROWS, LANES))
            log_ref[0, head : head + 1, pl.ds(start, QUERY_ROWS)] = logs.T[0:1, :]
        context_ref[pl.ds(start, QUERY_ROWS), :] = total.astype(LOW)
        return carry

    lax.fori_loop(0, rows // QUERY_ROWS, block, 0)


def attend(length, query, key, value, near):
    rows, width = query.shape
    pairs = width // LANES
    smem = pl.BlockSpec(memory_space=pltpu.SMEM)
    columns = pl.BlockSpec((rows, LANES), lambda pair: (0, pair))
    return pl.pallas_call(
        attend_kernel,
        grid=(pairs,),
        in_specs=[smem, columns, columns, columns]
        + [pl.BlockSpec((2, 1, 2 * QUERY_ROWS), lambda pair: (pair, 0, 0))],
        out_specs=[columns, pl.BlockSpec((1, 2, rows), lambda pair: (pair, 0, 0))],
        out_shape=[
            jax.ShapeDtypeStruct((rows, width), LOW),
            jax.ShapeDtypeStruct((pairs, 2, rows), WIDE),
        ],
        scratch_shapes=[
            pltpu.VMEM((2, QUERY_ROWS, 2 * rows - QUERY_ROWS), WIDE),
            pltpu.VMEM((2, rows, LANES), LOW),
            pltpu.VMEM((2, rows, LANES), LOW),
        ],
        compiler_params=pltpu.CompilerParams(vmem_limit_bytes=40 << 20),
        cost_estimate=pl.CostEstimate(
            flops=24 * rows * rows * width, bytes_accessed=8 * rows * width, transcendentals=2 * pairs * rows * rows
        ),
        name="attend",
    )(length, query, key, value, near)


def attend_grad_kernel(
    length_ref,
    query_ref,
    key_ref,
    value_ref,
    grad_ref,
    log_ref,
    near_ref,
    query_grad_ref,
    key_grad_ref,
    value_grad_ref,
    sums_ref,
    bias,
    keys,
    values,
    padded,
    key_total,
    value_total,
    tiles,
):
    rows = query_ref.shape[0]
    blocks = rows // QUERY_ROWS
    split_heads(key_ref[...], spare_lanes(length_ref[0], rows), keys)
    split_heads(value_ref[...], jnp.zeros((rows, LANES), LOW), values)
    near_start = rows - QUERY_ROWS - HALF_ROWS
    near_end = near_start + 2 * QUERY_ROWS
    for head in range(2):
        line = near_ref[head]
        bias[head, :near_start, :] = jnp.broadcast_to(line[:, :1], (near_start, QUERY_ROWS))
        bias[head, near_start:near_end, :] = near_block(line).T
        bias[head, near_end:, :] = jnp.broadcast_to(line[:, -1:], (bias.shape[1] - near_end, QUERY_ROWS))
        padded[head, :HALF_ROWS, :] = jnp.zeros((HALF_ROWS, QUERY_ROWS), LOW)
        padded[head, rows + HALF_ROWS :, :] = jnp.zeros((HALF_ROWS, QUERY_ROWS), LOW)
    key_total[...] = jnp.zeros_like(key_total)
    value_total[...] = jnp.zeros_like(value_total)
    tiles[...] = jnp.zeros_like(tiles)
    sums_ref[...] = jnp.zeros_like(sums_ref)
    spot = lax.broadcasted_iota(jnp.int32, (1, LANES), 1)
    lane = lax.broadcasted_iota(jnp.int32, (QUERY_ROWS, LANES), 1)
    ones = jnp.where(lax.rem(lane, HEAD_DIM) == 0, 1.0, 0.0).astype(LOW)
    zero = jnp.zeros((), LOW)

    def block(number, carry):
        start = pl.multiple_of(number * QUERY_ROWS, QUERY_ROWS)
        offset = pl.multiple_of(rows - QUERY_ROWS - number * QUERY_ROWS, LANES)
        both = query_ref[pl.ds(start, QUERY_ROWS), :]
        grad = grad_ref[pl.ds(start, QUERY_ROWS), :]
        parts = []
        for head in range(2):
            mine = lane < HEAD_DIM if head == 0 else lane >= HEAD_DIM
            logits = dot(keys[head], jnp.where(mine, both, ones), NT)
            logits = logits + bias[head, pl.ds(offset, rows), :]
            probs = jnp.exp(logits - log_ref[0, head : head + 1, pl.ds(start, QUERY_ROWS)])
            prob_grad = dot(values[head], grad, NT)
            weighted = probs * prob_grad
            inner = jnp.sum(weighted, axis=0, keepdims=True)
            score = (weighted - probs * inner).astype(LOW)
            value_total[...] += dot(probs.astype(LOW), jnp.where(mine, grad, zero))
            key_total[...] += dot(score, jnp.where(mine, both, zero))
            padded[head, HALF_ROWS : HALF_ROWS + rows, :] = score
            part = dot(score, keys[head], TN)
            parts.append(part)
            columns = jnp.sum(part, axis=0, keepdims=True)
            spare = HEAD_DIM * (1 - head) + 1 + number
            close = padded[head, pl.ds(start, 2 * QUERY_ROWS), :].astype(WIDE)
            quarter = [close[HALF_ROWS * step : HALF_ROWS * (step + 1)] for step in range(4)]
            for step in range(3):
                tiles[head, step] += quarter[step][:, :HALF_ROWS] + quarter[step + 1][:, HALF_ROWS:]
            left = jnp.sum(quarter[0][:, HALF_ROWS:], axis=0, keepdims=True)
            right = jnp.sum(quarter[3][:, :HALF_ROWS], axis=0, keepdims=True)
            left = left + jnp.where(spot == spare, columns, 0.0)
            right = right + jnp.where(spot == spare + blocks, columns, 0.0)
            sums_ref[0, 4 * head + 2 : 4 * head + 3, :] += left
            sums_ref[0, 4 * head + 3 : 4 * head + 4, :] += right
        chosen = jnp.where(lane < HEAD_DIM, parts[0], parts[1])
        query_grad_ref[pl.ds(start, QUERY_ROWS), :] = chosen.astype(LOW)
        return carry

    lax.fori_loop(0, blocks, block, 0)
    key_grad_ref[...] = key_total[...].astype(LOW)
    value_grad_ref[...] = value_total[...].astype(LOW)
    shape = (HALF_ROWS, HALF_ROWS)
    upper = lax.broadcasted_iota(jnp.int32, shape, 0) <= lax.broadcasted_iota(jnp.int32, shape, 1)
    for head in range(2):
        before, centre, behind = (tiles[head, step] for step in range(3))
        sums_ref[0, 4 * head : 4 * head + 1, :] = diagonal_sums(jnp.where(upper, centre, before))
        sums_ref[0, 4 * head + 1 : 4 * head + 2, :] = diagonal_sums(jnp.where(upper, behind, centre))
        left = jnp.sum(jnp.where(upper, before, 0.0), axis=0, keepdims=True)
        right = jnp.sum(jnp.where(upper, 0.0, behind), axis=0, keepdims=True)
        sums_ref[0, 4 * head + 2 : 4 * head + 3, :] += left
        sums_ref[0, 4 * head + 3 : 4 * head + 4, :] += right


def attend_grad(length, query, key, value, grad, logs, near):
    rows, width = query.shape
    pairs = width // LANES
    smem = pl.BlockSpec(memory_space=pltpu.SMEM)
    columns = pl.BlockSpec((rows, LANES), lambda pair: (0, pair))
    shape = jax.ShapeDtypeStruct
    return pl.pallas_call(
        attend_grad_kernel,
        grid=(pairs,),
        in_specs=[smem, columns, columns, columns, columns]
        + [pl.BlockSpec((1, 2, rows), lambda pair: (pair, 0, 0))]
        + [pl.BlockSpec((2, 1, 2 * QUERY_ROWS), lambda pair: (pair, 0, 0))],
        out_specs=[columns, columns, columns] + [pl.BlockSpec((1, 8, LANES), lambda pair: (pair, 0, 0))],
        out_shape=[shape((rows, width), LOW)] * 3 + [shape((pairs, 8, LANES), WIDE)],
        scratch_shapes=[
            pltpu.VMEM((2, 2 * rows - QUERY_ROWS, QUERY_ROWS), WIDE),
            pltpu.VMEM((2, rows, LANES), LOW),
            pltpu.VMEM((2, rows, LANES), LOW),
            pltpu.VMEM((2, rows + QUERY_ROWS, QUERY_ROWS), LOW),
            pltpu.VMEM((rows, LANES), WIDE),
            pltpu.VMEM((rows, LANES), WIDE),
            pltpu.VMEM((2, 3, HALF_ROWS, HALF_ROWS), WIDE),
        ],
        compiler_params=pltpu.CompilerParams(vmem_limit_bytes=48 << 20),
        cost_estimate=pl.CostEstimate(
            flops=44 * rows * rows * width, bytes_accessed=14 * rows * width, transcendentals=2 * pairs * rows * rows
        ),
        name="attend_grad",
    )(length, query, key, value, grad, logs, near)


def bucket_sums(sums):
    side = np.arange(LANES)
    far = np.full((LANES,), 2 * HALF_ROWS)
    chosen = bucket_columns(np.concatenate([-side, HALF_ROWS - side, -far, far]))
    return lax.dot_general(
        jnp.asarray(chosen), sums, NT, precision=lax.Precision.HIGHEST, preferred_element_type=WIDE
    )


def feed_kernel(normed_ref, grad_ref, up_ref, down_ref, up_part_ref, down_part_ref, out_ref, back_ref):
    @pl.when(pl.program_id(0) == 0)
    def _():
        out_ref[...] = jnp.zeros_like(out_ref)
        back_ref[...] = jnp.zeros_like(back_ref)

    up, down = (up_ref[...], down_ref[...])
    normed, grad = (normed_ref[...], grad_ref[...])
    active, slope = gelu_parts(dot(normed, up, NT))
    active = active.astype(LOW)
    pre_grad = (dot(grad, down, NT) * slope).astype(LOW)
    out_ref[...] += dot(active, down)
    back_ref[...] += dot(pre_grad, up)
    up_part_ref[...] = dot(pre_grad, normed, TN).astype(LOW)
    down_part_ref[...] = dot(active, grad, TN).astype(LOW)


def feed(normed, grad, up, down):
    rows, width = normed.shape
    unit = up.shape[0] // 4
    fixed = pl.BlockSpec((rows, width), lambda step: (0, 0))
    block = pl.BlockSpec((unit, width), lambda step: (step, 0))
    return pl.pallas_call(
        feed_kernel,
        grid=(4,),
        in_specs=[fixed, fixed, block, block],
        out_specs=[block, block, fixed, fixed],
        out_shape=[jax.ShapeDtypeStruct((4 * unit, width), LOW)] * 2
        + [jax.ShapeDtypeStruct((rows, width), WIDE)] * 2,
        compiler_params=pltpu.CompilerParams(vmem_limit_bytes=56 << 20),
        name="feed",
    )(normed, grad, up, down)


def push(source, target, sems, number, place, index, there=None):
    return pltpu.make_async_remote_copy(
        src_ref=source,
        dst_ref=target,
        send_sem=sems.at[(0,) + number],
        recv_sem=sems.at[(1,) + (there or number)],
        device_id={"seq": place, "fsdp": index},
        device_id_type=pl.DeviceIdType.MESH,
    )


def greet_column(depth):
    barrier = pltpu.get_barrier_semaphore()
    place, index = (lax.axis_index("seq"), lax.axis_index("fsdp"))

    def signal(there, which):
        pl.semaphore_signal(
            barrier, inc=1, device_id={"seq": there, "fsdp": which}, device_id_type=pl.DeviceIdType.MESH
        )

    signal(place, partner(ALONG_X))
    signal(place, partner(ALONG_Y))
    signal(place, partner(CORE))
    for step in range(1, depth):
        signal(lax.rem(place + step, depth), index)
        signal(lax.rem(place + step, depth), partner(CORE))
    pl.semaphore_wait(barrier, 2 * depth + 1)


def slots_moves(source, target, sems, depth, act):
    held = depth // 2
    place, index = (lax.axis_index("seq"), lax.axis_index("fsdp"))
    core = lax.rem(index, 2)
    slot = lax.rem(place, held)
    for sequence in range(held):
        there, which = (core * held + sequence, index - core + place // held)
        home = (there == place) & (which == index)

        @pl.when(home)
        def _():
            if act == "start":
                pltpu.make_async_copy(source.at[sequence], target.at[slot], sems.at[1, slot]).start()

        @pl.when(jnp.logical_not(home))
        def _():
            move = push(source.at[sequence], target.at[slot], sems, (sequence,), there, which, (slot,))
            if act == "start":
                move.start()
            else:
                move.wait_send()


def slots_came(target, sems, slot):
    push(target.at[slot], target.at[slot], sems, (slot,), lax.axis_index("seq"), partner(CORE)).wait_recv()


def enter_kernel(
    depth,
    inputs_ref,
    query_ref,
    key_ref,
    value_ref,
    up_ref,
    down_ref,
    gain_ref,
    normed_out_ref,
    query_out_ref,
    key_out_ref,
    value_out_ref,
    source_out_ref,
    weights_out_ref,
    up_out_ref,
    down_out_ref,
    normed_ref,
    source_ref,
    weights_ref,
    kept,
    slot_sems,
    near_sems,
    far_sems,
    cut_sems,
    row_sems,
    local_sems,
):
    held = depth // 2
    span = source_ref.shape[1]
    rows = normed_ref.shape[0]
    index = lax.axis_index("fsdp")
    core = lax.rem(index, 2)
    chip = chip_of()
    mine = (query_ref, key_ref, value_ref)
    half = query_ref.shape[0] // 2
    greet_column(depth)
    slots_moves(inputs_ref, source_ref, slot_sems, depth, "start")
    direct = [
        send(one, weights_ref.at[chip, kind], near_sems, 2 * kind + turn, bit)
        for kind, one in enumerate(mine)
        for turn, bit in enumerate((ALONG_X, ALONG_Y))
    ]
    for one in direct:
        one.start()
    local = [
        pltpu.make_async_copy(one, weights_ref.at[chip, kind], local_sems.at[kind]) for kind, one in enumerate(mine)
    ]
    cuts = []
    for kind, (whole_one, out) in enumerate(((up_ref, up_out_ref), (down_ref, down_out_ref))):
        cuts.append(send(whole_one.at[:, 1 - core], out.at[core], cut_sems, kind, CORE))
        local.append(pltpu.make_async_copy(whole_one.at[:, core], kept.at[kind], local_sems.at[3 + kind]))
    for one in cuts + local:
        one.start()
    for one in direct:
        one.wait_recv()
    onward = []
    for turn, (bit, came) in enumerate(((ALONG_X, ALONG_Y), (ALONG_Y, ALONG_X))):
        piece = weights_ref.at[chip_of(came), :, pl.ds(turn * half, half)]
        onward.append(send(piece, piece, far_sems, turn, bit))
    for one in onward:
        one.start()

    moves = []
    for slot in range(held):
        slots_came(source_ref, slot_sems, slot)
        source = source_ref[slot].astype(WIDE)
        rms = inverse_root(jnp.mean(source * source, axis=1, keepdims=True) + EPSILON)
        here = pl.ds(pl.multiple_of(core * (rows // 2) + slot * span, span), span)
        normed_ref[here, :] = (source * rms * gain_ref[...]).astype(LOW)
        moves.append(send(normed_ref.at[here], normed_ref.at[here], row_sems, slot, CORE))
        moves[-1].start()
    for one in moves:
        one.wait()
    for one in local:
        one.wait()

    def project(number):
        weight = weights_ref[number].reshape(-1, weights_ref.shape[3])
        product = dot(normed_ref[...], weight, NT).astype(LOW)
        lanes = pl.ds(pl.multiple_of(number * LANES, LANES), LANES)
        for kind, out in enumerate((query_out_ref, key_out_ref, value_out_ref)):
            out[:, lanes] = product[:, kind * LANES : (kind + 1) * LANES]

    def some(turn, carry):
        project(jnp.where(turn == 0, chip, jnp.where(turn == 1, chip_of(ALONG_X), chip_of(ALONG_Y))))
        return carry

    lax.fori_loop(0, 3, some, 0)
    for one in onward:
        one.wait()
    stored = [
        pltpu.make_async_copy(one, there, local_sems.at[5 + number])
        for number, (one, there) in enumerate(
            (
                (normed_ref, normed_out_ref),
                (source_ref, source_out_ref),
                (weights_ref, weights_out_ref),
                (kept.at[0], up_out_ref.at[core]),
                (kept.at[1], down_out_ref.at[core]),
            )
        )
    ]
    for one in stored:
        one.start()
    project(chip_of(ALONG_X, ALONG_Y))
    for one in stored:
        one.wait()
    for one in direct:
        one.wait_send()
    for one in cuts:
        one.wait()
    slots_moves(inputs_ref, source_ref, slot_sems, depth, "end")


def enter(inputs, projections, up, down, gain):
    held, span, width = inputs.shape
    depth = lax.axis_size("seq")
    rows = 2 * held * span
    slim = projections[0].shape[0]
    thick = up.shape[0] // 4
    vmem, anywhere = (pl.BlockSpec(memory_space=pltpu.VMEM), pl.BlockSpec(memory_space=pltpu.HBM))
    shape = jax.ShapeDtypeStruct
    return pl.pallas_call(
        functools.partial(enter_kernel, depth),
        in_specs=[anywhere] * 6 + [vmem],
        out_specs=[anywhere] + [vmem] * 3 + [anywhere] * 4,
        out_shape=[shape((rows, width), LOW)]
        + [shape((rows, 4 * slim), LOW)] * 3
        + [shape((held, span, width), LOW), shape((4, 3, slim, width), LOW)]
        + [shape((2, 2, thick, width), LOW)] * 2,
        scratch_shapes=[
            pltpu.VMEM((rows, width), LOW),
            pltpu.VMEM((held, span, width), LOW),
            pltpu.VMEM((4, 3, slim, width), LOW),
            pltpu.VMEM((2, 2, thick, width), LOW),
            pltpu.SemaphoreType.DMA((2, held)),
            pltpu.SemaphoreType.DMA((2, 6)),
            pltpu.SemaphoreType.DMA((2, 2)),
            pltpu.SemaphoreType.DMA((2, 2)),
            pltpu.SemaphoreType.DMA((2, held)),
            pltpu.SemaphoreType.DMA((10,)),
        ],
        compiler_params=pltpu.CompilerParams(vmem_limit_bytes=62 << 20, collective_id=4, has_side_effects=True),
        cost_estimate=pl.CostEstimate(flops=24 * rows * slim * width, bytes_accessed=16 << 20, transcendentals=0),
        name="enter",
    )(inputs, *projections, up.reshape(2, 2, thick, width), down.reshape(2, 2, thick, width), gain)


def through_kernel(
    depth,
    length_ref,
    query_ref,
    key_ref,
    value_ref,
    near_ref,
    source_ref,
    gain_ref,
    output_ref,
    up_ref,
    down_ref,
    cotangent_ref,
    log_ref,
    context_ref,
    hidden_ref,
    far_context_out_ref,
    own_output_out_ref,
    far_output_out_ref,
    normed_ref,
    grad_ref,
    ups_ref,
    downs_ref,
    bias,
    keys,
    values,
    context,
    came,
    far_context_ref,
    own_output_ref,
    far_output_ref,
    normed,
    grad,
    slot_sems,
    near_sems,
    far_sems,
    deep_sems,
    core_sems,
    context_sems,
    local,
):
    rows = query_ref.shape[0]
    width = source_ref.shape[1]
    pair = pl.program_id(0)
    last = depth - 1
    held = depth // 2
    core = lax.rem(lax.axis_index("fsdp"), 2)
    chip = chip_of()
    own = pl.ds(pl.multiple_of(core * (rows // 2), rows // 2), rows // 2)
    other = pl.ds(pl.multiple_of((1 - core) * (rows // 2), rows // 2), rows // 2)
    half = output_ref.shape[0] // 2
    place, index = (lax.axis_index("seq"), lax.axis_index("fsdp"))
    parity = lax.rem(place, 2)
    unit = down_ref.shape[0] // 2
    mine = pl.ds(pl.multiple_of(parity * unit, unit), unit)
    direct = []
    for one, there in (
        (output_ref, own_output_ref.at[chip]),
        (down_ref.at[mine], downs_ref.at[chip, mine]),
        (up_ref, ups_ref.at[chip]),
    ):
        for bit in (ALONG_X, ALONG_Y):
            direct.append(send(one, there, near_sems, len(direct), bit))
    exchange = [
        push(
            downs_ref.at[chip_of(bit), mine],
            downs_ref.at[chip_of(bit), mine],
            deep_sems,
            (number,),
            place + 1 - 2 * parity,
            index,
        )
        for number, bit in enumerate((ALONG_X, ALONG_Y))
    ]
    onward = []
    for turn, (bit, from_bit) in enumerate(((ALONG_X, ALONG_Y), (ALONG_Y, ALONG_X))):
        piece = own_output_ref.at[chip_of(from_bit), pl.ds(turn * half, half)]
        onward.append(send(piece, piece, far_sems, turn, bit))
    keep = pltpu.make_async_copy(output_ref, own_output_ref.at[chip], local.at[0])
    swap = send(own_output_ref, far_output_ref, core_sems, 0, CORE)
    both_cores = [
        (send(one, there.at[own], core_sems, 1 + number, CORE), pltpu.make_async_copy(one, there.at[own], local.at[1 + number]))
        for number, (one, there) in enumerate(((grad, grad_ref), (normed, normed_ref)))
    ]
    stored = [
        pltpu.make_async_copy(one, there, local.at[3 + number])
        for number, (one, there) in enumerate(
            (
                (own_output_ref, own_output_out_ref),
                (far_output_ref, far_output_out_ref),
                (far_context_ref, far_context_out_ref),
            )
        )
    ]

    def context_move(number):
        lanes = pl.ds(pl.multiple_of(number * LANES, LANES), LANES)
        return send(context.at[other, lanes], far_context_ref.at[:, lanes], context_sems, number, CORE)

    @pl.when(pair == 0)
    def _():
        greet_column(depth)
        for one in direct[:4]:
            one.start()
        keep.start()
        slots_moves(cotangent_ref, came, slot_sems, depth, "start")

    @pl.when(pair == 1)
    def _():
        for one in direct[:2]:
            one.wait_recv()
        for one in onward + direct[4:]:
            one.start()

    @pl.when(pair == last - 1)
    def _():
        for one in direct[2:4]:
            one.wait_recv()
        for one in exchange:
            one.start()

    @pl.when(pair == last)
    def _():
        for one in onward:
            one.wait()
        keep.wait()
        swap.start()
        stored[0].start()
        slot_ids = core * (rows // 2) + lax.broadcasted_iota(jnp.int32, (rows // 2, 1), 0)
        valid = (slot_ids < length_ref[0]).astype(WIDE)
        for slot in range(held):
            slots_came(came, slot_sems, slot)
        grad[...] = (came[...].reshape(rows // 2, width).astype(WIDE) * valid).astype(LOW)
        for one in both_cores[0]:
            one.start()

    lanes = pl.ds(pl.multiple_of(pair * LANES, LANES), LANES)
    split_heads(key_ref[...], spare_lanes(length_ref[0], rows), keys)
    split_heads(value_ref[...], jnp.zeros((rows, LANES), LOW), values)
    near_start = rows - QUERY_ROWS - HALF_ROWS
    near_end = near_start + 2 * QUERY_ROWS
    for head in range(2):
        line = near_ref[head]
        bias[head, :, :near_start] = jnp.broadcast_to(line[:, :1], (QUERY_ROWS, near_start))
        bias[head, :, near_start:near_end] = near_block(line)
        bias[head, :, near_end:] = jnp.broadcast_to(line[:, -1:], (QUERY_ROWS, bias.shape[2] - near_end))
    lane = lax.broadcasted_iota(jnp.int32, (QUERY_ROWS, LANES), 1)
    ones = jnp.where(lax.rem(lane, HEAD_DIM) == 0, 1.0, 0.0).astype(LOW)

    def block(number, carry):
        start = pl.multiple_of(number * QUERY_ROWS, QUERY_ROWS)
        offset = pl.multiple_of(rows - QUERY_ROWS - number * QUERY_ROWS, LANES)
        both = query_ref[pl.ds(start, QUERY_ROWS), :]
        total = jnp.zeros((QUERY_ROWS, LANES), WIDE)
        for head in range(2):
            mine = lane < HEAD_DIM if head == 0 else lane >= HEAD_DIM
            logits = dot(jnp.where(mine, both, ones), keys[head], NT)
            logits = logits + bias[head, :, pl.ds(offset, rows)]
            peak = jnp.max(logits, axis=1, keepdims=True)
            exponent = jnp.exp(logits - peak)
            row_sum = jnp.sum(exponent, axis=1, keepdims=True)
            weights_low = (exponent * (1.0 / row_sum)).astype(LOW)
            total = total + dot(weights_low, values[head])
            logs = jnp.broadcast_to(peak + jnp.log(row_sum), (QUERY_ROWS, LANES))
            log_ref[0, head : head + 1, pl.ds(start, QUERY_ROWS)] = logs.T[0:1, :]
        context[pl.ds(start, QUERY_ROWS), lanes] = total.astype(LOW)
        return carry

    lax.fori_loop(0, rows // QUERY_ROWS, block, 0)
    context_move(pair).start()
    context_ref[:, lanes] = context[own, lanes]

    @pl.when(pair == last)
    def _():
        swap.wait()
        for number in range(last + 1):
            context_move(number).wait()
        for one in stored[1:]:
            one.start()
        inner = context_ref.shape[1]
        attended = dot(context_ref[...], own_output_ref[...].reshape(inner, width))
        attended = attended + dot(far_context_ref[...], far_output_ref[...].reshape(inner, width))
        hidden = source_ref[...].astype(WIDE) + attended
        hidden_ref[...] = hidden
        rms = inverse_root(jnp.mean(hidden * hidden, axis=1, keepdims=True) + EPSILON)
        normed[...] = (hidden * rms * gain_ref[...]).astype(LOW)
        for one in both_cores[1]:
            one.start()
        for one in direct:
            one.wait_send()
        for one in direct[4:]:
            one.wait_recv()
        for one in exchange:
            one.wait()
        slots_moves(cotangent_ref, came, slot_sems, depth, "end")
        for one in both_cores[0] + both_cores[1]:
            one.wait()
        for one in stored:
            one.wait()


def through(length, query, key, value, near, source, gain, output, up, down, cotangent):
    rows, inner = query.shape
    held, span, width = cotangent.shape
    depth = lax.axis_size("seq")
    pairs = inner // LANES
    vmem, anywhere = (pl.BlockSpec(memory_space=pltpu.VMEM), pl.BlockSpec(memory_space=pltpu.HBM))
    columns = pl.BlockSpec((rows, LANES), lambda pair: (0, pair))
    shape = jax.ShapeDtypeStruct
    outputs = (4,) + output.shape
    return pl.pallas_call(
        functools.partial(through_kernel, depth),
        grid=(pairs,),
        in_specs=[pl.BlockSpec(memory_space=pltpu.SMEM), columns, columns, columns]
        + [pl.BlockSpec((2, 1, 2 * QUERY_ROWS), lambda pair: (pair, 0, 0)), vmem, vmem]
        + [anywhere] * 4,
        out_specs=[pl.BlockSpec((1, 2, rows), lambda pair: (pair, 0, 0))] + [vmem] * 2 + [anywhere] * 7,
        out_shape=[shape((pairs, 2, rows), WIDE)]
        + [shape((rows // 2, inner), LOW), shape((rows // 2, width), WIDE), shape((rows // 2, inner), LOW)]
        + [shape(outputs, LOW)] * 2
        + [shape((rows, width), LOW)] * 2
        + [shape((4,) + up.shape, LOW)] * 2,
        scratch_shapes=[
            pltpu.VMEM((2, QUERY_ROWS, 2 * rows - QUERY_ROWS), WIDE),
            pltpu.VMEM((2, rows, LANES), LOW),
            pltpu.VMEM((2, rows, LANES), LOW),
            pltpu.VMEM((rows, inner), LOW),
            pltpu.VMEM((held, span, width), LOW),
            pltpu.VMEM((rows // 2, inner), LOW),
            pltpu.VMEM(outputs, LOW),
            pltpu.VMEM(outputs, LOW),
            pltpu.VMEM((rows // 2, width), LOW),
            pltpu.VMEM((rows // 2, width), LOW),
            pltpu.SemaphoreType.DMA((2, held)),
            pltpu.SemaphoreType.DMA((2, 6)),
            pltpu.SemaphoreType.DMA((2, 2)),
            pltpu.SemaphoreType.DMA((2, 2)),
            pltpu.SemaphoreType.DMA((2, 3)),
            pltpu.SemaphoreType.DMA((2, pairs)),
            pltpu.SemaphoreType.DMA((6,)),
        ],
        compiler_params=pltpu.CompilerParams(vmem_limit_bytes=62 << 20, collective_id=1, has_side_effects=True),
        cost_estimate=pl.CostEstimate(
            flops=24 * rows * rows * inner, bytes_accessed=8 * rows * inner, transcendentals=2 * pairs * rows * rows
        ),
        name="through",
    )(length, query, key, value, near, source, gain, output, up, down, cotangent)


def row_moves(source, target, sems, depth, piece, started=True):
    held = depth // 2
    place, index = (lax.axis_index("seq"), lax.axis_index("fsdp"))
    core = lax.rem(index, 2)
    there, which = (core * held + piece, index - core + place // held)
    slot = lax.rem(place, held)
    home = (there == place) & (which == index)

    @pl.when(home)
    def _():
        if started:
            pltpu.make_async_copy(source, target.at[slot], sems.at[1, piece, slot]).start()

    @pl.when(jnp.logical_not(home))
    def _():
        move = push(source, target.at[slot], sems, (piece, slot), there, which)
        if started:
            move.start()
        else:
            move.wait_send()


def rows_came(target, sems, depth):
    held = depth // 2
    place = lax.axis_index("seq")
    for slot in range(held):
        number = (lax.rem(place, held), slot)
        push(target.at[slot], target.at[slot], sems, number, place, partner(CORE)).wait_recv()


def middle_kernel(
    depth,
    length_ref,
    normed_in_ref,
    grad_in_ref,
    hidden_in_ref,
    gain_ref,
    output_in_ref,
    far_output_in_ref,
    context_in_ref,
    far_context_in_ref,
    up_ref,
    down_ref,
    ups_ref,
    downs_ref,
    up_part_ref,
    down_part_ref,
    up_came_ref,
    down_came_ref,
    far_up_ref,
    far_down_ref,
    context_grad_ref,
    hidden_grad_ref,
    layer_ref,
    gain_part_ref,
    output_part_ref,
    normed_ref,
    grad_ref,
    hidden_ref,
    output_ref,
    far_output_ref,
    context_ref,
    far_context_ref,
    near_grad,
    out_total,
    back_total,
    fold_sent,
    fold_came,
    up_slots,
    down_slots,
    up_stages,
    down_stages,
    parts,
    parts_came,
    far_grad,
    arrived,
    stored,
    far_sems,
    unit_sems,
    fold_sems,
    core_sems,
    kept,
    later_sems,
):
    rows, width = normed_ref.shape
    mine, wholes, fars = ((up_ref, down_ref), (ups_ref, downs_ref), (far_up_ref, far_down_ref))
    results, came = ((up_part_ref, down_part_ref), (up_came_ref, down_came_ref))
    slots, stages = ((up_slots, down_slots), (up_stages, down_stages))
    kinds = range(2)
    step = pl.program_id(0)
    last = depth - 1
    index = lax.axis_index("fsdp")
    core, x, y = (lax.rem(index, 2), lax.rem(index // 2, 2), index // 4)
    unit = up_slots.shape[1]
    half = unit // 2
    slot = lax.rem(step, 2)
    places = [chip_of(), chip_of(ALONG_X), chip_of(ALONG_Y), chip_of(ALONG_X, ALONG_Y)]

    place = lax.axis_index("seq")
    parity = lax.rem(place, 2)
    moves, exchange = ([], [])
    for turn, (bit, from_bit) in enumerate(((ALONG_X, ALONG_Y), (ALONG_Y, ALONG_X))):
        there = pl.ds(pl.multiple_of(turn * half + parity * (half // 2), half // 2), half // 2)
        moves.append(send(downs_ref.at[chip_of(from_bit), there], far_down_ref.at[there], far_sems, turn, bit))
        far = far_down_ref.at[there]
        exchange.append(push(far, far, far_sems, (4 + turn,), place + 1 - 2 * parity, index))
    for turn, (bit, from_bit) in enumerate(((ALONG_X, ALONG_Y), (ALONG_Y, ALONG_X))):
        there = pl.ds(turn * half, half)
        moves.append(send(ups_ref.at[chip_of(from_bit), there], far_up_ref.at[there], far_sems, 2 + turn, bit))
    sources = [
        mine,
        [one.at[places[1]] for one in wholes],
        [one.at[places[2]] for one in wholes],
        fars,
    ]

    def fetch(block, into):
        for number, pair in enumerate(sources):

            @pl.when(block == number)
            def _():
                for kind in kinds:
                    pltpu.make_async_copy(pair[kind], slots[kind].at[into], arrived.at[kind, into]).start()

    def store(number, kind):
        return pltpu.make_async_copy(
            stages[kind].at[number % 2], results[kind].at[places[number]], stored.at[kind, number % 2]
        )

    def first_sum(number, kind):
        block = places[number]
        if kind == 0:
            source, bit = (results[0].at[block, :, 1 - x], ALONG_X)
        else:
            source, bit = (results[1].at[block, 1 - y], ALONG_Y)
        return send(source, came[kind].at[block], unit_sems, last * kind + number, bit)

    def own_rows(which):
        return pl.ds(pl.multiple_of(which * (rows // 2), rows // 2), rows // 2)

    folds = [send(fold_sent.at[number], fold_came.at[number], fold_sems, number, CORE) for number in range(2)]

    later = [
        pltpu.make_async_copy(one, there, later_sems.at[number])
        for number, (one, there) in enumerate(
            (
                (hidden_in_ref, hidden_ref),
                (output_in_ref, output_ref),
                (far_output_in_ref, far_output_ref),
                (context_in_ref, context_ref),
                (far_context_in_ref, far_context_ref),
            )
        )
    ]

    @pl.when(step == 0)
    def _():
        greet_column(depth)
        for one in moves:
            one.start()
        fetch(0, 0)
        soon = [
            pltpu.make_async_copy(one, there, later_sems.at[5 + number])
            for number, (one, there) in enumerate(((normed_in_ref, normed_ref), (grad_in_ref, grad_ref)))
        ]
        for one in soon + later:
            one.start()
        out_total[...] = jnp.zeros_like(out_total)
        back_total[...] = jnp.zeros_like(back_total)
        for one in soon:
            one.wait()

    @pl.when(step + 1 < last)
    def _():
        fetch(step + 1, 1 - slot)

    @pl.when(step == 1)
    def _():
        for one in moves[:2]:
            one.wait()
        for one in exchange:
            one.start()

    for number in range(last):

        @pl.when(step == number + 1)
        def _():
            for kind in kinds:
                store(number, kind).wait()
                first_sum(number, kind).start()

    for kind in kinds:
        pltpu.make_async_copy(slots[kind].at[slot], slots[kind].at[slot], arrived.at[kind, slot]).wait()
    up, down = (slots[0][slot], slots[1][slot])
    normed, grad = (normed_ref[...], grad_ref[...])
    active, slope = gelu_parts(dot(normed, up, NT))
    active = active.astype(LOW)
    pre_grad = (dot(grad, down, NT) * slope).astype(LOW)
    back_total[...] += dot(pre_grad, up)
    out_total[...] += dot(active, down)

    @pl.when(step == last)
    def _():
        for number, total in enumerate((back_total, out_total)):
            fold_sent[number] = total[own_rows(1 - core), :].astype(LOW)
            folds[number].start()

    shape = up_stages.shape[1:]
    stages[0][slot] = dot(pre_grad, normed, TN).astype(LOW).reshape(shape)
    stages[1][slot] = dot(active, grad, TN).astype(LOW).reshape(shape)
    for number in range(last + 1):

        @pl.when(step == number)
        def _():
            for kind in kinds:
                store(number, kind).start()

    @pl.when(step == last - 1)
    def _():
        for one in moves[2:] + exchange:
            one.wait()
        fetch(last, last % 2)

    @pl.when(step == last)
    def _():
        for one in later:
            one.wait()
        folds[0].wait()
        normed_grad = back_total[own_rows(core), :] + fold_came[0].astype(WIDE)
        hidden = hidden_ref[...]
        rms = inverse_root(jnp.mean(hidden * hidden, axis=1, keepdims=True) + EPSILON)
        scaled = hidden * rms
        gained = gain_ref[...] * normed_grad
        inside = jnp.mean(gained * scaled, axis=1, keepdims=True)
        hidden_grad = grad_ref[own_rows(core), :].astype(WIDE) + rms * (gained - scaled * inside)
        gain_part_ref[...] = jnp.sum(normed_grad * scaled, axis=0, keepdims=True)
        hidden_grad_ref[...] = hidden_grad
        hidden_low = hidden_grad.astype(LOW)
        far_grad[...] = dot(hidden_low, far_output_ref[...], NT).astype(LOW)
        move = send(far_grad, context_grad_ref.at[own_rows(core)], core_sems, 0, CORE)
        move.start()
        part_shape = parts.shape[1:]
        parts[0] = dot(context_ref[...], hidden_low, TN).astype(LOW).reshape(part_shape)
        parts[1] = dot(far_context_ref[...], hidden_low, TN).astype(LOW).reshape(part_shape)
        others = [
            send(parts.at[kind, :, :, 1 - core], parts_came.at[kind], core_sems, 1 + kind, CORE) for kind in kinds
        ]
        for one in others:
            one.start()
        near_grad[...] = dot(hidden_low, output_ref[...], NT).astype(LOW)
        keep = pltpu.make_async_copy(near_grad, context_grad_ref.at[own_rows(core)], kept)
        keep.start()
        folds[1].wait()
        slot_ids = core * (rows // 2) + lax.broadcasted_iota(jnp.int32, (rows // 2, 1), 0)
        valid = (slot_ids < length_ref[0]).astype(WIDE)
        layer_rows = (hidden + (out_total[own_rows(core), :] + fold_came[1].astype(WIDE))) * valid
        layer_ref[...] = layer_rows.astype(LOW).reshape(layer_ref.shape)
        for one in others:
            one.wait()
        for turn in range(depth):
            near = parts[0, turn, :, core].astype(WIDE) + parts_came[1, turn].astype(WIDE)
            output_part_ref[turn, core] = near.astype(LOW)
            far = parts[1, turn, :, core].astype(WIDE) + parts_came[0, turn].astype(WIDE)
            output_part_ref[turn, 1 - core] = far.astype(LOW)
        for kind in kinds:
            store(last, kind).wait()
        move.wait()
        keep.wait()
        for number in range(last):
            for kind in kinds:
                first_sum(number, kind).wait()


def middle(length, normed, grad, hidden, gain, outputs, contexts, mine, wholes):
    rows, width = normed.shape
    inner = outputs[0].shape[0]
    unit = mine[0].shape[0]
    depth = lax.axis_size("seq")
    held = depth // 2
    thick, slim = (unit // 4, inner // 16)
    vmem, anywhere = (pl.BlockSpec(memory_space=pltpu.VMEM), pl.BlockSpec(memory_space=pltpu.HBM))
    shape = jax.ShapeDtypeStruct
    part = (depth, 2, 2, thick, width)
    return pl.pallas_call(
        functools.partial(middle_kernel, depth),
        grid=(depth,),
        in_specs=[pl.BlockSpec(memory_space=pltpu.SMEM)] + [anywhere] * 3 + [vmem] + [anywhere] * 8,
        out_specs=[anywhere] * 7 + [vmem] * 4,
        out_shape=[shape(part, LOW)] * 2
        + [shape((depth, 2, thick, width), LOW)] * 2
        + [shape((unit, width), LOW)] * 2
        + [
            shape((rows, inner), LOW),
            shape((rows // 2, width), WIDE),
            shape((held, rows // depth, width), LOW),
            shape((1, width), WIDE),
            shape((4, 2, 2, slim, width), LOW),
        ],
        scratch_shapes=[pltpu.VMEM(one.shape, one.dtype) for one in (normed, grad, hidden, *outputs, *contexts)]
        + [pltpu.VMEM((rows // 2, inner), LOW)]
        + [pltpu.VMEM((rows, width), WIDE)] * 2
        + [pltpu.VMEM((2, rows // 2, width), LOW)] * 2
        + [pltpu.VMEM((2, unit, width), LOW)] * 2
        + [pltpu.VMEM((2, 2, 2, thick, width), LOW)] * 2
        + [
            pltpu.VMEM((2, 4, 2, 2, slim, width), LOW),
            pltpu.VMEM((2, 4, 2, slim, width), LOW),
            pltpu.VMEM((rows // 2, inner), LOW),
            pltpu.SemaphoreType.DMA((2, 2)),
            pltpu.SemaphoreType.DMA((2, 2)),
            pltpu.SemaphoreType.DMA((2, 6)),
            pltpu.SemaphoreType.DMA((2, 2 * (depth - 1))),
            pltpu.SemaphoreType.DMA((2, 2)),
            pltpu.SemaphoreType.DMA((2, 3)),
            pltpu.SemaphoreType.DMA,
            pltpu.SemaphoreType.DMA((7,)),
        ],
        compiler_params=pltpu.CompilerParams(vmem_limit_bytes=62 << 20, collective_id=2, has_side_effects=True),
        cost_estimate=pl.CostEstimate(
            flops=52 * unit * rows * width,
            bytes_accessed=32 * unit * width + 12 * rows * width,
            transcendentals=8 * unit * rows,
        ),
        name="middle",
    )(length, normed, grad, hidden, gain, *outputs, *contexts, *mine, *wholes)


def add_rows(target, source):
    target[...] = (target[...].astype(WIDE) + source[...].astype(WIDE)).astype(LOW)


def backward_kernel(
    depth,
    length_ref,
    query_in_ref,
    key_in_ref,
    value_in_ref,
    grad_in_ref,
    log_ref,
    near_ref,
    normed_in_ref,
    weight_in_ref,
    source_in_ref,
    hidden_in_ref,
    gain_ref,
    small_ref,
    output_ref,
    layer_ref,
    up_ref,
    down_ref,
    up_came_ref,
    down_came_ref,
    layer_out_ref,
    row_came,
    heads_out_ref,
    units_out_ref,
    gains_out_ref,
    sums_out_ref,
    query_ref,
    key_ref,
    value_ref,
    grad_ref,
    normed_ref,
    weight_ref,
    source_ref,
    hidden_ref,
    bias,
    spare,
    keys,
    values,
    padded,
    key_total,
    value_total,
    tiles,
    lows,
    part,
    x_block,
    y_block,
    x_came,
    y_came,
    x_last,
    y_last,
    heads_came,
    units,
    units_came,
    units_last,
    units_far,
    fold_sent,
    fold_came,
    row_sent,
    small,
    small_came,
    swap_sems,
    first_sems,
    second_sems,
    third_sems,
    late_sems,
    unit_second_sems,
    unit_third_sems,
    fold_sems,
    row_sems,
    layer_sems,
    small_sems,
    early_sems,
    local_sems,
    later_sems,
):
    rows = query_ref.shape[0]
    width = normed_ref.shape[1]
    held = depth // 2
    step = pl.program_id(0)
    last = depth - 1
    place, index = (lax.axis_index("seq"), lax.axis_index("fsdp"))
    core, x, y = (lax.rem(index, 2), lax.rem(index // 2, 2), index // 4)
    column = index - core

    def owner(block):
        return lax.rem(place + 1 + block, depth)

    def beside(source, target, sems, number, bit):
        return push(source, target, sems, number, place, partner(bit))


    def unit_place(hop):
        return chip_of(*(bit for bit in (ALONG_X, ALONG_Y) if hop & (bit // 2)))

    def unit_source(kind, hop):
        block = unit_place(hop)
        if kind == 0:
            return (up_ref.at[block, :, 1 - x], up_ref.at[block, :, x], ALONG_X)
        return (down_ref.at[block, 1 - y], down_ref.at[block, y], ALONG_Y)

    def unit_came(kind, hop):
        return units_came.at[kind, hop]

    def unit_own(kind, hop):
        return pltpu.make_async_copy(unit_source(kind, hop)[1], units.at[kind, hop], local_sems.at[kind, hop])

    def unit_early(kind, hop):
        there = (up_came_ref, down_came_ref)[kind].at[unit_place(hop)]
        return pltpu.make_async_copy(there, units_came.at[kind, hop], early_sems.at[kind, hop])

    def unit_late(kind, hop):
        away, _, bit = unit_source(kind, hop)
        return beside(away, units_came.at[kind, late[kind]], late_sems, (kind,), bit)

    late = (2, 1)

    def units_start():
        for kind in range(2):
            unit_late(kind, 3).start()
        for kind in range(2):
            for hop in range(4):
                unit_own(kind, hop).start()
                if hop != late[kind]:
                    unit_early(kind, hop).start()

    def unit_halves(kind, hop):
        if kind == 0:
            return (units.at[0, hop, 1 - y], units.at[0, hop, y], ALONG_Y)
        return (units.at[1, hop, 1 - x], units.at[1, hop, x], ALONG_X)

    def unit_second(kind, hop):
        away, _, bit = unit_halves(kind, hop)
        there = hop ^ (bit // 2)
        return push(
            away, units_last.at[kind, there], unit_second_sems, (kind, hop), place, partner(bit), (kind, there)
        )

    def unit_first(kind, hop):
        unit_own(kind, hop).wait()
        if hop == late[kind]:
            unit_late(kind, 3).wait()
        else:
            unit_early(kind, hop).wait()
        add_rows(units.at[kind, hop], units_came.at[kind, hop])
        unit_second(kind, hop).start()


    def unit_arrived(kind, block, slot):
        far = units_far.at[kind, block, slot]
        return push(far, far, unit_third_sems, (kind, block, slot), place, partner(CORE))

    def unit_direct(kind, hop):
        block = unit_place(hop)
        slot = lax.rem(block + 2 * depth - place - 1, depth)
        own = unit_halves(kind, hop)[1]
        return push(
            own, units_far.at[kind, block, slot], unit_third_sems, (kind, block, 0), block, index, (kind, block, slot)
        )

    def unit_summed(kind, hop):
        unit_second(kind, hop).wait_send()
        unit_second(kind, hop ^ (2 - kind)).wait_recv()
        add_rows(unit_halves(kind, hop)[1], units_last.at[kind, hop])

        @pl.when(unit_place(hop) != place)
        def _():
            unit_direct(kind, hop).start()

    def unit_finish(kind, hop):
        block = unit_place(hop)

        @pl.when(block != place)
        def _():
            unit_direct(kind, hop).wait_send()

        @pl.when(block == place)
        def _():
            total = unit_halves(kind, hop)[1][...].astype(WIDE)
            for slot in range(depth - 1):
                unit_arrived(kind, block, slot).wait_recv()
                total = total + units_far[kind, block, slot].astype(WIDE)
            units_out_ref[kind] = total


    def swaps(block):
        moves = [
            beside(part.at[kind, :, 1 - core], x_block.at[block, :, core, kind], swap_sems, (kind, block), CORE)
            for kind in range(2)
        ]
        moves.append(beside(part.at[2, :, 1 - core], y_block.at[block, core, :, 0], swap_sems, (2, block), CORE))
        return moves

    def output_copy(block):
        return pltpu.make_async_copy(output_ref.at[owner(block)], y_block.at[block, :, :, 1], local_sems.at[2, block])

    def firsts(block):
        return (
            beside(x_block.at[block, 1 - x], x_came.at[block], first_sems, (0, block), ALONG_X),
            beside(y_block.at[block, 1 - y], y_came.at[block], first_sems, (1, block), ALONG_Y),
        )

    def seconds(block):
        return (
            beside(x_block.at[block, x, 1 - y], x_last.at[block], second_sems, (0, block), ALONG_Y),
            beside(y_block.at[block, y, 1 - x], y_last.at[block], second_sems, (1, block), ALONG_X),
        )

    def thirds(block):
        return [
            push(own, heads_came.at[block, kind], third_sems, (kind, block), owner(block), index)
            for kind, own in enumerate((x_block.at[block, x, y], y_block.at[block, y, x]))
        ]

    def heads_start(block):
        for one in swaps(block):
            one.wait_recv()
        output_copy(block).wait()
        for one in firsts(block):
            one.start()

    def heads_first(block):
        for one in firsts(block):
            one.wait()
        add_rows(x_block.at[block, x], x_came.at[block])
        add_rows(y_block.at[block, y], y_came.at[block])
        for one in seconds(block):
            one.start()

    def heads_second(block, mine=False):
        for one in seconds(block):
            one.wait()
        add_rows(x_block.at[block, x, y], x_last.at[block])
        add_rows(y_block.at[block, y, x], y_last.at[block])
        if not mine:
            for one in thirds(block):
                one.start()

    later = [
        pltpu.make_async_copy(one, there, later_sems.at[number])
        for number, (one, there) in enumerate(
            (
                (normed_in_ref, normed_ref),
                (weight_in_ref, weight_ref),
                (source_in_ref, source_ref),
                (hidden_in_ref, hidden_ref),
            )
        )
    ]

    soon = [
        pltpu.make_async_copy(one, there, later_sems.at[4 + number])
        for number, (one, there) in enumerate(
            (
                (query_in_ref, query_ref),
                (key_in_ref, key_ref),
                (value_in_ref, value_ref),
                (grad_in_ref, grad_ref),
            )
        )
    ]

    @pl.when(step == 0)
    def _():
        greet_column(depth)
        for one in soon:
            one.start()
        units_start()
        for one in later:
            one.start()
        for block in range(depth):
            output_copy(block).start()
        for piece in range(held):
            row_moves(layer_ref.at[piece], layer_out_ref, layer_sems, depth, piece)
        spare[...] = spare_lanes(length_ref[0], rows)
        for one in soon:
            one.wait()
        for head in range(2):
            padded[head, :HALF_ROWS, :] = jnp.zeros((HALF_ROWS, QUERY_ROWS), LOW)
            padded[head, rows + HALF_ROWS :, :] = jnp.zeros((HALF_ROWS, QUERY_ROWS), LOW)

    both_ready = [(0, 1), (0, 3), (1, 2), (1, 3)]
    others = [(0, 0), (0, 2), (1, 0), (1, 1)]

    def advance(number):
        def at(turn, tick, act):
            @pl.when((step == turn) & (number == tick))
            def _():
                act()

        ready = both_ready + [(0, 0), (1, 0)]
        at(0, 1, lambda: [unit_first(*one) for one in ready])
        at(1, 0, lambda: [unit_first(kind, late[kind]) for kind in range(2)])
        at(1, 3, lambda: [unit_summed(*one) for one in both_ready])
        at(2, 3, lambda: [unit_summed(*one) for one in others])
        at(3, 1, lambda: heads_first(0))

        @pl.when((step >= 1) & (number == 1))
        def _():
            heads_start(step - 1)

    pair = owner(step)
    lanes = pl.ds(pl.multiple_of(pair * LANES, LANES), LANES)
    split_heads(key_ref[:, lanes], spare[...], keys)
    split_heads(value_ref[:, lanes], jnp.zeros((rows, LANES), LOW), values)

    def low_lanes(kind):
        return pl.ds(pl.multiple_of((3 * pair + kind) * LANES, LANES), LANES)

    near_start = rows - QUERY_ROWS - HALF_ROWS
    near_end = near_start + 2 * QUERY_ROWS
    for head in range(2):
        line = near_ref[2 * pair + head]
        bias[head, :near_start, :] = jnp.broadcast_to(line[:, :1], (near_start, QUERY_ROWS))
        bias[head, near_start:near_end, :] = near_block(line).T
        bias[head, near_end:, :] = jnp.broadcast_to(line[:, -1:], (bias.shape[1] - near_end, QUERY_ROWS))
    key_total[...] = jnp.zeros_like(key_total)
    value_total[...] = jnp.zeros_like(value_total)
    tiles[...] = jnp.zeros_like(tiles)
    sums = small.at[0, pl.ds(pl.multiple_of(16 + 8 * pair, 8), 8)]
    sums[...] = jnp.zeros((8, LANES), WIDE)
    spot = lax.broadcasted_iota(jnp.int32, (1, LANES), 1)
    lane = lax.broadcasted_iota(jnp.int32, (QUERY_ROWS, LANES), 1)
    ones = jnp.where(lax.rem(lane, HEAD_DIM) == 0, 1.0, 0.0).astype(LOW)
    zero = jnp.zeros((), LOW)
    blocks = rows // QUERY_ROWS

    def block(number, carry):
        start = pl.multiple_of(number * QUERY_ROWS, QUERY_ROWS)
        offset = pl.multiple_of(rows - QUERY_ROWS - number * QUERY_ROWS, LANES)
        advance(number)
        both = query_ref[pl.ds(start, QUERY_ROWS), lanes]
        grad = grad_ref[pl.ds(start, QUERY_ROWS), lanes]
        parts = []
        for head in range(2):
            mine = lane < HEAD_DIM if head == 0 else lane >= HEAD_DIM
            logits = dot(keys[head], jnp.where(mine, both, ones), NT)
            logits = logits + bias[head, pl.ds(offset, rows), :]
            probs = jnp.exp(logits - log_ref[pair, head : head + 1, pl.ds(start, QUERY_ROWS)])
            prob_grad = dot(values[head], grad, NT)
            weighted = probs * prob_grad
            total = jnp.sum(weighted, axis=0, keepdims=True)
            score = (weighted - probs * total).astype(LOW)
            value_total[...] += dot(probs.astype(LOW), jnp.where(mine, grad, zero))
            key_total[...] += dot(score, jnp.where(mine, both, zero))
            padded[head, HALF_ROWS : HALF_ROWS + rows, :] = score
            one = dot(score, keys[head], TN)
            parts.append(one)
            columns = jnp.sum(one, axis=0, keepdims=True)
            first = HEAD_DIM * (1 - head) + 1 + number
            close = padded[head, pl.ds(start, 2 * QUERY_ROWS), :].astype(WIDE)
            quarter = [close[HALF_ROWS * turn : HALF_ROWS * (turn + 1)] for turn in range(4)]
            for turn in range(3):
                tiles[head, turn] += quarter[turn][:, :HALF_ROWS] + quarter[turn + 1][:, HALF_ROWS:]
            left = jnp.sum(quarter[0][:, HALF_ROWS:], axis=0, keepdims=True)
            right = jnp.sum(quarter[3][:, :HALF_ROWS], axis=0, keepdims=True)
            left = left + jnp.where(spot == first, columns, 0.0)
            right = right + jnp.where(spot == first + blocks, columns, 0.0)
            sums[4 * head + 2 : 4 * head + 3, :] += left
            sums[4 * head + 3 : 4 * head + 4, :] += right
        chosen = jnp.where(lane < HEAD_DIM, parts[0], parts[1])
        lows[pl.ds(start, QUERY_ROWS), low_lanes(0)] = chosen.astype(LOW)
        return carry

    lax.fori_loop(0, blocks, block, 0)
    lows[:, low_lanes(1)] = key_total[...].astype(LOW)
    lows[:, low_lanes(2)] = value_total[...].astype(LOW)
    shape = (HALF_ROWS, HALF_ROWS)
    upper = lax.broadcasted_iota(jnp.int32, shape, 0) <= lax.broadcasted_iota(jnp.int32, shape, 1)
    for head in range(2):
        before, centre, behind = (tiles[head, turn] for turn in range(3))
        sums[4 * head : 4 * head + 1, :] = diagonal_sums(jnp.where(upper, centre, before))
        sums[4 * head + 1 : 4 * head + 2, :] = diagonal_sums(jnp.where(upper, behind, centre))
        sums[4 * head + 2 : 4 * head + 3, :] += jnp.sum(jnp.where(upper, before, 0.0), axis=0, keepdims=True)
        sums[4 * head + 3 : 4 * head + 4, :] += jnp.sum(jnp.where(upper, 0.0, behind), axis=0, keepdims=True)

    @pl.when(step >= 1)
    def _():
        for one in swaps(step - 1):
            one.wait_send()

    @pl.when(step == 0)
    def _():
        later[0].wait()

    for kind in range(3):
        product = dot(lows[:, low_lanes(kind)], normed_ref[...], TN).astype(LOW)
        part[kind] = product.reshape(part.shape[1:])
    for one in swaps(step):
        one.start()
    for half in range(2):
        for kind in range(2):
            x_block[step, half, core, kind] = part[kind, half, core]
        y_block[step, core, half, 0] = part[2, half, core]

    @pl.when(step == last)
    def _():
        span = rows // 2 // held
        for one in later[1:]:
            one.wait()
        for piece in range(held):
            away = pl.ds(pl.multiple_of((1 - core) * (rows // 2) + piece * span, span), span)
            fold_sent[piece] = dot(lows[away, :], weight_ref[...]).astype(LOW)
            beside(fold_sent.at[piece], fold_came.at[piece], fold_sems, (piece,), CORE).start()
        heads_second(0)
        heads_first(1)
        for one in swaps(last):
            one.wait_send()
        heads_start(last)

        gain_total = jnp.zeros((1, width), WIDE)
        for piece in range(held):
            here = pl.ds(pl.multiple_of(core * (rows // 2) + piece * span, span), span)
            product = dot(lows[here, :], weight_ref[...])
            beside(fold_sent.at[piece], fold_came.at[piece], fold_sems, (piece,), CORE).wait()
            product = product + fold_came[piece].astype(WIDE)
            local = slice(piece * span, (piece + 1) * span)
            source = source_ref[local, :].astype(WIDE)
            rms = inverse_root(jnp.mean(source * source, axis=1, keepdims=True) + EPSILON)
            scaled = source * rms
            gain_total = gain_total + jnp.sum(product * scaled, axis=0, keepdims=True)
            gained = gain_ref[...] * product
            inside = jnp.mean(gained * scaled, axis=1, keepdims=True)
            row_sent[piece] = (hidden_ref[local, :] + rms * (gained - scaled * inside)).astype(LOW)
            if piece == held - 1:
                for number in range(width // LANES):
                    small[0, number : number + 1, :] = gain_total[:, number * LANES : (number + 1) * LANES]
                small[0, 8:16, :] = small_ref[...]
                moves = [
                    push(small.at[0], small_came.at[turn], small_sems, (turn,), lax.rem(place + turn, depth), index)
                    for turn in range(1, depth)
                ]
                for one in moves:
                    one.start()
            row_moves(row_sent.at[piece], row_came, row_sems, depth, piece)
            if piece == 0:
                heads_first(last - 1)
                heads_second(1)
        heads_second(last - 1)
        heads_first(last)
        heads_second(last, True)

        for one in moves:
            one.wait()
        small[1] = small[0] + sum(small_came[turn] for turn in range(1, depth))
        for turn, bit in ((1, ALONG_X), (2, ALONG_Y)):
            move = beside(small.at[turn], small_came.at[depth + turn - 1], small_sems, (depth + turn - 1,), bit)
            move.start()
            move.wait()
            small[turn + 1] = small[turn] + small_came[depth + turn - 1]
        move = beside(small.at[3], small_came.at[0], small_sems, (0,), CORE)
        move.start()
        move.wait()
        lines = width // LANES
        for number in range(2):
            line = pl.ds(number * lines + index, 1)
            gains_out_ref[number : number + 1, :] = small[3, line, :] + small_came[0, line, :]
        sums_out_ref[core] = small[3, 2 * lines :, :]
        sums_out_ref[1 - core] = small_came[0, 2 * lines :, :]

        for block in range(last):
            for one in thirds(block):
                one.wait()
        for kind in range(2):
            for hop in range(4):
                unit_finish(kind, hop)
        heads_out_ref[0:2] = x_block[last, x, y].astype(WIDE) + sum(
            heads_came[one, 0].astype(WIDE) for one in range(depth - 1)
        )
        heads_out_ref[2:4] = y_block[last, y, x].astype(WIDE) + sum(
            heads_came[one, 1].astype(WIDE) for one in range(depth - 1)
        )
        for piece in range(held):
            row_moves(layer_ref.at[piece], layer_out_ref, layer_sems, depth, piece, False)
            row_moves(row_sent.at[piece], row_came, row_sems, depth, piece, False)
        rows_came(layer_out_ref, layer_sems, depth)
        rows_came(row_came, row_sems, depth)


def backward(
    length, query, key, value, grad, logs, near, normed, weights, source, hidden, gain, ffn_gain_part, output_part, layer, *units
):
    rows, inner = query.shape
    width = normed.shape[1]
    depth = lax.axis_size("seq")
    held = depth // 2
    span = rows // depth
    slim, thick = (output_part.shape[3], units[0].shape[3])
    vmem, anywhere = (pl.BlockSpec(memory_space=pltpu.VMEM), pl.BlockSpec(memory_space=pltpu.HBM))
    shape = jax.ShapeDtypeStruct
    small_rows = 2 * (width // LANES) + 8 * depth
    sems = [(3, depth), (2, depth), (2, depth), (2, depth), (2,), (2, depth), (2, depth, depth - 1)]
    sems += [(held,), (held, held), (held, held), (depth + 2,)]
    return pl.pallas_call(
        functools.partial(backward_kernel, depth),
        grid=(depth,),
        in_specs=[pl.BlockSpec(memory_space=pltpu.SMEM)] + [anywhere] * 4 + [vmem] * 2 + [anywhere] * 4 + [vmem] * 2 + [anywhere, vmem] + [anywhere] * 4,
        out_specs=[anywhere] * 2 + [vmem] * 4,
        out_shape=[
            shape((held, span, width), LOW),
            shape((held, span, width), LOW),
            shape((4, slim, width), WIDE),
            shape((2, thick, width), WIDE),
            shape((2, LANES), WIDE),
            shape((2, 8 * depth, LANES), WIDE),
        ],
        scratch_shapes=[
            pltpu.VMEM(query.shape, LOW),
            pltpu.VMEM(key.shape, LOW),
            pltpu.VMEM(value.shape, LOW),
            pltpu.VMEM(grad.shape, LOW),
            pltpu.VMEM(normed.shape, LOW),
            pltpu.VMEM(weights.shape, LOW),
            pltpu.VMEM(source.shape, LOW),
            pltpu.VMEM(hidden.shape, WIDE),
            pltpu.VMEM((2, 2 * rows - QUERY_ROWS, QUERY_ROWS), WIDE),
            pltpu.VMEM((rows, LANES), LOW),
            pltpu.VMEM((2, rows, LANES), LOW),
            pltpu.VMEM((2, rows, LANES), LOW),
            pltpu.VMEM((2, rows + QUERY_ROWS, QUERY_ROWS), LOW),
            pltpu.VMEM((rows, LANES), WIDE),
            pltpu.VMEM((rows, LANES), WIDE),
            pltpu.VMEM((2, 3, HALF_ROWS, HALF_ROWS), WIDE),
            pltpu.VMEM((rows, 3 * inner), LOW),
            pltpu.VMEM((3, 2, 2, slim, width), LOW),
        ]
        + [pltpu.VMEM((depth, 2, 2, 2, slim, width), LOW)] * 2
        + [pltpu.VMEM((depth, 2, 2, slim, width), LOW)] * 2
        + [pltpu.VMEM((depth, 2, slim, width), LOW)] * 2
        + [
            pltpu.VMEM((depth - 1, 2, 2, slim, width), LOW),
            pltpu.VMEM((2, depth, 2, thick, width), LOW),
            pltpu.VMEM((2, depth, 2, thick, width), LOW),
            pltpu.VMEM((2, depth, thick, width), LOW),
            pltpu.VMEM((2, depth, depth - 1, thick, width), LOW),
        ]
        + [pltpu.VMEM((held, span, width), LOW)] * 3
        + [pltpu.VMEM((4, small_rows, LANES), WIDE), pltpu.VMEM((depth + 2, small_rows, LANES), WIDE)]
        + [pltpu.SemaphoreType.DMA((2,) + one) for one in sems]
        + [pltpu.SemaphoreType.DMA((2, depth)), pltpu.SemaphoreType.DMA((3, depth)), pltpu.SemaphoreType.DMA((8,))],
        compiler_params=pltpu.CompilerParams(
            vmem_limit_bytes=62 << 20, collective_id=3, has_side_effects=True
        ),
        cost_estimate=pl.CostEstimate(
            flops=60 * rows * rows * inner, bytes_accessed=14 * rows * inner, transcendentals=rows * rows * inner // 64
        ),
        name="backward",
    )(length, query, key, value, grad, logs, near, normed, weights, source, hidden, gain, ffn_gain_part, output_part, layer, *units)


def flip(value, bit):
    size = lax.axis_size("fsdp")
    return lax.ppermute(value, "fsdp", [(one, one ^ bit) for one in range(size)])


def other_core(value):
    return flip(value, 1)


def rounds_of(inverse):
    depth, size = (lax.axis_size("seq"), lax.axis_size("fsdp"))
    held = depth // 2
    rounds = []
    for step in range(held):
        pairs = []
        for place in range(depth):
            for index in range(size):
                target = (index % 2) * held + (place + step) % held
                there = target * size + index - index % 2 + place // held
                here = place * size + index
                pairs.append((there, here) if inverse else (here, there))
        rounds.append(pairs)
    return rounds


def to_sequence(blocks):
    held, span, width = blocks.shape
    place = lax.axis_index("seq")
    out = jnp.zeros((held, span, width), blocks.dtype)
    for step, pairs in enumerate(rounds_of(False)):
        sent = lax.dynamic_index_in_dim(blocks, (place + step) % held, 0, keepdims=False)
        got = lax.ppermute(sent, BOTH, pairs)
        out = lax.dynamic_update_index_in_dim(out, got, (place + held - step) % held, 0)
    return out.reshape(held * span, width)


def to_slots(rows, held):
    span, width = (rows.shape[0] // held, rows.shape[1])
    place = lax.axis_index("seq")
    blocks = rows.reshape(held, span, width)
    out = jnp.zeros(blocks.shape, rows.dtype)
    for step, pairs in enumerate(rounds_of(True)):
        sent = lax.dynamic_index_in_dim(blocks, (place + held - step) % held, 0, keepdims=False)
        got = lax.ppermute(sent, BOTH, pairs)
        out = lax.dynamic_update_index_in_dim(out, got, (place + step) % held, 0)
    return out


def whole(mine, core):
    other = other_core(mine)
    return jnp.where(
        core == 0, jnp.concatenate([mine, other], axis=0), jnp.concatenate([other, mine], axis=0)
    )


def fold(partial, core):
    half = partial.shape[0] // 2
    sent = lax.dynamic_slice_in_dim(partial, (1 - core) * half, half, 0)
    kept = lax.dynamic_slice_in_dim(partial, core * half, half, 0)
    return kept + other_core(sent)


def fast_plane():
    return lax.axis_size("fsdp") == 8 and lax.axis_size("seq") == 4


def own_head_rows(weight, core):
    width = weight.shape[1]
    return lax.dynamic_index_in_dim(weight.reshape(4, 2, -1, width), core, 1, keepdims=False).reshape(-1, width)


def add_low(left, right):
    return (left.astype(WIDE) + right.astype(WIDE)).astype(LOW)


def pick(value, index, axis):
    return lax.dynamic_index_in_dim(value, index, axis, keepdims=False)


def shards(
    inputs,
    lengths,
    cotangent,
    query_weight,
    key_weight,
    value_weight,
    output_weight,
    up_weight,
    down_weight,
    attn_gain,
    ffn_gain,
    bias_table,
):
    held, span, width = inputs.shape
    depth, size = (lax.axis_size("seq"), lax.axis_size("fsdp"))
    place, index = (lax.axis_index("seq"), lax.axis_index("fsdp"))
    core = index % 2
    rows = held * span
    inner = HEADS * HEAD_DIM
    fast = fast_plane()

    near_lengths = jnp.where(
        core == 0,
        jnp.concatenate([lengths, other_core(lengths)]),
        jnp.concatenate([other_core(lengths), lengths]),
    )
    length = lax.dynamic_slice_in_dim(near_lengths, place, 1, 0)

    own_table = lax.dynamic_index_in_dim(bias_table.reshape(BUCKETS, 4, 2, 2), core, 2, keepdims=False)
    own_table = own_table.reshape(BUCKETS, HEADS // 2)
    near = near_bias(own_table)

    if fast:
        normed_one, query, key, value, source_low, weights, up_mine, down_mine = enter(
            inputs, (query_weight, key_weight, value_weight), up_weight, down_weight, attn_gain[None, :]
        )
        source_low = source_low.reshape(rows, width)
        mine = (up_mine.reshape(-1, width), down_mine.reshape(-1, width))
        logs, near_context, hidden_one, far_context, own_output, far_output, normed_two, grad_low, *wholes = through(
            length,
            query,
            key,
            value,
            near,
            source_low,
            ffn_gain[None, :],
            output_weight,
            *mine,
            cotangent,
        )
        own_output, far_output = (own_output.reshape(-1, width), far_output.reshape(-1, width))
    else:
        own_three = [
            own_head_rows(lax.all_gather(one, "fsdp", axis=0, tiled=True), core)
            for one in (query_weight, key_weight, value_weight)
        ]
        full = lax.all_gather(output_weight, "fsdp", axis=0, tiled=True)
        own_output = own_head_rows(full, core)
        far_output = own_head_rows(full, 1 - core)
        own_up, own_down = (
            pick(
                lax.all_gather(one, "fsdp", axis=0, tiled=True).reshape(depth, size // 2, 2, -1, width), core, 2
            ).reshape(-1, width)
            for one in (up_weight, down_weight)
        )
        mask_rows = (core * rows + jnp.arange(rows, dtype=jnp.int32) < length[0])[:, None].astype(WIDE)
        source_low = to_sequence(inputs)
        source = source_low.astype(WIDE)
        rms_one = lax.rsqrt(jnp.mean(source * source, axis=1, keepdims=True) + EPSILON)
        scaled_one = source * rms_one
        normed_one = whole((scaled_one * attn_gain).astype(LOW), core)
        query, key, value = [dot(normed_one, one, NT).astype(LOW) for one in own_three]
        context, logs = attend(length, query, key, value, near)
        mine = (own_up, own_down)
        near_context = lax.dynamic_slice_in_dim(context, core * rows, rows, 0)
        far_context = other_core(lax.dynamic_slice_in_dim(context, (1 - core) * rows, rows, 0))
        hidden_one = source + (dot(near_context, own_output) + dot(far_context, far_output))
        rms_two = lax.rsqrt(jnp.mean(hidden_one * hidden_one, axis=1, keepdims=True) + EPSILON)
        scaled_two = hidden_one * rms_two
        normed_two = whole((scaled_two * ffn_gain).astype(LOW), core)
        grad_out = to_sequence(cotangent).astype(WIDE) * mask_rows
        grad_low = whole(grad_out.astype(LOW), core)

    if fast:
        up_part, down_part, up_came, down_came, _, _, context_grad, hidden_grad, layer_rows, ffn_gain_part, output_part = middle(
            length,
            normed_two,
            grad_low,
            hidden_one,
            ffn_gain[None, :],
            (own_output, far_output),
            (near_context, far_context),
            mine,
            wholes,
        )
    else:
        up_part, down_part, mlp_part, normed_part = feed(normed_two, grad_low, *mine)
        normed_grad = fold(normed_part, core)
        layer_rows = ((hidden_one + fold(mlp_part, core)) * mask_rows).astype(LOW)
        gained_two = ffn_gain * normed_grad
        hidden_grad = grad_out + rms_two * (
            gained_two - scaled_two * jnp.mean(gained_two * scaled_two, axis=1, keepdims=True)
        )
        ffn_gain_part = jnp.sum(normed_grad * scaled_two, axis=0)
        hidden_low = hidden_grad.astype(LOW)
        near_grad = dot(hidden_low, own_output, NT).astype(LOW)
        far_grad = other_core(dot(hidden_low, far_output, NT).astype(LOW))
        context_grad = jnp.where(
            core == 0,
            jnp.concatenate([near_grad, far_grad], axis=0),
            jnp.concatenate([far_grad, near_grad], axis=0),
        )
        near_output_part = dot(near_context, hidden_low, TN).astype(LOW)
        far_output_part = dot(far_context, hidden_low, TN).astype(LOW)

    if fast:
        layer_out, input_grad, heads_grad, units_grad, gains, sums = backward(
            length,
            query,
            key,
            value,
            context_grad,
            logs,
            near,
            normed_one,
            weights.reshape(-1, width),
            source_low,
            hidden_grad,
            attn_gain[None, :],
            ffn_gain_part.reshape(-1, LANES),
            output_part,
            layer_rows,
            up_part,
            down_part,
            up_came,
            down_came,
        )
        query_grad, key_grad, value_grad, output_grad = (heads_grad[number] for number in range(4))
        up_grad, down_grad = (units_grad[0], units_grad[1])
        input_grad = input_grad.astype(WIDE)
        attn_gain_grad, ffn_gain_grad = (gains[0], gains[1])
        sums = jnp.swapaxes(sums.reshape(2, 4, 2, 4 * LANES), 0, 1)
        bias_sum = bucket_sums(sums.reshape(HEADS, 4 * LANES))
    else:
        query_low, key_low, value_low, distance_sums = attend_grad(
            length, query, key, value, context_grad, logs, near
        )
        lows = (query_low, key_low, value_low)
        normed_one_grad = dot(query_low, own_three[0]) + dot(key_low, own_three[1]) + dot(value_low, own_three[2])
        normed_one_grad = fold(normed_one_grad, core)
        three_parts = [dot(one, normed_one, TN).astype(LOW) for one in lows]
        gained_one = attn_gain * normed_one_grad
        input_grad = hidden_grad + rms_one * (
            gained_one - scaled_one * jnp.mean(gained_one * scaled_one, axis=1, keepdims=True)
        )
        attn_gain_part = jnp.sum(normed_one_grad * scaled_one, axis=0)
        input_grad = to_slots(input_grad.astype(LOW), held).astype(WIDE)
        layer_out = to_slots(layer_rows, held)

        def summed(value):
            return lax.psum_scatter(value, BOTH, scatter_dimension=0, tiled=True).astype(WIDE)

        def own_only(value):
            blank = jnp.zeros_like(value)
            pair = jnp.where(core == 0, jnp.stack([value, blank], axis=1), jnp.stack([blank, value], axis=1))
            return summed(pair.reshape(-1, width))

        up_grad, down_grad = [own_only(one.reshape(depth * (size // 2), -1, width)) for one in (up_part, down_part)]
        query_grad, key_grad, value_grad = [own_only(one.reshape(4, -1, width)) for one in three_parts]
        near_part, far_part = (near_output_part.reshape(4, -1, width), far_output_part.reshape(4, -1, width))
        pair = jnp.where(
            core == 0, jnp.stack([near_part, far_part], axis=1), jnp.stack([far_part, near_part], axis=1)
        )
        output_grad = summed(pair.reshape(-1, width))
        bias_own = bucket_sums(distance_sums.reshape(HEADS // 2, 4 * LANES)).reshape(BUCKETS, 4, 1, 2)
        bias_full = lax.dynamic_update_slice(
            jnp.zeros((BUCKETS, 4, 2, 2), WIDE), bias_own, (0, 0, core, 0)
        ).reshape(BUCKETS, HEADS)
        attn_gain_sum, ffn_gain_sum, bias_sum = lax.psum((attn_gain_part, ffn_gain_part, bias_full), BOTH)

        gain_rows = width // size
        attn_gain_grad = lax.dynamic_slice_in_dim(attn_gain_sum, index * gain_rows, gain_rows, 0)
        ffn_gain_grad = lax.dynamic_slice_in_dim(ffn_gain_sum, index * gain_rows, gain_rows, 0)
    bucket_rows = BUCKETS // size
    bias_grad = lax.dynamic_slice_in_dim(bias_sum, index * bucket_rows, bucket_rows, 0)
    return (
        layer_out,
        input_grad,
        query_grad,
        key_grad,
        value_grad,
        output_grad,
        up_grad,
        down_grad,
        attn_gain_grad,
        ffn_gain_grad,
        bias_grad,
    )


def solution(mesh):
    placed = (
        P("fsdp", "seq", None),
        P("fsdp"),
        P("fsdp", "seq", None),
        P("fsdp", None),
        P("fsdp", None),
        P("fsdp", None),
        P("fsdp", None),
        P("fsdp", None),
        P("fsdp", None),
        P(),
        P(),
        P(),
    )
    return jax.shard_map(
        shards,
        mesh=mesh,
        in_specs=placed,
        out_specs=(
            P("fsdp", "seq", None),
            P("fsdp", "seq", None),
            P(("seq", "fsdp"), None),
            P(("seq", "fsdp"), None),
            P(("seq", "fsdp"), None),
            P(("seq", "fsdp"), None),
            P(("seq", "fsdp"), None),
            P(("seq", "fsdp"), None),
            P("fsdp"),
            P("fsdp"),
            P("fsdp", None),
        ),
        check_vma=False,
    )
```
